256 devices in a mesh: region: 32 (over x, z), rep: 8 (over y, core).
Axes of the slice: x: 4, y: 4, z: 8, core: 2. Of those that a mesh axis runs over, the one named last changes fastest.
Arguments:
- features: bfloat16 [8, 512, 2048], P('rep', None, 'region'), may hold values from -6 to 6
- weight_first: bfloat16 [27, 32, 64], replicated, may hold values from -0.3125 to 0.3125
- weight_second: bfloat16 [27, 64, 64], replicated, may hold values from -0.21875 to 0.21875
- cotangent: bfloat16 [8, 512, 4096], P('rep', None, 'region'), may hold values from -6 to 6
- neighbours: int32 [8, 64, 27], P('rep', 'region'), may hold values from 0 to 6, as said below
- voxel_mask: int32 [8, 64, 512], P('rep', 'region'), may hold values from 0 to 1, as said below
Outputs:
- block_out: bfloat16 [8, 512, 4096], P('rep', None, 'region')
- grad_first: float32 [27, 32, 64], replicated
- grad_second: float32 [27, 64, 64], replicated
The draws below stay inside these ranges and needn't reach their ends.
Inputs may be any that keep to these rules, and one draw needn't show every extreme that they name: `neighbours`: tiles of region r (slots r * 2 to (r + 1) * 2 - 1 of an event) lie in one plane of tiles along the first dimension, regions in order. A value n from 2 to 3 is a tile of the same region; below 2 a tile of the region before, only at offsets with a = -1; from 4 to 5 a tile of the region after, only at offsets with a = 1; no tile outside the regions is named. Offset 13 names the tile itself for every used slot; neighbour relations are symmetric; unused slots name no tile. Some region of each event uses all its slots. `voxel_mask`: unused tile slots have no active voxel.
All inputs are finite; a program needn't handle non-finite values.
Results may differ from the reference program's by a relative error of at most 0.0057.
Values may be sent and summed in bfloat16 or wider, within the bound.
A program may use at most 128 MiB of HBM per device.

```python
import math
import jax
import jax.numpy as jnp
from jax import lax

CH_IN = 32
CH = 64
TILES_DEV = 2
EVENTS = 8
TILES = 64


def tile_layout(key):
    regions = TILES // TILES_DEV
    cells = 4 * TILES_DEV
    key_order, key_live, key_full = jax.random.split(key, 3)
    scores = jax.random.randint(key_order, (EVENTS, regions, cells), 0, 2 ** 20) * cells + jnp.arange(cells)
    order = jnp.argsort(scores, axis=-1).astype(jnp.int32)
    ranking = jnp.argsort(order, axis=-1).astype(jnp.int32)
    live_count = jax.random.randint(key_live, (EVENTS, regions), max(1, TILES_DEV // 4), TILES_DEV + 1)
    full_region = jax.random.randint(key_full, (EVENTS,), 0, regions)
    live_count = jnp.where(jnp.arange(regions)[None, :] == full_region[:, None], TILES_DEV, live_count)
    slot_of_cell = jnp.where(ranking < live_count[:, :, None], ranking, -1)
    cell = order[:, :, :TILES_DEV]
    alive = jnp.arange(TILES_DEV)[None, None, :] < live_count[:, :, None]
    cell_row = cell // TILES_DEV
    cell_col = cell % TILES_DEV
    event_ids = jnp.arange(EVENTS)[:, None, None]
    region_ids = jnp.arange(regions)[None, :, None]
    columns = []
    for offset in range(27):
        shift_x, shift_y, shift_z = (offset // 9 - 1, offset // 3 % 3 - 1, offset % 3 - 1)
        near_region = region_ids + shift_x
        near_row = cell_row + shift_y
        near_col = cell_col + shift_z
        valid = alive & (near_region >= 0) & (near_region < regions)
        valid = valid & (near_row >= 0) & (near_row < 4) & (near_col >= 0) & (near_col < TILES_DEV)
        found = slot_of_cell[event_ids, jnp.clip(near_region, 0, regions - 1), jnp.clip(near_row, 0, 3) * TILES_DEV + jnp.clip(near_col, 0, TILES_DEV - 1)]
        columns.append(jnp.where(valid & (found >= 0), (shift_x + 1) * TILES_DEV + found, 3 * TILES_DEV))
    links = jnp.stack(columns, -1).reshape(EVENTS, TILES, 27).astype(jnp.int32)
    return (links, alive.reshape(EVENTS, TILES))


def draw_neighbours(key, part):
    links, alive = tile_layout(key)
    return links


def draw_voxel_mask(key, part):
    links, alive = tile_layout(key)
    key = jax.random.fold_in(key, 7)
    key_rate, key_voxel = jax.random.split(key)
    rate = jax.random.randint(key_rate, (EVENTS, TILES, 1), 10, 71)
    draws = jax.random.randint(key_voxel, (EVENTS, TILES, 512), 0, 100)
    return ((draws < rate) & alive[:, :, None]).astype(jnp.int32)


def level_of(stream_key, dims, cuts, low, largest):
    loudness = 1.0
    for axis_at, parts in cuts:
        steps = jax.random.uniform(jax.random.fold_in(jax.random.fold_in(stream_key, 6), axis_at), (parts,), jnp.float32, low / len(cuts), largest / len(cuts))
        loudness = loudness * jnp.repeat(jnp.exp(steps), dims[axis_at] // parts).reshape((-1,) + (1,) * (len(dims) - 1 - axis_at))
    return loudness


def bell_draw(own_key, shape, spread, limit, cuts=(), held_as=jnp.bfloat16):
    level = level_of(own_key, shape, cuts, -0.22, 0.18) if cuts else 1.0
    values = jax.random.normal(own_key, shape, jnp.float32) * spread * level
    return jnp.minimum(jnp.maximum(values, -limit), limit).astype(held_as)


def setup_inputs(seed: int = 0) -> dict:
    streams_of = jax.random.split(jax.random.key(seed), 7)
    features = bell_draw(streams_of[0], (EVENTS, 512, TILES * CH_IN), 1.0, 6.0, ((0, 8), (2, 32)))
    weight_first = bell_draw(streams_of[1], (27, CH_IN, CH), (12 * CH_IN) ** -0.5, 0.3125)
    weight_second = bell_draw(streams_of[2], (27, CH, CH), (12 * CH) ** -0.5, 0.21875)
    cotangent = bell_draw(streams_of[3], (EVENTS, 512, TILES * CH), 1.0, 6.0, ((0, 8), (2, 32)))
    neighbours = draw_neighbours(jax.random.fold_in(streams_of[6], 71), 0)
    voxel_mask = draw_voxel_mask(jax.random.fold_in(streams_of[6], 71), 0)
    return dict(features=features, weight_first=weight_first, weight_second=weight_second, cotangent=cotangent, neighbours=neighbours, voxel_mask=voxel_mask)


def spans(step):
    if step < 0:
        return (slice(7, 8), slice(0, 1))
    if step == 0:
        return (slice(0, 8), slice(1, 9))
    return (slice(0, 1), slice(9, 10))

def assemble(extended, links, tile_count, channels):
    padded = jnp.zeros((10, 10, 10, tile_count, channels), extended.dtype)
    for offset in range(27):
        src_x, dst_x = spans(offset // 9 - 1)
        src_y, dst_y = spans(offset // 3 % 3 - 1)
        src_z, dst_z = spans(offset % 3 - 1)
        chosen = jnp.take(extended[src_x, src_y, src_z], links[:, offset], axis=3)
        padded = padded.at[dst_x, dst_y, dst_z].set(chosen)
    return padded

def pad_event(columns, global_links, channels):
    cube = columns.reshape(8, 8, 8, TILES, channels)
    empty = jnp.zeros((8, 8, 8, 1, channels), columns.dtype)
    extended = jnp.concatenate([cube, empty], axis=3)
    return assemble(extended, global_links, TILES, channels)

def forward_conv(padded, weight):
    padded32 = padded.astype(jnp.float32)
    weight32 = weight.astype(jnp.float32)
    summed = jnp.zeros((8, 8, 8, padded.shape[3], weight.shape[2]), jnp.float32)
    for offset in range(27):
        shift_x, shift_y, shift_z = (offset // 9, offset // 3 % 3, offset % 3)
        window = padded32[shift_x:shift_x + 8, shift_y:shift_y + 8, shift_z:shift_z + 8]
        summed = summed + jnp.einsum('xyztc,co->xyzto', window, weight32[offset])
    return summed

def transpose_conv(padded, weight):
    padded32 = padded.astype(jnp.float32)
    weight32 = weight.astype(jnp.float32)
    summed = jnp.zeros((8, 8, 8, padded.shape[3], weight.shape[1]), jnp.float32)
    for offset in range(27):
        shift_x, shift_y, shift_z = (2 - offset // 9, 2 - offset // 3 % 3, 2 - offset % 3)
        window = padded32[shift_x:shift_x + 8, shift_y:shift_y + 8, shift_z:shift_z + 8]
        summed = summed + jnp.einsum('xyzto,co->xyztc', window, weight32[offset])
    return summed

def kernel_grad(padded, delta):
    padded32 = padded.astype(jnp.float32)
    delta32 = delta.astype(jnp.float32)
    grads = []
    for offset in range(27):
        shift_x, shift_y, shift_z = (offset // 9, offset // 3 % 3, offset % 3)
        window = padded32[shift_x:shift_x + 8, shift_y:shift_y + 8, shift_z:shift_z + 8]
        grads.append(jnp.einsum('xyztc,xyzto->co', window, delta32))
    return jnp.stack(grads)

def one_event(weight_first, weight_second, features_one, cotangent_one, links, mask_one):
    tile_ids = jnp.arange(TILES, dtype=jnp.int32)
    region = tile_ids // TILES_DEV
    target = (region[:, None] + links // TILES_DEV - 1) * TILES_DEV + links % TILES_DEV
    global_links = jnp.where(links == 3 * TILES_DEV, TILES, target).astype(jnp.int32)
    live = mask_one.T.astype(jnp.float32)[:, :, None]
    live_low = mask_one.T.astype(jnp.bfloat16)[:, :, None]
    masked = features_one.reshape(512, TILES, CH_IN) * live_low
    pad_first = pad_event(masked.reshape(512, TILES * CH_IN), global_links, CH_IN)
    pre_first = forward_conv(pad_first, weight_first).reshape(512, TILES, CH)
    sig_first = jax.nn.sigmoid(pre_first)
    hidden = (live * pre_first * sig_first).astype(jnp.bfloat16)
    pad_second = pad_event(hidden.reshape(512, TILES * CH), global_links, CH)
    pre_second = forward_conv(pad_second, weight_second).reshape(512, TILES, CH)
    sig_second = jax.nn.sigmoid(pre_second)
    block_out = (live * pre_second * sig_second).astype(jnp.bfloat16)
    upstream = cotangent_one.reshape(512, TILES, CH).astype(jnp.float32)
    delta_second = (upstream * live * sig_second * (1.0 + pre_second * (1.0 - sig_second))).astype(jnp.bfloat16)
    grad_second = kernel_grad(pad_second, delta_second.reshape(8, 8, 8, TILES, CH))
    pad_delta = pad_event(delta_second.reshape(512, TILES * CH), global_links, CH)
    back_hidden = transpose_conv(pad_delta, weight_second).reshape(512, TILES, CH)
    delta_first = (back_hidden * live * sig_first * (1.0 + pre_first * (1.0 - sig_first))).astype(jnp.bfloat16)
    grad_first = kernel_grad(pad_first, delta_first.reshape(8, 8, 8, TILES, CH))
    return (block_out.reshape(512, TILES * CH), grad_first, grad_second)

def reference(features, weight_first, weight_second, cotangent, neighbours, voxel_mask):

    def step(items):
        return one_event(weight_first, weight_second, items[0], items[1], items[2], items[3])
    block_out, grads_first, grads_second = lax.map(step, (features, cotangent, neighbours, voxel_mask))
    normaliser = 1.0 / math.sqrt(EVENTS * TILES * 512)
    grad_first = lax.optimization_barrier(jnp.sum(grads_first, axis=0)) * normaliser
    grad_second = lax.optimization_barrier(jnp.sum(grads_second, axis=0)) * normaliser
    return (block_out, grad_first, grad_second)
```

```python
import functools
import math

import jax
import jax.numpy as jnp
from jax import lax
from jax.experimental import pallas as pl
from jax.experimental.pallas import tpu as pltpu
from jax.sharding import PartitionSpec as P

MESH = pl.DeviceIdType.MESH
F32 = jnp.float32
BF16 = jnp.bfloat16
ROWS = (0, 80, 16)
ROWS_FIRST = (0, 80, 16, 144, 208)
PAIRS_SECOND = 16
PAIRS_FIRST = 8


def iota(shape, axis):
    return lax.broadcasted_iota(jnp.int32, shape, axis)


def dot(a, b):
    return jnp.dot(a, b, preferred_element_type=F32)


def kernel(
    sizes,
    scale,
    feat_ref,
    w1_ref,
    w2_ref,
    cot_ref,
    nbr_ref,
    mask_ref,
    out_ref,
    g1_ref,
    g2_ref,
    live_ref,
    field_ref,
    face_ref,
    halo_ref,
    side_ref,
    far_ref,
    c1_ref,
    c2_ref,
    c3_ref,
    w1b_ref,
    w2b_ref,
    w2t_ref,
    acc_ref,
    slope_ref,
    full1_ref,
    full2_ref,
    send1_ref,
    send2_ref,
    pair1_ref,
    pair2_ref,
    half1_ref,
    half2_ref,
    mine1_ref,
    mine2_ref,
    plane1_ref,
    plane2_ref,
    line1_ref,
    line2_ref,
    fin1_ref,
    fin2_ref,
    halo_send,
    halo_recv,
    pair_send,
    pair_recv,
    plane_send,
    plane_recv,
    line_send,
    line_recv,
    back_send,
    back_recv,
    twin_send,
    twin_recv,
):
    nx, nz, ny = sizes
    n_region = nx * nz
    n_plane = nx * ny
    region = lax.axis_index("region")
    rep = lax.axis_index("rep")
    my_x = region // nz
    my_z = lax.rem(region, nz)
    my_y = rep // 2
    core = lax.rem(rep, 2)
    member = my_x * ny + my_y
    right = lax.rem(region + 1, n_region)
    left = lax.rem(region + n_region - 1, n_region)

    def plane_peer(step):
        other = lax.rem(member + step, n_plane)
        return other, {"region": (other // ny) * nz + my_z, "rep": lax.rem(other, ny) * 2 + core}

    def line_peer(step):
        other = lax.rem(my_z + step, nz)
        return other, {"region": my_x * nz + other, "rep": rep}

    twin = {"region": region, "rep": my_y * 2 + 1 - core}

    barrier = pltpu.get_barrier_semaphore()
    pl.semaphore_signal(barrier, inc=1, device_id={"region": right, "rep": rep}, device_id_type=MESH)
    pl.semaphore_signal(barrier, inc=1, device_id={"region": left, "rep": rep}, device_id_type=MESH)
    pl.semaphore_signal(barrier, inc=1, device_id=twin, device_id_type=MESH)

    @pl.loop(1, n_plane)
    def _(step):
        pl.semaphore_signal(barrier, inc=1, device_id=plane_peer(step)[1], device_id_type=MESH)

    @pl.loop(1, nz)
    def _(step):
        pl.semaphore_signal(barrier, inc=1, device_id=line_peer(step)[1], device_id_type=MESH)

    mask = jnp.concatenate([mask_ref[...].astype(F32), jnp.zeros((6, 512), F32)], axis=0).T
    tile_of = (iota((8, 128), 1) // 64 == iota((8, 128), 0)).astype(F32)
    tile_of_first = (lax.rem(iota((8, 128), 1) // 32, 2) == iota((8, 128), 0)).astype(F32)
    live_ref[...] = dot(mask, tile_of).reshape(8, 64, 128)
    twice = (iota((64, 128), 0) == lax.rem(iota((64, 128), 1), 64)).astype(BF16)
    spread = dot(feat_ref[...], twice) * dot(mask, tile_of_first)
    field_ref[...] = spread.reshape(8, 64, 128)
    face_ref[...] = spread.astype(BF16).reshape(8, 64, 128)

    def halo_copies(which):
        return [
            pltpu.make_async_remote_copy(
                src_ref=face_ref.at[x],
                dst_ref=halo_ref.at[which, side],
                send_sem=halo_send.at[which, side],
                recv_sem=halo_recv.at[which, side],
                device_id={"region": to, "rep": rep},
                device_id_type=MESH,
            )
            for side, x, to in ((0, 7, right), (1, 0, left))
        ]

    pl.semaphore_wait(barrier, 3 + n_plane - 1 + nz - 1)
    halo = halo_copies(0)
    for copy in halo:
        copy.start()

    eye = iota((64, 256), 0)
    put = ((eye == iota((64, 256), 1)) | (eye == iota((64, 256), 1) - 192)).astype(BF16)
    spread1 = dot(w1_ref[...].reshape(27 * 32, 64), put).astype(BF16)
    top = spread1[:, :128].reshape(3, 3, 3, 32, 128)
    low = spread1[:, 128:].reshape(3, 3, 3, 32, 128)
    for b in range(3):
        for at, c in ((0, 0), (64, 2)):
            w1b_ref[:, b, at : at + 32, :] = top[:, b, c]
            w1b_ref[:, b, at + 32 : at + 64, :] = low[:, b, c]
    for at, b in ((0, 0), (64, 2)):
        w1b_ref[:, 3, at : at + 32, :] = top[:, b, 1]
        w1b_ref[:, 3, at + 32 : at + 64, :] = low[:, b, 1]
    w1b_ref[:, 4, 0:32, :] = top[:, 1, 1]
    w1b_ref[:, 4, 32:64, :] = low[:, 1, 1]
    w1b_ref[:, 4, 64:128, :] = jnp.zeros((3, 64, 128), BF16)
    spread2 = dot(w2_ref[...].reshape(27 * 64, 64), put).astype(BF16)
    w2b_ref[:, 0:64, :] = spread2[:, :128].reshape(27, 64, 128)
    w2b_ref[:, 64:128, :] = spread2[:, 128:].reshape(27, 64, 128)

    @pl.loop(0, 27)
    def _(k):
        w2t_ref[26 - k] = w2b_ref[k].T

    side_ref[2] = jnp.zeros((8, 64, 128), F32)
    far_ref[:, 2] = jnp.zeros((2, 64, 128), F32)
    lane = iota((8, 128), 1)
    first_half = lane < 64
    even_quarter = lax.rem(lane // 32, 2) == 0
    z_row = iota((8, 128), 0)
    z_first, z_last = z_row == 0, z_row == 7

    def rows_of(masked, count):
        return jnp.concatenate([masked] * count, axis=0) if count > 1 else masked

    def split_first():
        source, target = iota((128, 256), 0), iota((128, 256), 1)
        return (source == (target // 128) * 32 + lax.rem(target, 32)).astype(BF16)

    def split_second():
        source, target = iota((128, 256), 0), iota((128, 256), 1)
        return (source == (target // 128) * 64 + lax.rem(target, 64)).astype(BF16)

    def shifted(middle, load, tile_lane):
        ext = []
        for c in range(3):
            groups = [load(0, c, 56, 64)]
            if c == 1 and middle is not None:
                mid = middle
            else:
                mid = load(1, c, 0, 64)
            groups += [mid[8 * y : 8 * y + 8] for y in range(8)]
            groups.append(load(2, c, 0, 8))
            ext.append(groups)
        down = [pltpu.roll(jnp.where(z_last, ext[0][y], ext[1][y]), 1, 0) for y in range(10)]
        up = [pltpu.roll(jnp.where(z_first, ext[2][y], ext[1][y]), 7, 0) for y in range(10)]
        return down, ext[1], up

    def store_first(c_ref, slab, down, mid, up):
        both = [jnp.where(first_half, d, u) for d, u in zip(down, up)]
        c_ref[slab, 0:80, :] = jnp.concatenate(both, axis=0).astype(BF16)
        c_ref[slab, 80:144, :] = jnp.concatenate(both[1:9], axis=0).astype(BF16)
        ends = [jnp.where(first_half, mid[y], mid[y + 2]) for y in range(8)]
        c_ref[slab, 144:208, :] = jnp.concatenate(ends, axis=0).astype(BF16)
        c_ref[slab, 208:272, :] = jnp.concatenate(mid[1:9], axis=0).astype(BF16)

    def store_second(c_ref, slab, down, mid, up):
        for c, groups in enumerate((down, mid, up)):
            c_ref[c, slab, 0:80, :] = jnp.concatenate(groups, axis=0).astype(BF16)
            c_ref[c, slab, 80:144, :] = jnp.concatenate(groups[1:9], axis=0).astype(BF16)

    def build_inner(c_ref, store, splitter, tile_lane):
        whole = dot(face_ref[...].reshape(512, 128), splitter)
        side_ref[0] = whole[:, :128].reshape(8, 64, 128)
        side_ref[1] = whole[:, 128:].reshape(8, 64, 128)
        named = [
            [jnp.minimum(jnp.maximum(nbr_ref[t, 9 + k] - 2, 0), 2) for k in range(9)]
            for t in range(2)
        ]

        @pl.loop(0, 8)
        def _(x):
            def load(b, c, start, stop):
                k = 3 * b + c
                return jnp.where(
                    rows_of(tile_lane, (stop - start) // 8),
                    side_ref[named[0][k], x, start:stop, :],
                    side_ref[named[1][k], x, start:stop, :],
                )

            store(c_ref, x + 1, *shifted(field_ref[x], load, tile_lane))

    def build_faces(which, c_ref, store, splitter, tile_lane):
        for side in range(2):
            whole = dot(halo_ref[which, side], splitter)
            far_ref[side, 0] = whole[:, :128]
            far_ref[side, 1] = whole[:, 128:]
            named = [
                [
                    jnp.minimum(jnp.maximum(nbr_ref[t, 18 * side + k] - 4 * side, 0), 2)
                    for k in range(9)
                ]
                for t in range(2)
            ]

            def load(b, c, start, stop):
                k = 3 * b + c
                return jnp.where(
                    rows_of(tile_lane, (stop - start) // 8),
                    far_ref[side, named[0][k], start:stop, :],
                    far_ref[side, named[1][k], start:stop, :],
                )

            store(c_ref, 9 * side, *shifted(None, load, tile_lane))

    def windows_first(start, count):
        return [
            c1_ref[start : start + count, r : r + 64, :].reshape(count * 64, 128)
            for r in ROWS_FIRST
        ]

    def windows_second(c_ref, start, count):
        return [
            c_ref[c, start : start + count, ROWS[b] : ROWS[b] + 64, :].reshape(count * 64, 128)
            for b in range(3)
            for c in range(3)
        ]

    def conv_inner(windows, weight):
        acc_ref[...] = dot(jnp.concatenate(windows(1, 8), axis=1), weight(1))
        acc_ref[64:512] += dot(jnp.concatenate(windows(1, 7), axis=1), weight(0))
        acc_ref[0:448] += dot(jnp.concatenate(windows(2, 7), axis=1), weight(2))

    def conv_faces(windows, weight):
        acc_ref[0:64] += dot(jnp.concatenate(windows(0, 1), axis=1), weight(0))
        acc_ref[448:512] += dot(jnp.concatenate(windows(9, 1), axis=1), weight(2))

    def weight_first(a):
        return w1b_ref[a].reshape(5 * 128, 128)

    def weight_second(a):
        return w2b_ref[9 * a : 9 * a + 9].reshape(9 * 128, 128)

    def weight_back(a):
        return w2t_ref[9 * a : 9 * a + 9].reshape(9 * 128, 128)

    build_inner(c1_ref, store_first, split_first(), even_quarter)
    conv_inner(windows_first, weight_first)
    for copy in halo:
        copy.wait()
    build_faces(0, c1_ref, store_first, split_first(), even_quarter)
    conv_faces(windows_first, weight_first)

    @pl.loop(0, 8)
    def _(x):
        rows = pl.ds(pl.multiple_of(x * 64, 64), 64)
        pre = acc_ref[rows, :]
        live = live_ref[x]
        sig = jax.nn.sigmoid(pre)
        hidden = (live * pre * sig).astype(BF16)
        face_ref[x] = hidden
        field_ref[x] = hidden.astype(F32)
        slope_ref[x] = live * sig * (1.0 + pre * (1.0 - sig))

    halo = halo_copies(1)
    for copy in halo:
        copy.start()

    second = functools.partial(windows_second, c2_ref)
    build_inner(c2_ref, store_second, split_second(), first_half)
    conv_inner(second, weight_second)
    for copy in halo:
        copy.wait()
    build_faces(1, c2_ref, store_second, split_second(), first_half)
    conv_faces(second, weight_second)

    @pl.loop(0, 8)
    def _(x):
        rows = pl.ds(pl.multiple_of(x * 64, 64), 64)
        pre = acc_ref[rows, :]
        live = live_ref[x]
        sig = jax.nn.sigmoid(pre)
        out_ref[rows, :] = (live * pre * sig).astype(BF16)
        upstream = cot_ref[rows, :].astype(F32)
        delta = (upstream * live * sig * (1.0 + pre * (1.0 - sig))).astype(BF16)
        face_ref[x] = delta
        field_ref[x] = delta.astype(F32)

    halo = halo_copies(2)
    for copy in halo:
        copy.start()

    wide_half = iota((64, 128), 1) < 64
    wide_quarter = lax.rem(iota((64, 128), 1) // 32, 2) == 0
    per_core1, per_core2 = PAIRS_FIRST // 2, PAIRS_SECOND // 2

    def put_gradient(full, send, per_core, pair, value):
        value = value.reshape(4, 16, 128)
        units = pl.ds((pair % per_core) * 4, 4)
        full[pair // per_core, units] = value
        send[pair // per_core, units] = value.astype(BF16)

    delta_t = face_ref[...].reshape(512, 128).T
    for pair in range(14):
        both = []
        for k in (2 * pair, min(2 * pair + 1, 26)):
            a, b, c = k // 9, k // 3 % 3, k % 3
            window = c2_ref[c, a : a + 8, ROWS[b] : ROWS[b] + 64, :]
            both.append(window.reshape(512, 128))
        got = dot(delta_t, jnp.concatenate(both, axis=1))
        one, two = got[:, :128], got[:, 128:]
        straight = jnp.where(wide_half, one[0:64], two[64:128])
        crossed = jnp.where(wide_half, two[0:64], one[64:128])
        put_gradient(full2_ref, send2_ref, per_core2, pair, straight + pltpu.roll(crossed, 64, 1))
    for pair in range(14, PAIRS_SECOND):
        put_gradient(full2_ref, send2_ref, per_core2, pair, jnp.zeros((64, 128), F32))

    unit1, unit2 = 4 * per_core1 // n_plane, 4 * per_core2 // n_plane

    def reducer(which, unit, full, send, pair, half, mine, plane, line, fin):
        def pair_copy():
            return pltpu.make_async_remote_copy(
                src_ref=send.at[1 - core],
                dst_ref=pair,
                send_sem=pair_send.at[which],
                recv_sem=pair_recv.at[which],
                device_id=twin,
                device_id_type=MESH,
            )

        def plane_copy(step):
            other, device = plane_peer(step)
            return pltpu.make_async_remote_copy(
                src_ref=half.at[pl.ds(other * unit, unit)],
                dst_ref=plane.at[step],
                send_sem=plane_send.at[which, step],
                recv_sem=plane_recv.at[which, step],
                device_id=device,
                device_id_type=MESH,
            )

        def line_copy(step):
            _, device = line_peer(step)
            return pltpu.make_async_remote_copy(
                src_ref=line.at[my_z],
                dst_ref=line.at[my_z],
                send_sem=line_send.at[which, step],
                recv_sem=line_recv.at[which, step],
                device_id=device,
                device_id_type=MESH,
            )

        def back_copy(step):
            _, device = plane_peer(step)
            place = fin.at[core, pl.ds(member * unit, unit)]
            return pltpu.make_async_remote_copy(
                src_ref=place,
                dst_ref=place,
                send_sem=back_send.at[which, step],
                recv_sem=back_recv.at[which, step],
                device_id=device,
                device_id_type=MESH,
            )

        def twin_copy():
            return pltpu.make_async_remote_copy(
                src_ref=fin.at[core],
                dst_ref=fin.at[core],
                send_sem=twin_send.at[which],
                recv_sem=twin_recv.at[which],
                device_id=twin,
                device_id_type=MESH,
            )

        def start_pair():
            pair_copy().start()

        def start_plane():
            pair_copy().wait()
            total = full[core] + pair[...].astype(F32)
            half[...] = total.astype(BF16)
            mine[...] = total

            @pl.loop(1, n_plane)
            def _(step):
                plane_copy(step).start()

        def start_line():
            @pl.loop(1, n_plane)
            def _(step):
                plane_copy(step).wait()

            total = mine[pl.ds(member * unit, unit)]
            for step in range(1, n_plane):
                total = total + plane[step].astype(F32)
            line[my_z] = total.astype(BF16)

            @pl.loop(1, nz)
            def _(step):
                line_copy(step).start()

        def start_back():
            @pl.loop(1, nz)
            def _(step):
                line_copy(step).wait()

            total = line[0].astype(F32)
            for z in range(1, nz):
                total = total + line[z].astype(F32)
            fin[core, pl.ds(member * unit, unit)] = (total * scale).astype(BF16)

            @pl.loop(1, n_plane)
            def _(step):
                back_copy(step).start()

        def start_twin():
            @pl.loop(1, n_plane)
            def _(step):
                back_copy(step).wait()

            twin_copy().start()

        def finish():
            twin_copy().wait()

        return start_pair, start_plane, start_line, start_back, start_twin, finish

    sum1 = reducer(
        0, unit1, full1_ref, send1_ref, pair1_ref, half1_ref, mine1_ref, plane1_ref, line1_ref, fin1_ref
    )
    sum2 = reducer(
        1, unit2, full2_ref, send2_ref, pair2_ref, half2_ref, mine2_ref, plane2_ref, line2_ref, fin2_ref
    )

    sum2[0]()

    third = functools.partial(windows_second, c3_ref)
    build_inner(c3_ref, store_second, split_second(), first_half)
    sum2[1]()
    conv_inner(third, weight_back)
    for copy in halo:
        copy.wait()
    build_faces(2, c3_ref, store_second, split_second(), first_half)
    conv_faces(third, weight_back)
    sum2[2]()
    delta_t = (acc_ref[...] * slope_ref[...].reshape(512, 128)).astype(BF16).T
    for pair in range(PAIRS_FIRST):
        both = []
        for block in (2 * pair, min(2 * pair + 1, 14)):
            a, r = block // 5, ROWS_FIRST[block % 5]
            both.append(c1_ref[a : a + 8, r : r + 64, :].reshape(512, 128))
        got = dot(delta_t, jnp.concatenate(both, axis=1))
        one, two = got[:, :128], got[:, 128:]
        straight = jnp.where(wide_quarter, one[0:64], two[64:128])
        crossed = jnp.where(wide_quarter, two[0:64], one[64:128])
        swapped = jnp.where(wide_quarter, pltpu.roll(crossed, 96, 1), pltpu.roll(crossed, 32, 1))
        put_gradient(full1_ref, send1_ref, per_core1, pair, straight + swapped)
    sum1[0]()
    sum2[3]()
    sum1[1]()
    sum2[4]()
    sum1[2]()
    sum2[5]()
    sum1[3]()
    for pair in range(14):
        units = pl.ds((pair % per_core2) * 4, 4)
        value = fin2_ref[pair // per_core2, units].reshape(64, 128).astype(F32).T
        g2_ref[2 * pair] = value[0:64]
        if pair < 13:
            g2_ref[2 * pair + 1] = value[64:128]
    sum1[4]()
    sum1[5]()
    for pair in range(PAIRS_FIRST):
        units = pl.ds((pair % per_core1) * 4, 4)
        value = fin1_ref[pair // per_core1, units].reshape(64, 128).astype(F32).T
        for j in range(2):
            block = 2 * pair + j
            if block > 14:
                continue
            a, kind = block // 5, block % 5
            if kind < 3:
                offsets = (9 * a + 3 * kind, 9 * a + 3 * kind + 2)
            elif kind == 3:
                offsets = (9 * a + 1, 9 * a + 7)
            else:
                offsets = (9 * a + 4,)
            for i, k in enumerate(offsets):
                g1_ref[k] = value[64 * i + 32 * j : 64 * i + 32 * j + 32]


def solution(mesh):
    n_region, n_rep = mesh.shape["region"], mesh.shape["rep"]
    nx, ny = (4, 4) if n_region == 32 else (2, n_rep // 2)
    nz = n_region // nx
    n_plane = nx * ny
    core1, core2 = 2 * PAIRS_FIRST, 2 * PAIRS_SECOND
    unit1, unit2 = core1 // n_plane, core2 // n_plane
    vmem = pl.BlockSpec(memory_space=pltpu.VMEM)
    smem = pl.BlockSpec(memory_space=pltpu.SMEM)

    def body(features, weight_first, weight_second, cotangent, neighbours, voxel_mask):
        scale = 1.0 / math.sqrt(n_rep * 2 * n_region * 512)
        out, g1, g2 = pl.pallas_call(
            functools.partial(kernel, (nx, nz, ny), scale),
            out_shape=(
                jax.ShapeDtypeStruct((512, 128), BF16),
                jax.ShapeDtypeStruct((27, 32, 64), F32),
                jax.ShapeDtypeStruct((27, 64, 64), F32),
            ),
            in_specs=[vmem, vmem, vmem, vmem, smem, vmem],
            out_specs=(vmem, vmem, vmem),
            scratch_shapes=[
                pltpu.VMEM((8, 64, 128), F32),
                pltpu.VMEM((8, 64, 128), F32),
                pltpu.VMEM((8, 64, 128), BF16),
                pltpu.VMEM((3, 2, 64, 128), BF16),
                pltpu.VMEM((3, 8, 64, 128), F32),
                pltpu.VMEM((2, 3, 64, 128), F32),
                pltpu.VMEM((10, 272, 128), BF16),
                pltpu.VMEM((3, 10, 144, 128), BF16),
                pltpu.VMEM((3, 10, 144, 128), BF16),
                pltpu.VMEM((3, 5, 128, 128), BF16),
                pltpu.VMEM((27, 128, 128), BF16),
                pltpu.VMEM((27, 128, 128), BF16),
                pltpu.VMEM((512, 128), F32),
                pltpu.VMEM((8, 64, 128), F32),
                pltpu.VMEM((2, core1, 16, 128), F32),
                pltpu.VMEM((2, core2, 16, 128), F32),
                pltpu.VMEM((2, core1, 16, 128), BF16),
                pltpu.VMEM((2, core2, 16, 128), BF16),
                pltpu.VMEM((core1, 16, 128), BF16),
                pltpu.VMEM((core2, 16, 128), BF16),
                pltpu.VMEM((core1, 16, 128), BF16),
                pltpu.VMEM((core2, 16, 128), BF16),
                pltpu.VMEM((core1, 16, 128), F32),
                pltpu.VMEM((core2, 16, 128), F32),
                pltpu.VMEM((n_plane, unit1, 16, 128), BF16),
                pltpu.VMEM((n_plane, unit2, 16, 128), BF16),
                pltpu.VMEM((nz, unit1, 16, 128), BF16),
                pltpu.VMEM((nz, unit2, 16, 128), BF16),
                pltpu.VMEM((2, core1, 16, 128), BF16),
                pltpu.VMEM((2, core2, 16, 128), BF16),
                pltpu.SemaphoreType.DMA((3, 2)),
                pltpu.SemaphoreType.DMA((3, 2)),
                pltpu.SemaphoreType.DMA((2,)),
                pltpu.SemaphoreType.DMA((2,)),
                pltpu.SemaphoreType.DMA((2, n_plane)),
                pltpu.SemaphoreType.DMA((2, n_plane)),
                pltpu.SemaphoreType.DMA((2, nz)),
                pltpu.SemaphoreType.DMA((2, nz)),
                pltpu.SemaphoreType.DMA((2, n_plane)),
                pltpu.SemaphoreType.DMA((2, n_plane)),
                pltpu.SemaphoreType.DMA((2,)),
                pltpu.SemaphoreType.DMA((2,)),
            ],
            compiler_params=pltpu.CompilerParams(
                collective_id=0, has_side_effects=True, vmem_limit_bytes=40 * 2**20
            ),
        )(
            features.reshape(512, 64),
            weight_first,
            weight_second,
            cotangent.reshape(512, 128),
            neighbours.reshape(2, 27),
            voxel_mask.reshape(2, 512),
        )
        return out.reshape(1, 512, 128), g1, g2

    in_specs = (
        P("rep", None, "region"),
        P(),
        P(),
        P("rep", None, "region"),
        P("rep", "region", None),
        P("rep", "region", None),
    )
    out_specs = (P("rep", None, "region"), P(), P())
    return jax.shard_map(body, mesh=mesh, in_specs=in_specs, out_specs=out_specs, check_vma=False)
```

```python
import functools
import math

import jax
import jax.numpy as jnp
from jax import lax
from jax.experimental import pallas as pl
from jax.experimental.pallas import tpu as pltpu
from jax.sharding import PartitionSpec as P

MESH = pl.DeviceIdType.MESH
F32 = jnp.float32
BF16 = jnp.bfloat16
ROWS = (0, 80, 16)
ROWS_FIRST = (0, 80, 16, 144, 208)
PAIRS_SECOND = 16
PAIRS_FIRST = 8
HALF = (PAIRS_SECOND + PAIRS_FIRST) // 2


def iota(shape, axis):
    return lax.broadcasted_iota(jnp.int32, shape, axis)


def dot(a, b):
    return jnp.dot(a, b, preferred_element_type=F32)


def dot_nt(a, b):
    return lax.dot_general(a, b, (((1,), (1,)), ((), ())), preferred_element_type=F32)


def places(sizes):
    nx, nz, ny = sizes
    region = lax.axis_index("region")
    rep = lax.axis_index("rep")
    return region // nz, lax.rem(region, nz), rep // 2, lax.rem(rep, 2), region, rep


def compute_kernel(
    sizes,
    feat_hbm,
    w1_hbm,
    w2_hbm,
    cot_hbm,
    nbr_ref,
    mask_hbm,
    out_ref,
    grad_ref,
    feat_ref,
    w1_ref,
    w2_ref,
    cot_ref,
    mask_ref,
    live_ref,
    field_ref,
    face_ref,
    halo_ref,
    side_ref,
    far_ref,
    c1_ref,
    c2_ref,
    c3_ref,
    w1b_ref,
    w2b_ref,
    acc_ref,
    slope_ref,
    load_sem,
    halo_send,
    halo_recv,
):
    n_region = sizes[0] * sizes[1]
    region, rep = places(sizes)[4:]
    right = lax.rem(region + 1, n_region)
    left = lax.rem(region + n_region - 1, n_region)

    barrier = pltpu.get_barrier_semaphore()
    for to in (right, left):
        pl.semaphore_signal(barrier, inc=1, device_id={"region": to, "rep": rep}, device_id_type=MESH)
    loads = [
        pltpu.make_async_copy(src, dst, load_sem.at[i])
        for i, (src, dst) in enumerate(
            (
                (mask_hbm, mask_ref),
                (feat_hbm, feat_ref),
                (w1_hbm, w1_ref),
                (w2_hbm, w2_ref),
                (cot_hbm, cot_ref),
            )
        )
    ]
    for load in loads:
        load.start()
    loads[0].wait()
    loads[1].wait()

    mask = jnp.concatenate([mask_ref[...].astype(F32), jnp.zeros((6, 512), F32)], axis=0).T
    tile_of = (iota((8, 128), 1) // 64 == iota((8, 128), 0)).astype(F32)
    tile_of_first = (lax.rem(iota((8, 128), 1) // 32, 2) == iota((8, 128), 0)).astype(F32)
    live_ref[...] = dot(mask, tile_of).reshape(8, 64, 128)
    twice = (iota((64, 128), 0) == lax.rem(iota((64, 128), 1), 64)).astype(BF16)
    spread = dot(feat_ref[...].T, twice) * dot(mask, tile_of_first)
    field_ref[...] = spread.reshape(8, 64, 128)
    face_ref[...] = spread.astype(BF16).reshape(8, 64, 128)

    def halo_copies(which):
        return [
            pltpu.make_async_remote_copy(
                src_ref=face_ref.at[x],
                dst_ref=halo_ref.at[which, side],
                send_sem=halo_send.at[which, side],
                recv_sem=halo_recv.at[which, side],
                device_id={"region": to, "rep": rep},
                device_id_type=MESH,
            )
            for side, x, to in ((0, 7, right), (1, 0, left))
        ]

    pl.semaphore_wait(barrier, 2)
    halo = halo_copies(0)
    for copy in halo:
        copy.start()

    loads[2].wait()
    eye = iota((64, 256), 0)
    put = ((eye == iota((64, 256), 1)) | (eye == iota((64, 256), 1) - 192)).astype(BF16)
    spread1 = dot(w1_ref[...].reshape(27 * 32, 64), put).astype(BF16)
    top = spread1[:, :128].reshape(3, 3, 3, 32, 128)
    low = spread1[:, 128:].reshape(3, 3, 3, 32, 128)
    for b in range(3):
        for at, c in ((0, 0), (64, 2)):
            w1b_ref[:, b, at : at + 32, :] = top[:, b, c]
            w1b_ref[:, b, at + 32 : at + 64, :] = low[:, b, c]
    for at, b in ((0, 0), (64, 2)):
        w1b_ref[:, 3, at : at + 32, :] = top[:, b, 1]
        w1b_ref[:, 3, at + 32 : at + 64, :] = low[:, b, 1]
    w1b_ref[:, 4, 0:32, :] = top[:, 1, 1]
    w1b_ref[:, 4, 32:64, :] = low[:, 1, 1]
    w1b_ref[:, 4, 64:128, :] = jnp.zeros((3, 64, 128), BF16)
    loads[3].wait()
    spread2 = dot(w2_ref[...].reshape(27 * 64, 64), put).astype(BF16)
    w2b_ref[:, 0:64, :] = spread2[:, :128].reshape(27, 64, 128)
    w2b_ref[:, 64:128, :] = spread2[:, 128:].reshape(27, 64, 128)

    side_ref[2] = jnp.zeros((8, 64, 128), F32)
    far_ref[:, 2] = jnp.zeros((2, 64, 128), F32)
    lane = iota((8, 128), 1)
    first_half = lane < 64
    even_quarter = lax.rem(lane // 32, 2) == 0
    z_row = iota((8, 128), 0)
    z_first, z_last = z_row == 0, z_row == 7

    def rows_of(masked, count):
        return jnp.concatenate([masked] * count, axis=0) if count > 1 else masked

    def split_first():
        source, target = iota((128, 256), 0), iota((128, 256), 1)
        return (source == (target // 128) * 32 + lax.rem(target, 32)).astype(BF16)

    def split_second():
        source, target = iota((128, 256), 0), iota((128, 256), 1)
        return (source == (target // 128) * 64 + lax.rem(target, 64)).astype(BF16)

    def shifted(middle, load, tile_lane):
        ext = []
        for c in range(3):
            groups = [load(0, c, 56, 64)]
            if c == 1 and middle is not None:
                mid = middle
            else:
                mid = load(1, c, 0, 64)
            groups += [mid[8 * y : 8 * y + 8] for y in range(8)]
            groups.append(load(2, c, 0, 8))
            ext.append(groups)
        down = [pltpu.roll(jnp.where(z_last, ext[0][y], ext[1][y]), 1, 0) for y in range(10)]
        up = [pltpu.roll(jnp.where(z_first, ext[2][y], ext[1][y]), 7, 0) for y in range(10)]
        return down, ext[1], up

    def store_first(c_ref, slab, down, mid, up):
        both = [jnp.where(first_half, d, u) for d, u in zip(down, up)]
        c_ref[slab, 0:80, :] = jnp.concatenate(both, axis=0).astype(BF16)
        c_ref[slab, 80:144, :] = jnp.concatenate(both[1:9], axis=0).astype(BF16)
        ends = [jnp.where(first_half, mid[y], mid[y + 2]) for y in range(8)]
        c_ref[slab, 144:208, :] = jnp.concatenate(ends, axis=0).astype(BF16)
        c_ref[slab, 208:272, :] = jnp.concatenate(mid[1:9], axis=0).astype(BF16)

    def store_second(c_ref, slab, down, mid, up):
        for c, groups in enumerate((down, mid, up)):
            c_ref[c, slab, 0:80, :] = jnp.concatenate(groups, axis=0).astype(BF16)
            c_ref[c, slab, 80:144, :] = jnp.concatenate(groups[1:9], axis=0).astype(BF16)

    def build_inner(c_ref, store, splitter, tile_lane):
        whole = dot(face_ref[...].reshape(512, 128), splitter)
        side_ref[0] = whole[:, :128].reshape(8, 64, 128)
        side_ref[1] = whole[:, 128:].reshape(8, 64, 128)
        named = [
            [jnp.minimum(jnp.maximum(nbr_ref[t, 9 + k] - 2, 0), 2) for k in range(9)]
            for t in range(2)
        ]

        @pl.loop(0, 8)
        def _(x):
            def load(b, c, start, stop):
                k = 3 * b + c
                return jnp.where(
                    rows_of(tile_lane, (stop - start) // 8),
                    side_ref[named[0][k], x, start:stop, :],
                    side_ref[named[1][k], x, start:stop, :],
                )

            store(c_ref, x + 1, *shifted(field_ref[x], load, tile_lane))

    def build_faces(which, c_ref, store, splitter, tile_lane):
        for side in range(2):
            whole = dot(halo_ref[which, side], splitter)
            far_ref[side, 0] = whole[:, :128]
            far_ref[side, 1] = whole[:, 128:]
            named = [
                [
                    jnp.minimum(jnp.maximum(nbr_ref[t, 18 * side + k] - 4 * side, 0), 2)
                    for k in range(9)
                ]
                for t in range(2)
            ]

            def load(b, c, start, stop):
                k = 3 * b + c
                return jnp.where(
                    rows_of(tile_lane, (stop - start) // 8),
                    far_ref[side, named[0][k], start:stop, :],
                    far_ref[side, named[1][k], start:stop, :],
                )

            store(c_ref, 9 * side, *shifted(None, load, tile_lane))

    def windows_first(start, count):
        return [
            c1_ref[start : start + count, r : r + 64, :].reshape(count * 64, 128)
            for r in ROWS_FIRST
        ]

    def windows_second(c_ref, start, count):
        return [
            c_ref[c, start : start + count, ROWS[b] : ROWS[b] + 64, :].reshape(count * 64, 128)
            for b in range(3)
            for c in range(3)
        ]

    def conv_inner(windows, weight, product=dot):
        acc_ref[...] = product(jnp.concatenate(windows(1, 8), axis=1), weight(1))
        acc_ref[64:512] += product(jnp.concatenate(windows(1, 7), axis=1), weight(0))
        acc_ref[0:448] += product(jnp.concatenate(windows(2, 7), axis=1), weight(2))

    def conv_faces(windows, weight, product=dot):
        acc_ref[0:64] += product(jnp.concatenate(windows(0, 1), axis=1), weight(0))
        acc_ref[448:512] += product(jnp.concatenate(windows(9, 1), axis=1), weight(2))

    def weight_first(a):
        return w1b_ref[a].reshape(5 * 128, 128)

    def weight_second(a):
        return w2b_ref[9 * a : 9 * a + 9].reshape(9 * 128, 128)

    def weight_back(a):
        return jnp.concatenate([w2b_ref[26 - k] for k in range(9 * a, 9 * a + 9)], axis=1)

    def layer(which, c_ref, store, splitter, tile_lane, windows, weight, product, activate, halo):
        build_inner(c_ref, store, splitter, tile_lane)
        conv_inner(windows, weight, product)
        pl.loop(1, 7)(activate)
        for copy in halo:
            copy.wait()
        build_faces(which, c_ref, store, splitter, tile_lane)
        conv_faces(windows, weight, product)
        pl.loop(0, 2)(lambda i: activate(7 * i))

    def hidden_of(x):
        rows = pl.ds(pl.multiple_of(x * 64, 64), 64)
        pre = acc_ref[rows, :]
        live = live_ref[x]
        sig = jax.nn.sigmoid(pre)
        hidden = (live * pre * sig).astype(BF16)
        face_ref[x] = hidden
        field_ref[x] = hidden.astype(F32)
        slope_ref[x] = live * sig * (1.0 + pre * (1.0 - sig))

    def outputs_of(x):
        rows = pl.ds(pl.multiple_of(x * 64, 64), 64)
        pre = acc_ref[rows, :]
        live = live_ref[x]
        sig = jax.nn.sigmoid(pre)
        out_ref[rows, :] = (live * pre * sig).astype(BF16)
        upstream = cot_ref[rows, :].astype(F32)
        delta = (upstream * live * sig * (1.0 + pre * (1.0 - sig))).astype(BF16)
        face_ref[x] = delta
        field_ref[x] = delta.astype(F32)

    def back_of(x):
        rows = pl.ds(pl.multiple_of(x * 64, 64), 64)
        face_ref[x] = (acc_ref[rows, :] * slope_ref[x]).astype(BF16)

    layer(0, c1_ref, store_first, split_first(), even_quarter, windows_first, weight_first, dot, hidden_of, halo)
    halo = halo_copies(1)
    for copy in halo:
        copy.start()

    second = functools.partial(windows_second, c2_ref)
    loads[4].wait()
    layer(1, c2_ref, store_second, split_second(), first_half, second, weight_second, dot, outputs_of, halo)
    halo = halo_copies(2)
    for copy in halo:
        copy.start()

    wide_half = iota((64, 128), 1) < 64
    wide_quarter = lax.rem(iota((64, 128), 1) // 32, 2) == 0

    def put_gradient(pair, value):
        grad_ref[pair // HALF, (pair % HALF) * 4 : (pair % HALF) * 4 + 4] = value.reshape(4, 16, 128)

    delta_t = face_ref[...].reshape(512, 128).T
    for pair in range(14):
        both = []
        for k in (2 * pair, min(2 * pair + 1, 26)):
            a, b, c = k // 9, k // 3 % 3, k % 3
            window = c2_ref[c, a : a + 8, ROWS[b] : ROWS[b] + 64, :]
            both.append(window.reshape(512, 128))
        got = dot(delta_t, jnp.concatenate(both, axis=1))
        one, two = got[:, :128], got[:, 128:]
        straight = jnp.where(wide_half, one[0:64], two[64:128])
        crossed = jnp.where(wide_half, two[0:64], one[64:128])
        put_gradient(pair, straight + pltpu.roll(crossed, 64, 1))
    for pair in range(14, PAIRS_SECOND):
        put_gradient(pair, jnp.zeros((64, 128), F32))

    third = functools.partial(windows_second, c3_ref)
    layer(2, c3_ref, store_second, split_second(), first_half, third, weight_back, dot_nt, back_of, halo)
    delta_t = face_ref[...].reshape(512, 128).T
    for pair in range(PAIRS_FIRST):
        both = []
        for block in (2 * pair, min(2 * pair + 1, 14)):
            a, r = block // 5, ROWS_FIRST[block % 5]
            both.append(c1_ref[a : a + 8, r : r + 64, :].reshape(512, 128))
        got = dot(delta_t, jnp.concatenate(both, axis=1))
        one, two = got[:, :128], got[:, 128:]
        straight = jnp.where(wide_quarter, one[0:64], two[64:128])
        crossed = jnp.where(wide_quarter, two[0:64], one[64:128])
        swapped = jnp.where(wide_quarter, pltpu.roll(crossed, 96, 1), pltpu.roll(crossed, 32, 1))
        put_gradient(PAIRS_SECOND + pair, straight + swapped)


def sum_kernel(
    sizes,
    scale,
    grad_ref,
    fin_ref,
    send_ref,
    pair_ref,
    half_ref,
    mine_ref,
    plane_ref,
    line_ref,
    pair_send,
    pair_recv,
    plane_send,
    plane_recv,
    line_send,
    line_recv,
    back_send,
    back_recv,
    twin_send,
    twin_recv,
):
    nx, nz, ny = sizes
    n_plane = nx * ny
    my_x, my_z, my_y, core, region, rep = places(sizes)
    member = my_x * ny + my_y
    unit = 4 * HALF // n_plane

    def plane_peer(step):
        other = lax.rem(member + step, n_plane)
        return other, {"region": (other // ny) * nz + my_z, "rep": lax.rem(other, ny) * 2 + core}

    def line_peer(step):
        return {"region": my_x * nz + lax.rem(my_z + step, nz), "rep": rep}

    twin = {"region": region, "rep": my_y * 2 + 1 - core}

    barrier = pltpu.get_barrier_semaphore()
    pl.semaphore_signal(barrier, inc=1, device_id=twin, device_id_type=MESH)

    @pl.loop(1, n_plane)
    def _(step):
        pl.semaphore_signal(barrier, inc=1, device_id=plane_peer(step)[1], device_id_type=MESH)

    @pl.loop(1, nz)
    def _(step):
        pl.semaphore_signal(barrier, inc=1, device_id=line_peer(step), device_id_type=MESH)

    def remote(src, dst, send_sem, recv_sem, device):
        return pltpu.make_async_remote_copy(
            src_ref=src,
            dst_ref=dst,
            send_sem=send_sem,
            recv_sem=recv_sem,
            device_id=device,
            device_id_type=MESH,
        )

    def plane_copy(step):
        other, device = plane_peer(step)
        source = half_ref.at[pl.ds(other * unit, unit)]
        return remote(source, plane_ref.at[step], plane_send.at[step], plane_recv.at[step], device)

    def line_copy(step):
        place = line_ref.at[my_z]
        return remote(place, place, line_send.at[step], line_recv.at[step], line_peer(step))

    def back_copy(step):
        place = fin_ref.at[core, pl.ds(member * unit, unit)]
        return remote(place, place, back_send.at[step], back_recv.at[step], plane_peer(step)[1])

    send_ref[...] = grad_ref[1 - core].astype(BF16)
    pl.semaphore_wait(barrier, 1 + n_plane - 1 + nz - 1)
    pair_copy = remote(send_ref, pair_ref, pair_send.at[0], pair_recv.at[0], twin)
    pair_copy.start()
    pair_copy.wait()
    total = grad_ref[core] + pair_ref[...].astype(F32)
    half_ref[...] = total.astype(BF16)
    mine_ref[...] = total

    @pl.loop(1, n_plane)
    def _(step):
        plane_copy(step).start()

    @pl.loop(1, n_plane)
    def _(step):
        plane_copy(step).wait()

    total = mine_ref[pl.ds(member * unit, unit)]
    for step in range(1, n_plane):
        total = total + plane_ref[step].astype(F32)
    line_ref[my_z] = total.astype(BF16)

    @pl.loop(1, nz)
    def _(step):
        line_copy(step).start()

    @pl.loop(1, nz)
    def _(step):
        line_copy(step).wait()

    total = line_ref[0].astype(F32)
    for z in range(1, nz):
        total = total + line_ref[z].astype(F32)
    fin_ref[core, pl.ds(member * unit, unit)] = (total * scale).astype(BF16)

    @pl.loop(1, n_plane)
    def _(step):
        back_copy(step).start()

    @pl.loop(1, n_plane)
    def _(step):
        back_copy(step).wait()

    twin_copy = remote(fin_ref.at[core], fin_ref.at[core], twin_send.at[0], twin_recv.at[0], twin)
    twin_copy.start()
    twin_copy.wait()


def unpack_kernel(block_ref, fin_ref, out_hbm, g1_hbm, g2_hbm, g1_ref, g2_ref, sem):
    block_copy = pltpu.make_async_copy(block_ref, out_hbm, sem.at[0])
    block_copy.start()
    for pair in range(PAIRS_SECOND + PAIRS_FIRST):
        if pair in (14, 15):
            continue
        at = (pair % HALF) * 4
        value = fin_ref[pair // HALF, at : at + 4].reshape(64, 128).astype(F32).T
        if pair < 14:
            g2_ref[2 * pair] = value[0:64]
            if pair < 13:
                g2_ref[2 * pair + 1] = value[64:128]
            continue
        if pair == PAIRS_SECOND:
            second_copy = pltpu.make_async_copy(g2_ref, g2_hbm, sem.at[1])
            second_copy.start()
        for j in range(2):
            block = 2 * (pair - PAIRS_SECOND) + j
            if block > 14:
                continue
            a, kind = block // 5, block % 5
            if kind < 3:
                offsets = (9 * a + 3 * kind, 9 * a + 3 * kind + 2)
            elif kind == 3:
                offsets = (9 * a + 1, 9 * a + 7)
            else:
                offsets = (9 * a + 4,)
            for i, k in enumerate(offsets):
                g1_ref[k] = value[64 * i + 32 * j : 64 * i + 32 * j + 32]
    first_copy = pltpu.make_async_copy(g1_ref, g1_hbm, sem.at[2])
    first_copy.start()
    block_copy.wait()
    second_copy.wait()
    first_copy.wait()


def solution(mesh):
    n_region, n_rep = mesh.shape["region"], mesh.shape["rep"]
    nx, ny = (4, 4) if n_region == 32 else (2, n_rep // 2)
    nz = n_region // nx
    sizes = (nx, nz, ny)
    n_plane = nx * ny
    units = 4 * HALF
    unit = units // n_plane
    vmem = pl.BlockSpec(memory_space=pltpu.VMEM)
    smem = pl.BlockSpec(memory_space=pltpu.SMEM)
    hbm = pl.BlockSpec(memory_space=pl.ANY)
    dma = pltpu.SemaphoreType.DMA

    def body(features, weight_first, weight_second, cotangent, neighbours, voxel_mask):
        scale = 1.0 / math.sqrt(n_rep * 2 * n_region * 512)
        block, grad = pl.pallas_call(
            functools.partial(compute_kernel, sizes),
            out_shape=(
                jax.ShapeDtypeStruct((512, 128), BF16),
                jax.ShapeDtypeStruct((2, units, 16, 128), F32),
            ),
            in_specs=[hbm, hbm, hbm, hbm, smem, hbm],
            out_specs=(vmem, vmem),
            scratch_shapes=[
                pltpu.VMEM((64, 512), BF16),
                pltpu.VMEM((27, 32, 64), BF16),
                pltpu.VMEM((27, 64, 64), BF16),
                pltpu.VMEM((512, 128), BF16),
                pltpu.VMEM((2, 512), jnp.int32),
                pltpu.VMEM((8, 64, 128), F32),
                pltpu.VMEM((8, 64, 128), F32),
                pltpu.VMEM((8, 64, 128), BF16),
                pltpu.VMEM((3, 2, 64, 128), BF16),
                pltpu.VMEM((3, 8, 64, 128), F32),
                pltpu.VMEM((2, 3, 64, 128), F32),
                pltpu.VMEM((10, 272, 128), BF16),
                pltpu.VMEM((3, 10, 144, 128), BF16),
                pltpu.VMEM((3, 10, 144, 128), BF16),
                pltpu.VMEM((3, 5, 128, 128), BF16),
                pltpu.VMEM((27, 128, 128), BF16),
                pltpu.VMEM((512, 128), F32),
                pltpu.VMEM((8, 64, 128), F32),
                dma((5,)),
                dma((3, 2)),
                dma((3, 2)),
            ],
            compiler_params=pltpu.CompilerParams(
                collective_id=0, has_side_effects=True, vmem_limit_bytes=56 * 2**20
            ),
        )(
            jnp.swapaxes(features, 1, 2).reshape(64, 512),
            weight_first,
            weight_second,
            cotangent.reshape(512, 128),
            neighbours.reshape(2, 27),
            voxel_mask.reshape(2, 512),
        )
        fin = pl.pallas_call(
            functools.partial(sum_kernel, sizes, scale),
            out_shape=jax.ShapeDtypeStruct((2, units, 16, 128), BF16),
            in_specs=[vmem],
            out_specs=vmem,
            scratch_shapes=[
                pltpu.VMEM((units, 16, 128), BF16),
                pltpu.VMEM((units, 16, 128), BF16),
                pltpu.VMEM((units, 16, 128), BF16),
                pltpu.VMEM((units, 16, 128), F32),
                pltpu.VMEM((n_plane, unit, 16, 128), BF16),
                pltpu.VMEM((nz, unit, 16, 128), BF16),
                dma((1,)),
                dma((1,)),
                dma((n_plane,)),
                dma((n_plane,)),
                dma((nz,)),
                dma((nz,)),
                dma((n_plane,)),
                dma((n_plane,)),
                dma((1,)),
                dma((1,)),
            ],
            compiler_params=pltpu.CompilerParams(
                collective_id=1, has_side_effects=True, vmem_limit_bytes=40 * 2**20
            ),
        )(grad)
        out, g1, g2 = pl.pallas_call(
            unpack_kernel,
            out_shape=(
                jax.ShapeDtypeStruct((512, 128), BF16),
                jax.ShapeDtypeStruct((27, 32, 64), F32),
                jax.ShapeDtypeStruct((27, 64, 64), F32),
            ),
            in_specs=[vmem, vmem],
            out_specs=(hbm, hbm, hbm),
            scratch_shapes=[
                pltpu.VMEM((27, 32, 64), F32),
                pltpu.VMEM((27, 64, 64), F32),
                dma((3,)),
            ],
            compiler_params=pltpu.CompilerParams(vmem_limit_bytes=40 * 2**20),
        )(block, fin)
        return out.reshape(1, 512, 128), g1, g2

    in_specs = (
        P("rep", None, "region"),
        P(),
        P(),
        P("rep", None, "region"),
        P("rep", "region", None),
        P("rep", "region", None),
    )
    out_specs = (P("rep", None, "region"), P(), P())
    return jax.shard_map(body, mesh=mesh, in_specs=in_specs, out_specs=out_specs, check_vma=False)
```

```python
import functools
import math

import jax
import jax.numpy as jnp
from jax import lax
from jax.experimental import pallas as pl
from jax.experimental.pallas import tpu as pltpu
from jax.sharding import PartitionSpec as P

MESH = pl.DeviceIdType.MESH
F32 = jnp.float32
BF16 = jnp.bfloat16
ROWS = (0, 80, 16)
ROWS_FIRST = (0, 80, 16, 144, 208)
PAIRS_SECOND = 16
PAIRS_FIRST = 8


def iota(shape, axis):
    return lax.broadcasted_iota(jnp.int32, shape, axis)


def dot(a, b):
    return jnp.dot(a, b, preferred_element_type=F32)


def dot_nt(a, b):
    return lax.dot_general(a, b, (((1,), (1,)), ((), ())), preferred_element_type=F32)


def places(sizes):
    nx, nz, ny = sizes
    region = lax.axis_index("region")
    rep = lax.axis_index("rep")
    return region // nz, lax.rem(region, nz), rep // 2, lax.rem(rep, 2), region, rep


def main_kernel(
    sizes,
    scale,
    feat_hbm,
    w1_hbm,
    w2_hbm,
    cot_hbm,
    nbr_ref,
    mask_hbm,
    out_hbm,
    fin1_hbm,
    fin2_hbm,
    feat_ref,
    w1_ref,
    w2_ref,
    cot_ref,
    mask_ref,
    live_ref,
    field_ref,
    face_ref,
    halo_ref,
    side_ref,
    far_ref,
    c1_ref,
    c2_ref,
    c3_ref,
    w1b_ref,
    w2b_ref,
    acc_ref,
    slope_ref,
    full1_ref,
    full2_ref,
    send1_ref,
    send2_ref,
    pair1_ref,
    pair2_ref,
    half1_ref,
    half2_ref,
    plane1_ref,
    plane2_ref,
    line1_ref,
    line2_ref,
    fin1_ref,
    fin2_ref,
    out_ref,
    load_sem,
    store_sem,
    halo_send,
    halo_recv,
    sum_send,
    sum_recv,
):
    nx, nz, ny = sizes
    n_region, n_plane = nx * nz, nx * ny
    my_x, my_z, my_y, core, region, rep = places(sizes)
    member = my_x * ny + my_y
    right = lax.rem(region + 1, n_region)
    left = lax.rem(region + n_region - 1, n_region)
    twin = {"region": region, "rep": my_y * 2 + 1 - core}
    plane_peers = []
    for step in range(1, n_plane):
        other = lax.rem(member + step, n_plane)
        at = {"region": (other // ny) * nz + my_z, "rep": lax.rem(other, ny) * 2 + core}
        plane_peers.append((step, other, at))
    line_peers = [
        {"region": my_x * nz + lax.rem(my_z + step, nz), "rep": rep} for step in range(1, nz)
    ]

    halo_ref[...] = jnp.zeros((3, 2, 64, 128), BF16)

    barrier = pltpu.get_barrier_semaphore()
    partners = [{"region": right, "rep": rep}, {"region": left, "rep": rep}, twin]
    partners += [at for _, _, at in plane_peers] + line_peers
    for at in partners:
        pl.semaphore_signal(barrier, inc=1, device_id=at, device_id_type=MESH)
    loads = [
        pltpu.make_async_copy(src, dst, load_sem.at[i])
        for i, (src, dst) in enumerate(
            (
                (mask_hbm, mask_ref),
                (feat_hbm, feat_ref),
                (w1_hbm, w1_ref),
                (w2_hbm, w2_ref),
                (cot_hbm, cot_ref),
            )
        )
    ]
    for load in loads:
        load.start()
    loads[0].wait()
    loads[1].wait()

    mask = jnp.concatenate([mask_ref[...].astype(F32), jnp.zeros((6, 512), F32)], axis=0).T
    tile_of = (iota((8, 128), 1) // 64 == iota((8, 128), 0)).astype(F32)
    tile_of_first = (lax.rem(iota((8, 128), 1) // 32, 2) == iota((8, 128), 0)).astype(F32)
    live_ref[...] = dot(mask, tile_of).reshape(8, 64, 128)
    twice = (iota((64, 128), 0) == lax.rem(iota((64, 128), 1), 64)).astype(BF16)
    spread = dot(feat_ref[...].T, twice) * dot(mask, tile_of_first)
    field_ref[...] = spread.reshape(8, 64, 128)
    face_ref[...] = spread.astype(BF16).reshape(8, 64, 128)

    def halo_copy(which, side):
        return pltpu.make_async_remote_copy(
            src_ref=face_ref.at[7 if side == 0 else 0],
            dst_ref=halo_ref.at[which, side],
            send_sem=halo_send.at[which, side],
            recv_sem=halo_recv.at[which, side],
            device_id={"region": right if side == 0 else left, "rep": rep},
            device_id_type=MESH,
        )

    has_right, has_left = region < n_region - 1, region > 0

    def halo_start(which):
        pl.when(has_right)(lambda: halo_copy(which, 0).start())
        pl.when(has_left)(lambda: halo_copy(which, 1).start())

    def halo_wait(which):
        @pl.when(has_left)
        def _():
            halo_copy(which, 0).wait_recv()

        @pl.when(has_right)
        def _():
            halo_copy(which, 1).wait_recv()

        pl.when(has_right)(lambda: halo_copy(which, 0).wait_send())
        pl.when(has_left)(lambda: halo_copy(which, 1).wait_send())

    pl.semaphore_wait(barrier, len(partners))
    halo_start(0)

    loads[2].wait()
    eye = iota((64, 256), 0)
    put = ((eye == iota((64, 256), 1)) | (eye == iota((64, 256), 1) - 192)).astype(BF16)
    spread1 = dot(w1_ref[...].reshape(27 * 32, 64), put).astype(BF16)
    top = spread1[:, :128].reshape(3, 3, 3, 32, 128)
    low = spread1[:, 128:].reshape(3, 3, 3, 32, 128)
    for b in range(3):
        for at, c in ((0, 0), (64, 2)):
            w1b_ref[:, b, at : at + 32, :] = top[:, b, c]
            w1b_ref[:, b, at + 32 : at + 64, :] = low[:, b, c]
    for at, b in ((0, 0), (64, 2)):
        w1b_ref[:, 3, at : at + 32, :] = top[:, b, 1]
        w1b_ref[:, 3, at + 32 : at + 64, :] = low[:, b, 1]
    w1b_ref[:, 4, 0:32, :] = top[:, 1, 1]
    w1b_ref[:, 4, 32:64, :] = low[:, 1, 1]
    w1b_ref[:, 4, 64:128, :] = jnp.zeros((3, 64, 128), BF16)
    loads[3].wait()
    spread2 = dot(w2_ref[...].reshape(27 * 64, 64), put).astype(BF16)
    w2b_ref[:, 0:64, :] = spread2[:, :128].reshape(27, 64, 128)
    w2b_ref[:, 64:128, :] = spread2[:, 128:].reshape(27, 64, 128)

    side_ref[2] = jnp.zeros((8, 64, 128), F32)
    far_ref[:, 2] = jnp.zeros((2, 64, 128), F32)
    lane = iota((8, 128), 1)
    first_half = lane < 64
    even_quarter = lax.rem(lane // 32, 2) == 0
    z_row = iota((8, 128), 0)
    z_first, z_last = z_row == 0, z_row == 7

    def rows_of(masked, count):
        return jnp.concatenate([masked] * count, axis=0) if count > 1 else masked

    def split_first():
        source, target = iota((128, 256), 0), iota((128, 256), 1)
        return (source == (target // 128) * 32 + lax.rem(target, 32)).astype(BF16)

    def split_second():
        source, target = iota((128, 256), 0), iota((128, 256), 1)
        return (source == (target // 128) * 64 + lax.rem(target, 64)).astype(BF16)

    def shifted(middle, load, tile_lane):
        ext = []
        for c in range(3):
            groups = [load(0, c, 56, 64)]
            if c == 1 and middle is not None:
                mid = middle
            else:
                mid = load(1, c, 0, 64)
            groups += [mid[8 * y : 8 * y + 8] for y in range(8)]
            groups.append(load(2, c, 0, 8))
            ext.append(groups)
        down = [pltpu.roll(jnp.where(z_last, ext[0][y], ext[1][y]), 1, 0) for y in range(10)]
        up = [pltpu.roll(jnp.where(z_first, ext[2][y], ext[1][y]), 7, 0) for y in range(10)]
        return down, ext[1], up

    def store_first(c_ref, slab, down, mid, up):
        both = [jnp.where(first_half, d, u) for d, u in zip(down, up)]
        c_ref[slab, 0:80, :] = jnp.concatenate(both, axis=0).astype(BF16)
        c_ref[slab, 80:144, :] = jnp.concatenate(both[1:9], axis=0).astype(BF16)
        ends = [jnp.where(first_half, mid[y], mid[y + 2]) for y in range(8)]
        c_ref[slab, 144:208, :] = jnp.concatenate(ends, axis=0).astype(BF16)
        c_ref[slab, 208:272, :] = jnp.concatenate(mid[1:9], axis=0).astype(BF16)

    def store_second(c_ref, slab, down, mid, up):
        for c, groups in enumerate((down, mid, up)):
            c_ref[c, slab, 0:80, :] = jnp.concatenate(groups, axis=0).astype(BF16)
            c_ref[c, slab, 80:144, :] = jnp.concatenate(groups[1:9], axis=0).astype(BF16)

    def build_inner(c_ref, store, splitter, tile_lane):
        whole = dot(face_ref[...].reshape(512, 128), splitter)
        side_ref[0] = whole[:, :128].reshape(8, 64, 128)
        side_ref[1] = whole[:, 128:].reshape(8, 64, 128)
        named = [
            [jnp.minimum(jnp.maximum(nbr_ref[t, 9 + k] - 2, 0), 2) for k in range(9)]
            for t in range(2)
        ]

        @pl.loop(0, 8)
        def _(x):
            def load(b, c, start, stop):
                k = 3 * b + c
                return jnp.where(
                    rows_of(tile_lane, (stop - start) // 8),
                    side_ref[named[0][k], x, start:stop, :],
                    side_ref[named[1][k], x, start:stop, :],
                )

            store(c_ref, x + 1, *shifted(field_ref[x], load, tile_lane))

    def build_faces(which, c_ref, store, splitter, tile_lane):
        for side in range(2):
            whole = dot(halo_ref[which, side], splitter)
            far_ref[side, 0] = whole[:, :128]
            far_ref[side, 1] = whole[:, 128:]
            named = [
                [
                    jnp.minimum(jnp.maximum(nbr_ref[t, 18 * side + k] - 4 * side, 0), 2)
                    for k in range(9)
                ]
                for t in range(2)
            ]

            def load(b, c, start, stop):
                k = 3 * b + c
                return jnp.where(
                    rows_of(tile_lane, (stop - start) // 8),
                    far_ref[side, named[0][k], start:stop, :],
                    far_ref[side, named[1][k], start:stop, :],
                )

            store(c_ref, 9 * side, *shifted(None, load, tile_lane))

    def windows_first(start, count):
        return [
            c1_ref[start : start + count, r : r + 64, :].reshape(count * 64, 128)
            for r in ROWS_FIRST
        ]

    def windows_second(c_ref, start, count):
        return [
            c_ref[c, start : start + count, ROWS[b] : ROWS[b] + 64, :].reshape(count * 64, 128)
            for b in range(3)
            for c in range(3)
        ]

    def conv_inner(windows, weight, product=dot):
        acc_ref[...] = product(jnp.concatenate(windows(1, 8), axis=1), weight(1))
        acc_ref[64:512] += product(jnp.concatenate(windows(1, 7), axis=1), weight(0))
        acc_ref[0:448] += product(jnp.concatenate(windows(2, 7), axis=1), weight(2))

    def conv_faces(windows, weight, product=dot):
        acc_ref[0:64] += product(jnp.concatenate(windows(0, 1), axis=1), weight(0))
        acc_ref[448:512] += product(jnp.concatenate(windows(9, 1), axis=1), weight(2))

    def weight_first(a):
        return w1b_ref[a].reshape(5 * 128, 128)

    def weight_second(a):
        return w2b_ref[9 * a : 9 * a + 9].reshape(9 * 128, 128)

    def weight_back(a):
        return jnp.concatenate([w2b_ref[26 - k] for k in range(9 * a, 9 * a + 9)], axis=1)

    def layer(which, c_ref, store, splitter, tile_lane, windows, weight, product, activate, between=None):
        build_inner(c_ref, store, splitter, tile_lane)
        conv_inner(windows, weight, product)
        if between is not None:
            between()
        pl.loop(1, 7)(activate)
        halo_wait(which)
        build_faces(which, c_ref, store, splitter, tile_lane)
        conv_faces(windows, weight, product)
        pl.loop(0, 2)(lambda i: activate(7 * i))

    def hidden_of(x):
        rows = pl.ds(pl.multiple_of(x * 64, 64), 64)
        pre = acc_ref[rows, :]
        live = live_ref[x]
        sig = jax.nn.sigmoid(pre)
        hidden = (live * pre * sig).astype(BF16)
        face_ref[x] = hidden
        field_ref[x] = hidden.astype(F32)
        slope_ref[x] = live * sig * (1.0 + pre * (1.0 - sig))

    def outputs_of(x):
        rows = pl.ds(pl.multiple_of(x * 64, 64), 64)
        pre = acc_ref[rows, :]
        live = live_ref[x]
        sig = jax.nn.sigmoid(pre)
        out_ref[rows, :] = (live * pre * sig).astype(BF16)
        upstream = cot_ref[rows, :].astype(F32)
        delta = (upstream * live * sig * (1.0 + pre * (1.0 - sig))).astype(BF16)
        face_ref[x] = delta
        field_ref[x] = delta.astype(F32)

    def back_of(x):
        rows = pl.ds(pl.multiple_of(x * 64, 64), 64)
        face_ref[x] = (acc_ref[rows, :] * slope_ref[x]).astype(BF16)

    layer(0, c1_ref, store_first, split_first(), even_quarter, windows_first, weight_first, dot, hidden_of)
    halo_start(1)

    second = functools.partial(windows_second, c2_ref)
    loads[4].wait()
    layer(1, c2_ref, store_second, split_second(), first_half, second, weight_second, dot, outputs_of)
    halo_start(2)
    block_store = pltpu.make_async_copy(out_ref, out_hbm, store_sem.at[0])
    block_store.start()

    wide_half = iota((64, 128), 1) < 64
    wide_quarter = lax.rem(iota((64, 128), 1) // 32, 2) == 0
    per_core1, per_core2 = PAIRS_FIRST // 2, PAIRS_SECOND // 2

    def put_gradient(full, send, per_core, pair, value):
        value = value.reshape(4, 16, 128)
        units = pl.ds((pair % per_core) * 4, 4)
        full[pair // per_core, units] = value
        send[pair // per_core, units] = value.astype(BF16)

    delta_t = face_ref[...].reshape(512, 128).T
    for pair in range(14):
        both = []
        for k in (2 * pair, min(2 * pair + 1, 26)):
            a, b, c = k // 9, k // 3 % 3, k % 3
            window = c2_ref[c, a : a + 8, ROWS[b] : ROWS[b] + 64, :]
            both.append(window.reshape(512, 128))
        got = dot(delta_t, jnp.concatenate(both, axis=1))
        one, two = got[:, :128], got[:, 128:]
        straight = jnp.where(wide_half, one[0:64], two[64:128])
        crossed = jnp.where(wide_half, two[0:64], one[64:128])
        put_gradient(full2_ref, send2_ref, per_core2, pair, straight + pltpu.roll(crossed, 64, 1))
    for pair in range(14, PAIRS_SECOND):
        put_gradient(full2_ref, send2_ref, per_core2, pair, jnp.zeros((64, 128), F32))

    def reducer(which, per_core, full, send, pair, half, plane, line, fin):
        unit = 4 * per_core // n_plane

        def remote(stage, src, dst, device):
            return pltpu.make_async_remote_copy(
                src_ref=src,
                dst_ref=dst,
                send_sem=sum_send.at[which, stage],
                recv_sem=sum_recv.at[which, stage],
                device_id=device,
                device_id_type=MESH,
            )

        mine = fin.at[core, pl.ds(member * unit, unit)]
        plane_part = plane.at[pl.ds(1, n_plane - 1)]
        line_part = line.at[pl.ds(0, nz - 1)]
        back_part = fin.at[core, pl.ds(0, (n_plane - 1) * unit)]
        whole = [
            remote(0, send.at[1 - core], pair, twin),
            remote(1, plane_part, plane_part, twin),
            remote(2, line_part, line_part, twin),
            remote(3, back_part, back_part, twin),
            remote(4, fin.at[core], fin.at[core], twin),
        ]

        def start_pair():
            whole[0].start()

        def start_plane():
            whole[0].wait_recv()
            total = full[core] + pair[...].astype(F32)
            full[core] = total
            half[...] = total.astype(BF16)
            for step, other, at in plane_peers:
                remote(1, half.at[pl.ds(other * unit, unit)], plane.at[step], at).start()

        def start_line():
            whole[1].wait_recv()
            total = full[core, pl.ds(member * unit, unit)]
            for step in range(1, n_plane):
                total = total + plane[step].astype(F32)
            line[my_z] = total.astype(BF16)
            for at in line_peers:
                remote(2, line.at[my_z], line.at[my_z], at).start()

        def start_back():
            whole[2].wait_recv()
            total = line[0].astype(F32)
            for z in range(1, nz):
                total = total + line[z].astype(F32)
            fin[core, pl.ds(member * unit, unit)] = (total * scale).astype(BF16)
            for _, _, at in plane_peers:
                remote(3, mine, mine, at).start()

        def start_twin():
            whole[3].wait_recv()
            whole[4].start()

        def finish():
            whole[4].wait_recv()

        def sent():
            for copy in whole:
                copy.wait_send()

        return start_pair, start_plane, start_line, start_back, start_twin, finish, sent

    sum1 = reducer(
        0, per_core1, full1_ref, send1_ref, pair1_ref, half1_ref, plane1_ref, line1_ref, fin1_ref
    )
    sum2 = reducer(
        1, per_core2, full2_ref, send2_ref, pair2_ref, half2_ref, plane2_ref, line2_ref, fin2_ref
    )
    sum2[0]()

    third = functools.partial(windows_second, c3_ref)
    layer(2, c3_ref, store_second, split_second(), first_half, third, weight_back, dot_nt, back_of, sum2[1])
    delta_t = face_ref[...].reshape(512, 128).T
    for pair in range(PAIRS_FIRST):
        both = []
        for block in (2 * pair, min(2 * pair + 1, 14)):
            a, r = block // 5, ROWS_FIRST[block % 5]
            both.append(c1_ref[a : a + 8, r : r + 64, :].reshape(512, 128))
        got = dot(delta_t, jnp.concatenate(both, axis=1))
        one, two = got[:, :128], got[:, 128:]
        straight = jnp.where(wide_quarter, one[0:64], two[64:128])
        crossed = jnp.where(wide_quarter, two[0:64], one[64:128])
        swapped = jnp.where(wide_quarter, pltpu.roll(crossed, 96, 1), pltpu.roll(crossed, 32, 1))
        put_gradient(full1_ref, send1_ref, per_core1, pair, straight + swapped)
    sum1[0]()
    sum2[2]()
    sum1[1]()
    sum2[3]()
    sum1[2]()
    sum2[4]()
    sum1[3]()
    sum2[5]()
    second_store = pltpu.make_async_copy(fin2_ref, fin2_hbm, store_sem.at[1])
    second_store.start()
    sum1[4]()
    sum2[6]()
    block_store.wait()
    sum1[5]()
    first_store = pltpu.make_async_copy(fin1_ref, fin1_hbm, store_sem.at[2])
    first_store.start()
    sum1[6]()
    second_store.wait()
    first_store.wait()


def unpack_kernel(
    block_hbm, fin1_hbm, fin2_hbm, out_hbm, g1_hbm, g2_hbm, block_ref, fin1_ref, fin2_ref, g1_ref, g2_ref, sem
):
    loads = [
        pltpu.make_async_copy(src, dst, sem.at[i])
        for i, (src, dst) in enumerate(
            ((fin2_hbm, fin2_ref), (fin1_hbm, fin1_ref), (block_hbm, block_ref))
        )
    ]
    for load in loads:
        load.start()
    loads[0].wait()
    for pair in range(14):
        at = (pair % (PAIRS_SECOND // 2)) * 4
        value = fin2_ref[pair // (PAIRS_SECOND // 2), at : at + 4].reshape(64, 128).astype(F32).T
        g2_ref[2 * pair] = value[0:64]
        if pair < 13:
            g2_ref[2 * pair + 1] = value[64:128]
    second_copy = pltpu.make_async_copy(g2_ref, g2_hbm, sem.at[3])
    second_copy.start()
    loads[2].wait()
    block_copy = pltpu.make_async_copy(block_ref, out_hbm, sem.at[4])
    block_copy.start()
    loads[1].wait()
    for pair in range(PAIRS_FIRST):
        at = (pair % (PAIRS_FIRST // 2)) * 4
        value = fin1_ref[pair // (PAIRS_FIRST // 2), at : at + 4].reshape(64, 128).astype(F32).T
        for j in range(2):
            block = 2 * pair + j
            if block > 14:
                continue
            a, kind = block // 5, block % 5
            if kind < 3:
                offsets = (9 * a + 3 * kind, 9 * a + 3 * kind + 2)
            elif kind == 3:
                offsets = (9 * a + 1, 9 * a + 7)
            else:
                offsets = (9 * a + 4,)
            for i, k in enumerate(offsets):
                g1_ref[k] = value[64 * i + 32 * j : 64 * i + 32 * j + 32]
    first_copy = pltpu.make_async_copy(g1_ref, g1_hbm, sem.at[5])
    first_copy.start()
    second_copy.wait()
    block_copy.wait()
    first_copy.wait()


def solution(mesh):
    n_region, n_rep = mesh.shape["region"], mesh.shape["rep"]
    nx, ny = (4, 4) if n_region == 32 else (2, n_rep // 2)
    nz = n_region // nx
    sizes = (nx, nz, ny)
    n_plane = nx * ny
    core1, core2 = 2 * PAIRS_FIRST, 2 * PAIRS_SECOND
    unit1, unit2 = core1 // n_plane, core2 // n_plane
    vmem = pl.BlockSpec(memory_space=pltpu.VMEM)
    smem = pl.BlockSpec(memory_space=pltpu.SMEM)
    anywhere = pl.BlockSpec(memory_space=pl.ANY)
    dma = pltpu.SemaphoreType.DMA

    def body(features, weight_first, weight_second, cotangent, neighbours, voxel_mask):
        scale = 1.0 / math.sqrt(n_rep * 2 * n_region * 512)
        block, fin1, fin2 = pl.pallas_call(
            functools.partial(main_kernel, sizes, scale),
            out_shape=(
                jax.ShapeDtypeStruct((512, 128), BF16),
                jax.ShapeDtypeStruct((2, core1, 16, 128), BF16),
                jax.ShapeDtypeStruct((2, core2, 16, 128), BF16),
            ),
            in_specs=[anywhere, anywhere, anywhere, anywhere, smem, anywhere],
            out_specs=(anywhere, anywhere, anywhere),
            scratch_shapes=[
                pltpu.VMEM((64, 512), BF16),
                pltpu.VMEM((27, 32, 64), BF16),
                pltpu.VMEM((27, 64, 64), BF16),
                pltpu.VMEM((512, 128), BF16),
                pltpu.VMEM((2, 512), jnp.int32),
                pltpu.VMEM((8, 64, 128), F32),
                pltpu.VMEM((8, 64, 128), F32),
                pltpu.VMEM((8, 64, 128), BF16),
                pltpu.VMEM((3, 2, 64, 128), BF16),
                pltpu.VMEM((3, 8, 64, 128), F32),
                pltpu.VMEM((2, 3, 64, 128), F32),
                pltpu.VMEM((10, 272, 128), BF16),
                pltpu.VMEM((3, 10, 144, 128), BF16),
                pltpu.VMEM((3, 10, 144, 128), BF16),
                pltpu.VMEM((3, 5, 128, 128), BF16),
                pltpu.VMEM((27, 128, 128), BF16),
                pltpu.VMEM((512, 128), F32),
                pltpu.VMEM((8, 64, 128), F32),
                pltpu.VMEM((2, core1, 16, 128), F32),
                pltpu.VMEM((2, core2, 16, 128), F32),
                pltpu.VMEM((2, core1, 16, 128), BF16),
                pltpu.VMEM((2, core2, 16, 128), BF16),
                pltpu.VMEM((core1, 16, 128), BF16),
                pltpu.VMEM((core2, 16, 128), BF16),
                pltpu.VMEM((core1, 16, 128), BF16),
                pltpu.VMEM((core2, 16, 128), BF16),
                pltpu.VMEM((n_plane, unit1, 16, 128), BF16),
                pltpu.VMEM((n_plane, unit2, 16, 128), BF16),
                pltpu.VMEM((nz, unit1, 16, 128), BF16),
                pltpu.VMEM((nz, unit2, 16, 128), BF16),
                pltpu.VMEM((2, core1, 16, 128), BF16),
                pltpu.VMEM((2, core2, 16, 128), BF16),
                pltpu.VMEM((512, 128), BF16),
                dma((5,)),
                dma((3,)),
                dma((3, 2)),
                dma((3, 2)),
                dma((2, 5)),
                dma((2, 5)),
            ],
            compiler_params=pltpu.CompilerParams(
                collective_id=0, has_side_effects=True, vmem_limit_bytes=56 * 2**20
            ),
        )(
            jnp.swapaxes(features, 1, 2).reshape(64, 512),
            weight_first,
            weight_second,
            cotangent.reshape(512, 128),
            neighbours.reshape(2, 27),
            voxel_mask.reshape(2, 512),
        )
        out, g1, g2 = pl.pallas_call(
            unpack_kernel,
            out_shape=(
                jax.ShapeDtypeStruct((512, 128), BF16),
                jax.ShapeDtypeStruct((27, 32, 64), F32),
                jax.ShapeDtypeStruct((27, 64, 64), F32),
            ),
            in_specs=[anywhere, anywhere, anywhere],
            out_specs=(anywhere, anywhere, anywhere),
            scratch_shapes=[
                pltpu.VMEM((512, 128), BF16),
                pltpu.VMEM((2, core1, 16, 128), BF16),
                pltpu.VMEM((2, core2, 16, 128), BF16),
                pltpu.VMEM((27, 32, 64), F32),
                pltpu.VMEM((27, 64, 64), F32),
                dma((6,)),
            ],
            compiler_params=pltpu.CompilerParams(vmem_limit_bytes=56 * 2**20),
        )(block, fin1, fin2)
        return out.reshape(1, 512, 128), g1, g2

    in_specs = (
        P("rep", None, "region"),
        P(),
        P(),
        P("rep", None, "region"),
        P("rep", "region", None),
        P("rep", "region", None),
    )
    out_specs = (P("rep", None, "region"), P(), P())
    return jax.shard_map(body, mesh=mesh, in_specs=in_specs, out_specs=out_specs, check_vma=False)
```

```python
import functools
import math

import jax
import jax.numpy as jnp
from jax import lax
from jax.experimental import pallas as pl
from jax.experimental.pallas import tpu as pltpu
from jax.sharding import PartitionSpec as P

MESH = pl.DeviceIdType.MESH
F32 = jnp.float32
BF16 = jnp.bfloat16
ROWS = (0, 80, 16)
ROWS_FIRST = (0, 80, 16, 144, 208)
PAIRS_SECOND = 16
PAIRS_FIRST = 8


def iota(shape, axis):
    return lax.broadcasted_iota(jnp.int32, shape, axis)


def dot(a, b):
    return jnp.dot(a, b, preferred_element_type=F32)


def dot_nt(a, b):
    return lax.dot_general(a, b, (((1,), (1,)), ((), ())), preferred_element_type=F32)


def places(sizes):
    nx, nz, ny = sizes
    region = lax.axis_index("region")
    rep = lax.axis_index("rep")
    return region // nz, lax.rem(region, nz), rep // 2, lax.rem(rep, 2), region, rep


def main_kernel(
    sizes,
    scale,
    feat_hbm,
    w1_hbm,
    w2_hbm,
    cot_hbm,
    nbr_ref,
    mask_hbm,
    out_ref,
    fin1_ref,
    g2_ref,
    feat_ref,
    w1_ref,
    w2_ref,
    cot_ref,
    mask_ref,
    live_ref,
    field_ref,
    face_ref,
    halo_ref,
    side_ref,
    far_ref,
    c1_ref,
    c2_ref,
    c3_ref,
    w1b_ref,
    w2b_ref,
    acc_ref,
    slope_ref,
    full1_ref,
    full2_ref,
    send1_ref,
    send2_ref,
    pair1_ref,
    pair2_ref,
    half1_ref,
    half2_ref,
    plane1_ref,
    plane2_ref,
    line1_ref,
    line2_ref,
    fin2_ref,
    load_sem,
    halo_send,
    halo_recv,
    sum_send,
    sum_recv,
):
    nx, nz, ny = sizes
    n_region, n_plane = nx * nz, nx * ny
    my_x, my_z, my_y, core, region, rep = places(sizes)
    member = my_x * ny + my_y
    right = lax.rem(region + 1, n_region)
    left = lax.rem(region + n_region - 1, n_region)
    twin = {"region": region, "rep": my_y * 2 + 1 - core}
    plane_peers = []
    for step in range(1, n_plane):
        other = lax.rem(member + step, n_plane)
        at = {"region": (other // ny) * nz + my_z, "rep": lax.rem(other, ny) * 2 + core}
        plane_peers.append((step, other, at))
    line_peers = [
        {"region": my_x * nz + lax.rem(my_z + step, nz), "rep": rep} for step in range(1, nz)
    ]

    halo_ref[...] = jnp.zeros((3, 2, 64, 128), BF16)

    barrier = pltpu.get_barrier_semaphore()
    partners = [{"region": right, "rep": rep}, {"region": left, "rep": rep}, twin]
    partners += [at for _, _, at in plane_peers] + line_peers
    for at in partners:
        pl.semaphore_signal(barrier, inc=1, device_id=at, device_id_type=MESH)
    loads = [
        pltpu.make_async_copy(src, dst, load_sem.at[i])
        for i, (src, dst) in enumerate(
            (
                (mask_hbm, mask_ref),
                (feat_hbm, feat_ref),
                (w1_hbm, w1_ref),
                (w2_hbm, w2_ref),
                (cot_hbm, cot_ref),
            )
        )
    ]
    for load in loads:
        load.start()
    loads[0].wait()
    loads[1].wait()

    mask = jnp.concatenate([mask_ref[...].astype(F32), jnp.zeros((6, 512), F32)], axis=0).T
    tile_of = (iota((8, 128), 1) // 64 == iota((8, 128), 0)).astype(F32)
    tile_of_first = (lax.rem(iota((8, 128), 1) // 32, 2) == iota((8, 128), 0)).astype(F32)
    live_ref[...] = dot(mask, tile_of).reshape(8, 64, 128)
    twice = (iota((64, 128), 0) == lax.rem(iota((64, 128), 1), 64)).astype(BF16)
    spread = dot(feat_ref[...].T, twice) * dot(mask, tile_of_first)
    field_ref[...] = spread.reshape(8, 64, 128)
    face_ref[...] = spread.astype(BF16).reshape(8, 64, 128)

    def halo_copy(which, side):
        return pltpu.make_async_remote_copy(
            src_ref=face_ref.at[7 if side == 0 else 0],
            dst_ref=halo_ref.at[which, side],
            send_sem=halo_send.at[which, side],
            recv_sem=halo_recv.at[which, side],
            device_id={"region": right if side == 0 else left, "rep": rep},
            device_id_type=MESH,
        )

    has_right, has_left = region < n_region - 1, region > 0

    def halo_start(which):
        pl.when(has_right)(lambda: halo_copy(which, 0).start())
        pl.when(has_left)(lambda: halo_copy(which, 1).start())

    def halo_wait(which):
        @pl.when(has_left)
        def _():
            halo_copy(which, 0).wait_recv()

        @pl.when(has_right)
        def _():
            halo_copy(which, 1).wait_recv()

        pl.when(has_right)(lambda: halo_copy(which, 0).wait_send())
        pl.when(has_left)(lambda: halo_copy(which, 1).wait_send())

    pl.semaphore_wait(barrier, len(partners))
    halo_start(0)

    loads[2].wait()
    eye = iota((64, 256), 0)
    put = ((eye == iota((64, 256), 1)) | (eye == iota((64, 256), 1) - 192)).astype(BF16)
    spread1 = dot(w1_ref[...].reshape(27 * 32, 64), put).astype(BF16)
    top = spread1[:, :128].reshape(3, 3, 3, 32, 128)
    low = spread1[:, 128:].reshape(3, 3, 3, 32, 128)
    for b in range(3):
        for at, c in ((0, 0), (64, 2)):
            w1b_ref[:, b, at : at + 32, :] = top[:, b, c]
            w1b_ref[:, b, at + 32 : at + 64, :] = low[:, b, c]
    for at, b in ((0, 0), (64, 2)):
        w1b_ref[:, 3, at : at + 32, :] = top[:, b, 1]
        w1b_ref[:, 3, at + 32 : at + 64, :] = low[:, b, 1]
    w1b_ref[:, 4, 0:32, :] = top[:, 1, 1]
    w1b_ref[:, 4, 32:64, :] = low[:, 1, 1]
    w1b_ref[:, 4, 64:128, :] = jnp.zeros((3, 64, 128), BF16)
    loads[3].wait()
    spread2 = dot(w2_ref[...].reshape(27 * 64, 64), put).astype(BF16)
    w2b_ref[:, 0:64, :] = spread2[:, :128].reshape(27, 64, 128)
    w2b_ref[:, 64:128, :] = spread2[:, 128:].reshape(27, 64, 128)

    side_ref[2] = jnp.zeros((8, 64, 128), F32)
    far_ref[:, 2] = jnp.zeros((2, 64, 128), F32)
    lane = iota((8, 128), 1)
    first_half = lane < 64
    even_quarter = lax.rem(lane // 32, 2) == 0
    z_row = iota((8, 128), 0)
    z_first, z_last = z_row == 0, z_row == 7

    def rows_of(masked, count):
        return jnp.concatenate([masked] * count, axis=0) if count > 1 else masked

    def split_first():
        source, target = iota((128, 256), 0), iota((128, 256), 1)
        return (source == (target // 128) * 32 + lax.rem(target, 32)).astype(BF16)

    def split_second():
        source, target = iota((128, 256), 0), iota((128, 256), 1)
        return (source == (target // 128) * 64 + lax.rem(target, 64)).astype(BF16)

    def shifted(middle, load, tile_lane):
        ext = []
        for c in range(3):
            groups = [load(0, c, 56, 64)]
            if c == 1 and middle is not None:
                mid = middle
            else:
                mid = load(1, c, 0, 64)
            groups += [mid[8 * y : 8 * y + 8] for y in range(8)]
            groups.append(load(2, c, 0, 8))
            ext.append(groups)
        down = [pltpu.roll(jnp.where(z_last, ext[0][y], ext[1][y]), 1, 0) for y in range(10)]
        up = [pltpu.roll(jnp.where(z_first, ext[2][y], ext[1][y]), 7, 0) for y in range(10)]
        return down, ext[1], up

    def store_first(c_ref, slab, down, mid, up):
        both = [jnp.where(first_half, d, u) for d, u in zip(down, up)]
        c_ref[slab, 0:80, :] = jnp.concatenate(both, axis=0).astype(BF16)
        c_ref[slab, 80:144, :] = jnp.concatenate(both[1:9], axis=0).astype(BF16)
        ends = [jnp.where(first_half, mid[y], mid[y + 2]) for y in range(8)]
        c_ref[slab, 144:208, :] = jnp.concatenate(ends, axis=0).astype(BF16)
        c_ref[slab, 208:272, :] = jnp.concatenate(mid[1:9], axis=0).astype(BF16)

    def store_second(c_ref, slab, down, mid, up):
        for c, groups in enumerate((down, mid, up)):
            c_ref[c, slab, 0:80, :] = jnp.concatenate(groups, axis=0).astype(BF16)
            c_ref[c, slab, 80:144, :] = jnp.concatenate(groups[1:9], axis=0).astype(BF16)

    def build_inner(c_ref, store, splitter, tile_lane):
        whole = dot(face_ref[...].reshape(512, 128), splitter)
        side_ref[0] = whole[:, :128].reshape(8, 64, 128)
        side_ref[1] = whole[:, 128:].reshape(8, 64, 128)
        named = [
            [jnp.minimum(jnp.maximum(nbr_ref[t, 9 + k] - 2, 0), 2) for k in range(9)]
            for t in range(2)
        ]

        @pl.loop(0, 8, unroll=4)
        def _(x):
            def load(b, c, start, stop):
                k = 3 * b + c
                return jnp.where(
                    rows_of(tile_lane, (stop - start) // 8),
                    side_ref[named[0][k], x, start:stop, :],
                    side_ref[named[1][k], x, start:stop, :],
                )

            store(c_ref, x + 1, *shifted(field_ref[x], load, tile_lane))

    def build_faces(which, c_ref, store, splitter, tile_lane):
        for side in range(2):
            whole = dot(halo_ref[which, side], splitter)
            far_ref[side, 0] = whole[:, :128]
            far_ref[side, 1] = whole[:, 128:]
            named = [
                [
                    jnp.minimum(jnp.maximum(nbr_ref[t, 18 * side + k] - 4 * side, 0), 2)
                    for k in range(9)
                ]
                for t in range(2)
            ]

            def load(b, c, start, stop):
                k = 3 * b + c
                return jnp.where(
                    rows_of(tile_lane, (stop - start) // 8),
                    far_ref[side, named[0][k], start:stop, :],
                    far_ref[side, named[1][k], start:stop, :],
                )

            store(c_ref, 9 * side, *shifted(None, load, tile_lane))

    def windows_first(start, count):
        return [
            c1_ref[start : start + count, r : r + 64, :].reshape(count * 64, 128)
            for r in ROWS_FIRST
        ]

    def windows_second(c_ref, start, count):
        return [
            c_ref[c, start : start + count, ROWS[b] : ROWS[b] + 64, :].reshape(count * 64, 128)
            for b in range(3)
            for c in range(3)
        ]

    def conv_inner(windows, weight, product=dot):
        acc_ref[...] = product(jnp.concatenate(windows(1, 8), axis=1), weight(1))
        acc_ref[64:512] += product(jnp.concatenate(windows(1, 7), axis=1), weight(0))
        acc_ref[0:448] += product(jnp.concatenate(windows(2, 7), axis=1), weight(2))

    def conv_faces(windows, weight, product=dot):
        acc_ref[0:64] += product(jnp.concatenate(windows(0, 1), axis=1), weight(0))
        acc_ref[448:512] += product(jnp.concatenate(windows(9, 1), axis=1), weight(2))

    def weight_first(a):
        return w1b_ref[a].reshape(5 * 128, 128)

    def weight_second(a):
        return w2b_ref[9 * a : 9 * a + 9].reshape(9 * 128, 128)

    def weight_back(a):
        return jnp.concatenate([w2b_ref[26 - k] for k in range(9 * a, 9 * a + 9)], axis=1)

    def layer(which, c_ref, store, splitter, tile_lane, windows, weight, product, activate, between=None):
        build_inner(c_ref, store, splitter, tile_lane)
        conv_inner(windows, weight, product)
        if between is not None:
            between()
        pl.loop(1, 7, unroll=3)(activate)
        halo_wait(which)
        build_faces(which, c_ref, store, splitter, tile_lane)
        conv_faces(windows, weight, product)
        pl.loop(0, 2, unroll=2)(lambda i: activate(7 * i))

    def hidden_of(x):
        rows = pl.ds(pl.multiple_of(x * 64, 64), 64)
        pre = acc_ref[rows, :]
        live = live_ref[x]
        sig = jax.nn.sigmoid(pre)
        hidden = (live * pre * sig).astype(BF16)
        face_ref[x] = hidden
        field_ref[x] = hidden.astype(F32)
        slope_ref[x] = live * sig * (1.0 + pre * (1.0 - sig))

    def outputs_of(x):
        rows = pl.ds(pl.multiple_of(x * 64, 64), 64)
        pre = acc_ref[rows, :]
        live = live_ref[x]
        sig = jax.nn.sigmoid(pre)
        out_ref[rows, :] = (live * pre * sig).astype(BF16)
        upstream = cot_ref[rows, :].astype(F32)
        delta = (upstream * live * sig * (1.0 + pre * (1.0 - sig))).astype(BF16)
        face_ref[x] = delta
        field_ref[x] = delta.astype(F32)

    def back_of(x):
        rows = pl.ds(pl.multiple_of(x * 64, 64), 64)
        face_ref[x] = (acc_ref[rows, :] * slope_ref[x]).astype(BF16)

    layer(0, c1_ref, store_first, split_first(), even_quarter, windows_first, weight_first, dot, hidden_of)
    halo_start(1)

    second = functools.partial(windows_second, c2_ref)
    loads[4].wait()
    layer(1, c2_ref, store_second, split_second(), first_half, second, weight_second, dot, outputs_of)
    halo_start(2)

    wide_half = iota((64, 128), 1) < 64
    wide_quarter = lax.rem(iota((64, 128), 1) // 32, 2) == 0
    per_core1, per_core2 = PAIRS_FIRST // 2, PAIRS_SECOND // 2

    def put_gradient(full, send, per_core, pair, value):
        value = value.reshape(4, 16, 128)
        units = pl.ds((pair % per_core) * 4, 4)
        full[pair // per_core, units] = value
        send[pair // per_core, units] = value.astype(BF16)

    delta_t = face_ref[...].reshape(512, 128).T
    for pair in range(14):
        both = []
        for k in (2 * pair, min(2 * pair + 1, 26)):
            a, b, c = k // 9, k // 3 % 3, k % 3
            window = c2_ref[c, a : a + 8, ROWS[b] : ROWS[b] + 64, :]
            both.append(window.reshape(512, 128))
        got = dot(delta_t, jnp.concatenate(both, axis=1))
        one, two = got[:, :128], got[:, 128:]
        straight = jnp.where(wide_half, one[0:64], two[64:128])
        crossed = jnp.where(wide_half, two[0:64], one[64:128])
        put_gradient(full2_ref, send2_ref, per_core2, pair, straight + pltpu.roll(crossed, 64, 1))
    for pair in range(14, PAIRS_SECOND):
        put_gradient(full2_ref, send2_ref, per_core2, pair, jnp.zeros((64, 128), F32))

    def reducer(which, per_core, full, send, pair, half, plane, line, fin):
        unit = 4 * per_core // n_plane

        def remote(stage, src, dst, device):
            return pltpu.make_async_remote_copy(
                src_ref=src,
                dst_ref=dst,
                send_sem=sum_send.at[which, stage],
                recv_sem=sum_recv.at[which, stage],
                device_id=device,
                device_id_type=MESH,
            )

        mine = fin.at[core, pl.ds(member * unit, unit)]
        plane_part = plane.at[pl.ds(1, n_plane - 1)]
        line_part = line.at[pl.ds(0, nz - 1)]
        back_part = fin.at[core, pl.ds(0, (n_plane - 1) * unit)]
        whole = [
            remote(0, send.at[1 - core], pair, twin),
            remote(1, plane_part, plane_part, twin),
            remote(2, line_part, line_part, twin),
            remote(3, back_part, back_part, twin),
            remote(4, fin.at[core], fin.at[core], twin),
        ]

        def start_pair():
            whole[0].start()

        def start_plane():
            whole[0].wait_recv()
            total = full[core] + pair[...].astype(F32)
            full[core] = total
            half[...] = total.astype(BF16)
            for step, other, at in plane_peers:
                remote(1, half.at[pl.ds(other * unit, unit)], plane.at[step], at).start()

        def start_line():
            whole[1].wait_recv()
            total = full[core, pl.ds(member * unit, unit)]
            for step in range(1, n_plane):
                total = total + plane[step].astype(F32)
            line[my_z] = total.astype(BF16)
            for at in line_peers:
                remote(2, line.at[my_z], line.at[my_z], at).start()

        def start_back():
            whole[2].wait_recv()
            total = line[0].astype(F32)
            for z in range(1, nz):
                total = total + line[z].astype(F32)
            fin[core, pl.ds(member * unit, unit)] = (total * scale).astype(BF16)
            for _, _, at in plane_peers:
                remote(3, mine, mine, at).start()

        def start_twin():
            whole[3].wait_recv()
            whole[4].start()

        def finish():
            whole[4].wait_recv()

        def sent():
            for copy in whole:
                copy.wait_send()

        return start_pair, start_plane, start_line, start_back, start_twin, finish, sent

    sum1 = reducer(
        0, per_core1, full1_ref, send1_ref, pair1_ref, half1_ref, plane1_ref, line1_ref, fin1_ref
    )
    sum2 = reducer(
        1, per_core2, full2_ref, send2_ref, pair2_ref, half2_ref, plane2_ref, line2_ref, fin2_ref
    )
    sum2[0]()

    third = functools.partial(windows_second, c3_ref)
    layer(2, c3_ref, store_second, split_second(), first_half, third, weight_back, dot_nt, back_of, sum2[1])
    delta_t = face_ref[...].reshape(512, 128).T
    for pair in range(PAIRS_FIRST):
        both = []
        for block in (2 * pair, min(2 * pair + 1, 14)):
            a, r = block // 5, ROWS_FIRST[block % 5]
            both.append(c1_ref[a : a + 8, r : r + 64, :].reshape(512, 128))
        got = dot(delta_t, jnp.concatenate(both, axis=1))
        one, two = got[:, :128], got[:, 128:]
        straight = jnp.where(wide_quarter, one[0:64], two[64:128])
        crossed = jnp.where(wide_quarter, two[0:64], one[64:128])
        swapped = jnp.where(wide_quarter, pltpu.roll(crossed, 96, 1), pltpu.roll(crossed, 32, 1))
        put_gradient(full1_ref, send1_ref, per_core1, pair, straight + swapped)
    sum1[0]()
    sum2[2]()
    sum1[1]()
    sum2[3]()
    sum1[2]()
    sum2[4]()
    sum1[3]()
    sum2[5]()
    for pair in range(14):
        units = pl.ds((pair % per_core2) * 4, 4)
        value = fin2_ref[pair // per_core2, units].reshape(64, 128).astype(F32).T
        g2_ref[2 * pair] = value[0:64]
        if pair < 13:
            g2_ref[2 * pair + 1] = value[64:128]
    sum1[4]()
    sum2[6]()
    sum1[5]()
    sum1[6]()


def unpack_kernel(block_ref, fin_ref, g2_ref, out_hbm, g1_hbm, g2_hbm, g1_ref, sem):
    block_copy = pltpu.make_async_copy(block_ref, out_hbm, sem.at[0])
    second_copy = pltpu.make_async_copy(g2_ref, g2_hbm, sem.at[1])
    first_copy = pltpu.make_async_copy(g1_ref, g1_hbm, sem.at[2])
    second_copy.start()
    block_copy.start()
    for pair in range(PAIRS_FIRST):
        at = (pair % (PAIRS_FIRST // 2)) * 4
        value = fin_ref[pair // (PAIRS_FIRST // 2), at : at + 4].reshape(64, 128).astype(F32).T
        for j in range(2):
            block = 2 * pair + j
            if block > 14:
                continue
            a, kind = block // 5, block % 5
            if kind < 3:
                offsets = (9 * a + 3 * kind, 9 * a + 3 * kind + 2)
            elif kind == 3:
                offsets = (9 * a + 1, 9 * a + 7)
            else:
                offsets = (9 * a + 4,)
            for i, k in enumerate(offsets):
                g1_ref[k] = value[64 * i + 32 * j : 64 * i + 32 * j + 32]
    first_copy.start()
    second_copy.wait()
    block_copy.wait()
    first_copy.wait()


def solution(mesh):
    n_region, n_rep = mesh.shape["region"], mesh.shape["rep"]
    nx, ny = (4, 4) if n_region == 32 else (2, n_rep // 2)
    nz = n_region // nx
    sizes = (nx, nz, ny)
    n_plane = nx * ny
    core1, core2 = 2 * PAIRS_FIRST, 2 * PAIRS_SECOND
    unit1, unit2 = core1 // n_plane, core2 // n_plane
    vmem = pl.BlockSpec(memory_space=pltpu.VMEM)
    smem = pl.BlockSpec(memory_space=pltpu.SMEM)
    hbm = pl.BlockSpec(memory_space=pltpu.HBM)
    anywhere = pl.BlockSpec(memory_space=pl.ANY)
    dma = pltpu.SemaphoreType.DMA

    def body(features, weight_first, weight_second, cotangent, neighbours, voxel_mask):
        scale = 1.0 / math.sqrt(n_rep * 2 * n_region * 512)
        block, fin1, g2 = pl.pallas_call(
            functools.partial(main_kernel, sizes, scale),
            out_shape=(
                jax.ShapeDtypeStruct((512, 128), BF16),
                jax.ShapeDtypeStruct((2, core1, 16, 128), BF16),
                jax.ShapeDtypeStruct((27, 64, 64), F32),
            ),
            in_specs=[hbm, hbm, hbm, hbm, smem, hbm],
            out_specs=(vmem, vmem, vmem),
            scratch_shapes=[
                pltpu.VMEM((64, 512), BF16),
                pltpu.VMEM((27, 32, 64), BF16),
                pltpu.VMEM((27, 64, 64), BF16),
                pltpu.VMEM((512, 128), BF16),
                pltpu.VMEM((2, 512), jnp.int32),
                pltpu.VMEM((8, 64, 128), F32),
                pltpu.VMEM((8, 64, 128), F32),
                pltpu.VMEM((8, 64, 128), BF16),
                pltpu.VMEM((3, 2, 64, 128), BF16),
                pltpu.VMEM((3, 8, 64, 128), F32),
                pltpu.VMEM((2, 3, 64, 128), F32),
                pltpu.VMEM((10, 272, 128), BF16),
                pltpu.VMEM((3, 10, 144, 128), BF16),
                pltpu.VMEM((3, 10, 144, 128), BF16),
                pltpu.VMEM((3, 5, 128, 128), BF16),
                pltpu.VMEM((27, 128, 128), BF16),
                pltpu.VMEM((512, 128), F32),
                pltpu.VMEM((8, 64, 128), F32),
                pltpu.VMEM((2, core1, 16, 128), F32),
                pltpu.VMEM((2, core2, 16, 128), F32),
                pltpu.VMEM((2, core1, 16, 128), BF16),
                pltpu.VMEM((2, core2, 16, 128), BF16),
                pltpu.VMEM((core1, 16, 128), BF16),
                pltpu.VMEM((core2, 16, 128), BF16),
                pltpu.VMEM((core1, 16, 128), BF16),
                pltpu.VMEM((core2, 16, 128), BF16),
                pltpu.VMEM((n_plane, unit1, 16, 128), BF16),
                pltpu.VMEM((n_plane, unit2, 16, 128), BF16),
                pltpu.VMEM((nz, unit1, 16, 128), BF16),
                pltpu.VMEM((nz, unit2, 16, 128), BF16),
                pltpu.VMEM((2, core2, 16, 128), BF16),
                dma((5,)),
                dma((3, 2)),
                dma((3, 2)),
                dma((2, 5)),
                dma((2, 5)),
            ],
            compiler_params=pltpu.CompilerParams(
                collective_id=0, has_side_effects=True, vmem_limit_bytes=40 * 2**20
            ),
        )(
            *(
                pltpu.with_memory_space_constraint(x, pltpu.HBM)
                for x in (
                    jnp.swapaxes(features, 1, 2).reshape(64, 512),
                    weight_first,
                    weight_second,
                    cotangent.reshape(512, 128),
                    neighbours.reshape(2, 27),
                    voxel_mask.reshape(2, 512),
                )
            )
        )
        out, g1, g2 = pl.pallas_call(
            unpack_kernel,
            out_shape=(
                jax.ShapeDtypeStruct((512, 128), BF16),
                jax.ShapeDtypeStruct((27, 32, 64), F32),
                jax.ShapeDtypeStruct((27, 64, 64), F32),
            ),
            in_specs=[vmem, vmem, vmem],
            out_specs=(anywhere, anywhere, anywhere),
            scratch_shapes=[
                pltpu.VMEM((27, 32, 64), F32),
                dma((3,)),
            ],
            compiler_params=pltpu.CompilerParams(vmem_limit_bytes=40 * 2**20),
        )(block, fin1, g2)
        return out.reshape(1, 512, 128), g1, g2

    in_specs = (
        P("rep", None, "region"),
        P(),
        P(),
        P("rep", None, "region"),
        P("rep", "region", None),
        P("rep", "region", None),
    )
    out_specs = (P("rep", None, "region"), P(), P())
    return jax.shard_map(body, mesh=mesh, in_specs=in_specs, out_specs=out_specs, check_vma=False)
```

```python
import functools
import math

import jax
import jax.numpy as jnp
from jax import lax
from jax.experimental import pallas as pl
from jax.experimental.pallas import tpu as pltpu
from jax.sharding import PartitionSpec as P

MESH = pl.DeviceIdType.MESH
F32 = jnp.float32
BF16 = jnp.bfloat16
ROWS = (0, 80, 16)
ROWS_FIRST = (0, 80, 16, 144, 208)
PAIRS_SECOND = 16
PAIRS_FIRST = 8


def iota(shape, axis):
    return lax.broadcasted_iota(jnp.int32, shape, axis)


def dot(a, b):
    return jnp.dot(a, b, preferred_element_type=F32)


def dot_nt(a, b):
    return lax.dot_general(a, b, (((1,), (1,)), ((), ())), preferred_element_type=F32)


def places(sizes):
    nx, nz, ny = sizes
    region = lax.axis_index("region")
    rep = lax.axis_index("rep")
    return region // nz, lax.rem(region, nz), rep // 2, lax.rem(rep, 2), region, rep


def main_kernel(
    sizes,
    scale,
    feat_hbm,
    w1_hbm,
    w2_hbm,
    cot_hbm,
    nbr_ref,
    mask_hbm,
    out_ref,
    fin1_ref,
    g2_ref,
    feat_ref,
    w1_ref,
    w2_ref,
    cot_ref,
    mask_ref,
    live_ref,
    field_ref,
    face_ref,
    halo_ref,
    side_ref,
    far_ref,
    c1_ref,
    c2_ref,
    c3_ref,
    w1b_ref,
    w2b_ref,
    acc_ref,
    slope_ref,
    full1_ref,
    full2_ref,
    send1_ref,
    send2_ref,
    pair1_ref,
    pair2_ref,
    half1_ref,
    half2_ref,
    plane1_ref,
    plane2_ref,
    line1_ref,
    line2_ref,
    fin2_ref,
    load_sem,
    halo_send,
    halo_recv,
    sum_send,
    sum_recv,
):
    nx, nz, ny = sizes
    n_region, n_plane = nx * nz, nx * ny
    my_x, my_z, my_y, core, region, rep = places(sizes)
    member = my_x * ny + my_y
    right = lax.rem(region + 1, n_region)
    left = lax.rem(region + n_region - 1, n_region)
    twin = {"region": region, "rep": my_y * 2 + 1 - core}
    plane_peers = []
    for step in range(1, n_plane):
        other = lax.rem(member + step, n_plane)
        at = {"region": (other // ny) * nz + my_z, "rep": lax.rem(other, ny) * 2 + core}
        plane_peers.append((step, other, at))
    line_peers = [
        {"region": my_x * nz + lax.rem(my_z + step, nz), "rep": rep} for step in range(1, nz)
    ]

    halo_ref[...] = jnp.zeros((3, 2, 64, 128), BF16)

    barrier = pltpu.get_barrier_semaphore()
    partners = [{"region": right, "rep": rep}, {"region": left, "rep": rep}, twin]
    partners += [at for _, _, at in plane_peers] + line_peers
    for at in partners:
        pl.semaphore_signal(barrier, inc=1, device_id=at, device_id_type=MESH)
    loads = [
        pltpu.make_async_copy(src, dst, load_sem.at[i])
        for i, (src, dst) in enumerate(
            (
                (mask_hbm, mask_ref),
                (feat_hbm, feat_ref),
                (w1_hbm, w1_ref),
                (w2_hbm, w2_ref),
                (cot_hbm, cot_ref),
            )
        )
    ]
    for load in loads:
        load.start()
    loads[0].wait()
    loads[1].wait()

    mask = jnp.concatenate([mask_ref[...].astype(F32), jnp.zeros((6, 512), F32)], axis=0).T
    tile_of = (iota((8, 128), 1) // 64 == iota((8, 128), 0)).astype(F32)
    tile_of_first = (lax.rem(iota((8, 128), 1) // 32, 2) == iota((8, 128), 0)).astype(F32)
    live_ref[...] = dot(mask, tile_of).reshape(8, 64, 128)
    twice = (iota((64, 128), 0) == lax.rem(iota((64, 128), 1), 64)).astype(BF16)
    spread = dot(feat_ref[...].T, twice) * dot(mask, tile_of_first)
    field_ref[...] = spread.reshape(8, 64, 128)
    face_ref[...] = spread.astype(BF16).reshape(8, 64, 128)

    def halo_copy(which, side):
        return pltpu.make_async_remote_copy(
            src_ref=face_ref.at[7 if side == 0 else 0],
            dst_ref=halo_ref.at[which, side],
            send_sem=halo_send.at[which, side],
            recv_sem=halo_recv.at[which, side],
            device_id={"region": right if side == 0 else left, "rep": rep},
            device_id_type=MESH,
        )

    has_right, has_left = region < n_region - 1, region > 0

    def halo_start(which):
        pl.when(has_right)(lambda: halo_copy(which, 0).start())
        pl.when(has_left)(lambda: halo_copy(which, 1).start())

    def halo_wait(which):
        @pl.when(has_left)
        def _():
            halo_copy(which, 0).wait_recv()

        @pl.when(has_right)
        def _():
            halo_copy(which, 1).wait_recv()

        pl.when(has_right)(lambda: halo_copy(which, 0).wait_send())
        pl.when(has_left)(lambda: halo_copy(which, 1).wait_send())

    pl.semaphore_wait(barrier, len(partners))
    halo_start(0)

    loads[2].wait()
    eye = iota((64, 256), 0)
    put = ((eye == iota((64, 256), 1)) | (eye == iota((64, 256), 1) - 192)).astype(BF16)
    spread1 = dot(w1_ref[...].reshape(27 * 32, 64), put).astype(BF16)
    top = spread1[:, :128].reshape(3, 3, 3, 32, 128)
    low = spread1[:, 128:].reshape(3, 3, 3, 32, 128)
    for b in range(3):
        for at, c in ((0, 0), (64, 2)):
            w1b_ref[:, b, at : at + 32, :] = top[:, b, c]
            w1b_ref[:, b, at + 32 : at + 64, :] = low[:, b, c]
    for at, b in ((0, 0), (64, 2)):
        w1b_ref[:, 3, at : at + 32, :] = top[:, b, 1]
        w1b_ref[:, 3, at + 32 : at + 64, :] = low[:, b, 1]
    w1b_ref[:, 4, 0:32, :] = top[:, 1, 1]
    w1b_ref[:, 4, 32:64, :] = low[:, 1, 1]
    w1b_ref[:, 4, 64:128, :] = jnp.zeros((3, 64, 128), BF16)
    loads[3].wait()
    spread2 = dot(w2_ref[...].reshape(27 * 64, 64), put).astype(BF16)
    top = spread2[:, :128].reshape(27, 64, 128)
    low = spread2[:, 128:].reshape(27, 64, 128)
    for k in range(27):
        a, b, c = k // 9, k // 3 % 3, k % 3
        w2b_ref[b, 3 * c + a, 0:64, :] = top[k]
        w2b_ref[b, 3 * c + a, 64:128, :] = low[k]

    side_ref[2] = jnp.zeros((8, 64, 128), F32)
    far_ref[:, 2] = jnp.zeros((2, 64, 128), F32)
    lane = iota((8, 128), 1)
    first_half = lane < 64
    even_quarter = lax.rem(lane // 32, 2) == 0
    z_row = iota((8, 128), 0)
    z_first, z_last = z_row == 0, z_row == 7

    def rows_of(masked, count):
        return jnp.concatenate([masked] * count, axis=0) if count > 1 else masked

    def split_first():
        source, target = iota((128, 256), 0), iota((128, 256), 1)
        return (source == (target // 128) * 32 + lax.rem(target, 32)).astype(BF16)

    def split_second():
        source, target = iota((128, 256), 0), iota((128, 256), 1)
        return (source == (target // 128) * 64 + lax.rem(target, 64)).astype(BF16)

    def shifted(middle, load, tile_lane):
        ext = []
        for c in range(3):
            groups = [load(0, c, 56, 64)]
            if c == 1 and middle is not None:
                mid = middle
            else:
                mid = load(1, c, 0, 64)
            groups += [mid[8 * y : 8 * y + 8] for y in range(8)]
            groups.append(load(2, c, 0, 8))
            ext.append(groups)
        down = [pltpu.roll(jnp.where(z_last, ext[0][y], ext[1][y]), 1, 0) for y in range(10)]
        up = [pltpu.roll(jnp.where(z_first, ext[2][y], ext[1][y]), 7, 0) for y in range(10)]
        return down, ext[1], up

    def store_first(c_ref, slab, down, mid, up):
        both = [jnp.where(first_half, d, u) for d, u in zip(down, up)]
        c_ref[slab, 0:80, :] = jnp.concatenate(both, axis=0).astype(BF16)
        c_ref[slab, 80:144, :] = jnp.concatenate(both[1:9], axis=0).astype(BF16)
        ends = [jnp.where(first_half, mid[y], mid[y + 2]) for y in range(8)]
        c_ref[slab, 144:208, :] = jnp.concatenate(ends, axis=0).astype(BF16)
        c_ref[slab, 208:272, :] = jnp.concatenate(mid[1:9], axis=0).astype(BF16)

    def store_second(c_ref, slab, down, mid, up):
        for c, groups in enumerate((down, mid, up)):
            c_ref[c, slab, 0:80, :] = jnp.concatenate(groups, axis=0).astype(BF16)
            c_ref[c, slab, 80:144, :] = jnp.concatenate(groups[1:9], axis=0).astype(BF16)

    def build_inner(c_ref, store, splitter, tile_lane):
        whole = dot(face_ref[...].reshape(512, 128), splitter)
        side_ref[0] = whole[:, :128].reshape(8, 64, 128)
        side_ref[1] = whole[:, 128:].reshape(8, 64, 128)
        named = [
            [jnp.minimum(jnp.maximum(nbr_ref[t, 9 + k] - 2, 0), 2) for k in range(9)]
            for t in range(2)
        ]

        @pl.loop(0, 8, unroll=4)
        def _(x):
            def load(b, c, start, stop):
                k = 3 * b + c
                return jnp.where(
                    rows_of(tile_lane, (stop - start) // 8),
                    side_ref[named[0][k], x, start:stop, :],
                    side_ref[named[1][k], x, start:stop, :],
                )

            store(c_ref, x + 1, *shifted(field_ref[x], load, tile_lane))

    def build_faces(which, c_ref, store, splitter, tile_lane):
        for side in range(2):
            whole = dot(halo_ref[which, side], splitter)
            far_ref[side, 0] = whole[:, :128]
            far_ref[side, 1] = whole[:, 128:]
            named = [
                [
                    jnp.minimum(jnp.maximum(nbr_ref[t, 18 * side + k] - 4 * side, 0), 2)
                    for k in range(9)
                ]
                for t in range(2)
            ]

            def load(b, c, start, stop):
                k = 3 * b + c
                return jnp.where(
                    rows_of(tile_lane, (stop - start) // 8),
                    far_ref[side, named[0][k], start:stop, :],
                    far_ref[side, named[1][k], start:stop, :],
                )

            store(c_ref, 9 * side, *shifted(None, load, tile_lane))

    for x in (0, 9):
        c1_ref[x] = jnp.zeros((272, 128), BF16)
        c2_ref[:, x] = jnp.zeros((3, 144, 128), BF16)
        c3_ref[:, x] = jnp.zeros((3, 144, 128), BF16)

    def conv_first():
        acc_ref[...] = jnp.zeros((512, 128), F32)

        @pl.loop(0, 3)
        def _(a):
            windows = [c1_ref[pl.ds(a, 8), r : r + 64, :].reshape(512, 128) for r in ROWS_FIRST]
            acc_ref[...] += dot(jnp.concatenate(windows, axis=1), w1b_ref[a].reshape(5 * 128, 128))

    def faces_first():
        for a, slab, at in ((0, 0, 0), (2, 9, 448)):
            windows = [c1_ref[slab, r : r + 64, :] for r in ROWS_FIRST]
            acc_ref[at : at + 64] += dot(
                jnp.concatenate(windows, axis=1), w1b_ref[a].reshape(5 * 128, 128)
            )

    def weight_second(b, blocks):
        return jnp.concatenate([w2b_ref[b, n] for n in blocks], axis=0)

    def weight_back(b, blocks):
        return jnp.concatenate([w2b_ref[2 - b, 8 - n] for n in blocks], axis=1)

    def conv_second(c_ref, weight, product):
        acc_ref[...] = jnp.zeros((512, 128), F32)

        @pl.loop(0, 3)
        def _(b):
            rows = pl.ds(pl.multiple_of(80 * b * (2 - b) + 8 * b * (b - 1), 16), 64)
            windows = [
                c_ref[c, a : a + 8, rows, :].reshape(512, 128) for c in range(3) for a in range(3)
            ]
            acc_ref[...] += product(jnp.concatenate(windows, axis=1), weight(b, range(9)))

    def faces_second(c_ref, weight, product, join):
        for a, slab, at in ((0, 0, 0), (2, 9, 448)):
            windows = [
                c_ref[c, slab, ROWS[b] : ROWS[b] + 64, :] for b in range(3) for c in range(3)
            ]
            weights = [weight(b, range(a, 9, 3)) for b in range(3)]
            acc_ref[at : at + 64] += product(
                jnp.concatenate(windows, axis=1), jnp.concatenate(weights, axis=join)
            )

    def layer(which, c_ref, store, splitter, tile_lane, inner, faces, activate, between=None):
        build_inner(c_ref, store, splitter, tile_lane)
        inner()
        if between is not None:
            between()
        pl.loop(1, 7, unroll=3)(activate)
        halo_wait(which)
        build_faces(which, c_ref, store, splitter, tile_lane)
        faces()
        pl.loop(0, 2, unroll=2)(lambda i: activate(7 * i))

    def hidden_of(x):
        rows = pl.ds(pl.multiple_of(x * 64, 64), 64)
        pre = acc_ref[rows, :]
        live = live_ref[x]
        sig = jax.nn.sigmoid(pre)
        hidden = (live * pre * sig).astype(BF16)
        face_ref[x] = hidden
        field_ref[x] = hidden.astype(F32)
        slope_ref[x] = live * sig * (1.0 + pre * (1.0 - sig))

    def outputs_of(x):
        rows = pl.ds(pl.multiple_of(x * 64, 64), 64)
        pre = acc_ref[rows, :]
        live = live_ref[x]
        sig = jax.nn.sigmoid(pre)
        out_ref[rows, :] = (live * pre * sig).astype(BF16)
        upstream = cot_ref[rows, :].astype(F32)
        delta = (upstream * live * sig * (1.0 + pre * (1.0 - sig))).astype(BF16)
        face_ref[x] = delta
        field_ref[x] = delta.astype(F32)

    def back_of(x):
        rows = pl.ds(pl.multiple_of(x * 64, 64), 64)
        face_ref[x] = (acc_ref[rows, :] * slope_ref[x]).astype(BF16)

    layer(0, c1_ref, store_first, split_first(), even_quarter, conv_first, faces_first, hidden_of)
    halo_start(1)

    loads[4].wait()
    layer(
        1,
        c2_ref,
        store_second,
        split_second(),
        first_half,
        lambda: conv_second(c2_ref, weight_second, dot),
        lambda: faces_second(c2_ref, weight_second, dot, 0),
        outputs_of,
    )
    halo_start(2)

    wide_half = iota((64, 128), 1) < 64
    wide_quarter = lax.rem(iota((64, 128), 1) // 32, 2) == 0
    per_core1, per_core2 = PAIRS_FIRST // 2, PAIRS_SECOND // 2

    def put_gradient(full, send, per_core, pair, value):
        value = value.reshape(4, 16, 128)
        units = pl.ds((pair % per_core) * 4, 4)
        full[pair // per_core, units] = value
        send[pair // per_core, units] = value.astype(BF16)

    delta_t = face_ref[...].reshape(512, 128).T
    for pair in range(14):
        both = []
        for k in (2 * pair, min(2 * pair + 1, 26)):
            a, b, c = k // 9, k // 3 % 3, k % 3
            window = c2_ref[c, a : a + 8, ROWS[b] : ROWS[b] + 64, :]
            both.append(window.reshape(512, 128))
        got = dot(delta_t, jnp.concatenate(both, axis=1))
        one, two = got[:, :128], got[:, 128:]
        straight = jnp.where(wide_half, one[0:64], two[64:128])
        crossed = jnp.where(wide_half, two[0:64], one[64:128])
        put_gradient(full2_ref, send2_ref, per_core2, pair, straight + pltpu.roll(crossed, 64, 1))
    for pair in range(14, PAIRS_SECOND):
        put_gradient(full2_ref, send2_ref, per_core2, pair, jnp.zeros((64, 128), F32))

    def reducer(which, per_core, full, send, pair, half, plane, line, fin):
        unit = 4 * per_core // n_plane

        def remote(stage, src, dst, device):
            return pltpu.make_async_remote_copy(
                src_ref=src,
                dst_ref=dst,
                send_sem=sum_send.at[which, stage],
                recv_sem=sum_recv.at[which, stage],
                device_id=device,
                device_id_type=MESH,
            )

        mine = fin.at[core, pl.ds(member * unit, unit)]
        plane_part = plane.at[pl.ds(1, n_plane - 1)]
        line_part = line.at[pl.ds(0, nz - 1)]
        back_part = fin.at[core, pl.ds(0, (n_plane - 1) * unit)]
        whole = [
            remote(0, send.at[1 - core], pair, twin),
            remote(1, plane_part, plane_part, twin),
            remote(2, line_part, line_part, twin),
            remote(3, back_part, back_part, twin),
            remote(4, fin.at[core], fin.at[core], twin),
        ]

        def start_pair():
            whole[0].start()

        def start_plane():
            whole[0].wait_recv()
            total = full[core] + pair[...].astype(F32)
            full[core] = total
            half[...] = total.astype(BF16)
            for step, other, at in plane_peers:
                remote(1, half.at[pl.ds(other * unit, unit)], plane.at[step], at).start()

        def start_line():
            whole[1].wait_recv()
            total = full[core, pl.ds(member * unit, unit)]
            for step in range(1, n_plane):
                total = total + plane[step].astype(F32)
            line[my_z] = total.astype(BF16)
            for at in line_peers:
                remote(2, line.at[my_z], line.at[my_z], at).start()

        def start_back():
            whole[2].wait_recv()
            total = line[0].astype(F32)
            for z in range(1, nz):
                total = total + line[z].astype(F32)
            fin[core, pl.ds(member * unit, unit)] = (total * scale).astype(BF16)
            for _, _, at in plane_peers:
                remote(3, mine, mine, at).start()

        def start_twin():
            whole[3].wait_recv()
            whole[4].start()

        def finish():
            whole[4].wait_recv()

        def sent():
            for copy in whole:
                copy.wait_send()

        return start_pair, start_plane, start_line, start_back, start_twin, finish, sent

    sum1 = reducer(
        0, per_core1, full1_ref, send1_ref, pair1_ref, half1_ref, plane1_ref, line1_ref, fin1_ref
    )
    sum2 = reducer(
        1, per_core2, full2_ref, send2_ref, pair2_ref, half2_ref, plane2_ref, line2_ref, fin2_ref
    )
    sum2[0]()

    layer(
        2,
        c3_ref,
        store_second,
        split_second(),
        first_half,
        lambda: conv_second(c3_ref, weight_back, dot_nt),
        lambda: faces_second(c3_ref, weight_back, dot_nt, 1),
        back_of,
        sum2[1],
    )
    delta_t = face_ref[...].reshape(512, 128).T
    for pair in range(PAIRS_FIRST):
        both = []
        for block in (2 * pair, min(2 * pair + 1, 14)):
            a, r = block // 5, ROWS_FIRST[block % 5]
            both.append(c1_ref[a : a + 8, r : r + 64, :].reshape(512, 128))
        got = dot(delta_t, jnp.concatenate(both, axis=1))
        one, two = got[:, :128], got[:, 128:]
        straight = jnp.where(wide_quarter, one[0:64], two[64:128])
        crossed = jnp.where(wide_quarter, two[0:64], one[64:128])
        swapped = jnp.where(wide_quarter, pltpu.roll(crossed, 96, 1), pltpu.roll(crossed, 32, 1))
        put_gradient(full1_ref, send1_ref, per_core1, pair, straight + swapped)
    sum1[0]()
    sum2[2]()
    sum1[1]()
    sum2[3]()
    sum1[2]()
    sum2[4]()
    sum1[3]()
    sum2[5]()
    for pair in range(14):
        units = pl.ds((pair % per_core2) * 4, 4)
        value = fin2_ref[pair // per_core2, units].reshape(64, 128).astype(F32).T
        g2_ref[2 * pair] = value[0:64]
        if pair < 13:
            g2_ref[2 * pair + 1] = value[64:128]
    sum1[4]()
    sum2[6]()
    sum1[5]()
    sum1[6]()


def unpack_kernel(block_ref, fin_ref, g2_ref, out_hbm, g1_hbm, g2_hbm, g1_ref, sem):
    block_copy = pltpu.make_async_copy(block_ref, out_hbm, sem.at[0])
    second_copy = pltpu.make_async_copy(g2_ref, g2_hbm, sem.at[1])
    first_copy = pltpu.make_async_copy(g1_ref, g1_hbm, sem.at[2])
    second_copy.start()
    block_copy.start()
    for pair in range(PAIRS_FIRST):
        at = (pair % (PAIRS_FIRST // 2)) * 4
        value = fin_ref[pair // (PAIRS_FIRST // 2), at : at + 4].reshape(64, 128).astype(F32).T
        for j in range(2):
            block = 2 * pair + j
            if block > 14:
                continue
            a, kind = block // 5, block % 5
            if kind < 3:
                offsets = (9 * a + 3 * kind, 9 * a + 3 * kind + 2)
            elif kind == 3:
                offsets = (9 * a + 1, 9 * a + 7)
            else:
                offsets = (9 * a + 4,)
            for i, k in enumerate(offsets):
                g1_ref[k] = value[64 * i + 32 * j : 64 * i + 32 * j + 32]
    first_copy.start()
    second_copy.wait()
    block_copy.wait()
    first_copy.wait()


def solution(mesh):
    n_region, n_rep = mesh.shape["region"], mesh.shape["rep"]
    nx, ny = (4, 4) if n_region == 32 else (2, n_rep // 2)
    nz = n_region // nx
    sizes = (nx, nz, ny)
    n_plane = nx * ny
    core1, core2 = 2 * PAIRS_FIRST, 2 * PAIRS_SECOND
    unit1, unit2 = core1 // n_plane, core2 // n_plane
    vmem = pl.BlockSpec(memory_space=pltpu.VMEM)
    smem = pl.BlockSpec(memory_space=pltpu.SMEM)
    hbm = pl.BlockSpec(memory_space=pltpu.HBM)
    anywhere = pl.BlockSpec(memory_space=pl.ANY)
    dma = pltpu.SemaphoreType.DMA

    def body(features, weight_first, weight_second, cotangent, neighbours, voxel_mask):
        scale = 1.0 / math.sqrt(n_rep * 2 * n_region * 512)
        block, fin1, g2 = pl.pallas_call(
            functools.partial(main_kernel, sizes, scale),
            out_shape=(
                jax.ShapeDtypeStruct((512, 128), BF16),
                jax.ShapeDtypeStruct((2, core1, 16, 128), BF16),
                jax.ShapeDtypeStruct((27, 64, 64), F32),
            ),
            in_specs=[hbm, hbm, hbm, hbm, smem, hbm],
            out_specs=(vmem, vmem, vmem),
            scratch_shapes=[
                pltpu.VMEM((64, 512), BF16),
                pltpu.VMEM((27, 32, 64), BF16),
                pltpu.VMEM((27, 64, 64), BF16),
                pltpu.VMEM((512, 128), BF16),
                pltpu.VMEM((2, 512), jnp.int32),
                pltpu.VMEM((8, 64, 128), F32),
                pltpu.VMEM((8, 64, 128), F32),
                pltpu.VMEM((8, 64, 128), BF16),
                pltpu.VMEM((3, 2, 64, 128), BF16),
                pltpu.VMEM((3, 8, 64, 128), F32),
                pltpu.VMEM((2, 3, 64, 128), F32),
                pltpu.VMEM((10, 272, 128), BF16),
                pltpu.VMEM((3, 10, 144, 128), BF16),
                pltpu.VMEM((3, 10, 144, 128), BF16),
                pltpu.VMEM((3, 5, 128, 128), BF16),
                pltpu.VMEM((3, 9, 128, 128), BF16),
                pltpu.VMEM((512, 128), F32),
                pltpu.VMEM((8, 64, 128), F32),
                pltpu.VMEM((2, core1, 16, 128), F32),
                pltpu.VMEM((2, core2, 16, 128), F32),
                pltpu.VMEM((2, core1, 16, 128), BF16),
                pltpu.VMEM((2, core2, 16, 128), BF16),
                pltpu.VMEM((core1, 16, 128), BF16),
                pltpu.VMEM((core2, 16, 128), BF16),
                pltpu.VMEM((core1, 16, 128), BF16),
                pltpu.VMEM((core2, 16, 128), BF16),
                pltpu.VMEM((n_plane, unit1, 16, 128), BF16),
                pltpu.VMEM((n_plane, unit2, 16, 128), BF16),
                pltpu.VMEM((nz, unit1, 16, 128), BF16),
                pltpu.VMEM((nz, unit2, 16, 128), BF16),
                pltpu.VMEM((2, core2, 16, 128), BF16),
                dma((5,)),
                dma((3, 2)),
                dma((3, 2)),
                dma((2, 5)),
                dma((2, 5)),
            ],
            compiler_params=pltpu.CompilerParams(
                collective_id=0, has_side_effects=True, vmem_limit_bytes=40 * 2**20
            ),
        )(
            *(
                pltpu.with_memory_space_constraint(x, pltpu.HBM)
                for x in (
                    jnp.swapaxes(features, 1, 2).reshape(64, 512),
                    weight_first,
                    weight_second,
                    cotangent.reshape(512, 128),
                    neighbours.reshape(2, 27),
                    voxel_mask.reshape(2, 512),
                )
            )
        )
        out, g1, g2 = pl.pallas_call(
            unpack_kernel,
            out_shape=(
                jax.ShapeDtypeStruct((512, 128), BF16),
                jax.ShapeDtypeStruct((27, 32, 64), F32),
                jax.ShapeDtypeStruct((27, 64, 64), F32),
            ),
            in_specs=[vmem, vmem, vmem],
            out_specs=(anywhere, anywhere, anywhere),
            scratch_shapes=[
                pltpu.VMEM((27, 32, 64), F32),
                dma((3,)),
            ],
            compiler_params=pltpu.CompilerParams(vmem_limit_bytes=40 * 2**20),
        )(block, fin1, g2)
        return out.reshape(1, 512, 128), g1, g2

    in_specs = (
        P("rep", None, "region"),
        P(),
        P(),
        P("rep", None, "region"),
        P("rep", "region", None),
        P("rep", "region", None),
    )
    out_specs = (P("rep", None, "region"), P(), P())
    return jax.shard_map(body, mesh=mesh, in_specs=in_specs, out_specs=out_specs, check_vma=False)
```

```python
import functools
import math

import jax
import jax.numpy as jnp
from jax import lax
from jax.experimental import pallas as pl
from jax.experimental.pallas import tpu as pltpu
from jax.sharding import PartitionSpec as P

MESH = pl.DeviceIdType.MESH
F32 = jnp.float32
BF16 = jnp.bfloat16
ROWS = (0, 80, 16)
ROWS_FIRST = (0, 80, 16, 144, 208)
PAIRS_SECOND = 16
PAIRS_FIRST = 8


def iota(shape, axis):
    return lax.broadcasted_iota(jnp.int32, shape, axis)


def dot(a, b):
    return jnp.dot(a, b, preferred_element_type=F32)


def dot_nt(a, b):
    return lax.dot_general(a, b, (((1,), (1,)), ((), ())), preferred_element_type=F32)


def places(sizes):
    nx, nz, ny = sizes
    region = lax.axis_index("region")
    rep = lax.axis_index("rep")
    return region // nz, lax.rem(region, nz), rep // 2, lax.rem(rep, 2), region, rep


def main_kernel(
    sizes,
    scale,
    feat_hbm,
    w1_hbm,
    w2_hbm,
    cot_hbm,
    nbr_ref,
    mask_hbm,
    out_ref,
    fin1_ref,
    g2_ref,
    feat_ref,
    w1_ref,
    w2_ref,
    cot_ref,
    mask_ref,
    live_ref,
    field_ref,
    face_ref,
    halo_ref,
    side_ref,
    far_ref,
    c1_ref,
    c2_ref,
    c3_ref,
    w1b_ref,
    w2b_ref,
    acc_ref,
    slope_ref,
    full1_ref,
    full2_ref,
    send1_ref,
    send2_ref,
    pair2_ref,
    half2_ref,
    mine2_ref,
    parts1_ref,
    parts2_ref,
    line1_ref,
    line2_ref,
    fin2_ref,
    load_sem,
    halo_send,
    halo_recv,
    pair_sem,
    sum_send,
    sum_recv,
):
    nx, nz, ny = sizes
    n_region, n_plane = nx * nz, nx * ny
    my_x, my_z, my_y, core, region, rep = places(sizes)
    member = my_x * ny + my_y
    right = lax.rem(region + 1, n_region)
    left = lax.rem(region + n_region - 1, n_region)
    twin = {"region": region, "rep": my_y * 2 + 1 - core}

    def apart(offset, size):
        return min(offset, size - offset)

    offsets = sorted(
        ((dx, dy, dc) for dx in range(nx) for dy in range(ny) for dc in range(2)),
        key=lambda d: (-apart(d[0], nx) - apart(d[1], ny), d),
    )
    plane_peers, all_peers = [], []
    for dx, dy, dc in offsets:
        if (dx, dy, dc) == (0, 0, 0):
            continue
        x, y, c = lax.rem(my_x + dx, nx), lax.rem(my_y + dy, ny), lax.rem(core + dc, 2)
        at = {"region": x * nz + my_z, "rep": y * 2 + c}
        all_peers.append((c * n_plane + x * ny + y, at))
        if dc == 0:
            plane_peers.append((x * ny + y, at))
    line_peers = [
        {"region": my_x * nz + lax.rem(my_z + step, nz), "rep": rep}
        for step in sorted(range(1, nz), key=lambda d: -apart(d, nz))
    ]

    halo_ref[...] = jnp.zeros((3, 2, 64, 128), BF16)

    barrier = pltpu.get_barrier_semaphore()
    partners = [{"region": right, "rep": rep}, {"region": left, "rep": rep}]
    partners += [at for _, at in all_peers] + line_peers
    for at in partners:
        pl.semaphore_signal(barrier, inc=1, device_id=at, device_id_type=MESH)
    loads = [
        pltpu.make_async_copy(src, dst, load_sem.at[i])
        for i, (src, dst) in enumerate(
            (
                (mask_hbm, mask_ref),
                (feat_hbm, feat_ref),
                (w1_hbm, w1_ref),
                (w2_hbm, w2_ref),
                (cot_hbm, cot_ref),
            )
        )
    ]
    for load in loads:
        load.start()
    loads[0].wait()
    loads[1].wait()

    mask = jnp.concatenate([mask_ref[...].astype(F32), jnp.zeros((6, 512), F32)], axis=0).T
    tile_of = (iota((8, 128), 1) // 64 == iota((8, 128), 0)).astype(F32)
    tile_of_first = (lax.rem(iota((8, 128), 1) // 32, 2) == iota((8, 128), 0)).astype(F32)
    live_ref[...] = dot(mask, tile_of).reshape(8, 64, 128)
    twice = (iota((64, 128), 0) == lax.rem(iota((64, 128), 1), 64)).astype(BF16)
    spread = dot(feat_ref[...].T, twice) * dot(mask, tile_of_first)
    field_ref[...] = spread.reshape(8, 64, 128)
    face_ref[...] = spread.astype(BF16).reshape(8, 64, 128)

    def halo_copy(which, side):
        return pltpu.make_async_remote_copy(
            src_ref=face_ref.at[7 if side == 0 else 0],
            dst_ref=halo_ref.at[which, side],
            send_sem=halo_send.at[which, side],
            recv_sem=halo_recv.at[which, side],
            device_id={"region": right if side == 0 else left, "rep": rep},
            device_id_type=MESH,
        )

    has_right, has_left = region < n_region - 1, region > 0

    def halo_start(which):
        pl.when(has_right)(lambda: halo_copy(which, 0).start())
        pl.when(has_left)(lambda: halo_copy(which, 1).start())

    def halo_wait(which):
        @pl.when(has_left)
        def _():
            halo_copy(which, 0).wait_recv()

        @pl.when(has_right)
        def _():
            halo_copy(which, 1).wait_recv()

        pl.when(has_right)(lambda: halo_copy(which, 0).wait_send())
        pl.when(has_left)(lambda: halo_copy(which, 1).wait_send())

    pl.semaphore_wait(barrier, len(partners))
    halo_start(0)

    loads[2].wait()
    eye = iota((64, 256), 0)
    put = ((eye == iota((64, 256), 1)) | (eye == iota((64, 256), 1) - 192)).astype(BF16)
    spread1 = dot(w1_ref[...].reshape(27 * 32, 64), put).astype(BF16)
    top = spread1[:, :128].reshape(3, 3, 3, 32, 128)
    low = spread1[:, 128:].reshape(3, 3, 3, 32, 128)
    for b in range(3):
        for at, c in ((0, 0), (64, 2)):
            w1b_ref[:, b, at : at + 32, :] = top[:, b, c]
            w1b_ref[:, b, at + 32 : at + 64, :] = low[:, b, c]
    for at, b in ((0, 0), (64, 2)):
        w1b_ref[:, 3, at : at + 32, :] = top[:, b, 1]
        w1b_ref[:, 3, at + 32 : at + 64, :] = low[:, b, 1]
    w1b_ref[:, 4, 0:32, :] = top[:, 1, 1]
    w1b_ref[:, 4, 32:64, :] = low[:, 1, 1]
    w1b_ref[:, 4, 64:128, :] = jnp.zeros((3, 64, 128), BF16)
    side_ref[2] = jnp.zeros((8, 64, 128), F32)
    far_ref[:, 2] = jnp.zeros((2, 64, 128), F32)
    lane = iota((8, 128), 1)
    first_half = lane < 64
    even_quarter = lax.rem(lane // 32, 2) == 0
    z_row = iota((8, 128), 0)
    z_first, z_last = z_row == 0, z_row == 7

    def rows_of(masked, count):
        return jnp.concatenate([masked] * count, axis=0) if count > 1 else masked

    def split_first():
        source, target = iota((128, 256), 0), iota((128, 256), 1)
        return (source == (target // 128) * 32 + lax.rem(target, 32)).astype(BF16)

    def split_second():
        source, target = iota((128, 256), 0), iota((128, 256), 1)
        return (source == (target // 128) * 64 + lax.rem(target, 64)).astype(BF16)

    def shifted(middle, load, tile_lane):
        ext = []
        for c in range(3):
            groups = [load(0, c, 56, 64)]
            if c == 1 and middle is not None:
                mid = middle
            else:
                mid = load(1, c, 0, 64)
            groups += [mid[8 * y : 8 * y + 8] for y in range(8)]
            groups.append(load(2, c, 0, 8))
            ext.append(groups)
        down = [pltpu.roll(jnp.where(z_last, ext[0][y], ext[1][y]), 1, 0) for y in range(10)]
        up = [pltpu.roll(jnp.where(z_first, ext[2][y], ext[1][y]), 7, 0) for y in range(10)]
        return down, ext[1], up

    def store_first(c_ref, slab, down, mid, up):
        both = [jnp.where(first_half, d, u) for d, u in zip(down, up)]
        c_ref[slab, 0:80, :] = jnp.concatenate(both, axis=0).astype(BF16)
        c_ref[slab, 80:144, :] = jnp.concatenate(both[1:9], axis=0).astype(BF16)
        ends = [jnp.where(first_half, mid[y], mid[y + 2]) for y in range(8)]
        c_ref[slab, 144:208, :] = jnp.concatenate(ends, axis=0).astype(BF16)
        c_ref[slab, 208:272, :] = jnp.concatenate(mid[1:9], axis=0).astype(BF16)

    def store_second(c_ref, slab, down, mid, up):
        for c, groups in enumerate((down, mid, up)):
            c_ref[c, slab, 0:80, :] = jnp.concatenate(groups, axis=0).astype(BF16)
            c_ref[c, slab, 80:144, :] = jnp.concatenate(groups[1:9], axis=0).astype(BF16)

    def build_inner(c_ref, store, splitter, tile_lane):
        whole = dot(face_ref[...].reshape(512, 128), splitter)
        side_ref[0] = whole[:, :128].reshape(8, 64, 128)
        side_ref[1] = whole[:, 128:].reshape(8, 64, 128)
        named = [
            [jnp.minimum(jnp.maximum(nbr_ref[t, 9 + k] - 2, 0), 2) for k in range(9)]
            for t in range(2)
        ]

        @pl.loop(0, 8, unroll=4)
        def _(x):
            def load(b, c, start, stop):
                k = 3 * b + c
                return jnp.where(
                    rows_of(tile_lane, (stop - start) // 8),
                    side_ref[named[0][k], x, start:stop, :],
                    side_ref[named[1][k], x, start:stop, :],
                )

            store(c_ref, x + 1, *shifted(field_ref[x], load, tile_lane))

    def build_faces(which, c_ref, store, splitter, tile_lane):
        for side in range(2):
            whole = dot(halo_ref[which, side], splitter)
            far_ref[side, 0] = whole[:, :128]
            far_ref[side, 1] = whole[:, 128:]
            named = [
                [
                    jnp.minimum(jnp.maximum(nbr_ref[t, 18 * side + k] - 4 * side, 0), 2)
                    for k in range(9)
                ]
                for t in range(2)
            ]

            def load(b, c, start, stop):
                k = 3 * b + c
                return jnp.where(
                    rows_of(tile_lane, (stop - start) // 8),
                    far_ref[side, named[0][k], start:stop, :],
                    far_ref[side, named[1][k], start:stop, :],
                )

            store(c_ref, 9 * side, *shifted(None, load, tile_lane))

    def windows_first(start, count):
        return [
            c1_ref[start : start + count, r : r + 64, :].reshape(count * 64, 128)
            for r in ROWS_FIRST
        ]

    def windows_second(c_ref, start, count):
        return [
            c_ref[c, start : start + count, ROWS[b] : ROWS[b] + 64, :].reshape(count * 64, 128)
            for b in range(3)
            for c in range(3)
        ]

    def conv_inner(windows, weight, product=dot):
        acc_ref[...] = product(jnp.concatenate(windows(1, 8), axis=1), weight(1))
        acc_ref[64:512] += product(jnp.concatenate(windows(1, 7), axis=1), weight(0))
        acc_ref[0:448] += product(jnp.concatenate(windows(2, 7), axis=1), weight(2))

    def conv_faces(windows, weight, product=dot):
        acc_ref[0:64] += product(jnp.concatenate(windows(0, 1), axis=1), weight(0))
        acc_ref[448:512] += product(jnp.concatenate(windows(9, 1), axis=1), weight(2))

    def weight_first(a):
        return w1b_ref[a].reshape(5 * 128, 128)

    def weight_second(a):
        return w2b_ref[9 * a : 9 * a + 9].reshape(9 * 128, 128)

    def weight_back(a):
        return jnp.concatenate([w2b_ref[26 - k] for k in range(9 * a, 9 * a + 9)], axis=1)

    def layer(which, c_ref, store, splitter, tile_lane, windows, weight, product, activate, between=None):
        build_inner(c_ref, store, splitter, tile_lane)
        conv_inner(windows, weight, product)
        if between is not None:
            between()
        pl.loop(1, 7, unroll=3)(activate)
        halo_wait(which)
        build_faces(which, c_ref, store, splitter, tile_lane)
        conv_faces(windows, weight, product)
        pl.loop(0, 2, unroll=2)(lambda i: activate(7 * i))

    def hidden_of(x):
        rows = pl.ds(pl.multiple_of(x * 64, 64), 64)
        pre = acc_ref[rows, :]
        live = live_ref[x]
        sig = jax.nn.sigmoid(pre)
        hidden = (live * pre * sig).astype(BF16)
        face_ref[x] = hidden
        field_ref[x] = hidden.astype(F32)
        slope_ref[x] = live * sig * (1.0 + pre * (1.0 - sig))

    def outputs_of(x):
        rows = pl.ds(pl.multiple_of(x * 64, 64), 64)
        pre = acc_ref[rows, :]
        live = live_ref[x]
        sig = jax.nn.sigmoid(pre)
        out_ref[rows, :] = (live * pre * sig).astype(BF16)
        upstream = cot_ref[rows, :].astype(F32)
        delta = (upstream * live * sig * (1.0 + pre * (1.0 - sig))).astype(BF16)
        face_ref[x] = delta
        field_ref[x] = delta.astype(F32)

    def back_of(x):
        rows = pl.ds(pl.multiple_of(x * 64, 64), 64)
        face_ref[x] = (acc_ref[rows, :] * slope_ref[x]).astype(BF16)

    layer(0, c1_ref, store_first, split_first(), even_quarter, windows_first, weight_first, dot, hidden_of)
    halo_start(1)

    loads[3].wait()
    spread2 = dot(w2_ref[...].reshape(27 * 64, 64), put).astype(BF16)
    w2b_ref[:, 0:64, :] = spread2[:, :128].reshape(27, 64, 128)
    w2b_ref[:, 64:128, :] = spread2[:, 128:].reshape(27, 64, 128)
    second = functools.partial(windows_second, c2_ref)
    loads[4].wait()
    layer(1, c2_ref, store_second, split_second(), first_half, second, weight_second, dot, outputs_of)
    halo_start(2)

    wide_half = iota((64, 128), 1) < 64
    wide_quarter = lax.rem(iota((64, 128), 1) // 32, 2) == 0
    per_core1, per_core2 = PAIRS_FIRST // 2, PAIRS_SECOND // 2

    def put_gradient(full, send, pair, value):
        value = value.reshape(4, 16, 128)
        full[4 * pair : 4 * pair + 4] = value
        send[4 * pair : 4 * pair + 4] = value.astype(BF16)

    delta_t = face_ref[...].reshape(512, 128).T
    for pair in range(14):
        both = []
        for k in (2 * pair, min(2 * pair + 1, 26)):
            a, b, c = k // 9, k // 3 % 3, k % 3
            window = c2_ref[c, a : a + 8, ROWS[b] : ROWS[b] + 64, :]
            both.append(window.reshape(512, 128))
        got = dot(delta_t, jnp.concatenate(both, axis=1))
        one, two = got[:, :128], got[:, 128:]
        straight = jnp.where(wide_half, one[0:64], two[64:128])
        crossed = jnp.where(wide_half, two[0:64], one[64:128])
        put_gradient(full2_ref, send2_ref, pair, straight + pltpu.roll(crossed, 64, 1))
    for pair in range(14, PAIRS_SECOND):
        put_gradient(full2_ref, send2_ref, pair, jnp.zeros((64, 128), F32))

    def reducer(which, unit, send, parts, line, fin):
        half = n_plane * unit

        def remote(stage, src, dst, device):
            return pltpu.make_async_remote_copy(
                src_ref=src,
                dst_ref=dst,
                send_sem=sum_send.at[which, stage],
                recv_sem=sum_recv.at[which, stage],
                device_id=device,
                device_id_type=MESH,
            )

        place = pl.ds((core * n_plane + member) * unit, unit)
        parts_whole = parts.at[pl.ds(1, parts.shape[0] - 1)]
        line_whole = line.at[pl.ds(0, nz - 1)]
        fin_whole = fin.at[pl.ds(0, (2 * n_plane - 1) * unit)]
        whole = [
            remote(0, parts_whole, parts_whole, twin),
            remote(1, line_whole, line_whole, twin),
            remote(2, fin_whole, fin_whole, twin),
        ]

        def start_parts(peers):
            for i, (other, at) in enumerate(peers):
                remote(0, send.at[pl.ds(other * unit, unit)], parts.at[i + 1], at).start()

        def start_line(own):
            whole[0].wait_recv()
            total = own
            for i in range(1, parts.shape[0]):
                total = total + parts[i].astype(F32)
            line[my_z] = total.astype(BF16)
            for at in line_peers:
                remote(1, line.at[my_z], line.at[my_z], at).start()

        def start_back():
            whole[1].wait_recv()
            total = line[0].astype(F32)
            for z in range(1, nz):
                total = total + line[z].astype(F32)
            fin[place] = (total * scale).astype(BF16)
            for _, at in all_peers:
                remote(2, fin.at[place], fin.at[place], at).start()

        def finish():
            whole[2].wait_recv()

        def sent():
            for copy in whole:
                copy.wait_send()

        return start_parts, start_line, start_back, finish, sent

    unit1, unit2 = 4 * per_core1 // n_plane, 4 * per_core2 // n_plane
    place1 = pl.ds((core * n_plane + member) * unit1, unit1)
    sum1 = reducer(0, unit1, send1_ref, parts1_ref, line1_ref, fin1_ref)
    sum2 = reducer(1, unit2, half2_ref, parts2_ref, line2_ref, fin2_ref)

    def half_units(which_core):
        return pl.ds(which_core * 4 * per_core2, 4 * per_core2)

    pair_copy = pltpu.make_async_remote_copy(
        src_ref=send2_ref.at[half_units(1 - core)],
        dst_ref=pair2_ref,
        send_sem=pair_sem.at[0],
        recv_sem=pair_sem.at[1],
        device_id=twin,
        device_id_type=MESH,
    )
    pair_copy.start()

    def start_second():
        pair_copy.wait_recv()
        total = full2_ref[half_units(core)] + pair2_ref[...].astype(F32)
        mine2_ref[...] = total
        half2_ref[...] = total.astype(BF16)
        sum2[0](plane_peers)

    third = functools.partial(windows_second, c3_ref)
    layer(2, c3_ref, store_second, split_second(), first_half, third, weight_back, dot_nt, back_of, start_second)
    delta_t = face_ref[...].reshape(512, 128).T
    for pair in range(PAIRS_FIRST):
        both = []
        for block in (2 * pair, min(2 * pair + 1, 14)):
            a, r = block // 5, ROWS_FIRST[block % 5]
            both.append(c1_ref[a : a + 8, r : r + 64, :].reshape(512, 128))
        got = dot(delta_t, jnp.concatenate(both, axis=1))
        one, two = got[:, :128], got[:, 128:]
        straight = jnp.where(wide_quarter, one[0:64], two[64:128])
        crossed = jnp.where(wide_quarter, two[0:64], one[64:128])
        swapped = jnp.where(wide_quarter, pltpu.roll(crossed, 96, 1), pltpu.roll(crossed, 32, 1))
        put_gradient(full1_ref, send1_ref, pair, straight + swapped)
    sum1[0](all_peers)
    sum2[1](mine2_ref[pl.ds(member * unit2, unit2)])
    sum1[1](full1_ref[place1])
    sum2[2]()
    sum1[2]()
    sum2[3]()
    for pair in range(14):
        value = fin2_ref[4 * pair : 4 * pair + 4].reshape(64, 128).astype(F32).T
        g2_ref[2 * pair] = value[0:64]
        if pair < 13:
            g2_ref[2 * pair + 1] = value[64:128]
    sum1[3]()
    pair_copy.wait_send()
    sum2[4]()
    sum1[4]()


def unpack_kernel(block_ref, fin_ref, g2_ref, out_hbm, g1_hbm, g2_hbm, g1_ref, sem):
    block_copy = pltpu.make_async_copy(block_ref, out_hbm, sem.at[0])
    second_copy = pltpu.make_async_copy(g2_ref, g2_hbm, sem.at[1])
    first_copy = pltpu.make_async_copy(g1_ref, g1_hbm, sem.at[2])
    second_copy.start()
    block_copy.start()
    for pair in range(PAIRS_FIRST):
        value = fin_ref[4 * pair : 4 * pair + 4].reshape(64, 128).astype(F32).T
        for j in range(2):
            block = 2 * pair + j
            if block > 14:
                continue
            a, kind = block // 5, block % 5
            if kind < 3:
                offsets = (9 * a + 3 * kind, 9 * a + 3 * kind + 2)
            elif kind == 3:
                offsets = (9 * a + 1, 9 * a + 7)
            else:
                offsets = (9 * a + 4,)
            for i, k in enumerate(offsets):
                g1_ref[k] = value[64 * i + 32 * j : 64 * i + 32 * j + 32]
    first_copy.start()
    second_copy.wait()
    block_copy.wait()
    first_copy.wait()


def solution(mesh):
    n_region, n_rep = mesh.shape["region"], mesh.shape["rep"]
    nx, ny = (4, 4) if n_region == 32 else (2, n_rep // 2)
    nz = n_region // nx
    sizes = (nx, nz, ny)
    n_plane = nx * ny
    core1, core2 = 2 * PAIRS_FIRST, 2 * PAIRS_SECOND
    unit1, unit2 = core1 // n_plane, core2 // n_plane
    vmem = pl.BlockSpec(memory_space=pltpu.VMEM)
    smem = pl.BlockSpec(memory_space=pltpu.SMEM)
    hbm = pl.BlockSpec(memory_space=pltpu.HBM)
    anywhere = pl.BlockSpec(memory_space=pl.ANY)
    dma = pltpu.SemaphoreType.DMA

    def body(features, weight_first, weight_second, cotangent, neighbours, voxel_mask):
        scale = 1.0 / math.sqrt(n_rep * 2 * n_region * 512)
        block, fin1, g2 = pl.pallas_call(
            functools.partial(main_kernel, sizes, scale),
            out_shape=(
                jax.ShapeDtypeStruct((512, 128), BF16),
                jax.ShapeDtypeStruct((2 * core1, 16, 128), BF16),
                jax.ShapeDtypeStruct((27, 64, 64), F32),
            ),
            in_specs=[hbm, hbm, hbm, hbm, smem, hbm],
            out_specs=(vmem, vmem, vmem),
            scratch_shapes=[
                pltpu.VMEM((64, 512), BF16),
                pltpu.VMEM((27, 32, 64), BF16),
                pltpu.VMEM((27, 64, 64), BF16),
                pltpu.VMEM((512, 128), BF16),
                pltpu.VMEM((2, 512), jnp.int32),
                pltpu.VMEM((8, 64, 128), F32),
                pltpu.VMEM((8, 64, 128), F32),
                pltpu.VMEM((8, 64, 128), BF16),
                pltpu.VMEM((3, 2, 64, 128), BF16),
                pltpu.VMEM((3, 8, 64, 128), F32),
                pltpu.VMEM((2, 3, 64, 128), F32),
                pltpu.VMEM((10, 272, 128), BF16),
                pltpu.VMEM((3, 10, 144, 128), BF16),
                pltpu.VMEM((3, 10, 144, 128), BF16),
                pltpu.VMEM((3, 5, 128, 128), BF16),
                pltpu.VMEM((27, 128, 128), BF16),
                pltpu.VMEM((512, 128), F32),
                pltpu.VMEM((8, 64, 128), F32),
                pltpu.VMEM((2 * core1, 16, 128), F32),
                pltpu.VMEM((2 * core2, 16, 128), F32),
                pltpu.VMEM((2 * core1, 16, 128), BF16),
                pltpu.VMEM((2 * core2, 16, 128), BF16),
                pltpu.VMEM((core2, 16, 128), BF16),
                pltpu.VMEM((core2, 16, 128), BF16),
                pltpu.VMEM((core2, 16, 128), F32),
                pltpu.VMEM((2 * n_plane, unit1, 16, 128), BF16),
                pltpu.VMEM((n_plane, unit2, 16, 128), BF16),
                pltpu.VMEM((nz, unit1, 16, 128), BF16),
                pltpu.VMEM((nz, unit2, 16, 128), BF16),
                pltpu.VMEM((2 * core2, 16, 128), BF16),
                dma((5,)),
                dma((3, 2)),
                dma((3, 2)),
                dma((2,)),
                dma((2, 3)),
                dma((2, 3)),
            ],
            compiler_params=pltpu.CompilerParams(
                collective_id=0, has_side_effects=True, vmem_limit_bytes=40 * 2**20
            ),
        )(
            *(
                pltpu.with_memory_space_constraint(x, pltpu.HBM)
                for x in (
                    jnp.swapaxes(features, 1, 2).reshape(64, 512),
                    weight_first,
                    weight_second,
                    cotangent.reshape(512, 128),
                    neighbours.reshape(2, 27),
                    voxel_mask.reshape(2, 512),
                )
            )
        )
        out, g1, g2 = pl.pallas_call(
            unpack_kernel,
            out_shape=(
                jax.ShapeDtypeStruct((512, 128), BF16),
                jax.ShapeDtypeStruct((27, 32, 64), F32),
                jax.ShapeDtypeStruct((27, 64, 64), F32),
            ),
            in_specs=[vmem, vmem, vmem],
            out_specs=(anywhere, anywhere, anywhere),
            scratch_shapes=[
                pltpu.VMEM((27, 32, 64), F32),
                dma((3,)),
            ],
            compiler_params=pltpu.CompilerParams(vmem_limit_bytes=40 * 2**20),
        )(block, fin1, g2)
        return out.reshape(1, 512, 128), g1, g2

    in_specs = (
        P("rep", None, "region"),
        P(),
        P(),
        P("rep", None, "region"),
        P("rep", "region", None),
        P("rep", "region", None),
    )
    out_specs = (P("rep", None, "region"), P(), P())
    return jax.shard_map(body, mesh=mesh, in_specs=in_specs, out_specs=out_specs, check_vma=False)
```

```python
import functools
import math

import jax
import jax.numpy as jnp
from jax import lax
from jax.experimental import pallas as pl
from jax.experimental.pallas import tpu as pltpu
from jax.sharding import PartitionSpec as P

MESH = pl.DeviceIdType.MESH
F32 = jnp.float32
BF16 = jnp.bfloat16
ROWS = (0, 80, 16)
ROWS_FIRST = (0, 80, 16, 144, 208)
PAIRS_SECOND = 16
PAIRS_FIRST = 8


def iota(shape, axis):
    return lax.broadcasted_iota(jnp.int32, shape, axis)


def dot(a, b):
    return jnp.dot(a, b, preferred_element_type=F32)


def dot_nt(a, b):
    return lax.dot_general(a, b, (((1,), (1,)), ((), ())), preferred_element_type=F32)


def places(sizes):
    nx, nz, ny = sizes
    region = lax.axis_index("region")
    rep = lax.axis_index("rep")
    return region // nz, lax.rem(region, nz), rep // 2, lax.rem(rep, 2), region, rep


def main_kernel(
    sizes,
    scale,
    feat_hbm,
    w1_hbm,
    w2_hbm,
    cot_hbm,
    nbr_ref,
    mask_hbm,
    out_ref,
    fin1_ref,
    g2_ref,
    feat_ref,
    w1_ref,
    w2_ref,
    cot_ref,
    mask_ref,
    live_ref,
    field_ref,
    face_ref,
    halo_ref,
    side_ref,
    far_ref,
    c1_ref,
    c2_ref,
    c3_ref,
    w1b_ref,
    w2b_ref,
    acc_ref,
    slope_ref,
    full1_ref,
    full2_ref,
    send1_ref,
    send2_ref,
    parts1_ref,
    parts2_ref,
    line1_ref,
    line2_ref,
    fin2_ref,
    load_sem,
    halo_send,
    halo_recv,
    sum_send,
    sum_recv,
):
    nx, nz, ny = sizes
    n_region, n_plane = nx * nz, nx * ny
    my_x, my_z, my_y, core, region, rep = places(sizes)
    member = my_x * ny + my_y
    right = lax.rem(region + 1, n_region)
    left = lax.rem(region + n_region - 1, n_region)
    twin = {"region": region, "rep": my_y * 2 + 1 - core}

    def apart(offset, size):
        return min(offset, size - offset)

    offsets = sorted(
        ((dx, dy, dc) for dx in range(nx) for dy in range(ny) for dc in range(2)),
        key=lambda d: (-apart(d[0], nx) - apart(d[1], ny), d),
    )
    all_peers = []
    for dx, dy, dc in offsets:
        if (dx, dy, dc) == (0, 0, 0):
            continue
        x, y, c = lax.rem(my_x + dx, nx), lax.rem(my_y + dy, ny), lax.rem(core + dc, 2)
        at = {"region": x * nz + my_z, "rep": y * 2 + c}
        all_peers.append((c * n_plane + x * ny + y, at))
    line_peers = [
        {"region": my_x * nz + lax.rem(my_z + step, nz), "rep": rep}
        for step in sorted(range(1, nz), key=lambda d: -apart(d, nz))
    ]

    halo_ref[...] = jnp.zeros((3, 2, 64, 128), BF16)

    barrier = pltpu.get_barrier_semaphore()
    partners = [{"region": right, "rep": rep}, {"region": left, "rep": rep}]
    partners += [at for _, at in all_peers] + line_peers
    for at in partners:
        pl.semaphore_signal(barrier, inc=1, device_id=at, device_id_type=MESH)
    loads = [
        pltpu.make_async_copy(src, dst, load_sem.at[i])
        for i, (src, dst) in enumerate(
            (
                (mask_hbm, mask_ref),
                (feat_hbm, feat_ref),
                (w1_hbm, w1_ref),
                (w2_hbm, w2_ref),
                (cot_hbm, cot_ref),
            )
        )
    ]
    for load in loads:
        load.start()
    loads[0].wait()
    loads[1].wait()

    mask = jnp.concatenate([mask_ref[...].astype(F32), jnp.zeros((6, 512), F32)], axis=0).T
    tile_of = (iota((8, 128), 1) // 64 == iota((8, 128), 0)).astype(F32)
    tile_of_first = (lax.rem(iota((8, 128), 1) // 32, 2) == iota((8, 128), 0)).astype(F32)
    live_ref[...] = dot(mask, tile_of).reshape(8, 64, 128)
    twice = (iota((64, 128), 0) == lax.rem(iota((64, 128), 1), 64)).astype(BF16)
    spread = dot(feat_ref[...].T, twice) * dot(mask, tile_of_first)
    field_ref[...] = spread.reshape(8, 64, 128)
    face_ref[...] = spread.astype(BF16).reshape(8, 64, 128)

    def halo_copy(which, side):
        return pltpu.make_async_remote_copy(
            src_ref=face_ref.at[7 if side == 0 else 0],
            dst_ref=halo_ref.at[which, side],
            send_sem=halo_send.at[which, side],
            recv_sem=halo_recv.at[which, side],
            device_id={"region": right if side == 0 else left, "rep": rep},
            device_id_type=MESH,
        )

    has_right, has_left = region < n_region - 1, region > 0

    def halo_start(which):
        pl.when(has_right)(lambda: halo_copy(which, 0).start())
        pl.when(has_left)(lambda: halo_copy(which, 1).start())

    def halo_wait(which):
        @pl.when(has_left)
        def _():
            halo_copy(which, 0).wait_recv()

        @pl.when(has_right)
        def _():
            halo_copy(which, 1).wait_recv()

        pl.when(has_right)(lambda: halo_copy(which, 0).wait_send())
        pl.when(has_left)(lambda: halo_copy(which, 1).wait_send())

    pl.semaphore_wait(barrier, len(partners))
    halo_start(0)

    loads[2].wait()
    eye = iota((64, 256), 0)
    put = ((eye == iota((64, 256), 1)) | (eye == iota((64, 256), 1) - 192)).astype(BF16)
    spread1 = dot(w1_ref[...].reshape(27 * 32, 64), put).astype(BF16)
    top = spread1[:, :128].reshape(3, 3, 3, 32, 128)
    low = spread1[:, 128:].reshape(3, 3, 3, 32, 128)
    for b in range(3):
        for at, c in ((0, 0), (64, 2)):
            w1b_ref[:, b, at : at + 32, :] = top[:, b, c]
            w1b_ref[:, b, at + 32 : at + 64, :] = low[:, b, c]
    for at, b in ((0, 0), (64, 2)):
        w1b_ref[:, 3, at : at + 32, :] = top[:, b, 1]
        w1b_ref[:, 3, at + 32 : at + 64, :] = low[:, b, 1]
    w1b_ref[:, 4, 0:32, :] = top[:, 1, 1]
    w1b_ref[:, 4, 32:64, :] = low[:, 1, 1]
    w1b_ref[:, 4, 64:128, :] = jnp.zeros((3, 64, 128), BF16)
    side_ref[2] = jnp.zeros((8, 64, 128), F32)
    far_ref[:, 2] = jnp.zeros((2, 64, 128), F32)
    lane = iota((8, 128), 1)
    first_half = lane < 64
    even_quarter = lax.rem(lane // 32, 2) == 0
    z_row = iota((8, 128), 0)
    z_first, z_last = z_row == 0, z_row == 7

    def rows_of(masked, count):
        return jnp.concatenate([masked] * count, axis=0) if count > 1 else masked

    def split_first():
        source, target = iota((128, 256), 0), iota((128, 256), 1)
        return (source == (target // 128) * 32 + lax.rem(target, 32)).astype(BF16)

    def split_second():
        source, target = iota((128, 256), 0), iota((128, 256), 1)
        return (source == (target // 128) * 64 + lax.rem(target, 64)).astype(BF16)

    def shifted(middle, load, tile_lane):
        ext = []
        for c in range(3):
            groups = [load(0, c, 56, 64)]
            if c == 1 and middle is not None:
                mid = middle
            else:
                mid = load(1, c, 0, 64)
            groups += [mid[8 * y : 8 * y + 8] for y in range(8)]
            groups.append(load(2, c, 0, 8))
            ext.append(groups)
        down = [pltpu.roll(jnp.where(z_last, ext[0][y], ext[1][y]), 1, 0) for y in range(10)]
        up = [pltpu.roll(jnp.where(z_first, ext[2][y], ext[1][y]), 7, 0) for y in range(10)]
        return down, ext[1], up

    def store_first(c_ref, slab, down, mid, up):
        both = [jnp.where(first_half, d, u) for d, u in zip(down, up)]
        c_ref[slab, 0:80, :] = jnp.concatenate(both, axis=0).astype(BF16)
        c_ref[slab, 80:144, :] = jnp.concatenate(both[1:9], axis=0).astype(BF16)
        ends = [jnp.where(first_half, mid[y], mid[y + 2]) for y in range(8)]
        c_ref[slab, 144:208, :] = jnp.concatenate(ends, axis=0).astype(BF16)
        c_ref[slab, 208:272, :] = jnp.concatenate(mid[1:9], axis=0).astype(BF16)

    def store_second(c_ref, slab, down, mid, up):
        for c, groups in enumerate((down, mid, up)):
            c_ref[c, slab, 0:80, :] = jnp.concatenate(groups, axis=0).astype(BF16)
            c_ref[c, slab, 80:144, :] = jnp.concatenate(groups[1:9], axis=0).astype(BF16)

    def build_inner(c_ref, store, splitter, tile_lane):
        whole = dot(face_ref[...].reshape(512, 128), splitter)
        side_ref[0] = whole[:, :128].reshape(8, 64, 128)
        side_ref[1] = whole[:, 128:].reshape(8, 64, 128)
        named = [
            [jnp.minimum(jnp.maximum(nbr_ref[t, 9 + k] - 2, 0), 2) for k in range(9)]
            for t in range(2)
        ]

        @pl.loop(0, 8, unroll=4)
        def _(x):
            def load(b, c, start, stop):
                k = 3 * b + c
                return jnp.where(
                    rows_of(tile_lane, (stop - start) // 8),
                    side_ref[named[0][k], x, start:stop, :],
                    side_ref[named[1][k], x, start:stop, :],
                )

            store(c_ref, x + 1, *shifted(field_ref[x], load, tile_lane))

    def build_faces(which, c_ref, store, splitter, tile_lane):
        whole = dot(halo_ref[which].reshape(128, 128), splitter)
        for side in range(2):
            far_ref[side, 0] = whole[64 * side : 64 * side + 64, :128]
            far_ref[side, 1] = whole[64 * side : 64 * side + 64, 128:]
            named = [
                [
                    jnp.minimum(jnp.maximum(nbr_ref[t, 18 * side + k] - 4 * side, 0), 2)
                    for k in range(9)
                ]
                for t in range(2)
            ]

            def load(b, c, start, stop):
                k = 3 * b + c
                return jnp.where(
                    rows_of(tile_lane, (stop - start) // 8),
                    far_ref[side, named[0][k], start:stop, :],
                    far_ref[side, named[1][k], start:stop, :],
                )

            store(c_ref, 9 * side, *shifted(None, load, tile_lane))

    def windows_first(start, count):
        return [
            c1_ref[start : start + count, r : r + 64, :].reshape(count * 64, 128)
            for r in ROWS_FIRST
        ]

    def windows_second(c_ref, start, count):
        return [
            c_ref[c, start : start + count, ROWS[b] : ROWS[b] + 64, :].reshape(count * 64, 128)
            for b in range(3)
            for c in range(3)
        ]

    def conv_inner(windows, weight, product=dot, columns=1):
        weights = jnp.concatenate([weight(0), weight(2), weight(1)], axis=columns)
        got = product(jnp.concatenate(windows(1, 8), axis=1), weights)
        acc_ref[...] = got[:, 256:384]
        acc_ref[64:512] += got[0:448, 0:128]
        acc_ref[0:448] += got[64:512, 128:256]

    def conv_faces(windows, weight, product=dot, columns=1):
        weights = jnp.concatenate([weight(0), weight(2)], axis=columns)
        rows = [jnp.concatenate(both, axis=0) for both in zip(windows(0, 1), windows(9, 1))]
        got = product(jnp.concatenate(rows, axis=1), weights)
        acc_ref[0:64] += got[0:64, 0:128]
        acc_ref[448:512] += got[64:128, 128:256]

    def weight_first(a):
        return w1b_ref[a].reshape(5 * 128, 128)

    def weight_second(a):
        return w2b_ref[9 * a : 9 * a + 9].reshape(9 * 128, 128)

    def weight_back(a):
        return jnp.concatenate([w2b_ref[26 - k] for k in range(9 * a, 9 * a + 9)], axis=1)

    def layer(which, c_ref, store, splitter, tile_lane, windows, weight, product, columns, activate, between=None):
        build_inner(c_ref, store, splitter, tile_lane)
        conv_inner(windows, weight, product, columns)
        if between is not None:
            between()
        pl.loop(1, 7, unroll=3)(activate)
        halo_wait(which)
        build_faces(which, c_ref, store, splitter, tile_lane)
        conv_faces(windows, weight, product, columns)
        pl.loop(0, 2, unroll=2)(lambda i: activate(7 * i))

    def hidden_of(x):
        rows = pl.ds(pl.multiple_of(x * 64, 64), 64)
        pre = acc_ref[rows, :]
        live = live_ref[x]
        sig = jax.nn.sigmoid(pre)
        hidden = (live * pre * sig).astype(BF16)
        face_ref[x] = hidden
        field_ref[x] = hidden.astype(F32)
        slope_ref[x] = live * sig * (1.0 + pre * (1.0 - sig))

    def outputs_of(x):
        rows = pl.ds(pl.multiple_of(x * 64, 64), 64)
        pre = acc_ref[rows, :]
        live = live_ref[x]
        sig = jax.nn.sigmoid(pre)
        out_ref[rows, :] = (live * pre * sig).astype(BF16)
        upstream = cot_ref[rows, :].astype(F32)
        delta = (upstream * live * sig * (1.0 + pre * (1.0 - sig))).astype(BF16)
        face_ref[x] = delta
        field_ref[x] = delta.astype(F32)

    def back_of(x):
        rows = pl.ds(pl.multiple_of(x * 64, 64), 64)
        face_ref[x] = (acc_ref[rows, :] * slope_ref[x]).astype(BF16)

    layer(0, c1_ref, store_first, split_first(), even_quarter, windows_first, weight_first, dot, 1, hidden_of)
    halo_start(1)

    loads[3].wait()
    spread2 = dot(w2_ref[...].reshape(27 * 64, 64), put).astype(BF16)
    w2b_ref[:, 0:64, :] = spread2[:, :128].reshape(27, 64, 128)
    w2b_ref[:, 64:128, :] = spread2[:, 128:].reshape(27, 64, 128)
    second = functools.partial(windows_second, c2_ref)
    loads[4].wait()
    layer(1, c2_ref, store_second, split_second(), first_half, second, weight_second, dot, 1, outputs_of)
    halo_start(2)

    wide_half = iota((64, 128), 1) < 64
    wide_quarter = lax.rem(iota((64, 128), 1) // 32, 2) == 0
    per_core1, per_core2 = PAIRS_FIRST // 2, PAIRS_SECOND // 2

    def put_gradient(full, send, pair, value):
        value = value.reshape(4, 16, 128)
        full[4 * pair : 4 * pair + 4] = value
        send[4 * pair : 4 * pair + 4] = value.astype(BF16)

    delta_t = face_ref[...].reshape(512, 128).T
    for pair in range(14):
        both = []
        for k in (2 * pair, min(2 * pair + 1, 26)):
            a, b, c = k // 9, k // 3 % 3, k % 3
            window = c2_ref[c, a : a + 8, ROWS[b] : ROWS[b] + 64, :]
            both.append(window.reshape(512, 128))
        got = dot(delta_t, jnp.concatenate(both, axis=1))
        one, two = got[:, :128], got[:, 128:]
        straight = jnp.where(wide_half, one[0:64], two[64:128])
        crossed = jnp.where(wide_half, two[0:64], one[64:128])
        put_gradient(full2_ref, send2_ref, pair, straight + pltpu.roll(crossed, 64, 1))
    for pair in range(14, PAIRS_SECOND):
        put_gradient(full2_ref, send2_ref, pair, jnp.zeros((64, 128), F32))

    def reducer(which, unit, full, send, parts, line, fin):

        def remote(stage, src, dst, device):
            return pltpu.make_async_remote_copy(
                src_ref=src,
                dst_ref=dst,
                send_sem=sum_send.at[which, stage],
                recv_sem=sum_recv.at[which, stage],
                device_id=device,
                device_id_type=MESH,
            )

        place = pl.ds((core * n_plane + member) * unit, unit)
        parts_whole = parts.at[pl.ds(1, parts.shape[0] - 1)]
        line_whole = line.at[pl.ds(0, nz - 1)]
        fin_whole = fin.at[pl.ds(0, (2 * n_plane - 1) * unit)]
        whole = [
            remote(0, parts_whole, parts_whole, twin),
            remote(1, line_whole, line_whole, twin),
            remote(2, fin_whole, fin_whole, twin),
        ]

        def start_parts():
            for i, (other, at) in enumerate(all_peers):
                remote(0, send.at[pl.ds(other * unit, unit)], parts.at[i + 1], at).start()

        def start_line():
            whole[0].wait_recv()
            total = full[place]
            for i in range(1, parts.shape[0]):
                total = total + parts[i].astype(F32)
            line[my_z] = total.astype(BF16)
            for at in line_peers:
                remote(1, line.at[my_z], line.at[my_z], at).start()

        def start_back():
            whole[1].wait_recv()
            total = line[0].astype(F32)
            for z in range(1, nz):
                total = total + line[z].astype(F32)
            fin[place] = (total * scale).astype(BF16)
            for _, at in all_peers:
                remote(2, fin.at[place], fin.at[place], at).start()

        def finish():
            whole[2].wait_recv()

        def sent():
            for copy in whole:
                copy.wait_send()

        return start_parts, start_line, start_back, finish, sent

    unit1, unit2 = 4 * per_core1 // n_plane, 4 * per_core2 // n_plane
    sum1 = reducer(0, unit1, full1_ref, send1_ref, parts1_ref, line1_ref, fin1_ref)
    sum2 = reducer(1, unit2, full2_ref, send2_ref, parts2_ref, line2_ref, fin2_ref)
    sum2[0]()

    third = functools.partial(windows_second, c3_ref)
    layer(2, c3_ref, store_second, split_second(), first_half, third, weight_back, dot_nt, 0, back_of)
    delta_t = face_ref[...].reshape(512, 128).T
    for pair in range(PAIRS_FIRST):
        both = []
        for block in (2 * pair, min(2 * pair + 1, 14)):
            a, r = block // 5, ROWS_FIRST[block % 5]
            both.append(c1_ref[a : a + 8, r : r + 64, :].reshape(512, 128))
        got = dot(delta_t, jnp.concatenate(both, axis=1))
        one, two = got[:, :128], got[:, 128:]
        straight = jnp.where(wide_quarter, one[0:64], two[64:128])
        crossed = jnp.where(wide_quarter, two[0:64], one[64:128])
        swapped = jnp.where(wide_quarter, pltpu.roll(crossed, 96, 1), pltpu.roll(crossed, 32, 1))
        put_gradient(full1_ref, send1_ref, pair, straight + swapped)
    sum1[0]()
    sum2[1]()
    sum1[1]()
    sum2[2]()
    sum1[2]()
    sum2[3]()
    for pair in range(14):
        value = fin2_ref[4 * pair : 4 * pair + 4].reshape(64, 128).astype(F32).T
        g2_ref[2 * pair] = value[0:64]
        if pair < 13:
            g2_ref[2 * pair + 1] = value[64:128]
    sum1[3]()
    sum2[4]()
    sum1[4]()


def unpack_kernel(block_ref, fin_ref, g2_ref, out_hbm, g1_hbm, g2_hbm, g1_ref, sem):
    block_copy = pltpu.make_async_copy(block_ref, out_hbm, sem.at[0])
    second_copies = [
        pltpu.make_async_copy(g2_ref.at[pl.ds(k, 9)], g2_hbm.at[pl.ds(k, 9)], sem.at[3 + k // 9])
        for k in (0, 9, 18)
    ]
    first_copy = pltpu.make_async_copy(g1_ref, g1_hbm, sem.at[2])
    for copy in second_copies:
        copy.start()
    block_copy.start()
    for pair in range(PAIRS_FIRST):
        value = fin_ref[4 * pair : 4 * pair + 4].reshape(64, 128).astype(F32).T
        for j in range(2):
            block = 2 * pair + j
            if block > 14:
                continue
            a, kind = block // 5, block % 5
            if kind < 3:
                offsets = (9 * a + 3 * kind, 9 * a + 3 * kind + 2)
            elif kind == 3:
                offsets = (9 * a + 1, 9 * a + 7)
            else:
                offsets = (9 * a + 4,)
            for i, k in enumerate(offsets):
                g1_ref[k] = value[64 * i + 32 * j : 64 * i + 32 * j + 32]
    first_copy.start()
    for copy in second_copies:
        copy.wait()
    block_copy.wait()
    first_copy.wait()


def solution(mesh):
    n_region, n_rep = mesh.shape["region"], mesh.shape["rep"]
    nx, ny = (4, 4) if n_region == 32 else (2, n_rep // 2)
    nz = n_region // nx
    sizes = (nx, nz, ny)
    n_plane = nx * ny
    core1, core2 = 2 * PAIRS_FIRST, 2 * PAIRS_SECOND
    unit1, unit2 = core1 // n_plane, core2 // n_plane
    vmem = pl.BlockSpec(memory_space=pltpu.VMEM)
    smem = pl.BlockSpec(memory_space=pltpu.SMEM)
    hbm = pl.BlockSpec(memory_space=pltpu.HBM)
    anywhere = pl.BlockSpec(memory_space=pl.ANY)
    dma = pltpu.SemaphoreType.DMA

    def body(features, weight_first, weight_second, cotangent, neighbours, voxel_mask):
        scale = 1.0 / math.sqrt(n_rep * 2 * n_region * 512)
        block, fin1, g2 = pl.pallas_call(
            functools.partial(main_kernel, sizes, scale),
            out_shape=(
                jax.ShapeDtypeStruct((512, 128), BF16),
                jax.ShapeDtypeStruct((2 * core1, 16, 128), BF16),
                jax.ShapeDtypeStruct((27, 64, 64), F32),
            ),
            in_specs=[hbm, hbm, hbm, hbm, smem, hbm],
            out_specs=(vmem, vmem, vmem),
            scratch_shapes=[
                pltpu.VMEM((64, 512), BF16),
                pltpu.VMEM((27, 32, 64), BF16),
                pltpu.VMEM((27, 64, 64), BF16),
                pltpu.VMEM((512, 128), BF16),
                pltpu.VMEM((2, 512), jnp.int32),
                pltpu.VMEM((8, 64, 128), F32),
                pltpu.VMEM((8, 64, 128), F32),
                pltpu.VMEM((8, 64, 128), BF16),
                pltpu.VMEM((3, 2, 64, 128), BF16),
                pltpu.VMEM((3, 8, 64, 128), F32),
                pltpu.VMEM((2, 3, 64, 128), F32),
                pltpu.VMEM((10, 272, 128), BF16),
                pltpu.VMEM((3, 10, 144, 128), BF16),
                pltpu.VMEM((3, 10, 144, 128), BF16),
                pltpu.VMEM((3, 5, 128, 128), BF16),
                pltpu.VMEM((27, 128, 128), BF16),
                pltpu.VMEM((512, 128), F32),
                pltpu.VMEM((8, 64, 128), F32),
                pltpu.VMEM((2 * core1, 16, 128), F32),
                pltpu.VMEM((2 * core2, 16, 128), F32),
                pltpu.VMEM((2 * core1, 16, 128), BF16),
                pltpu.VMEM((2 * core2, 16, 128), BF16),
                pltpu.VMEM((2 * n_plane, unit1, 16, 128), BF16),
                pltpu.VMEM((2 * n_plane, unit2, 16, 128), BF16),
                pltpu.VMEM((nz, unit1, 16, 128), BF16),
                pltpu.VMEM((nz, unit2, 16, 128), BF16),
                pltpu.VMEM((2 * core2, 16, 128), BF16),
                dma((5,)),
                dma((3, 2)),
                dma((3, 2)),
                dma((2, 3)),
                dma((2, 3)),
            ],
            compiler_params=pltpu.CompilerParams(
                collective_id=0, has_side_effects=True, vmem_limit_bytes=40 * 2**20
            ),
        )(
            *(
                pltpu.with_memory_space_constraint(x, pltpu.HBM)
                for x in (
                    jnp.swapaxes(features, 1, 2).reshape(64, 512),
                    weight_first,
                    weight_second,
                    cotangent.reshape(512, 128),
                    neighbours.reshape(2, 27),
                    voxel_mask.reshape(2, 512),
                )
            )
        )
        out, g1, g2 = pl.pallas_call(
            unpack_kernel,
            out_shape=(
                jax.ShapeDtypeStruct((512, 128), BF16),
                jax.ShapeDtypeStruct((27, 32, 64), F32),
                jax.ShapeDtypeStruct((27, 64, 64), F32),
            ),
            in_specs=[vmem, vmem, vmem],
            out_specs=(anywhere, anywhere, anywhere),
            scratch_shapes=[
                pltpu.VMEM((27, 32, 64), F32),
                dma((6,)),
            ],
            compiler_params=pltpu.CompilerParams(vmem_limit_bytes=40 * 2**20),
        )(block, fin1, g2)
        return out.reshape(1, 512, 128), g1, g2

    in_specs = (
        P("rep", None, "region"),
        P(),
        P(),
        P("rep", None, "region"),
        P("rep", "region", None),
        P("rep", "region", None),
    )
    out_specs = (P("rep", None, "region"), P(), P())
    return jax.shard_map(body, mesh=mesh, in_specs=in_specs, out_specs=out_specs, check_vma=False)
```

```python
import functools
import math

import jax
import jax.numpy as jnp
from jax import lax
from jax.experimental import pallas as pl
from jax.experimental.pallas import tpu as pltpu
from jax.sharding import PartitionSpec as P

MESH = pl.DeviceIdType.MESH
F32 = jnp.float32
BF16 = jnp.bfloat16
ROWS = (0, 80, 16)
ROWS_FIRST = (0, 80, 16, 144, 208)
PAIRS_SECOND = 16
PAIRS_FIRST = 8


def iota(shape, axis):
    return lax.broadcasted_iota(jnp.int32, shape, axis)


def dot(a, b):
    return jnp.dot(a, b, preferred_element_type=F32)


def dot_nt(a, b):
    return lax.dot_general(a, b, (((1,), (1,)), ((), ())), preferred_element_type=F32)


def places(sizes):
    nx, nz, ny = sizes
    region = lax.axis_index("region")
    rep = lax.axis_index("rep")
    return region // nz, lax.rem(region, nz), rep // 2, lax.rem(rep, 2), region, rep


def main_kernel(
    sizes,
    scale,
    feat_hbm,
    w1_hbm,
    w2_hbm,
    cot_hbm,
    nbr_ref,
    mask_hbm,
    out_ref,
    fin1_ref,
    g2_ref,
    feat_ref,
    w1_ref,
    w2_ref,
    cot_ref,
    mask_ref,
    live_ref,
    field_ref,
    face_ref,
    halo_ref,
    side_ref,
    far_ref,
    c1_ref,
    c2_ref,
    c3_ref,
    w1b_ref,
    w2b_ref,
    acc_ref,
    slope_ref,
    full1_ref,
    full2_ref,
    send1_ref,
    send2_ref,
    parts1_ref,
    parts2_ref,
    line1_ref,
    line2_ref,
    fin2_ref,
    load_sem,
    halo_send,
    halo_recv,
    sum_send,
    sum_recv,
):
    nx, nz, ny = sizes
    n_region, n_plane = nx * nz, nx * ny
    my_x, my_z, my_y, core, region, rep = places(sizes)
    member = my_x * ny + my_y
    right = lax.rem(region + 1, n_region)
    left = lax.rem(region + n_region - 1, n_region)
    twin = {"region": region, "rep": my_y * 2 + 1 - core}

    def apart(offset, size):
        return min(offset, size - offset)

    offsets = sorted(
        ((dx, dy, dc) for dx in range(nx) for dy in range(ny) for dc in range(2)),
        key=lambda d: (-apart(d[0], nx) - apart(d[1], ny), d),
    )
    plane_peers, all_peers = [], []
    for dx, dy, dc in offsets:
        if (dx, dy, dc) == (0, 0, 0):
            continue
        x, y, c = lax.rem(my_x + dx, nx), lax.rem(my_y + dy, ny), lax.rem(core + dc, 2)
        at = {"region": x * nz + my_z, "rep": y * 2 + c}
        all_peers.append((c * n_plane + x * ny + y, at))
        if dc == 0:
            plane_peers.append(at)
    line_peers = [
        {"region": my_x * nz + lax.rem(my_z + step, nz), "rep": rep}
        for step in sorted(range(1, nz), key=lambda d: -apart(d, nz))
    ]

    halo_ref[...] = jnp.zeros((3, 2, 64, 128), BF16)

    barrier = pltpu.get_barrier_semaphore()
    partners = [{"region": right, "rep": rep}, {"region": left, "rep": rep}]
    partners += [at for _, at in all_peers] + line_peers
    for at in partners:
        pl.semaphore_signal(barrier, inc=1, device_id=at, device_id_type=MESH)
    loads = [
        pltpu.make_async_copy(src, dst, load_sem.at[i])
        for i, (src, dst) in enumerate(
            (
                (mask_hbm, mask_ref),
                (feat_hbm, feat_ref),
                (w1_hbm, w1_ref),
                (w2_hbm, w2_ref),
                (cot_hbm, cot_ref),
            )
        )
    ]
    for load in loads:
        load.start()
    loads[0].wait()
    loads[1].wait()

    mask = jnp.concatenate([mask_ref[...].astype(F32), jnp.zeros((6, 512), F32)], axis=0).T
    tile_of = (iota((8, 128), 1) // 64 == iota((8, 128), 0)).astype(F32)
    tile_of_first = (lax.rem(iota((8, 128), 1) // 32, 2) == iota((8, 128), 0)).astype(F32)
    live_ref[...] = dot(mask, tile_of).reshape(8, 64, 128)
    twice = (iota((64, 128), 0) == lax.rem(iota((64, 128), 1), 64)).astype(BF16)
    spread = dot(feat_ref[...].T, twice) * dot(mask, tile_of_first)
    field_ref[...] = spread.reshape(8, 64, 128)
    face_ref[...] = spread.astype(BF16).reshape(8, 64, 128)

    def halo_copy(which, side):
        return pltpu.make_async_remote_copy(
            src_ref=face_ref.at[7 if side == 0 else 0],
            dst_ref=halo_ref.at[which, side],
            send_sem=halo_send.at[which, side],
            recv_sem=halo_recv.at[which, side],
            device_id={"region": right if side == 0 else left, "rep": rep},
            device_id_type=MESH,
        )

    has_right, has_left = region < n_region - 1, region > 0

    def halo_start(which):
        pl.when(has_right)(lambda: halo_copy(which, 0).start())
        pl.when(has_left)(lambda: halo_copy(which, 1).start())

    def halo_wait(which):
        @pl.when(has_left)
        def _():
            halo_copy(which, 0).wait_recv()

        @pl.when(has_right)
        def _():
            halo_copy(which, 1).wait_recv()

        pl.when(has_right)(lambda: halo_copy(which, 0).wait_send())
        pl.when(has_left)(lambda: halo_copy(which, 1).wait_send())

    pl.semaphore_wait(barrier, len(partners))
    halo_start(0)

    loads[2].wait()
    eye = iota((64, 256), 0)
    put = ((eye == iota((64, 256), 1)) | (eye == iota((64, 256), 1) - 192)).astype(BF16)
    spread1 = dot(w1_ref[...].reshape(27 * 32, 64), put).astype(BF16)
    top = spread1[:, :128].reshape(3, 3, 3, 32, 128)
    low = spread1[:, 128:].reshape(3, 3, 3, 32, 128)
    for b in range(3):
        for at, c in ((0, 0), (64, 2)):
            w1b_ref[:, b, at : at + 32, :] = top[:, b, c]
            w1b_ref[:, b, at + 32 : at + 64, :] = low[:, b, c]
    for at, b in ((0, 0), (64, 2)):
        w1b_ref[:, 3, at : at + 32, :] = top[:, b, 1]
        w1b_ref[:, 3, at + 32 : at + 64, :] = low[:, b, 1]
    w1b_ref[:, 4, 0:32, :] = top[:, 1, 1]
    w1b_ref[:, 4, 32:64, :] = low[:, 1, 1]
    w1b_ref[:, 4, 64:128, :] = jnp.zeros((3, 64, 128), BF16)
    side_ref[2] = jnp.zeros((8, 64, 128), F32)
    far_ref[:, 2] = jnp.zeros((2, 64, 128), F32)
    lane = iota((8, 128), 1)
    first_half = lane < 64
    even_quarter = lax.rem(lane // 32, 2) == 0
    z_row = iota((8, 128), 0)
    z_first, z_last = z_row == 0, z_row == 7

    def rows_of(masked, count):
        return jnp.concatenate([masked] * count, axis=0) if count > 1 else masked

    def split_first():
        source, target = iota((128, 256), 0), iota((128, 256), 1)
        return (source == (target // 128) * 32 + lax.rem(target, 32)).astype(BF16)

    def split_second():
        source, target = iota((128, 256), 0), iota((128, 256), 1)
        return (source == (target // 128) * 64 + lax.rem(target, 64)).astype(BF16)

    def shifted(middle, load, tile_lane):
        ext = []
        for c in range(3):
            groups = [load(0, c, 56, 64)]
            if c == 1 and middle is not None:
                mid = middle
            else:
                mid = load(1, c, 0, 64)
            groups += [mid[8 * y : 8 * y + 8] for y in range(8)]
            groups.append(load(2, c, 0, 8))
            ext.append(groups)
        down = [pltpu.roll(jnp.where(z_last, ext[0][y], ext[1][y]), 1, 0) for y in range(10)]
        up = [pltpu.roll(jnp.where(z_first, ext[2][y], ext[1][y]), 7, 0) for y in range(10)]
        return down, ext[1], up

    def store_first(c_ref, slab, down, mid, up):
        both = [jnp.where(first_half, d, u) for d, u in zip(down, up)]
        c_ref[slab, 0:80, :] = jnp.concatenate(both, axis=0).astype(BF16)
        c_ref[slab, 80:144, :] = jnp.concatenate(both[1:9], axis=0).astype(BF16)
        ends = [jnp.where(first_half, mid[y], mid[y + 2]) for y in range(8)]
        c_ref[slab, 144:208, :] = jnp.concatenate(ends, axis=0).astype(BF16)
        c_ref[slab, 208:272, :] = jnp.concatenate(mid[1:9], axis=0).astype(BF16)

    def store_second(c_ref, slab, down, mid, up):
        for c, groups in enumerate((down, mid, up)):
            c_ref[c, slab, 0:80, :] = jnp.concatenate(groups, axis=0).astype(BF16)
            c_ref[c, slab, 80:144, :] = jnp.concatenate(groups[1:9], axis=0).astype(BF16)

    def build_inner(c_ref, store, splitter, tile_lane):
        whole = dot(face_ref[...].reshape(512, 128), splitter)
        side_ref[0] = whole[:, :128].reshape(8, 64, 128)
        side_ref[1] = whole[:, 128:].reshape(8, 64, 128)
        named = [
            [jnp.minimum(jnp.maximum(nbr_ref[t, 9 + k] - 2, 0), 2) for k in range(9)]
            for t in range(2)
        ]

        @pl.loop(0, 8, unroll=4)
        def _(x):
            def load(b, c, start, stop):
                k = 3 * b + c
                return jnp.where(
                    rows_of(tile_lane, (stop - start) // 8),
                    side_ref[named[0][k], x, start:stop, :],
                    side_ref[named[1][k], x, start:stop, :],
                )

            store(c_ref, x + 1, *shifted(field_ref[x], load, tile_lane))

    def build_faces(which, c_ref, store, splitter, tile_lane):
        whole = dot(halo_ref[which].reshape(128, 128), splitter)
        for side in range(2):
            far_ref[side, 0] = whole[64 * side : 64 * side + 64, :128]
            far_ref[side, 1] = whole[64 * side : 64 * side + 64, 128:]
            named = [
                [
                    jnp.minimum(jnp.maximum(nbr_ref[t, 18 * side + k] - 4 * side, 0), 2)
                    for k in range(9)
                ]
                for t in range(2)
            ]

            def load(b, c, start, stop):
                k = 3 * b + c
                return jnp.where(
                    rows_of(tile_lane, (stop - start) // 8),
                    far_ref[side, named[0][k], start:stop, :],
                    far_ref[side, named[1][k], start:stop, :],
                )

            store(c_ref, 9 * side, *shifted(None, load, tile_lane))

    def windows_first(start, count):
        return [
            c1_ref[start : start + count, r : r + 64, :].reshape(count * 64, 128)
            for r in ROWS_FIRST
        ]

    def windows_second(c_ref, start, count):
        return [
            c_ref[c, start : start + count, ROWS[b] : ROWS[b] + 64, :].reshape(count * 64, 128)
            for b in range(3)
            for c in range(3)
        ]

    def conv_inner(windows, weight, product=dot, columns=1):
        weights = jnp.concatenate([weight(0), weight(2), weight(1)], axis=columns)
        got = product(jnp.concatenate(windows(1, 8), axis=1), weights)
        acc_ref[...] = got[:, 256:384]
        acc_ref[64:512] += got[0:448, 0:128]
        acc_ref[0:448] += got[64:512, 128:256]

    def conv_faces(windows, weight, product=dot, columns=1):
        weights = jnp.concatenate([weight(0), weight(2)], axis=columns)
        rows = [jnp.concatenate(both, axis=0) for both in zip(windows(0, 1), windows(9, 1))]
        got = product(jnp.concatenate(rows, axis=1), weights)
        acc_ref[0:64] += got[0:64, 0:128]
        acc_ref[448:512] += got[64:128, 128:256]

    def weight_first(a):
        return w1b_ref[a].reshape(5 * 128, 128)

    def weight_second(a):
        return w2b_ref[9 * a : 9 * a + 9].reshape(9 * 128, 128)

    def weight_back(a):
        return jnp.concatenate([w2b_ref[26 - k] for k in range(9 * a, 9 * a + 9)], axis=1)

    def layer(which, c_ref, store, splitter, tile_lane, windows, weight, product, columns, activate, between=None):
        build_inner(c_ref, store, splitter, tile_lane)
        conv_inner(windows, weight, product, columns)
        if between is not None:
            between()
        pl.loop(1, 7, unroll=3)(activate)
        halo_wait(which)
        build_faces(which, c_ref, store, splitter, tile_lane)
        conv_faces(windows, weight, product, columns)
        pl.loop(0, 2, unroll=2)(lambda i: activate(7 * i))

    def hidden_of(x):
        rows = pl.ds(pl.multiple_of(x * 64, 64), 64)
        pre = acc_ref[rows, :]
        live = live_ref[x]
        sig = jax.nn.sigmoid(pre)
        hidden = (live * pre * sig).astype(BF16)
        face_ref[x] = hidden
        field_ref[x] = hidden.astype(F32)
        slope_ref[x] = live * sig * (1.0 + pre * (1.0 - sig))

    def outputs_of(x):
        rows = pl.ds(pl.multiple_of(x * 64, 64), 64)
        pre = acc_ref[rows, :]
        live = live_ref[x]
        sig = jax.nn.sigmoid(pre)
        out_ref[rows, :] = (live * pre * sig).astype(BF16)
        upstream = cot_ref[rows, :].astype(F32)
        delta = (upstream * live * sig * (1.0 + pre * (1.0 - sig))).astype(BF16)
        face_ref[x] = delta
        field_ref[x] = delta.astype(F32)

    def back_of(x):
        rows = pl.ds(pl.multiple_of(x * 64, 64), 64)
        face_ref[x] = (acc_ref[rows, :] * slope_ref[x]).astype(BF16)

    layer(0, c1_ref, store_first, split_first(), even_quarter, windows_first, weight_first, dot, 1, hidden_of)
    halo_start(1)

    loads[3].wait()
    spread2 = dot(w2_ref[...].reshape(27 * 64, 64), put).astype(BF16)
    w2b_ref[:, 0:64, :] = spread2[:, :128].reshape(27, 64, 128)
    w2b_ref[:, 64:128, :] = spread2[:, 128:].reshape(27, 64, 128)
    second = functools.partial(windows_second, c2_ref)
    loads[4].wait()
    layer(1, c2_ref, store_second, split_second(), first_half, second, weight_second, dot, 1, outputs_of)
    halo_start(2)

    wide_half = iota((64, 128), 1) < 64
    wide_quarter = lax.rem(iota((64, 128), 1) // 32, 2) == 0
    per_core1, per_core2 = PAIRS_FIRST // 2, PAIRS_SECOND // 2

    def put_gradient(full, send, pair, value):
        value = value.reshape(4, 16, 128)
        full[4 * pair : 4 * pair + 4] = value
        send[4 * pair : 4 * pair + 4] = value.astype(BF16)

    delta_t = face_ref[...].reshape(512, 128).T
    for pair in range(14):
        both = []
        for k in (2 * pair, min(2 * pair + 1, 26)):
            a, b, c = k // 9, k // 3 % 3, k % 3
            window = c2_ref[c, a : a + 8, ROWS[b] : ROWS[b] + 64, :]
            both.append(window.reshape(512, 128))
        got = dot(delta_t, jnp.concatenate(both, axis=1))
        one, two = got[:, :128], got[:, 128:]
        straight = jnp.where(wide_half, one[0:64], two[64:128])
        crossed = jnp.where(wide_half, two[0:64], one[64:128])
        put_gradient(full2_ref, send2_ref, pair, straight + pltpu.roll(crossed, 64, 1))
    for pair in range(14, PAIRS_SECOND):
        put_gradient(full2_ref, send2_ref, pair, jnp.zeros((64, 128), F32))

    def reducer(which, unit, full, send, parts, line, fin, back_peers):

        def remote(stage, src, dst, device):
            return pltpu.make_async_remote_copy(
                src_ref=src,
                dst_ref=dst,
                send_sem=sum_send.at[which, stage],
                recv_sem=sum_recv.at[which, stage],
                device_id=device,
                device_id_type=MESH,
            )

        place = pl.ds((core * n_plane + member) * unit, unit)
        parts_whole = parts.at[pl.ds(1, parts.shape[0] - 1)]
        line_whole = line.at[pl.ds(0, nz - 1)]
        fin_whole = fin.at[pl.ds(0, len(back_peers) * unit)]
        fin_half = fin.at[pl.ds(core * n_plane * unit, n_plane * unit)]
        whole = [
            remote(0, parts_whole, parts_whole, twin),
            remote(1, line_whole, line_whole, twin),
            remote(2, fin_whole, fin_whole, twin),
        ]

        def twin_copy():
            return remote(3, fin_half, fin_half, twin)

        def start_parts():
            for i, (other, at) in enumerate(all_peers):
                remote(0, send.at[pl.ds(other * unit, unit)], parts.at[i + 1], at).start()

        def start_line():
            whole[0].wait_recv()
            total = full[place]
            for i in range(1, parts.shape[0]):
                total = total + parts[i].astype(F32)
            line[my_z] = total.astype(BF16)
            for at in line_peers:
                remote(1, line.at[my_z], line.at[my_z], at).start()

        def start_back():
            whole[1].wait_recv()
            total = line[0].astype(F32)
            for z in range(1, nz):
                total = total + line[z].astype(F32)
            fin[place] = (total * scale).astype(BF16)
            for at in back_peers:
                remote(2, fin.at[place], fin.at[place], at).start()

        def finish():
            whole[2].wait_recv()

        def sent():
            for copy in whole:
                copy.wait_send()

        return start_parts, start_line, start_back, finish, sent, twin_copy

    unit1, unit2 = 4 * per_core1 // n_plane, 4 * per_core2 // n_plane
    sum1 = reducer(0, unit1, full1_ref, send1_ref, parts1_ref, line1_ref, fin1_ref, [at for _, at in all_peers])
    sum2 = reducer(1, unit2, full2_ref, send2_ref, parts2_ref, line2_ref, fin2_ref, plane_peers)
    sum2[0]()

    third = functools.partial(windows_second, c3_ref)
    layer(2, c3_ref, store_second, split_second(), first_half, third, weight_back, dot_nt, 0, back_of)
    delta_t = face_ref[...].reshape(512, 128).T
    for pair in range(PAIRS_FIRST):
        both = []
        for block in (2 * pair, min(2 * pair + 1, 14)):
            a, r = block // 5, ROWS_FIRST[block % 5]
            both.append(c1_ref[a : a + 8, r : r + 64, :].reshape(512, 128))
        got = dot(delta_t, jnp.concatenate(both, axis=1))
        one, two = got[:, :128], got[:, 128:]
        straight = jnp.where(wide_quarter, one[0:64], two[64:128])
        crossed = jnp.where(wide_quarter, two[0:64], one[64:128])
        swapped = jnp.where(wide_quarter, pltpu.roll(crossed, 96, 1), pltpu.roll(crossed, 32, 1))
        put_gradient(full1_ref, send1_ref, pair, straight + swapped)
    sum1[0]()
    sum2[1]()
    sum1[1]()
    sum2[2]()
    sum1[2]()
    sum2[3]()
    sum2[5]().start()

    def unpack_half(which_core):
        for i in range(per_core2):
            pair = which_core * per_core2 + i
            value = fin2_ref[pl.ds(4 * pair, 4)].reshape(64, 128).astype(F32).T
            g2_ref[pl.ds(2 * pair, 2)] = value.reshape(2, 64, 64)

    unpack_half(core)
    sum2[5]().wait_recv()
    unpack_half(1 - core)
    sum1[3]()
    sum2[4]()
    sum2[5]().wait_send()
    sum1[4]()


def unpack_kernel(block_ref, fin_ref, g2_ref, out_hbm, g1_hbm, g2_hbm, g1_ref, sem):
    block_copy = pltpu.make_async_copy(block_ref, out_hbm, sem.at[0])
    second_copies = [
        pltpu.make_async_copy(g2_ref.at[pl.ds(k, 9)], g2_hbm.at[pl.ds(k, 9)], sem.at[3 + k // 9])
        for k in (0, 9, 18)
    ]
    first_copy = pltpu.make_async_copy(g1_ref, g1_hbm, sem.at[2])
    for copy in second_copies:
        copy.start()
    block_copy.start()
    for pair in range(PAIRS_FIRST):
        value = fin_ref[4 * pair : 4 * pair + 4].reshape(64, 128).astype(F32).T
        for j in range(2):
            block = 2 * pair + j
            if block > 14:
                continue
            a, kind = block // 5, block % 5
            if kind < 3:
                offsets = (9 * a + 3 * kind, 9 * a + 3 * kind + 2)
            elif kind == 3:
                offsets = (9 * a + 1, 9 * a + 7)
            else:
                offsets = (9 * a + 4,)
            for i, k in enumerate(offsets):
                g1_ref[k] = value[64 * i + 32 * j : 64 * i + 32 * j + 32]
    first_copy.start()
    for copy in second_copies:
        copy.wait()
    block_copy.wait()
    first_copy.wait()


def solution(mesh):
    n_region, n_rep = mesh.shape["region"], mesh.shape["rep"]
    nx, ny = (4, 4) if n_region == 32 else (2, n_rep // 2)
    nz = n_region // nx
    sizes = (nx, nz, ny)
    n_plane = nx * ny
    core1, core2 = 2 * PAIRS_FIRST, 2 * PAIRS_SECOND
    unit1, unit2 = core1 // n_plane, core2 // n_plane
    vmem = pl.BlockSpec(memory_space=pltpu.VMEM)
    smem = pl.BlockSpec(memory_space=pltpu.SMEM)
    hbm = pl.BlockSpec(memory_space=pltpu.HBM)
    anywhere = pl.BlockSpec(memory_space=pl.ANY)
    dma = pltpu.SemaphoreType.DMA

    def body(features, weight_first, weight_second, cotangent, neighbours, voxel_mask):
        scale = 1.0 / math.sqrt(n_rep * 2 * n_region * 512)
        block, fin1, g2 = pl.pallas_call(
            functools.partial(main_kernel, sizes, scale),
            out_shape=(
                jax.ShapeDtypeStruct((512, 128), BF16),
                jax.ShapeDtypeStruct((2 * core1, 16, 128), BF16),
                jax.ShapeDtypeStruct((2 * PAIRS_SECOND, 64, 64), F32),
            ),
            in_specs=[hbm, hbm, hbm, hbm, smem, hbm],
            out_specs=(vmem, vmem, vmem),
            scratch_shapes=[
                pltpu.VMEM((64, 512), BF16),
                pltpu.VMEM((27, 32, 64), BF16),
                pltpu.VMEM((27, 64, 64), BF16),
                pltpu.VMEM((512, 128), BF16),
                pltpu.VMEM((2, 512), jnp.int32),
                pltpu.VMEM((8, 64, 128), F32),
                pltpu.VMEM((8, 64, 128), F32),
                pltpu.VMEM((8, 64, 128), BF16),
                pltpu.VMEM((3, 2, 64, 128), BF16),
                pltpu.VMEM((3, 8, 64, 128), F32),
                pltpu.VMEM((2, 3, 64, 128), F32),
                pltpu.VMEM((10, 272, 128), BF16),
                pltpu.VMEM((3, 10, 144, 128), BF16),
                pltpu.VMEM((3, 10, 144, 128), BF16),
                pltpu.VMEM((3, 5, 128, 128), BF16),
                pltpu.VMEM((27, 128, 128), BF16),
                pltpu.VMEM((512, 128), F32),
                pltpu.VMEM((8, 64, 128), F32),
                pltpu.VMEM((2 * core1, 16, 128), F32),
                pltpu.VMEM((2 * core2, 16, 128), F32),
                pltpu.VMEM((2 * core1, 16, 128), BF16),
                pltpu.VMEM((2 * core2, 16, 128), BF16),
                pltpu.VMEM((2 * n_plane, unit1, 16, 128), BF16),
                pltpu.VMEM((2 * n_plane, unit2, 16, 128), BF16),
                pltpu.VMEM((nz, unit1, 16, 128), BF16),
                pltpu.VMEM((nz, unit2, 16, 128), BF16),
                pltpu.VMEM((2 * core2, 16, 128), BF16),
                dma((5,)),
                dma((3, 2)),
                dma((3, 2)),
                dma((2, 4)),
                dma((2, 4)),
            ],
            compiler_params=pltpu.CompilerParams(
                collective_id=0, has_side_effects=True, vmem_limit_bytes=40 * 2**20
            ),
        )(
            *(
                pltpu.with_memory_space_constraint(x, pltpu.HBM)
                for x in (
                    jnp.swapaxes(features, 1, 2).reshape(64, 512),
                    weight_first,
                    weight_second,
                    cotangent.reshape(512, 128),
                    neighbours.reshape(2, 27),
                    voxel_mask.reshape(2, 512),
                )
            )
        )
        out, g1, g2 = pl.pallas_call(
            unpack_kernel,
            out_shape=(
                jax.ShapeDtypeStruct((512, 128), BF16),
                jax.ShapeDtypeStruct((27, 32, 64), F32),
                jax.ShapeDtypeStruct((27, 64, 64), F32),
            ),
            in_specs=[vmem, vmem, vmem],
            out_specs=(anywhere, anywhere, anywhere),
            scratch_shapes=[
                pltpu.VMEM((27, 32, 64), F32),
                dma((6,)),
            ],
            compiler_params=pltpu.CompilerParams(vmem_limit_bytes=40 * 2**20),
        )(block, fin1, g2)
        return out.reshape(1, 512, 128), g1, g2

    in_specs = (
        P("rep", None, "region"),
        P(),
        P(),
        P("rep", None, "region"),
        P("rep", "region", None),
        P("rep", "region", None),
    )
    out_specs = (P("rep", None, "region"), P(), P())
    return jax.shard_map(body, mesh=mesh, in_specs=in_specs, out_specs=out_specs, check_vma=False)
```

```python
import functools
import math

import jax
import jax.numpy as jnp
from jax import lax
from jax.experimental import pallas as pl
from jax.experimental.pallas import tpu as pltpu
from jax.sharding import PartitionSpec as P

MESH = pl.DeviceIdType.MESH
F32 = jnp.float32
BF16 = jnp.bfloat16
ROWS = (0, 80, 16)
ROWS_FIRST = (0, 80, 16, 144, 208)
PAIRS_SECOND = 16
PAIRS_FIRST = 8


def iota(shape, axis):
    return lax.broadcasted_iota(jnp.int32, shape, axis)


def dot(a, b):
    return jnp.dot(a, b, preferred_element_type=F32)


def dot_nt(a, b):
    return lax.dot_general(a, b, (((1,), (1,)), ((), ())), preferred_element_type=F32)


def places(sizes):
    nx, nz, ny = sizes
    region = lax.axis_index("region")
    rep = lax.axis_index("rep")
    return region // nz, lax.rem(region, nz), rep // 2, lax.rem(rep, 2), region, rep


def main_kernel(
    sizes,
    scale,
    feat_hbm,
    w1_hbm,
    w2_hbm,
    cot_hbm,
    nbr_ref,
    mask_hbm,
    out_ref,
    fin1_ref,
    g2_ref,
    feat_ref,
    w1_ref,
    w2_ref,
    cot_ref,
    mask_ref,
    live_ref,
    field_ref,
    face_ref,
    halo_ref,
    side_ref,
    far_ref,
    c1_ref,
    c2_ref,
    c3_ref,
    w1b_ref,
    w2b_ref,
    acc_ref,
    slope_ref,
    full1_ref,
    full2_ref,
    send1_ref,
    send2_ref,
    parts1_ref,
    parts2_ref,
    line1_ref,
    line2_ref,
    fin2_ref,
    load_sem,
    halo_send,
    halo_recv,
    sum_send,
    sum_recv,
):
    nx, nz, ny = sizes
    n_region, n_plane = nx * nz, nx * ny
    my_x, my_z, my_y, core, region, rep = places(sizes)
    member = my_x * ny + my_y
    right = lax.rem(region + 1, n_region)
    left = lax.rem(region + n_region - 1, n_region)
    twin = {"region": region, "rep": my_y * 2 + 1 - core}

    def apart(offset, size):
        return min(offset, size - offset)

    offsets = sorted(
        ((dx, dy, dc) for dx in range(nx) for dy in range(ny) for dc in range(2)),
        key=lambda d: (-apart(d[0], nx) - apart(d[1], ny), d),
    )
    all_peers = []
    for dx, dy, dc in offsets:
        if (dx, dy, dc) == (0, 0, 0):
            continue
        x, y, c = lax.rem(my_x + dx, nx), lax.rem(my_y + dy, ny), lax.rem(core + dc, 2)
        at = {"region": x * nz + my_z, "rep": y * 2 + c}
        all_peers.append((len(all_peers) + 1, c * n_plane + x * ny + y, at))
    line_peers = [
        {"region": my_x * nz + lax.rem(my_z + step, nz), "rep": rep}
        for step in sorted(range(1, nz), key=lambda d: -apart(d, nz))
    ]

    halo_ref[...] = jnp.zeros((3, 2, 64, 128), BF16)

    barrier = pltpu.get_barrier_semaphore()
    partners = [{"region": right, "rep": rep}, {"region": left, "rep": rep}]
    partners += [at for _, _, at in all_peers] + line_peers
    for at in partners[:2]:
        pl.semaphore_signal(barrier, inc=1, device_id=at, device_id_type=MESH)
    loads = [
        pltpu.make_async_copy(src, dst, load_sem.at[i])
        for i, (src, dst) in enumerate(
            (
                (mask_hbm, mask_ref),
                (feat_hbm, feat_ref),
                (w1_hbm, w1_ref),
                (w2_hbm, w2_ref),
                (cot_hbm, cot_ref),
            )
        )
    ]
    for load in loads:
        load.start()
    for at in partners[2:]:
        pl.semaphore_signal(barrier, inc=1, device_id=at, device_id_type=MESH)
    loads[0].wait()
    loads[1].wait()

    mask = jnp.concatenate([mask_ref[...].astype(F32), jnp.zeros((6, 512), F32)], axis=0).T
    tile_of = (iota((8, 128), 1) // 64 == iota((8, 128), 0)).astype(F32)
    tile_of_first = (lax.rem(iota((8, 128), 1) // 32, 2) == iota((8, 128), 0)).astype(F32)
    live_ref[...] = dot(mask, tile_of).reshape(8, 64, 128)
    twice = (iota((64, 128), 0) == lax.rem(iota((64, 128), 1), 64)).astype(BF16)
    spread = dot(feat_ref[...].T, twice) * dot(mask, tile_of_first)
    field_ref[...] = spread.reshape(8, 64, 128)
    face_ref[...] = spread.astype(BF16).reshape(8, 64, 128)

    def halo_copy(which, side):
        return pltpu.make_async_remote_copy(
            src_ref=face_ref.at[7 if side == 0 else 0],
            dst_ref=halo_ref.at[which, side],
            send_sem=halo_send.at[which, side],
            recv_sem=halo_recv.at[which, side],
            device_id={"region": right if side == 0 else left, "rep": rep},
            device_id_type=MESH,
        )

    has_right, has_left = region < n_region - 1, region > 0

    def halo_start(which):
        pl.when(has_right)(lambda: halo_copy(which, 0).start())
        pl.when(has_left)(lambda: halo_copy(which, 1).start())

    def halo_wait(which):
        @pl.when(has_left)
        def _():
            halo_copy(which, 0).wait_recv()

        @pl.when(has_right)
        def _():
            halo_copy(which, 1).wait_recv()

        pl.when(has_right)(lambda: halo_copy(which, 0).wait_send())
        pl.when(has_left)(lambda: halo_copy(which, 1).wait_send())

    pl.semaphore_wait(barrier, len(partners))
    halo_start(0)

    loads[2].wait()
    eye = iota((64, 256), 0)
    put = ((eye == iota((64, 256), 1)) | (eye == iota((64, 256), 1) - 192)).astype(BF16)
    spread1 = dot(w1_ref[...].reshape(27 * 32, 64), put).astype(BF16)
    top = spread1[:, :128].reshape(3, 3, 3, 32, 128)
    low = spread1[:, 128:].reshape(3, 3, 3, 32, 128)
    for b in range(3):
        for at, c in ((0, 0), (64, 2)):
            w1b_ref[:, b, at : at + 32, :] = top[:, b, c]
            w1b_ref[:, b, at + 32 : at + 64, :] = low[:, b, c]
    for at, b in ((0, 0), (64, 2)):
        w1b_ref[:, 3, at : at + 32, :] = top[:, b, 1]
        w1b_ref[:, 3, at + 32 : at + 64, :] = low[:, b, 1]
    w1b_ref[:, 4, 0:32, :] = top[:, 1, 1]
    w1b_ref[:, 4, 32:64, :] = low[:, 1, 1]
    w1b_ref[:, 4, 64:128, :] = jnp.zeros((3, 64, 128), BF16)
    side_ref[2] = jnp.zeros((8, 64, 128), F32)
    far_ref[:, 2] = jnp.zeros((2, 64, 128), F32)
    lane = iota((8, 128), 1)
    first_half = lane < 64
    even_quarter = lax.rem(lane // 32, 2) == 0
    z_row = iota((8, 128), 0)
    z_first, z_last = z_row == 0, z_row == 7

    def rows_of(masked, count):
        return jnp.concatenate([masked] * count, axis=0) if count > 1 else masked

    def split_first():
        source, target = iota((128, 256), 0), iota((128, 256), 1)
        return (source == (target // 128) * 32 + lax.rem(target, 32)).astype(BF16)

    def split_second():
        source, target = iota((128, 256), 0), iota((128, 256), 1)
        return (source == (target // 128) * 64 + lax.rem(target, 64)).astype(BF16)

    def shifted(middle, load, tile_lane):
        ext = []
        for c in range(3):
            groups = [load(0, c, 56, 64)]
            if c == 1 and middle is not None:
                mid = middle
            else:
                mid = load(1, c, 0, 64)
            groups += [mid[8 * y : 8 * y + 8] for y in range(8)]
            groups.append(load(2, c, 0, 8))
            ext.append(groups)
        down = [pltpu.roll(jnp.where(z_last, ext[0][y], ext[1][y]), 1, 0) for y in range(10)]
        up = [pltpu.roll(jnp.where(z_first, ext[2][y], ext[1][y]), 7, 0) for y in range(10)]
        return down, ext[1], up

    def store_first(c_ref, slab, down, mid, up):
        both = [jnp.where(first_half, d, u) for d, u in zip(down, up)]
        c_ref[slab, 0:80, :] = jnp.concatenate(both, axis=0).astype(BF16)
        c_ref[slab, 80:144, :] = jnp.concatenate(both[1:9], axis=0).astype(BF16)
        ends = [jnp.where(first_half, mid[y], mid[y + 2]) for y in range(8)]
        c_ref[slab, 144:208, :] = jnp.concatenate(ends, axis=0).astype(BF16)
        c_ref[slab, 208:272, :] = jnp.concatenate(mid[1:9], axis=0).astype(BF16)

    def store_second(c_ref, slab, down, mid, up):
        for c, groups in enumerate((down, mid, up)):
            c_ref[c, slab, 0:80, :] = jnp.concatenate(groups, axis=0).astype(BF16)
            c_ref[c, slab, 80:144, :] = jnp.concatenate(groups[1:9], axis=0).astype(BF16)

    def build_inner(c_ref, store, splitter, tile_lane):
        whole = dot(face_ref[...].reshape(512, 128), splitter)
        side_ref[0] = whole[:, :128].reshape(8, 64, 128)
        side_ref[1] = whole[:, 128:].reshape(8, 64, 128)
        named = [
            [jnp.minimum(jnp.maximum(nbr_ref[t, 9 + k] - 2, 0), 2) for k in range(9)]
            for t in range(2)
        ]

        @pl.loop(0, 8, unroll=4)
        def _(x):
            def load(b, c, start, stop):
                k = 3 * b + c
                return jnp.where(
                    rows_of(tile_lane, (stop - start) // 8),
                    side_ref[named[0][k], x, start:stop, :],
                    side_ref[named[1][k], x, start:stop, :],
                )

            store(c_ref, x + 1, *shifted(field_ref[x], load, tile_lane))

    def build_faces(which, c_ref, store, splitter, tile_lane):
        whole = dot(halo_ref[which].reshape(128, 128), splitter)
        for side in range(2):
            far_ref[side, 0] = whole[64 * side : 64 * side + 64, :128]
            far_ref[side, 1] = whole[64 * side : 64 * side + 64, 128:]
            named = [
                [
                    jnp.minimum(jnp.maximum(nbr_ref[t, 18 * side + k] - 4 * side, 0), 2)
                    for k in range(9)
                ]
                for t in range(2)
            ]

            def load(b, c, start, stop):
                k = 3 * b + c
                return jnp.where(
                    rows_of(tile_lane, (stop - start) // 8),
                    far_ref[side, named[0][k], start:stop, :],
                    far_ref[side, named[1][k], start:stop, :],
                )

            store(c_ref, 9 * side, *shifted(None, load, tile_lane))

    def windows_first(start, count):
        return [
            c1_ref[start : start + count, r : r + 64, :].reshape(count * 64, 128)
            for r in ROWS_FIRST
        ]

    def windows_second(c_ref, start, count):
        return [
            c_ref[c, start : start + count, ROWS[b] : ROWS[b] + 64, :].reshape(count * 64, 128)
            for b in range(3)
            for c in range(3)
        ]

    def conv_inner(windows, weight, product=dot, columns=1):
        weights = jnp.concatenate([weight(0), weight(2), weight(1)], axis=columns)
        got = product(jnp.concatenate(windows(1, 8), axis=1), weights)
        acc_ref[...] = got[:, 256:384]
        acc_ref[64:512] += got[0:448, 0:128]
        acc_ref[0:448] += got[64:512, 128:256]

    def conv_faces(windows, weight, product=dot, columns=1):
        weights = jnp.concatenate([weight(0), weight(2)], axis=columns)
        rows = [jnp.concatenate(both, axis=0) for both in zip(windows(0, 1), windows(9, 1))]
        got = product(jnp.concatenate(rows, axis=1), weights)
        acc_ref[0:64] += got[0:64, 0:128]
        acc_ref[448:512] += got[64:128, 128:256]

    def weight_first(a):
        return w1b_ref[a].reshape(5 * 128, 128)

    def weight_second(a):
        return w2b_ref[9 * a : 9 * a + 9].reshape(9 * 128, 128)

    def weight_back(a):
        return jnp.concatenate([w2b_ref[26 - k] for k in range(9 * a, 9 * a + 9)], axis=1)

    def layer(which, c_ref, store, splitter, tile_lane, windows, weight, product, columns, activate, between=None):
        build_inner(c_ref, store, splitter, tile_lane)
        conv_inner(windows, weight, product, columns)
        if between is not None:
            between()
        pl.loop(1, 7, unroll=3)(activate)
        halo_wait(which)
        build_faces(which, c_ref, store, splitter, tile_lane)
        conv_faces(windows, weight, product, columns)
        pl.loop(0, 2, unroll=2)(lambda i: activate(7 * i))

    def hidden_of(x):
        rows = pl.ds(pl.multiple_of(x * 64, 64), 64)
        pre = acc_ref[rows, :]
        live = live_ref[x]
        sig = jax.nn.sigmoid(pre)
        hidden = (live * pre * sig).astype(BF16)
        face_ref[x] = hidden
        field_ref[x] = hidden.astype(F32)
        slope_ref[x] = live * sig * (1.0 + pre * (1.0 - sig))

    def outputs_of(x):
        rows = pl.ds(pl.multiple_of(x * 64, 64), 64)
        pre = acc_ref[rows, :]
        live = live_ref[x]
        sig = jax.nn.sigmoid(pre)
        out_ref[rows, :] = (live * pre * sig).astype(BF16)
        upstream = cot_ref[rows, :].astype(F32)
        delta = (upstream * live * sig * (1.0 + pre * (1.0 - sig))).astype(BF16)
        face_ref[x] = delta
        field_ref[x] = delta.astype(F32)

    def back_of(x):
        rows = pl.ds(pl.multiple_of(x * 64, 64), 64)
        face_ref[x] = (acc_ref[rows, :] * slope_ref[x]).astype(BF16)

    layer(0, c1_ref, store_first, split_first(), even_quarter, windows_first, weight_first, dot, 1, hidden_of)
    halo_start(1)

    loads[3].wait()
    spread2 = dot(w2_ref[...].reshape(27 * 64, 64), put).astype(BF16)
    w2b_ref[:, 0:64, :] = spread2[:, :128].reshape(27, 64, 128)
    w2b_ref[:, 64:128, :] = spread2[:, 128:].reshape(27, 64, 128)
    second = functools.partial(windows_second, c2_ref)
    loads[4].wait()
    layer(1, c2_ref, store_second, split_second(), first_half, second, weight_second, dot, 1, outputs_of)
    halo_start(2)

    wide_half = iota((64, 128), 1) < 64
    wide_quarter = lax.rem(iota((64, 128), 1) // 32, 2) == 0
    per_core1, per_core2 = PAIRS_FIRST // 2, PAIRS_SECOND // 2

    def put_gradient(full, send, pair, value):
        value = value.reshape(4, 16, 128)
        full[4 * pair : 4 * pair + 4] = value
        send[4 * pair : 4 * pair + 4] = value.astype(BF16)

    delta_t = face_ref[...].reshape(512, 128).T
    for pair in range(14):
        both = []
        for k in (2 * pair, min(2 * pair + 1, 26)):
            a, b, c = k // 9, k // 3 % 3, k % 3
            window = c2_ref[c, a : a + 8, ROWS[b] : ROWS[b] + 64, :]
            both.append(window.reshape(512, 128))
        got = dot(delta_t, jnp.concatenate(both, axis=1))
        one, two = got[:, :128], got[:, 128:]
        straight = jnp.where(wide_half, one[0:64], two[64:128])
        crossed = jnp.where(wide_half, two[0:64], one[64:128])
        put_gradient(full2_ref, send2_ref, pair, straight + pltpu.roll(crossed, 64, 1))
    for pair in range(14, PAIRS_SECOND):
        put_gradient(full2_ref, send2_ref, pair, jnp.zeros((64, 128), F32))

    def reducer(which, unit, full, send, parts, line, fin):

        def remote(stage, src, dst, device):
            return pltpu.make_async_remote_copy(
                src_ref=src,
                dst_ref=dst,
                send_sem=sum_send.at[which, stage],
                recv_sem=sum_recv.at[which, stage],
                device_id=device,
                device_id_type=MESH,
            )

        place = pl.ds((core * n_plane + member) * unit, unit)
        parts_whole = parts.at[pl.ds(1, parts.shape[0] - 1)]
        line_whole = line.at[pl.ds(0, nz - 1)]
        fin_whole = fin.at[pl.ds(0, (2 * n_plane - 1) * unit)]
        whole = [
            remote(0, parts_whole, parts_whole, twin),
            remote(1, line_whole, line_whole, twin),
            remote(2, fin_whole, fin_whole, twin),
        ]

        def start_parts(peers):
            for slot, other, at in peers:
                remote(0, send.at[pl.ds(other * unit, unit)], parts.at[slot], at).start()

        def start_line():
            whole[0].wait_recv()
            total = full[place]
            for i in range(1, parts.shape[0]):
                total = total + parts[i].astype(F32)
            line[my_z] = total.astype(BF16)
            for at in line_peers:
                remote(1, line.at[my_z], line.at[my_z], at).start()

        def start_back():
            whole[1].wait_recv()
            total = line[0].astype(F32)
            for z in range(1, nz):
                total = total + line[z].astype(F32)
            fin[place] = (total * scale).astype(BF16)
            for _, _, at in all_peers:
                remote(2, fin.at[place], fin.at[place], at).start()

        def finish():
            whole[2].wait_recv()

        def sent():
            for copy in whole:
                copy.wait_send()

        return start_parts, start_line, start_back, finish, sent

    unit1, unit2 = 4 * per_core1 // n_plane, 4 * per_core2 // n_plane
    sum1 = reducer(0, unit1, full1_ref, send1_ref, parts1_ref, line1_ref, fin1_ref)
    sum2 = reducer(1, unit2, full2_ref, send2_ref, parts2_ref, line2_ref, fin2_ref)
    sum2[0](all_peers)

    third = functools.partial(windows_second, c3_ref)
    layer(2, c3_ref, store_second, split_second(), first_half, third, weight_back, dot_nt, 0, back_of)
    delta_t = face_ref[...].reshape(512, 128).T
    def first_gradient(pair):
        both = []
        for j in range(2):
            block = jnp.minimum(2 * pair + j, 14)
            a, kind = block // 5, lax.rem(block, 5)
            row = jnp.where(kind < 3, 80 * kind * (2 - kind) + 8 * kind * (kind - 1), 64 * kind - 48)
            rows = pl.ds(pl.multiple_of(row, 16), 64)
            both.append(c1_ref[pl.ds(a, 8), rows, :].reshape(512, 128))
        got = dot(delta_t, jnp.concatenate(both, axis=1))
        one, two = got[:, :128], got[:, 128:]
        straight = jnp.where(wide_quarter, one[0:64], two[64:128])
        crossed = jnp.where(wide_quarter, two[0:64], one[64:128])
        swapped = jnp.where(wide_quarter, pltpu.roll(crossed, 96, 1), pltpu.roll(crossed, 32, 1))
        value = (straight + swapped).reshape(4, 16, 128)
        full1_ref[pl.ds(4 * pair, 4)] = value
        send1_ref[pl.ds(4 * pair, 4)] = value.astype(BF16)

    for i in range(per_core1):
        first_gradient((1 - core) * per_core1 + i)
    sum1[0]([peer for peer, offset in zip(all_peers, offsets) if offset[2] == 1])
    for i in range(per_core1):
        first_gradient(core * per_core1 + i)
    sum1[0]([peer for peer, offset in zip(all_peers, offsets) if offset[2] == 0])
    sum2[1]()
    sum1[1]()
    sum2[2]()
    sum1[2]()
    sum2[3]()
    for pair in range(14):
        value = fin2_ref[4 * pair : 4 * pair + 4].reshape(64, 128).T.astype(F32)
        g2_ref[2 * pair] = value[0:64]
        if pair < 13:
            g2_ref[2 * pair + 1] = value[64:128]
    sum1[3]()
    sum2[4]()
    sum1[4]()


def unpack_kernel(block_ref, fin_ref, g2_ref, out_hbm, g1_hbm, g2_hbm, g1_ref, sem):
    block_copy = pltpu.make_async_copy(block_ref, out_hbm, sem.at[0])
    second_copies = [
        pltpu.make_async_copy(g2_ref.at[pl.ds(k, 9)], g2_hbm.at[pl.ds(k, 9)], sem.at[3 + k // 9])
        for k in (0, 9, 18)
    ]
    first_copy = pltpu.make_async_copy(g1_ref, g1_hbm, sem.at[2])
    for copy in second_copies:
        copy.start()
    block_copy.start()
    for pair in range(PAIRS_FIRST):
        value = fin_ref[4 * pair : 4 * pair + 4].reshape(64, 128).T.astype(F32)
        for j in range(2):
            block = 2 * pair + j
            if block > 14:
                continue
            a, kind = block // 5, block % 5
            if kind < 3:
                offsets = (9 * a + 3 * kind, 9 * a + 3 * kind + 2)
            elif kind == 3:
                offsets = (9 * a + 1, 9 * a + 7)
            else:
                offsets = (9 * a + 4,)
            for i, k in enumerate(offsets):
                g1_ref[k] = value[64 * i + 32 * j : 64 * i + 32 * j + 32]
    first_copy.start()
    for copy in second_copies:
        copy.wait()
    block_copy.wait()
    first_copy.wait()


def solution(mesh):
    n_region, n_rep = mesh.shape["region"], mesh.shape["rep"]
    nx, ny = (4, 4) if n_region == 32 else (2, n_rep // 2)
    nz = n_region // nx
    sizes = (nx, nz, ny)
    n_plane = nx * ny
    core1, core2 = 2 * PAIRS_FIRST, 2 * PAIRS_SECOND
    unit1, unit2 = core1 // n_plane, core2 // n_plane
    vmem = pl.BlockSpec(memory_space=pltpu.VMEM)
    smem = pl.BlockSpec(memory_space=pltpu.SMEM)
    hbm = pl.BlockSpec(memory_space=pltpu.HBM)
    anywhere = pl.BlockSpec(memory_space=pl.ANY)
    dma = pltpu.SemaphoreType.DMA

    def body(features, weight_first, weight_second, cotangent, neighbours, voxel_mask):
        scale = 1.0 / math.sqrt(n_rep * 2 * n_region * 512)
        block, fin1, g2 = pl.pallas_call(
            functools.partial(main_kernel, sizes, scale),
            out_shape=(
                jax.ShapeDtypeStruct((512, 128), BF16),
                jax.ShapeDtypeStruct((2 * core1, 16, 128), BF16),
                jax.ShapeDtypeStruct((27, 64, 64), F32),
            ),
            in_specs=[hbm, hbm, hbm, hbm, smem, hbm],
            out_specs=(vmem, vmem, vmem),
            scratch_shapes=[
                pltpu.VMEM((64, 512), BF16),
                pltpu.VMEM((27, 32, 64), BF16),
                pltpu.VMEM((27, 64, 64), BF16),
                pltpu.VMEM((512, 128), BF16),
                pltpu.VMEM((2, 512), jnp.int32),
                pltpu.VMEM((8, 64, 128), F32),
                pltpu.VMEM((8, 64, 128), F32),
                pltpu.VMEM((8, 64, 128), BF16),
                pltpu.VMEM((3, 2, 64, 128), BF16),
                pltpu.VMEM((3, 8, 64, 128), F32),
                pltpu.VMEM((2, 3, 64, 128), F32),
                pltpu.VMEM((10, 272, 128), BF16),
                pltpu.VMEM((3, 10, 144, 128), BF16),
                pltpu.VMEM((3, 10, 144, 128), BF16),
                pltpu.VMEM((3, 5, 128, 128), BF16),
                pltpu.VMEM((27, 128, 128), BF16),
                pltpu.VMEM((512, 128), F32),
                pltpu.VMEM((8, 64, 128), F32),
                pltpu.VMEM((2 * core1, 16, 128), F32),
                pltpu.VMEM((2 * core2, 16, 128), F32),
                pltpu.VMEM((2 * core1, 16, 128), BF16),
                pltpu.VMEM((2 * core2, 16, 128), BF16),
                pltpu.VMEM((2 * n_plane, unit1, 16, 128), BF16),
                pltpu.VMEM((2 * n_plane, unit2, 16, 128), BF16),
                pltpu.VMEM((nz, unit1, 16, 128), BF16),
                pltpu.VMEM((nz, unit2, 16, 128), BF16),
                pltpu.VMEM((2 * core2, 16, 128), BF16),
                dma((5,)),
                dma((3, 2)),
                dma((3, 2)),
                dma((2, 3)),
                dma((2, 3)),
            ],
            compiler_params=pltpu.CompilerParams(
                collective_id=0, has_side_effects=True, vmem_limit_bytes=40 * 2**20
            ),
        )(
            *(
                pltpu.with_memory_space_constraint(x, pltpu.HBM)
                for x in (
                    jnp.swapaxes(features, 1, 2).reshape(64, 512),
                    weight_first,
                    weight_second,
                    cotangent.reshape(512, 128),
                    neighbours.reshape(2, 27),
                    voxel_mask.reshape(2, 512),
                )
            )
        )
        out, g1, g2 = pl.pallas_call(
            unpack_kernel,
            out_shape=(
                jax.ShapeDtypeStruct((512, 128), BF16),
                jax.ShapeDtypeStruct((27, 32, 64), F32),
                jax.ShapeDtypeStruct((27, 64, 64), F32),
            ),
            in_specs=[vmem, vmem, vmem],
            out_specs=(anywhere, anywhere, anywhere),
            scratch_shapes=[
                pltpu.VMEM((27, 32, 64), F32),
                dma((6,)),
            ],
            compiler_params=pltpu.CompilerParams(vmem_limit_bytes=40 * 2**20),
        )(block, fin1, g2)
        return out.reshape(1, 512, 128), g1, g2

    in_specs = (
        P("rep", None, "region"),
        P(),
        P(),
        P("rep", None, "region"),
        P("rep", "region", None),
        P("rep", "region", None),
    )
    out_specs = (P("rep", None, "region"), P(), P())
    return jax.shard_map(body, mesh=mesh, in_specs=in_specs, out_specs=out_specs, check_vma=False)
```

```python
import functools
import math

import jax
import jax.numpy as jnp
from jax import lax
from jax.experimental import pallas as pl
from jax.experimental.pallas import tpu as pltpu
from jax.sharding import PartitionSpec as P

MESH = pl.DeviceIdType.MESH
F32 = jnp.float32
BF16 = jnp.bfloat16
ROWS = (0, 80, 16)
ROWS_FIRST = (0, 80, 16, 144, 208)
PAIRS_SECOND = 16
PAIRS_FIRST = 8


def iota(shape, axis):
    return lax.broadcasted_iota(jnp.int32, shape, axis)


def dot(a, b):
    return jnp.dot(a, b, preferred_element_type=F32)


def dot_nt(a, b):
    return lax.dot_general(a, b, (((1,), (1,)), ((), ())), preferred_element_type=F32)


def places(sizes):
    nx, nz, ny = sizes
    region = lax.axis_index("region")
    rep = lax.axis_index("rep")
    return region // nz, lax.rem(region, nz), rep // 2, lax.rem(rep, 2), region, rep


def main_kernel(
    sizes,
    scale,
    feat_hbm,
    w1_hbm,
    w2_hbm,
    cot_hbm,
    nbr_ref,
    mask_hbm,
    out_ref,
    fin1_ref,
    g2_ref,
    feat_ref,
    w1_ref,
    w2_ref,
    cot_ref,
    mask_ref,
    live_ref,
    field_ref,
    face_ref,
    halo_ref,
    edge_ref,
    rim_ref,
    ext_ref,
    side_ref,
    far_ref,
    c1_ref,
    c2_ref,
    c3_ref,
    w1b_ref,
    w2b_ref,
    acc_ref,
    slope_ref,
    full1_ref,
    full2_ref,
    send1_ref,
    send2_ref,
    parts1_ref,
    parts2_ref,
    line1_ref,
    line2_ref,
    fin2_ref,
    load_sem,
    halo_send,
    halo_recv,
    sum_send,
    sum_recv,
):
    nx, nz, ny = sizes
    n_region, n_plane = nx * nz, nx * ny
    my_x, my_z, my_y, core, region, rep = places(sizes)
    member = my_x * ny + my_y
    right = lax.rem(region + 1, n_region)
    left = lax.rem(region + n_region - 1, n_region)
    twin = {"region": region, "rep": my_y * 2 + 1 - core}

    def apart(offset, size):
        return min(offset, size - offset)

    offsets = sorted(
        ((dx, dy, dc) for dx in range(nx) for dy in range(ny) for dc in range(2)),
        key=lambda d: (-apart(d[0], nx) - apart(d[1], ny), d),
    )
    all_peers = []
    for dx, dy, dc in offsets:
        if (dx, dy, dc) == (0, 0, 0):
            continue
        x, y, c = lax.rem(my_x + dx, nx), lax.rem(my_y + dy, ny), lax.rem(core + dc, 2)
        at = {"region": x * nz + my_z, "rep": y * 2 + c}
        all_peers.append((c * n_plane + x * ny + y, at))
    line_peers = [
        {"region": my_x * nz + lax.rem(my_z + step, nz), "rep": rep}
        for step in sorted(range(1, nz), key=lambda d: -apart(d, nz))
    ]

    halo_ref[...] = jnp.zeros((3, 2, 64, 128), BF16)
    rim_ref[...] = jnp.zeros((2, 3, 64, 128), BF16)

    barrier = pltpu.get_barrier_semaphore()
    partners = [{"region": right, "rep": rep}, {"region": left, "rep": rep}]
    partners += [at for _, at in all_peers] + line_peers
    for at in partners[:2]:
        pl.semaphore_signal(barrier, inc=1, device_id=at, device_id_type=MESH)
    loads = [
        pltpu.make_async_copy(src, dst, load_sem.at[i])
        for i, (src, dst) in enumerate(
            (
                (mask_hbm, mask_ref),
                (feat_hbm, feat_ref),
                (w1_hbm, w1_ref),
                (w2_hbm, w2_ref),
                (cot_hbm, cot_ref),
            )
        )
    ]
    for load in loads:
        load.start()
    for at in partners[2:]:
        pl.semaphore_signal(barrier, inc=1, device_id=at, device_id_type=MESH)
    loads[0].wait()
    loads[1].wait()

    mask = jnp.concatenate([mask_ref[...].astype(F32), jnp.zeros((6, 512), F32)], axis=0).T
    tile_of = (iota((8, 128), 1) // 64 == iota((8, 128), 0)).astype(F32)
    tile_of_first = (lax.rem(iota((8, 128), 1) // 32, 2) == iota((8, 128), 0)).astype(F32)
    live_ref[...] = dot(mask, tile_of).reshape(8, 64, 128)
    twice = (iota((64, 128), 0) == lax.rem(iota((64, 128), 1), 64)).astype(BF16)
    spread = dot(feat_ref[...].T, twice) * dot(mask, tile_of_first)
    field_ref[...] = spread.reshape(8, 64, 128)
    face_ref[...] = spread.astype(BF16).reshape(8, 64, 128)

    def halo_copy(which, side):
        return pltpu.make_async_remote_copy(
            src_ref=edge_ref.at[side] if which == 0 else face_ref.at[7 if side == 0 else 0],
            dst_ref=rim_ref.at[side] if which == 0 else halo_ref.at[which, side],
            send_sem=halo_send.at[which, side],
            recv_sem=halo_recv.at[which, side],
            device_id={"region": right if side == 0 else left, "rep": rep},
            device_id_type=MESH,
        )

    has_right, has_left = region < n_region - 1, region > 0

    def halo_start(which):
        pl.when(has_right)(lambda: halo_copy(which, 0).start())
        pl.when(has_left)(lambda: halo_copy(which, 1).start())

    def halo_wait(which):
        @pl.when(has_left)
        def _():
            halo_copy(which, 0).wait_recv()

        @pl.when(has_right)
        def _():
            halo_copy(which, 1).wait_recv()

    def halo_sent(which):
        pl.when(has_right)(lambda: halo_copy(which, 0).wait_send())
        pl.when(has_left)(lambda: halo_copy(which, 1).wait_send())

    wide_half = iota((64, 128), 1) < 64
    wide_quarter = lax.rem(iota((64, 128), 1) // 32, 2) == 0
    one_lane = wide_quarter[0:1]
    links = []
    for s in range(2):
        for k in range(9):
            named = [(nbr_ref[t, 9 + k] == 2 + s).astype(F32) for t in range(2)]
            links.append(jnp.where(one_lane, named[0], named[1]))
        links.append(jnp.zeros((23, 128), F32))
    links = jnp.concatenate(links, axis=0).astype(BF16)
    for side, face, inside in ((0, 7, 6), (1, 0, 1)):
        edge_ref[side, 0] = jnp.where(wide_half, face_ref[face], face_ref[inside])
        edge_ref[side, 1] = live_ref[face].astype(BF16)
        edge_ref[side, 2] = links
    pl.semaphore_wait(barrier, len(partners))
    halo_start(0)

    loads[2].wait()
    eye = iota((64, 256), 0)
    put = ((eye == iota((64, 256), 1)) | (eye == iota((64, 256), 1) - 192)).astype(BF16)
    spread1 = dot(w1_ref[...].reshape(27 * 32, 64), put).astype(BF16)
    top = spread1[:, :128].reshape(3, 3, 3, 32, 128)
    low = spread1[:, 128:].reshape(3, 3, 3, 32, 128)
    for b in range(3):
        for at, c in ((0, 0), (64, 2)):
            w1b_ref[:, b, at : at + 32, :] = top[:, b, c]
            w1b_ref[:, b, at + 32 : at + 64, :] = low[:, b, c]
    for at, b in ((0, 0), (64, 2)):
        w1b_ref[:, 3, at : at + 32, :] = top[:, b, 1]
        w1b_ref[:, 3, at + 32 : at + 64, :] = low[:, b, 1]
    w1b_ref[:, 4, 0:32, :] = top[:, 1, 1]
    w1b_ref[:, 4, 32:64, :] = low[:, 1, 1]
    w1b_ref[:, 4, 64:128, :] = jnp.zeros((3, 64, 128), BF16)
    side_ref[2] = jnp.zeros((8, 64, 128), F32)
    far_ref[:, 2] = jnp.zeros((2, 64, 128), F32)
    lane = iota((8, 128), 1)
    first_half = lane < 64
    even_quarter = lax.rem(lane // 32, 2) == 0
    z_row = iota((8, 128), 0)
    z_first, z_last = z_row == 0, z_row == 7

    def rows_of(masked, count):
        return jnp.concatenate([masked] * count, axis=0) if count > 1 else masked

    def split_first():
        source, target = iota((128, 256), 0), iota((128, 256), 1)
        return (source == (target // 128) * 32 + lax.rem(target, 32)).astype(BF16)

    def split_second():
        source, target = iota((128, 256), 0), iota((128, 256), 1)
        return (source == (target // 128) * 64 + lax.rem(target, 64)).astype(BF16)

    def shifted(middle, load, tile_lane):
        ext = []
        for c in range(3):
            groups = [load(0, c, 56, 64)]
            if c == 1 and middle is not None:
                mid = middle
            else:
                mid = load(1, c, 0, 64)
            groups += [mid[8 * y : 8 * y + 8] for y in range(8)]
            groups.append(load(2, c, 0, 8))
            ext.append(groups)
        down = [pltpu.roll(jnp.where(z_last, ext[0][y], ext[1][y]), 1, 0) for y in range(10)]
        up = [pltpu.roll(jnp.where(z_first, ext[2][y], ext[1][y]), 7, 0) for y in range(10)]
        return down, ext[1], up

    def store_first(c_ref, slab, down, mid, up):
        both = [jnp.where(first_half, d, u) for d, u in zip(down, up)]
        c_ref[slab, 0:80, :] = jnp.concatenate(both, axis=0).astype(BF16)
        c_ref[slab, 80:144, :] = jnp.concatenate(both[1:9], axis=0).astype(BF16)
        ends = [jnp.where(first_half, mid[y], mid[y + 2]) for y in range(8)]
        c_ref[slab, 144:208, :] = jnp.concatenate(ends, axis=0).astype(BF16)
        c_ref[slab, 208:272, :] = jnp.concatenate(mid[1:9], axis=0).astype(BF16)

    def store_second(c_ref, slab, down, mid, up):
        for c, groups in enumerate((down, mid, up)):
            c_ref[c, slab, 0:80, :] = jnp.concatenate(groups, axis=0).astype(BF16)
            c_ref[c, slab, 80:144, :] = jnp.concatenate(groups[1:9], axis=0).astype(BF16)

    def build_inner(c_ref, store, splitter, tile_lane):
        whole = dot(face_ref[...].reshape(512, 128), splitter)
        side_ref[0] = whole[:, :128].reshape(8, 64, 128)
        side_ref[1] = whole[:, 128:].reshape(8, 64, 128)
        named = [
            [jnp.minimum(jnp.maximum(nbr_ref[t, 9 + k] - 2, 0), 2) for k in range(9)]
            for t in range(2)
        ]

        @pl.loop(0, 8, unroll=4)
        def _(x):
            def load(b, c, start, stop):
                k = 3 * b + c
                return jnp.where(
                    rows_of(tile_lane, (stop - start) // 8),
                    side_ref[named[0][k], x, start:stop, :],
                    side_ref[named[1][k], x, start:stop, :],
                )

            store(c_ref, x + 1, *shifted(field_ref[x], load, tile_lane))

    def build_faces(which, c_ref, store, splitter, tile_lane):
        source = rim_ref[:, 0] if which == 0 else halo_ref[which]
        whole = dot(source.reshape(128, 128), splitter)
        for side in range(2):
            far_ref[side, 0] = whole[64 * side : 64 * side + 64, :128]
            far_ref[side, 1] = whole[64 * side : 64 * side + 64, 128:]
            named = [
                [
                    jnp.minimum(jnp.maximum(nbr_ref[t, 18 * side + k] - 4 * side, 0), 2)
                    for k in range(9)
                ]
                for t in range(2)
            ]

            def load(b, c, start, stop):
                k = 3 * b + c
                return jnp.where(
                    rows_of(tile_lane, (stop - start) // 8),
                    far_ref[side, named[0][k], start:stop, :],
                    far_ref[side, named[1][k], start:stop, :],
                )

            store(c_ref, 9 * side, *shifted(None, load, tile_lane))

    def build_cross():
        for side, x, base, code in ((0, 0, 18, 0), (1, 7, 0, 4)):
            named = []
            for s in range(2):
                row = []
                for k in range(9):
                    link = [nbr_ref[t, 26 - base - k] == code + s for t in range(2)]
                    row.append(jnp.where(link[0], 0, jnp.where(link[1], 1, 2)))
                named.append(row)

            def load(b, c, start, stop):
                k = 3 * b + c
                return jnp.where(
                    rows_of(even_quarter, (stop - start) // 8),
                    side_ref[named[0][k], x, start:stop, :],
                    side_ref[named[1][k], x, start:stop, :],
                )

            store_first(ext_ref.at[side], 2 - 2 * side, *shifted(None, load, even_quarter))

    def build_rim():
        source, target = iota((128, 384), 0), iota((128, 384), 1)
        group, lane_in = target // 128, lax.rem(target, 128)
        wanted = jnp.where(group == 0, lax.rem(lane_in, 64), (group - 1) * 32 + lax.rem(lane_in, 32))
        for inside in range(2):
            spread_out = (source == wanted + 64 * inside).astype(BF16)
            whole = dot(rim_ref[:, 0].reshape(128, 128), spread_out)
            for side in range(2):
                part = whole[64 * side : 64 * side + 64]
                table = rim_ref[side, 2].astype(F32)

                def load(b, c, start, stop):
                    k = 3 * b + c
                    first = table[k : k + 1] * part[start:stop, 128:256]
                    return first + table[32 + k : 33 + k] * part[start:stop, 256:384]

                slab = 1 if inside == 0 else 2 * side
                store_first(ext_ref.at[side], slab, *shifted(part[:, 0:128], load, even_quarter))

    def hidden_beside():
        windows = []
        for a in range(3):
            for r in ROWS_FIRST:
                windows.append(ext_ref[:, a, r : r + 64, :].reshape(128, 128))
        pre = dot(jnp.concatenate(windows, axis=1), w1b_ref[...].reshape(15 * 128, 128))
        live = rim_ref[:, 1].reshape(128, 128).astype(F32)
        hidden = (live * pre * jax.nn.sigmoid(pre)).astype(BF16)
        halo_ref[1] = hidden.reshape(2, 64, 128)

    def windows_first(start, count):
        return [
            c1_ref[start : start + count, r : r + 64, :].reshape(count * 64, 128)
            for r in ROWS_FIRST
        ]

    def windows_second(c_ref, start, count):
        return [
            c_ref[c, start : start + count, ROWS[b] : ROWS[b] + 64, :].reshape(count * 64, 128)
            for b in range(3)
            for c in range(3)
        ]

    def conv_inner(windows, weight, product=dot, columns=1):
        weights = jnp.concatenate([weight(0), weight(2), weight(1)], axis=columns)
        got = product(jnp.concatenate(windows(1, 8), axis=1), weights)
        acc_ref[...] = got[:, 256:384]
        acc_ref[64:512] += got[0:448, 0:128]
        acc_ref[0:448] += got[64:512, 128:256]

    def conv_faces(windows, weight, product=dot, columns=1):
        weights = jnp.concatenate([weight(0), weight(2)], axis=columns)
        rows = [jnp.concatenate(both, axis=0) for both in zip(windows(0, 1), windows(9, 1))]
        got = product(jnp.concatenate(rows, axis=1), weights)
        acc_ref[0:64] += got[0:64, 0:128]
        acc_ref[448:512] += got[64:128, 128:256]

    def weight_first(a):
        return w1b_ref[a].reshape(5 * 128, 128)

    def weight_second(a):
        return w2b_ref[9 * a : 9 * a + 9].reshape(9 * 128, 128)

    def weight_back(a):
        return jnp.concatenate([w2b_ref[26 - k] for k in range(9 * a, 9 * a + 9)], axis=1)

    def layer(which, c_ref, store, splitter, tile_lane, windows, weight, product, columns, activate, between=None):
        build_inner(c_ref, store, splitter, tile_lane)
        conv_inner(windows, weight, product, columns)
        if between is not None:
            between()
        if which == 0:
            build_cross()
        pl.loop(1, 7, unroll=3)(activate)
        if which != 1:
            halo_wait(which)
        build_faces(which, c_ref, store, splitter, tile_lane)
        if which == 0:
            build_rim()
            hidden_beside()
        conv_faces(windows, weight, product, columns)
        if which == 2:
            halo_sent(2)
        pl.loop(0, 2, unroll=2)(lambda i: activate(7 * i))

    def hidden_of(x):
        rows = pl.ds(pl.multiple_of(x * 64, 64), 64)
        pre = acc_ref[rows, :]
        live = live_ref[x]
        sig = jax.nn.sigmoid(pre)
        hidden = (live * pre * sig).astype(BF16)
        face_ref[x] = hidden
        field_ref[x] = hidden.astype(F32)
        slope_ref[x] = live * sig * (1.0 + pre * (1.0 - sig))

    def outputs_of(x):
        rows = pl.ds(pl.multiple_of(x * 64, 64), 64)
        pre = acc_ref[rows, :]
        live = live_ref[x]
        sig = jax.nn.sigmoid(pre)
        out_ref[rows, :] = (live * pre * sig).astype(BF16)
        upstream = cot_ref[rows, :].astype(F32)
        delta = (upstream * live * sig * (1.0 + pre * (1.0 - sig))).astype(BF16)
        face_ref[x] = delta
        field_ref[x] = delta.astype(F32)

    def back_of(x):
        rows = pl.ds(pl.multiple_of(x * 64, 64), 64)
        face_ref[x] = (acc_ref[rows, :] * slope_ref[x]).astype(BF16)

    layer(0, c1_ref, store_first, split_first(), even_quarter, windows_first, weight_first, dot, 1, hidden_of)

    loads[3].wait()
    spread2 = dot(w2_ref[...].reshape(27 * 64, 64), put).astype(BF16)
    w2b_ref[:, 0:64, :] = spread2[:, :128].reshape(27, 64, 128)
    w2b_ref[:, 64:128, :] = spread2[:, 128:].reshape(27, 64, 128)
    second = functools.partial(windows_second, c2_ref)
    loads[4].wait()
    layer(1, c2_ref, store_second, split_second(), first_half, second, weight_second, dot, 1, outputs_of)
    halo_start(2)

    wide_half = iota((64, 128), 1) < 64
    wide_quarter = lax.rem(iota((64, 128), 1) // 32, 2) == 0
    per_core1, per_core2 = PAIRS_FIRST // 2, PAIRS_SECOND // 2

    def put_gradient(full, send, pair, value):
        value = value.reshape(4, 16, 128)
        full[4 * pair : 4 * pair + 4] = value
        send[4 * pair : 4 * pair + 4] = value.astype(BF16)

    delta_t = face_ref[...].reshape(512, 128).T
    for pair in range(14):
        both = []
        for k in (2 * pair, min(2 * pair + 1, 26)):
            a, b, c = k // 9, k // 3 % 3, k % 3
            window = c2_ref[c, a : a + 8, ROWS[b] : ROWS[b] + 64, :]
            both.append(window.reshape(512, 128))
        got = dot(delta_t, jnp.concatenate(both, axis=1))
        one, two = got[:, :128], got[:, 128:]
        straight = jnp.where(wide_half, one[0:64], two[64:128])
        crossed = jnp.where(wide_half, two[0:64], one[64:128])
        put_gradient(full2_ref, send2_ref, pair, straight + pltpu.roll(crossed, 64, 1))
    for pair in range(14, PAIRS_SECOND):
        put_gradient(full2_ref, send2_ref, pair, jnp.zeros((64, 128), F32))

    def reducer(which, unit, full, send, parts, line, fin):

        def remote(stage, src, dst, device):
            return pltpu.make_async_remote_copy(
                src_ref=src,
                dst_ref=dst,
                send_sem=sum_send.at[which, stage],
                recv_sem=sum_recv.at[which, stage],
                device_id=device,
                device_id_type=MESH,
            )

        place = pl.ds((core * n_plane + member) * unit, unit)
        parts_whole = parts.at[pl.ds(1, parts.shape[0] - 1)]
        line_whole = line.at[pl.ds(0, nz - 1)]
        fin_whole = fin.at[pl.ds(0, (2 * n_plane - 1) * unit)]
        whole = [
            remote(0, parts_whole, parts_whole, twin),
            remote(1, line_whole, line_whole, twin),
            remote(2, fin_whole, fin_whole, twin),
        ]

        def start_parts():
            for i, (other, at) in enumerate(all_peers):
                remote(0, send.at[pl.ds(other * unit, unit)], parts.at[i + 1], at).start()

        def start_line():
            whole[0].wait_recv()
            total = full[place]
            for i in range(1, parts.shape[0]):
                total = total + parts[i].astype(F32)
            line[my_z] = total.astype(BF16)
            for at in line_peers:
                remote(1, line.at[my_z], line.at[my_z], at).start()

        def start_back():
            whole[1].wait_recv()
            total = line[0].astype(F32)
            for z in range(1, nz):
                total = total + line[z].astype(F32)
            fin[place] = (total * scale).astype(BF16)
            for _, at in all_peers:
                remote(2, fin.at[place], fin.at[place], at).start()

        def finish():
            whole[2].wait_recv()

        def sent():
            for copy in whole:
                copy.wait_send()

        return start_parts, start_line, start_back, finish, sent

    unit1, unit2 = 4 * per_core1 // n_plane, 4 * per_core2 // n_plane
    sum1 = reducer(0, unit1, full1_ref, send1_ref, parts1_ref, line1_ref, fin1_ref)
    sum2 = reducer(1, unit2, full2_ref, send2_ref, parts2_ref, line2_ref, fin2_ref)
    sum2[0]()

    third = functools.partial(windows_second, c3_ref)
    layer(2, c3_ref, store_second, split_second(), first_half, third, weight_back, dot_nt, 0, back_of)
    delta_t = face_ref[...].reshape(512, 128).T
    for pair in range(PAIRS_FIRST):
        both = []
        for block in (2 * pair, min(2 * pair + 1, 14)):
            a, r = block // 5, ROWS_FIRST[block % 5]
            both.append(c1_ref[a : a + 8, r : r + 64, :].reshape(512, 128))
        got = dot(delta_t, jnp.concatenate(both, axis=1))
        one, two = got[:, :128], got[:, 128:]
        straight = jnp.where(wide_quarter, one[0:64], two[64:128])
        crossed = jnp.where(wide_quarter, two[0:64], one[64:128])
        swapped = jnp.where(wide_quarter, pltpu.roll(crossed, 96, 1), pltpu.roll(crossed, 32, 1))
        put_gradient(full1_ref, send1_ref, pair, straight + swapped)
    sum1[0]()
    sum2[1]()
    sum1[1]()
    sum2[2]()
    sum1[2]()
    sum2[3]()
    for pair in range(14):
        value = fin2_ref[4 * pair : 4 * pair + 4].reshape(64, 128).T.astype(F32)
        g2_ref[2 * pair] = value[0:64]
        if pair < 13:
            g2_ref[2 * pair + 1] = value[64:128]
    sum1[3]()
    sum2[4]()
    sum1[4]()
    halo_sent(0)


def unpack_kernel(block_ref, fin_ref, g2_ref, out_hbm, g1_hbm, g2_hbm, g1_ref, sem):
    block_copy = pltpu.make_async_copy(block_ref, out_hbm, sem.at[0])
    second_copies = [
        pltpu.make_async_copy(g2_ref.at[pl.ds(k, 9)], g2_hbm.at[pl.ds(k, 9)], sem.at[3 + k // 9])
        for k in (0, 9, 18)
    ]
    first_copy = pltpu.make_async_copy(g1_ref, g1_hbm, sem.at[2])
    for copy in second_copies:
        copy.start()
    block_copy.start()
    for pair in range(PAIRS_FIRST):
        value = fin_ref[4 * pair : 4 * pair + 4].reshape(64, 128).T.astype(F32)
        for j in range(2):
            block = 2 * pair + j
            if block > 14:
                continue
            a, kind = block // 5, block % 5
            if kind < 3:
                offsets = (9 * a + 3 * kind, 9 * a + 3 * kind + 2)
            elif kind == 3:
                offsets = (9 * a + 1, 9 * a + 7)
            else:
                offsets = (9 * a + 4,)
            for i, k in enumerate(offsets):
                g1_ref[k] = value[64 * i + 32 * j : 64 * i + 32 * j + 32]
    first_copy.start()
    for copy in second_copies:
        copy.wait()
    block_copy.wait()
    first_copy.wait()


def solution(mesh):
    n_region, n_rep = mesh.shape["region"], mesh.shape["rep"]
    nx, ny = (4, 4) if n_region == 32 else (2, n_rep // 2)
    nz = n_region // nx
    sizes = (nx, nz, ny)
    n_plane = nx * ny
    core1, core2 = 2 * PAIRS_FIRST, 2 * PAIRS_SECOND
    unit1, unit2 = core1 // n_plane, core2 // n_plane
    vmem = pl.BlockSpec(memory_space=pltpu.VMEM)
    smem = pl.BlockSpec(memory_space=pltpu.SMEM)
    hbm = pl.BlockSpec(memory_space=pltpu.HBM)
    anywhere = pl.BlockSpec(memory_space=pl.ANY)
    dma = pltpu.SemaphoreType.DMA

    def body(features, weight_first, weight_second, cotangent, neighbours, voxel_mask):
        scale = 1.0 / math.sqrt(n_rep * 2 * n_region * 512)
        block, fin1, g2 = pl.pallas_call(
            functools.partial(main_kernel, sizes, scale),
            out_shape=(
                jax.ShapeDtypeStruct((512, 128), BF16),
                jax.ShapeDtypeStruct((2 * core1, 16, 128), BF16),
                jax.ShapeDtypeStruct((27, 64, 64), F32),
            ),
            in_specs=[hbm, hbm, hbm, hbm, smem, hbm],
            out_specs=(vmem, vmem, vmem),
            scratch_shapes=[
                pltpu.VMEM((64, 512), BF16),
                pltpu.VMEM((27, 32, 64), BF16),
                pltpu.VMEM((27, 64, 64), BF16),
                pltpu.VMEM((512, 128), BF16),
                pltpu.VMEM((2, 512), jnp.int32),
                pltpu.VMEM((8, 64, 128), F32),
                pltpu.VMEM((8, 64, 128), F32),
                pltpu.VMEM((8, 64, 128), BF16),
                pltpu.VMEM((3, 2, 64, 128), BF16),
                pltpu.VMEM((2, 3, 64, 128), BF16),
                pltpu.VMEM((2, 3, 64, 128), BF16),
                pltpu.VMEM((2, 3, 272, 128), BF16),
                pltpu.VMEM((3, 8, 64, 128), F32),
                pltpu.VMEM((2, 3, 64, 128), F32),
                pltpu.VMEM((10, 272, 128), BF16),
                pltpu.VMEM((3, 10, 144, 128), BF16),
                pltpu.VMEM((3, 10, 144, 128), BF16),
                pltpu.VMEM((3, 5, 128, 128), BF16),
                pltpu.VMEM((27, 128, 128), BF16),
                pltpu.VMEM((512, 128), F32),
                pltpu.VMEM((8, 64, 128), F32),
                pltpu.VMEM((2 * core1, 16, 128), F32),
                pltpu.VMEM((2 * core2, 16, 128), F32),
                pltpu.VMEM((2 * core1, 16, 128), BF16),
                pltpu.VMEM((2 * core2, 16, 128), BF16),
                pltpu.VMEM((2 * n_plane, unit1, 16, 128), BF16),
                pltpu.VMEM((2 * n_plane, unit2, 16, 128), BF16),
                pltpu.VMEM((nz, unit1, 16, 128), BF16),
                pltpu.VMEM((nz, unit2, 16, 128), BF16),
                pltpu.VMEM((2 * core2, 16, 128), BF16),
                dma((5,)),
                dma((3, 2)),
                dma((3, 2)),
                dma((2, 3)),
                dma((2, 3)),
            ],
            compiler_params=pltpu.CompilerParams(
                collective_id=0, has_side_effects=True, vmem_limit_bytes=40 * 2**20
            ),
        )(
            *(
                pltpu.with_memory_space_constraint(x, pltpu.HBM)
                for x in (
                    jnp.swapaxes(features, 1, 2).reshape(64, 512),
                    weight_first,
                    weight_second,
                    cotangent.reshape(512, 128),
                    neighbours.reshape(2, 27),
                    voxel_mask.reshape(2, 512),
                )
            )
        )
        out, g1, g2 = pl.pallas_call(
            unpack_kernel,
            out_shape=(
                jax.ShapeDtypeStruct((512, 128), BF16),
                jax.ShapeDtypeStruct((27, 32, 64), F32),
                jax.ShapeDtypeStruct((27, 64, 64), F32),
            ),
            in_specs=[vmem, vmem, vmem],
            out_specs=(anywhere, anywhere, anywhere),
            scratch_shapes=[
                pltpu.VMEM((27, 32, 64), F32),
                dma((6,)),
            ],
            compiler_params=pltpu.CompilerParams(vmem_limit_bytes=40 * 2**20),
        )(block, fin1, g2)
        return out.reshape(1, 512, 128), g1, g2

    in_specs = (
        P("rep", None, "region"),
        P(),
        P(),
        P("rep", None, "region"),
        P("rep", "region", None),
        P("rep", "region", None),
    )
    out_specs = (P("rep", None, "region"), P(), P())
    return jax.shard_map(body, mesh=mesh, in_specs=in_specs, out_specs=out_specs, check_vma=False)
```

```python
import functools
import math

import jax
import jax.numpy as jnp
from jax import lax
from jax.experimental import pallas as pl
from jax.experimental.pallas import tpu as pltpu
from jax.sharding import PartitionSpec as P

MESH = pl.DeviceIdType.MESH
F32 = jnp.float32
BF16 = jnp.bfloat16
ROWS = (0, 80, 16)
ROWS_FIRST = (0, 80, 16, 144, 208)
PAIRS_SECOND = 16
PAIRS_FIRST = 8


def iota(shape, axis):
    return lax.broadcasted_iota(jnp.int32, shape, axis)


def dot(a, b):
    return jnp.dot(a, b, preferred_element_type=F32)


def dot_nt(a, b):
    return lax.dot_general(a, b, (((1,), (1,)), ((), ())), preferred_element_type=F32)


def places(sizes):
    nx, nz, ny = sizes
    region = lax.axis_index("region")
    rep = lax.axis_index("rep")
    return region // nz, lax.rem(region, nz), rep // 2, lax.rem(rep, 2), region, rep


def main_kernel(
    sizes,
    scale,
    feat_hbm,
    w1_hbm,
    w2_hbm,
    cot_hbm,
    nbr_ref,
    mask_hbm,
    out_ref,
    fin1_ref,
    g2_ref,
    feat_ref,
    w1_ref,
    w2_ref,
    cot_ref,
    mask_ref,
    live_ref,
    field_ref,
    face_ref,
    halo_ref,
    edge_ref,
    rim_ref,
    ext_ref,
    side_ref,
    far_ref,
    c1_ref,
    c2_ref,
    c3_ref,
    w1b_ref,
    w2b_ref,
    acc_ref,
    slope_ref,
    full1_ref,
    full2_ref,
    send1_ref,
    send2_ref,
    pair2_ref,
    half2_ref,
    mine2_ref,
    parts1_ref,
    parts2_ref,
    line1_ref,
    line2_ref,
    fin2_ref,
    load_sem,
    halo_send,
    halo_recv,
    pair_sem,
    sum_send,
    sum_recv,
):
    nx, nz, ny = sizes
    n_region, n_plane = nx * nz, nx * ny
    my_x, my_z, my_y, core, region, rep = places(sizes)
    member = my_x * ny + my_y
    right = lax.rem(region + 1, n_region)
    left = lax.rem(region + n_region - 1, n_region)
    twin = {"region": region, "rep": my_y * 2 + 1 - core}

    def apart(offset, size):
        return min(offset, size - offset)

    offsets = sorted(
        ((dx, dy, dc) for dx in range(nx) for dy in range(ny) for dc in range(2)),
        key=lambda d: (-apart(d[0], nx) - apart(d[1], ny), d),
    )
    plane_peers, all_peers = [], []
    for dx, dy, dc in offsets:
        if (dx, dy, dc) == (0, 0, 0):
            continue
        x, y, c = lax.rem(my_x + dx, nx), lax.rem(my_y + dy, ny), lax.rem(core + dc, 2)
        at = {"region": x * nz + my_z, "rep": y * 2 + c}
        all_peers.append((c * n_plane + x * ny + y, at))
        if dc == 0:
            plane_peers.append((x * ny + y, at))
    line_peers = [
        {"region": my_x * nz + lax.rem(my_z + step, nz), "rep": rep}
        for step in sorted(range(1, nz), key=lambda d: -apart(d, nz))
    ]

    halo_ref[...] = jnp.zeros((3, 2, 64, 128), BF16)
    rim_ref[...] = jnp.zeros((2, 3, 64, 128), BF16)

    barrier = pltpu.get_barrier_semaphore()
    partners = [{"region": right, "rep": rep}, {"region": left, "rep": rep}]
    partners += [at for _, at in all_peers] + line_peers
    for at in partners[:2]:
        pl.semaphore_signal(barrier, inc=1, device_id=at, device_id_type=MESH)
    loads = [
        pltpu.make_async_copy(src, dst, load_sem.at[i])
        for i, (src, dst) in enumerate(
            (
                (mask_hbm, mask_ref),
                (feat_hbm, feat_ref),
                (w1_hbm, w1_ref),
                (w2_hbm, w2_ref),
                (cot_hbm, cot_ref),
            )
        )
    ]
    for load in loads:
        load.start()
    for at in partners[2:]:
        pl.semaphore_signal(barrier, inc=1, device_id=at, device_id_type=MESH)
    loads[0].wait()
    loads[1].wait()

    mask = jnp.concatenate([mask_ref[...].astype(F32), jnp.zeros((6, 512), F32)], axis=0).T
    tile_of = (iota((8, 128), 1) // 64 == iota((8, 128), 0)).astype(F32)
    tile_of_first = (lax.rem(iota((8, 128), 1) // 32, 2) == iota((8, 128), 0)).astype(F32)
    live_ref[...] = dot(mask, tile_of).reshape(8, 64, 128)
    twice = (iota((64, 128), 0) == lax.rem(iota((64, 128), 1), 64)).astype(BF16)
    spread = dot(feat_ref[...].T, twice) * dot(mask, tile_of_first)
    field_ref[...] = spread.reshape(8, 64, 128)
    face_ref[...] = spread.astype(BF16).reshape(8, 64, 128)

    def halo_copy(which, side):
        return pltpu.make_async_remote_copy(
            src_ref=edge_ref.at[side] if which == 0 else face_ref.at[7 if side == 0 else 0],
            dst_ref=rim_ref.at[side] if which == 0 else halo_ref.at[which, side],
            send_sem=halo_send.at[which, side],
            recv_sem=halo_recv.at[which, side],
            device_id={"region": right if side == 0 else left, "rep": rep},
            device_id_type=MESH,
        )

    has_right, has_left = region < n_region - 1, region > 0

    def halo_start(which):
        pl.when(has_right)(lambda: halo_copy(which, 0).start())
        pl.when(has_left)(lambda: halo_copy(which, 1).start())

    def halo_wait(which):
        @pl.when(has_left)
        def _():
            halo_copy(which, 0).wait_recv()

        @pl.when(has_right)
        def _():
            halo_copy(which, 1).wait_recv()

    def halo_sent(which):
        pl.when(has_right)(lambda: halo_copy(which, 0).wait_send())
        pl.when(has_left)(lambda: halo_copy(which, 1).wait_send())

    wide_half = iota((64, 128), 1) < 64
    wide_quarter = lax.rem(iota((64, 128), 1) // 32, 2) == 0
    one_lane = wide_quarter[0:1]
    links = []
    for s in range(2):
        for k in range(9):
            named = [(nbr_ref[t, 9 + k] == 2 + s).astype(F32) for t in range(2)]
            links.append(jnp.where(one_lane, named[0], named[1]))
        links.append(jnp.zeros((23, 128), F32))
    links = jnp.concatenate(links, axis=0).astype(BF16)
    for side, face, inside in ((0, 7, 6), (1, 0, 1)):
        edge_ref[side, 0] = jnp.where(wide_half, face_ref[face], face_ref[inside])
        edge_ref[side, 1] = live_ref[face].astype(BF16)
        edge_ref[side, 2] = links
    pl.semaphore_wait(barrier, len(partners))
    halo_start(0)

    loads[2].wait()
    eye = iota((64, 256), 0)
    put = ((eye == iota((64, 256), 1)) | (eye == iota((64, 256), 1) - 192)).astype(BF16)
    spread1 = dot(w1_ref[...].reshape(27 * 32, 64), put).astype(BF16)
    top = spread1[:, :128].reshape(3, 3, 3, 32, 128)
    low = spread1[:, 128:].reshape(3, 3, 3, 32, 128)
    for b in range(3):
        for at, c in ((0, 0), (64, 2)):
            w1b_ref[:, b, at : at + 32, :] = top[:, b, c]
            w1b_ref[:, b, at + 32 : at + 64, :] = low[:, b, c]
    for at, b in ((0, 0), (64, 2)):
        w1b_ref[:, 3, at : at + 32, :] = top[:, b, 1]
        w1b_ref[:, 3, at + 32 : at + 64, :] = low[:, b, 1]
    w1b_ref[:, 4, 0:32, :] = top[:, 1, 1]
    w1b_ref[:, 4, 32:64, :] = low[:, 1, 1]
    w1b_ref[:, 4, 64:128, :] = jnp.zeros((3, 64, 128), BF16)
    side_ref[2] = jnp.zeros((8, 64, 128), F32)
    far_ref[:, 2] = jnp.zeros((2, 64, 128), F32)
    lane = iota((8, 128), 1)
    first_half = lane < 64
    even_quarter = lax.rem(lane // 32, 2) == 0
    z_row = iota((8, 128), 0)
    z_first, z_last = z_row == 0, z_row == 7

    def rows_of(masked, count):
        return jnp.concatenate([masked] * count, axis=0) if count > 1 else masked

    def split_first():
        source, target = iota((128, 256), 0), iota((128, 256), 1)
        return (source == (target // 128) * 32 + lax.rem(target, 32)).astype(BF16)

    def split_second():
        source, target = iota((128, 256), 0), iota((128, 256), 1)
        return (source == (target // 128) * 64 + lax.rem(target, 64)).astype(BF16)

    def shifted(middle, load, tile_lane):
        ext = []
        for c in range(3):
            groups = [load(0, c, 56, 64)]
            if c == 1 and middle is not None:
                mid = middle
            else:
                mid = load(1, c, 0, 64)
            groups += [mid[8 * y : 8 * y + 8] for y in range(8)]
            groups.append(load(2, c, 0, 8))
            ext.append(groups)
        down = [pltpu.roll(jnp.where(z_last, ext[0][y], ext[1][y]), 1, 0) for y in range(10)]
        up = [pltpu.roll(jnp.where(z_first, ext[2][y], ext[1][y]), 7, 0) for y in range(10)]
        return down, ext[1], up

    def store_first(c_ref, slab, down, mid, up):
        both = [jnp.where(first_half, d, u) for d, u in zip(down, up)]
        c_ref[slab, 0:80, :] = jnp.concatenate(both, axis=0).astype(BF16)
        c_ref[slab, 80:144, :] = jnp.concatenate(both[1:9], axis=0).astype(BF16)
        ends = [jnp.where(first_half, mid[y], mid[y + 2]) for y in range(8)]
        c_ref[slab, 144:208, :] = jnp.concatenate(ends, axis=0).astype(BF16)
        c_ref[slab, 208:272, :] = jnp.concatenate(mid[1:9], axis=0).astype(BF16)

    def store_second(c_ref, slab, down, mid, up):
        for c, groups in enumerate((down, mid, up)):
            c_ref[c, slab, 0:80, :] = jnp.concatenate(groups, axis=0).astype(BF16)
            c_ref[c, slab, 80:144, :] = jnp.concatenate(groups[1:9], axis=0).astype(BF16)

    def build_inner(c_ref, store, splitter, tile_lane):
        whole = dot(face_ref[...].reshape(512, 128), splitter)
        side_ref[0] = whole[:, :128].reshape(8, 64, 128)
        side_ref[1] = whole[:, 128:].reshape(8, 64, 128)
        named = [
            [jnp.minimum(jnp.maximum(nbr_ref[t, 9 + k] - 2, 0), 2) for k in range(9)]
            for t in range(2)
        ]

        @pl.loop(0, 8, unroll=4)
        def _(x):
            def load(b, c, start, stop):
                k = 3 * b + c
                return jnp.where(
                    rows_of(tile_lane, (stop - start) // 8),
                    side_ref[named[0][k], x, start:stop, :],
                    side_ref[named[1][k], x, start:stop, :],
                )

            store(c_ref, x + 1, *shifted(field_ref[x], load, tile_lane))

    def build_faces(which, c_ref, store, splitter, tile_lane):
        source = rim_ref[:, 0] if which == 0 else halo_ref[which]
        whole = dot(source.reshape(128, 128), splitter)
        for side in range(2):
            far_ref[side, 0] = whole[64 * side : 64 * side + 64, :128]
            far_ref[side, 1] = whole[64 * side : 64 * side + 64, 128:]
            named = [
                [
                    jnp.minimum(jnp.maximum(nbr_ref[t, 18 * side + k] - 4 * side, 0), 2)
                    for k in range(9)
                ]
                for t in range(2)
            ]

            def load(b, c, start, stop):
                k = 3 * b + c
                return jnp.where(
                    rows_of(tile_lane, (stop - start) // 8),
                    far_ref[side, named[0][k], start:stop, :],
                    far_ref[side, named[1][k], start:stop, :],
                )

            store(c_ref, 9 * side, *shifted(None, load, tile_lane))

    def build_cross():
        for side, x, base, code in ((0, 0, 18, 0), (1, 7, 0, 4)):
            named = []
            for s in range(2):
                row = []
                for k in range(9):
                    link = [nbr_ref[t, 26 - base - k] == code + s for t in range(2)]
                    row.append(jnp.where(link[0], 0, jnp.where(link[1], 1, 2)))
                named.append(row)

            def load(b, c, start, stop):
                k = 3 * b + c
                return jnp.where(
                    rows_of(even_quarter, (stop - start) // 8),
                    side_ref[named[0][k], x, start:stop, :],
                    side_ref[named[1][k], x, start:stop, :],
                )

            store_first(ext_ref.at[side], 2 - 2 * side, *shifted(None, load, even_quarter))

    def build_rim():
        source, target = iota((128, 384), 0), iota((128, 384), 1)
        group, lane_in = target // 128, lax.rem(target, 128)
        wanted = jnp.where(group == 0, lax.rem(lane_in, 64), (group - 1) * 32 + lax.rem(lane_in, 32))
        for inside in range(2):
            spread_out = (source == wanted + 64 * inside).astype(BF16)
            whole = dot(rim_ref[:, 0].reshape(128, 128), spread_out)
            for side in range(2):
                part = whole[64 * side : 64 * side + 64]
                table = rim_ref[side, 2].astype(F32)

                def load(b, c, start, stop):
                    k = 3 * b + c
                    first = table[k : k + 1] * part[start:stop, 128:256]
                    return first + table[32 + k : 33 + k] * part[start:stop, 256:384]

                slab = 1 if inside == 0 else 2 * side
                store_first(ext_ref.at[side], slab, *shifted(part[:, 0:128], load, even_quarter))

    def hidden_beside():
        windows = []
        for a in range(3):
            for r in ROWS_FIRST:
                windows.append(ext_ref[:, a, r : r + 64, :].reshape(128, 128))
        pre = dot(jnp.concatenate(windows, axis=1), w1b_ref[...].reshape(15 * 128, 128))
        live = rim_ref[:, 1].reshape(128, 128).astype(F32)
        hidden = (live * pre * jax.nn.sigmoid(pre)).astype(BF16)
        halo_ref[1] = hidden.reshape(2, 64, 128)

    def windows_first(start, count):
        return [
            c1_ref[start : start + count, r : r + 64, :].reshape(count * 64, 128)
            for r in ROWS_FIRST
        ]

    def windows_second(c_ref, start, count):
        return [
            c_ref[c, start : start + count, ROWS[b] : ROWS[b] + 64, :].reshape(count * 64, 128)
            for b in range(3)
            for c in range(3)
        ]

    def conv_inner(windows, weight, product=dot, columns=1):
        weights = jnp.concatenate([weight(0), weight(2), weight(1)], axis=columns)
        got = product(jnp.concatenate(windows(1, 8), axis=1), weights)
        acc_ref[...] = got[:, 256:384]
        acc_ref[64:512] += got[0:448, 0:128]
        acc_ref[0:448] += got[64:512, 128:256]

    def conv_faces(windows, weight, product=dot, columns=1):
        weights = jnp.concatenate([weight(0), weight(2)], axis=columns)
        rows = [jnp.concatenate(both, axis=0) for both in zip(windows(0, 1), windows(9, 1))]
        got = product(jnp.concatenate(rows, axis=1), weights)
        acc_ref[0:64] += got[0:64, 0:128]
        acc_ref[448:512] += got[64:128, 128:256]

    def weight_first(a):
        return w1b_ref[a].reshape(5 * 128, 128)

    def weight_second(a):
        return w2b_ref[9 * a : 9 * a + 9].reshape(9 * 128, 128)

    def weight_back(a):
        return jnp.concatenate([w2b_ref[26 - k] for k in range(9 * a, 9 * a + 9)], axis=1)

    def layer(which, c_ref, store, splitter, tile_lane, windows, weight, product, columns, activate, between=None):
        build_inner(c_ref, store, splitter, tile_lane)
        conv_inner(windows, weight, product, columns)
        if which == 0:
            build_cross()
        pl.loop(1, 7, unroll=3)(activate)
        if between is not None:
            between()
        if which != 1:
            halo_wait(which)
        build_faces(which, c_ref, store, splitter, tile_lane)
        if which == 0:
            build_rim()
            hidden_beside()
        conv_faces(windows, weight, product, columns)
        if which == 2:
            halo_sent(2)
        pl.loop(0, 2, unroll=2)(lambda i: activate(7 * i))

    def hidden_of(x):
        rows = pl.ds(pl.multiple_of(x * 64, 64), 64)
        pre = acc_ref[rows, :]
        live = live_ref[x]
        sig = jax.nn.sigmoid(pre)
        hidden = (live * pre * sig).astype(BF16)
        face_ref[x] = hidden
        field_ref[x] = hidden.astype(F32)
        slope_ref[x] = live * sig * (1.0 + pre * (1.0 - sig))

    def outputs_of(x):
        rows = pl.ds(pl.multiple_of(x * 64, 64), 64)
        pre = acc_ref[rows, :]
        live = live_ref[x]
        sig = jax.nn.sigmoid(pre)
        out_ref[rows, :] = (live * pre * sig).astype(BF16)
        upstream = cot_ref[rows, :].astype(F32)
        delta = (upstream * live * sig * (1.0 + pre * (1.0 - sig))).astype(BF16)
        face_ref[x] = delta
        field_ref[x] = delta.astype(F32)

    def back_of(x):
        rows = pl.ds(pl.multiple_of(x * 64, 64), 64)
        face_ref[x] = (acc_ref[rows, :] * slope_ref[x]).astype(BF16)

    layer(0, c1_ref, store_first, split_first(), even_quarter, windows_first, weight_first, dot, 1, hidden_of)

    loads[3].wait()
    spread2 = dot(w2_ref[...].reshape(27 * 64, 64), put).astype(BF16)
    w2b_ref[:, 0:64, :] = spread2[:, :128].reshape(27, 64, 128)
    w2b_ref[:, 64:128, :] = spread2[:, 128:].reshape(27, 64, 128)
    second = functools.partial(windows_second, c2_ref)
    loads[4].wait()
    layer(1, c2_ref, store_second, split_second(), first_half, second, weight_second, dot, 1, outputs_of)
    halo_start(2)

    wide_half = iota((64, 128), 1) < 64
    wide_quarter = lax.rem(iota((64, 128), 1) // 32, 2) == 0
    per_core1, per_core2 = PAIRS_FIRST // 2, PAIRS_SECOND // 2

    def put_gradient(full, send, pair, value):
        value = value.reshape(4, 16, 128)
        full[4 * pair : 4 * pair + 4] = value
        send[4 * pair : 4 * pair + 4] = value.astype(BF16)

    delta_t = face_ref[...].reshape(512, 128).T
    for pair in range(14):
        both = []
        for k in (2 * pair, min(2 * pair + 1, 26)):
            a, b, c = k // 9, k // 3 % 3, k % 3
            window = c2_ref[c, a : a + 8, ROWS[b] : ROWS[b] + 64, :]
            both.append(window.reshape(512, 128))
        got = dot(delta_t, jnp.concatenate(both, axis=1))
        one, two = got[:, :128], got[:, 128:]
        straight = jnp.where(wide_half, one[0:64], two[64:128])
        crossed = jnp.where(wide_half, two[0:64], one[64:128])
        put_gradient(full2_ref, send2_ref, pair, straight + pltpu.roll(crossed, 64, 1))
    for pair in range(14, PAIRS_SECOND):
        put_gradient(full2_ref, send2_ref, pair, jnp.zeros((64, 128), F32))

    def reducer(which, unit, send, parts, line, fin):

        def remote(stage, src, dst, device):
            return pltpu.make_async_remote_copy(
                src_ref=src,
                dst_ref=dst,
                send_sem=sum_send.at[which, stage],
                recv_sem=sum_recv.at[which, stage],
                device_id=device,
                device_id_type=MESH,
            )

        place = pl.ds((core * n_plane + member) * unit, unit)
        parts_whole = parts.at[pl.ds(1, parts.shape[0] - 1)]
        line_whole = line.at[pl.ds(0, nz - 1)]
        fin_whole = fin.at[pl.ds(0, (2 * n_plane - 1) * unit)]
        whole = [
            remote(0, parts_whole, parts_whole, twin),
            remote(1, line_whole, line_whole, twin),
            remote(2, fin_whole, fin_whole, twin),
        ]

        def start_parts(peers):
            for i, (other, at) in enumerate(peers):
                remote(0, send.at[pl.ds(other * unit, unit)], parts.at[i + 1], at).start()

        def start_line(total):
            whole[0].wait_recv()
            for i in range(1, parts.shape[0]):
                total = total + parts[i].astype(F32)
            line[my_z] = total.astype(BF16)
            for at in line_peers:
                remote(1, line.at[my_z], line.at[my_z], at).start()

        def start_back():
            whole[1].wait_recv()
            total = line[0].astype(F32)
            for z in range(1, nz):
                total = total + line[z].astype(F32)
            fin[place] = (total * scale).astype(BF16)
            for _, at in all_peers:
                remote(2, fin.at[place], fin.at[place], at).start()

        def finish():
            whole[2].wait_recv()

        def sent():
            for copy in whole:
                copy.wait_send()

        return start_parts, start_line, start_back, finish, sent

    unit1, unit2 = 4 * per_core1 // n_plane, 4 * per_core2 // n_plane
    sum1 = reducer(0, unit1, send1_ref, parts1_ref, line1_ref, fin1_ref)
    sum2 = reducer(1, unit2, half2_ref, parts2_ref, line2_ref, fin2_ref)
    place1 = pl.ds((core * n_plane + member) * unit1, unit1)

    def half_units(which_core):
        return pl.ds(which_core * 4 * per_core2, 4 * per_core2)

    pair_copy = pltpu.make_async_remote_copy(
        src_ref=send2_ref.at[half_units(1 - core)],
        dst_ref=pair2_ref,
        send_sem=pair_sem.at[0],
        recv_sem=pair_sem.at[1],
        device_id=twin,
        device_id_type=MESH,
    )
    pair_copy.start()

    def start_second():
        pair_copy.wait_recv()
        total = full2_ref[half_units(core)] + pair2_ref[...].astype(F32)
        mine2_ref[...] = total
        half2_ref[...] = total.astype(BF16)
        sum2[0](plane_peers)

    third = functools.partial(windows_second, c3_ref)
    layer(2, c3_ref, store_second, split_second(), first_half, third, weight_back, dot_nt, 0, back_of, start_second)
    delta_t = face_ref[...].reshape(512, 128).T
    for pair in range(PAIRS_FIRST):
        both = []
        for block in (2 * pair, min(2 * pair + 1, 14)):
            a, r = block // 5, ROWS_FIRST[block % 5]
            both.append(c1_ref[a : a + 8, r : r + 64, :].reshape(512, 128))
        got = dot(delta_t, jnp.concatenate(both, axis=1))
        one, two = got[:, :128], got[:, 128:]
        straight = jnp.where(wide_quarter, one[0:64], two[64:128])
        crossed = jnp.where(wide_quarter, two[0:64], one[64:128])
        swapped = jnp.where(wide_quarter, pltpu.roll(crossed, 96, 1), pltpu.roll(crossed, 32, 1))
        put_gradient(full1_ref, send1_ref, pair, straight + swapped)
    sum1[0](all_peers)
    sum2[1](mine2_ref[pl.ds(member * unit2, unit2)])
    sum1[1](full1_ref[place1])
    sum2[2]()
    sum1[2]()
    sum2[3]()
    for pair in range(14):
        value = fin2_ref[4 * pair : 4 * pair + 4].reshape(64, 128).T.astype(F32)
        g2_ref[2 * pair] = value[0:64]
        if pair < 13:
            g2_ref[2 * pair + 1] = value[64:128]
    sum1[3]()
    pair_copy.wait_send()
    sum2[4]()
    sum1[4]()
    halo_sent(0)


def unpack_kernel(block_ref, fin_ref, g2_ref, out_hbm, g1_hbm, g2_hbm, g1_ref, sem):
    block_copy = pltpu.make_async_copy(block_ref, out_hbm, sem.at[0])
    second_copies = [
        pltpu.make_async_copy(g2_ref.at[pl.ds(k, 9)], g2_hbm.at[pl.ds(k, 9)], sem.at[3 + k // 9])
        for k in (0, 9, 18)
    ]
    first_copy = pltpu.make_async_copy(g1_ref, g1_hbm, sem.at[2])
    for copy in second_copies:
        copy.start()
    block_copy.start()
    for pair in range(PAIRS_FIRST):
        value = fin_ref[4 * pair : 4 * pair + 4].reshape(64, 128).T.astype(F32)
        for j in range(2):
            block = 2 * pair + j
            if block > 14:
                continue
            a, kind = block // 5, block % 5
            if kind < 3:
                offsets = (9 * a + 3 * kind, 9 * a + 3 * kind + 2)
            elif kind == 3:
                offsets = (9 * a + 1, 9 * a + 7)
            else:
                offsets = (9 * a + 4,)
            for i, k in enumerate(offsets):
                g1_ref[k] = value[64 * i + 32 * j : 64 * i + 32 * j + 32]
    first_copy.start()
    for copy in second_copies:
        copy.wait()
    block_copy.wait()
    first_copy.wait()


def solution(mesh):
    n_region, n_rep = mesh.shape["region"], mesh.shape["rep"]
    nx, ny = (4, 4) if n_region == 32 else (2, n_rep // 2)
    nz = n_region // nx
    sizes = (nx, nz, ny)
    n_plane = nx * ny
    core1, core2 = 2 * PAIRS_FIRST, 2 * PAIRS_SECOND
    unit1, unit2 = core1 // n_plane, core2 // n_plane
    vmem = pl.BlockSpec(memory_space=pltpu.VMEM)
    smem = pl.BlockSpec(memory_space=pltpu.SMEM)
    hbm = pl.BlockSpec(memory_space=pltpu.HBM)
    anywhere = pl.BlockSpec(memory_space=pl.ANY)
    dma = pltpu.SemaphoreType.DMA

    def body(features, weight_first, weight_second, cotangent, neighbours, voxel_mask):
        scale = 1.0 / math.sqrt(n_rep * 2 * n_region * 512)
        block, fin1, g2 = pl.pallas_call(
            functools.partial(main_kernel, sizes, scale),
            out_shape=(
                jax.ShapeDtypeStruct((512, 128), BF16),
                jax.ShapeDtypeStruct((2 * core1, 16, 128), BF16),
                jax.ShapeDtypeStruct((27, 64, 64), F32),
            ),
            in_specs=[hbm, hbm, hbm, hbm, smem, hbm],
            out_specs=(vmem, vmem, vmem),
            scratch_shapes=[
                pltpu.VMEM((64, 512), BF16),
                pltpu.VMEM((27, 32, 64), BF16),
                pltpu.VMEM((27, 64, 64), BF16),
                pltpu.VMEM((512, 128), BF16),
                pltpu.VMEM((2, 512), jnp.int32),
                pltpu.VMEM((8, 64, 128), F32),
                pltpu.VMEM((8, 64, 128), F32),
                pltpu.VMEM((8, 64, 128), BF16),
                pltpu.VMEM((3, 2, 64, 128), BF16),
                pltpu.VMEM((2, 3, 64, 128), BF16),
                pltpu.VMEM((2, 3, 64, 128), BF16),
                pltpu.VMEM((2, 3, 272, 128), BF16),
                pltpu.VMEM((3, 8, 64, 128), F32),
                pltpu.VMEM((2, 3, 64, 128), F32),
                pltpu.VMEM((10, 272, 128), BF16),
                pltpu.VMEM((3, 10, 144, 128), BF16),
                pltpu.VMEM((3, 10, 144, 128), BF16),
                pltpu.VMEM((3, 5, 128, 128), BF16),
                pltpu.VMEM((27, 128, 128), BF16),
                pltpu.VMEM((512, 128), F32),
                pltpu.VMEM((8, 64, 128), F32),
                pltpu.VMEM((2 * core1, 16, 128), F32),
                pltpu.VMEM((2 * core2, 16, 128), F32),
                pltpu.VMEM((2 * core1, 16, 128), BF16),
                pltpu.VMEM((2 * core2, 16, 128), BF16),
                pltpu.VMEM((core2, 16, 128), BF16),
                pltpu.VMEM((core2, 16, 128), BF16),
                pltpu.VMEM((core2, 16, 128), F32),
                pltpu.VMEM((2 * n_plane, unit1, 16, 128), BF16),
                pltpu.VMEM((n_plane, unit2, 16, 128), BF16),
                pltpu.VMEM((nz, unit1, 16, 128), BF16),
                pltpu.VMEM((nz, unit2, 16, 128), BF16),
                pltpu.VMEM((2 * core2, 16, 128), BF16),
                dma((5,)),
                dma((3, 2)),
                dma((3, 2)),
                dma((2,)),
                dma((2, 3)),
                dma((2, 3)),
            ],
            compiler_params=pltpu.CompilerParams(
                collective_id=0, has_side_effects=True, vmem_limit_bytes=40 * 2**20
            ),
        )(
            *(
                pltpu.with_memory_space_constraint(x, pltpu.HBM)
                for x in (
                    jnp.swapaxes(features, 1, 2).reshape(64, 512),
                    weight_first,
                    weight_second,
                    cotangent.reshape(512, 128),
                    neighbours.reshape(2, 27),
                    voxel_mask.reshape(2, 512),
                )
            )
        )
        out, g1, g2 = pl.pallas_call(
            unpack_kernel,
            out_shape=(
                jax.ShapeDtypeStruct((512, 128), BF16),
                jax.ShapeDtypeStruct((27, 32, 64), F32),
                jax.ShapeDtypeStruct((27, 64, 64), F32),
            ),
            in_specs=[vmem, vmem, vmem],
            out_specs=(anywhere, anywhere, anywhere),
            scratch_shapes=[
                pltpu.VMEM((27, 32, 64), F32),
                dma((6,)),
            ],
            compiler_params=pltpu.CompilerParams(vmem_limit_bytes=40 * 2**20),
        )(block, fin1, g2)
        return out.reshape(1, 512, 128), g1, g2

    in_specs = (
        P("rep", None, "region"),
        P(),
        P(),
        P("rep", None, "region"),
        P("rep", "region", None),
        P("rep", "region", None),
    )
    out_specs = (P("rep", None, "region"), P(), P())
    return jax.shard_map(body, mesh=mesh, in_specs=in_specs, out_specs=out_specs, check_vma=False)
```

```python
import functools
import math

import jax
import jax.numpy as jnp
from jax import lax
from jax.experimental import pallas as pl
from jax.experimental.pallas import tpu as pltpu
from jax.sharding import PartitionSpec as P

MESH = pl.DeviceIdType.MESH
F32 = jnp.float32
BF16 = jnp.bfloat16
ROWS = (0, 80, 16)
ROWS_FIRST = (0, 80, 16, 144, 208)
PAIRS_SECOND = 16
PAIRS_FIRST = 8


def iota(shape, axis):
    return lax.broadcasted_iota(jnp.int32, shape, axis)


def dot(a, b):
    return jnp.dot(a, b, preferred_element_type=F32)


def dot_nt(a, b):
    return lax.dot_general(a, b, (((1,), (1,)), ((), ())), preferred_element_type=F32)


def places(sizes):
    nx, nz, ny = sizes
    region = lax.axis_index("region")
    rep = lax.axis_index("rep")
    return region // nz, lax.rem(region, nz), rep // 2, lax.rem(rep, 2), region, rep


def main_kernel(
    sizes,
    scale,
    feat_hbm,
    w1_hbm,
    w2_hbm,
    cot_hbm,
    nbr_ref,
    mask_hbm,
    out_ref,
    fin1_ref,
    g2_ref,
    feat_ref,
    w1_ref,
    w2_ref,
    cot_ref,
    mask_ref,
    live_ref,
    field_ref,
    face_ref,
    halo_ref,
    edge_ref,
    rim_ref,
    ext_ref,
    side_ref,
    far_ref,
    c1_ref,
    c2_ref,
    c3_ref,
    w1b_ref,
    w2b_ref,
    acc_ref,
    slope_ref,
    full1_ref,
    full2_ref,
    send1_ref,
    send2_ref,
    pair2_ref,
    half2_ref,
    mine2_ref,
    parts1_ref,
    parts2_ref,
    line1_ref,
    line2_ref,
    fin2_ref,
    load_sem,
    halo_send,
    halo_recv,
    pair_sem,
    sum_send,
    sum_recv,
):
    nx, nz, ny = sizes
    n_region, n_plane = nx * nz, nx * ny
    my_x, my_z, my_y, core, region, rep = places(sizes)
    member = my_x * ny + my_y
    right = lax.rem(region + 1, n_region)
    left = lax.rem(region + n_region - 1, n_region)
    twin = {"region": region, "rep": my_y * 2 + 1 - core}

    def apart(offset, size):
        return min(offset, size - offset)

    offsets = sorted(
        ((dx, dy, dc) for dx in range(nx) for dy in range(ny) for dc in range(2)),
        key=lambda d: (-apart(d[0], nx) - apart(d[1], ny), d),
    )
    plane_peers, all_peers = [], []
    for dx, dy, dc in offsets:
        if (dx, dy, dc) == (0, 0, 0):
            continue
        x, y, c = lax.rem(my_x + dx, nx), lax.rem(my_y + dy, ny), lax.rem(core + dc, 2)
        at = {"region": x * nz + my_z, "rep": y * 2 + c}
        all_peers.append((c * n_plane + x * ny + y, at))
        if dc == 0:
            plane_peers.append((x * ny + y, at))
    line_peers = [
        {"region": my_x * nz + lax.rem(my_z + step, nz), "rep": rep}
        for step in sorted(range(1, nz), key=lambda d: -apart(d, nz))
    ]

    halo_ref[...] = jnp.zeros((3, 2, 64, 128), BF16)
    rim_ref[...] = jnp.zeros((2, 3, 64, 128), BF16)

    barrier = pltpu.get_barrier_semaphore()
    partners = [{"region": right, "rep": rep}, {"region": left, "rep": rep}]
    partners += [at for _, at in all_peers] + line_peers
    for at in partners[:2]:
        pl.semaphore_signal(barrier, inc=1, device_id=at, device_id_type=MESH)
    loads = [
        pltpu.make_async_copy(src, dst, load_sem.at[i])
        for i, (src, dst) in enumerate(
            (
                (mask_hbm, mask_ref),
                (feat_hbm, feat_ref),
                (w1_hbm, w1_ref),
                (w2_hbm, w2_ref),
                (cot_hbm, cot_ref),
            )
        )
    ]
    for load in loads:
        load.start()
    for at in partners[2:]:
        pl.semaphore_signal(barrier, inc=1, device_id=at, device_id_type=MESH)
    loads[0].wait()
    loads[1].wait()

    mask = jnp.concatenate([mask_ref[...].astype(F32), jnp.zeros((6, 512), F32)], axis=0).T
    tile_of = (iota((8, 128), 1) // 64 == iota((8, 128), 0)).astype(F32)
    tile_of_first = (lax.rem(iota((8, 128), 1) // 32, 2) == iota((8, 128), 0)).astype(F32)
    live_ref[...] = dot(mask, tile_of).reshape(8, 64, 128)
    twice = (iota((64, 128), 0) == lax.rem(iota((64, 128), 1), 64)).astype(BF16)
    spread = dot(feat_ref[...].T, twice) * dot(mask, tile_of_first)
    field_ref[...] = spread.reshape(8, 64, 128)
    face_ref[...] = spread.astype(BF16).reshape(8, 64, 128)

    def halo_copy(which, side):
        return pltpu.make_async_remote_copy(
            src_ref=edge_ref.at[side] if which == 0 else face_ref.at[7 if side == 0 else 0],
            dst_ref=rim_ref.at[side] if which == 0 else halo_ref.at[which, side],
            send_sem=halo_send.at[which, side],
            recv_sem=halo_recv.at[which, side],
            device_id={"region": right if side == 0 else left, "rep": rep},
            device_id_type=MESH,
        )

    has_right, has_left = region < n_region - 1, region > 0

    def halo_start(which):
        pl.when(has_right)(lambda: halo_copy(which, 0).start())
        pl.when(has_left)(lambda: halo_copy(which, 1).start())

    def halo_wait(which):
        @pl.when(has_left)
        def _():
            halo_copy(which, 0).wait_recv()

        @pl.when(has_right)
        def _():
            halo_copy(which, 1).wait_recv()

    def halo_sent(which):
        pl.when(has_right)(lambda: halo_copy(which, 0).wait_send())
        pl.when(has_left)(lambda: halo_copy(which, 1).wait_send())

    wide_half = iota((64, 128), 1) < 64
    wide_quarter = lax.rem(iota((64, 128), 1) // 32, 2) == 0
    one_lane = wide_quarter[0:1]
    links = []
    for s in range(2):
        for k in range(9):
            named = [(nbr_ref[t, 9 + k] == 2 + s).astype(F32) for t in range(2)]
            links.append(jnp.where(one_lane, named[0], named[1]))
        links.append(jnp.zeros((23, 128), F32))
    links = jnp.concatenate(links, axis=0).astype(BF16)
    for side, face, inside in ((0, 7, 6), (1, 0, 1)):
        edge_ref[side, 0] = jnp.where(wide_half, face_ref[face], face_ref[inside])
        edge_ref[side, 1] = live_ref[face].astype(BF16)
        edge_ref[side, 2] = links
    pl.semaphore_wait(barrier, len(partners))
    halo_start(0)

    loads[2].wait()
    eye = iota((64, 256), 0)
    put = ((eye == iota((64, 256), 1)) | (eye == iota((64, 256), 1) - 192)).astype(BF16)
    spread1 = dot(w1_ref[...].reshape(27 * 32, 64), put).astype(BF16)
    top = spread1[:, :128].reshape(3, 3, 3, 32, 128)
    low = spread1[:, 128:].reshape(3, 3, 3, 32, 128)
    for b in range(3):
        for at, c in ((0, 0), (64, 2)):
            w1b_ref[:, b, at : at + 32, :] = top[:, b, c]
            w1b_ref[:, b, at + 32 : at + 64, :] = low[:, b, c]
    for at, b in ((0, 0), (64, 2)):
        w1b_ref[:, 3, at : at + 32, :] = top[:, b, 1]
        w1b_ref[:, 3, at + 32 : at + 64, :] = low[:, b, 1]
    w1b_ref[:, 4, 0:32, :] = top[:, 1, 1]
    w1b_ref[:, 4, 32:64, :] = low[:, 1, 1]
    w1b_ref[:, 4, 64:128, :] = jnp.zeros((3, 64, 128), BF16)
    side_ref[2] = jnp.zeros((8, 64, 128), F32)
    far_ref[:, 2] = jnp.zeros((2, 64, 128), F32)
    lane = iota((8, 128), 1)
    first_half = lane < 64
    even_quarter = lax.rem(lane // 32, 2) == 0
    z_row = iota((8, 128), 0)
    z_first, z_last = z_row == 0, z_row == 7

    def rows_of(masked, count):
        return jnp.concatenate([masked] * count, axis=0) if count > 1 else masked

    def split_first():
        source, target = iota((128, 256), 0), iota((128, 256), 1)
        return (source == (target // 128) * 32 + lax.rem(target, 32)).astype(BF16)

    def split_second():
        source, target = iota((128, 256), 0), iota((128, 256), 1)
        return (source == (target // 128) * 64 + lax.rem(target, 64)).astype(BF16)

    def shifted(middle, load, tile_lane):
        ext = []
        for c in range(3):
            groups = [load(0, c, 56, 64)]
            if c == 1 and middle is not None:
                mid = middle
            else:
                mid = load(1, c, 0, 64)
            groups += [mid[8 * y : 8 * y + 8] for y in range(8)]
            groups.append(load(2, c, 0, 8))
            ext.append(groups)
        down = [pltpu.roll(jnp.where(z_last, ext[0][y], ext[1][y]), 1, 0) for y in range(10)]
        up = [pltpu.roll(jnp.where(z_first, ext[2][y], ext[1][y]), 7, 0) for y in range(10)]
        return down, ext[1], up

    def store_first(c_ref, slab, down, mid, up):
        both = [jnp.where(first_half, d, u) for d, u in zip(down, up)]
        c_ref[slab, 0:80, :] = jnp.concatenate(both, axis=0).astype(BF16)
        c_ref[slab, 80:144, :] = jnp.concatenate(both[1:9], axis=0).astype(BF16)
        ends = [jnp.where(first_half, mid[y], mid[y + 2]) for y in range(8)]
        c_ref[slab, 144:208, :] = jnp.concatenate(ends, axis=0).astype(BF16)
        c_ref[slab, 208:272, :] = jnp.concatenate(mid[1:9], axis=0).astype(BF16)

    def store_second(c_ref, slab, down, mid, up):
        for c, groups in enumerate((down, mid, up)):
            c_ref[c, slab, 0:80, :] = jnp.concatenate(groups, axis=0).astype(BF16)
            c_ref[c, slab, 80:144, :] = jnp.concatenate(groups[1:9], axis=0).astype(BF16)

    def build_inner(c_ref, store, splitter, tile_lane):
        whole = dot(face_ref[...].reshape(512, 128), splitter)
        side_ref[0] = whole[:, :128].reshape(8, 64, 128)
        side_ref[1] = whole[:, 128:].reshape(8, 64, 128)
        named = [
            [jnp.minimum(jnp.maximum(nbr_ref[t, 9 + k] - 2, 0), 2) for k in range(9)]
            for t in range(2)
        ]

        @pl.loop(0, 8, unroll=4)
        def _(x):
            def load(b, c, start, stop):
                k = 3 * b + c
                return jnp.where(
                    rows_of(tile_lane, (stop - start) // 8),
                    side_ref[named[0][k], x, start:stop, :],
                    side_ref[named[1][k], x, start:stop, :],
                )

            store(c_ref, x + 1, *shifted(field_ref[x], load, tile_lane))

    def build_faces(which, c_ref, store, splitter, tile_lane):
        source = rim_ref[:, 0] if which == 0 else halo_ref[which]
        whole = dot(source.reshape(128, 128), splitter)
        for side in range(2):
            far_ref[side, 0] = whole[64 * side : 64 * side + 64, :128]
            far_ref[side, 1] = whole[64 * side : 64 * side + 64, 128:]
            named = [
                [
                    jnp.minimum(jnp.maximum(nbr_ref[t, 18 * side + k] - 4 * side, 0), 2)
                    for k in range(9)
                ]
                for t in range(2)
            ]

            def load(b, c, start, stop):
                k = 3 * b + c
                return jnp.where(
                    rows_of(tile_lane, (stop - start) // 8),
                    far_ref[side, named[0][k], start:stop, :],
                    far_ref[side, named[1][k], start:stop, :],
                )

            store(c_ref, 9 * side, *shifted(None, load, tile_lane))

    def build_cross():
        for side, x, base, code in ((0, 0, 18, 0), (1, 7, 0, 4)):
            named = []
            for s in range(2):
                row = []
                for k in range(9):
                    link = [nbr_ref[t, 26 - base - k] == code + s for t in range(2)]
                    row.append(jnp.where(link[0], 0, jnp.where(link[1], 1, 2)))
                named.append(row)

            def load(b, c, start, stop):
                k = 3 * b + c
                return jnp.where(
                    rows_of(even_quarter, (stop - start) // 8),
                    side_ref[named[0][k], x, start:stop, :],
                    side_ref[named[1][k], x, start:stop, :],
                )

            store_first(ext_ref.at[side], 2 - 2 * side, *shifted(None, load, even_quarter))

    def build_rim():
        source, target = iota((128, 384), 0), iota((128, 384), 1)
        group, lane_in = target // 128, lax.rem(target, 128)
        wanted = jnp.where(group == 0, lax.rem(lane_in, 64), (group - 1) * 32 + lax.rem(lane_in, 32))
        for inside in range(2):
            spread_out = (source == wanted + 64 * inside).astype(BF16)
            whole = dot(rim_ref[:, 0].reshape(128, 128), spread_out)
            for side in range(2):
                part = whole[64 * side : 64 * side + 64]
                table = rim_ref[side, 2].astype(F32)

                def load(b, c, start, stop):
                    k = 3 * b + c
                    first = table[k : k + 1] * part[start:stop, 128:256]
                    return first + table[32 + k : 33 + k] * part[start:stop, 256:384]

                slab = 1 if inside == 0 else 2 * side
                store_first(ext_ref.at[side], slab, *shifted(part[:, 0:128], load, even_quarter))

    def hidden_beside():
        windows = []
        for a in range(3):
            for r in ROWS_FIRST:
                windows.append(ext_ref[:, a, r : r + 64, :].reshape(128, 128))
        pre = dot(jnp.concatenate(windows, axis=1), w1b_ref[...].reshape(15 * 128, 128))
        live = rim_ref[:, 1].reshape(128, 128).astype(F32)
        hidden = (live * pre * jax.nn.sigmoid(pre)).astype(BF16)
        halo_ref[1] = hidden.reshape(2, 64, 128)

    def windows_first(start, count):
        return [
            c1_ref[start : start + count, r : r + 64, :].reshape(count * 64, 128)
            for r in ROWS_FIRST
        ]

    def windows_second(c_ref, start, count):
        return [
            c_ref[c, start : start + count, ROWS[b] : ROWS[b] + 64, :].reshape(count * 64, 128)
            for b in range(3)
            for c in range(3)
        ]

    def conv_inner(windows, weight, product=dot, columns=1):
        weights = jnp.concatenate([weight(0), weight(2), weight(1)], axis=columns)
        got = product(jnp.concatenate(windows(1, 8), axis=1), weights)
        acc_ref[...] = got[:, 256:384]
        acc_ref[64:512] += got[0:448, 0:128]
        acc_ref[0:448] += got[64:512, 128:256]

    def conv_faces(windows, weight, product=dot, columns=1):
        weights = jnp.concatenate([weight(0), weight(2)], axis=columns)
        rows = [jnp.concatenate(both, axis=0) for both in zip(windows(0, 1), windows(9, 1))]
        got = product(jnp.concatenate(rows, axis=1), weights)
        acc_ref[0:64] += got[0:64, 0:128]
        acc_ref[448:512] += got[64:128, 128:256]

    def weight_first(a):
        return w1b_ref[a].reshape(5 * 128, 128)

    def weight_second(a):
        return w2b_ref[9 * a : 9 * a + 9].reshape(9 * 128, 128)

    def weight_back(a):
        return jnp.concatenate([w2b_ref[26 - k] for k in range(9 * a, 9 * a + 9)], axis=1)

    def conv_whole(windows, weight):
        weights = jnp.concatenate([weight(0), weight(2), weight(1)], axis=1)
        got = dot(jnp.concatenate(windows(0, 10), axis=1), weights)
        acc_ref[...] = got[0:512, 0:128] + got[64:576, 256:384] + got[128:640, 128:256]

    def layer(which, c_ref, store, splitter, tile_lane, windows, weight, product, columns, activate, between=None):
        build_inner(c_ref, store, splitter, tile_lane)
        conv_inner(windows, weight, product, columns)
        if which == 0:
            build_cross()
        pl.loop(1, 7, unroll=3)(activate)
        if between is not None:
            between()
        halo_wait(which)
        build_faces(which, c_ref, store, splitter, tile_lane)
        if which == 0:
            build_rim()
            hidden_beside()
        conv_faces(windows, weight, product, columns)
        if which == 2:
            halo_sent(2)
        pl.loop(0, 2, unroll=2)(lambda i: activate(7 * i))

    def hidden_of(x):
        rows = pl.ds(pl.multiple_of(x * 64, 64), 64)
        pre = acc_ref[rows, :]
        live = live_ref[x]
        sig = jax.nn.sigmoid(pre)
        hidden = (live * pre * sig).astype(BF16)
        face_ref[x] = hidden
        field_ref[x] = hidden.astype(F32)
        slope_ref[x] = live * sig * (1.0 + pre * (1.0 - sig))

    def outputs_of(x):
        rows = pl.ds(pl.multiple_of(x * 64, 64), 64)
        pre = acc_ref[rows, :]
        live = live_ref[x]
        sig = jax.nn.sigmoid(pre)
        out_ref[rows, :] = (live * pre * sig).astype(BF16)
        upstream = cot_ref[rows, :].astype(F32)
        delta = (upstream * live * sig * (1.0 + pre * (1.0 - sig))).astype(BF16)
        face_ref[x] = delta
        field_ref[x] = delta.astype(F32)

    def back_of(x):
        rows = pl.ds(pl.multiple_of(x * 64, 64), 64)
        face_ref[x] = (acc_ref[rows, :] * slope_ref[x]).astype(BF16)

    layer(0, c1_ref, store_first, split_first(), even_quarter, windows_first, weight_first, dot, 1, hidden_of)

    loads[3].wait()
    spread2 = dot(w2_ref[...].reshape(27 * 64, 64), put).astype(BF16)
    w2b_ref[:, 0:64, :] = spread2[:, :128].reshape(27, 64, 128)
    w2b_ref[:, 64:128, :] = spread2[:, 128:].reshape(27, 64, 128)
    second = functools.partial(windows_second, c2_ref)
    loads[4].wait()
    build_inner(c2_ref, store_second, split_second(), first_half)
    build_faces(1, c2_ref, store_second, split_second(), first_half)
    conv_whole(second, weight_second)
    pl.loop(0, 2, unroll=2)(lambda i: outputs_of(7 * i))
    halo_start(2)
    pl.loop(1, 7, unroll=3)(outputs_of)

    wide_half = iota((64, 128), 1) < 64
    wide_quarter = lax.rem(iota((64, 128), 1) // 32, 2) == 0
    per_core1, per_core2 = PAIRS_FIRST // 2, PAIRS_SECOND // 2

    def put_gradient(full, send, pair, value):
        value = value.reshape(4, 16, 128)
        full[4 * pair : 4 * pair + 4] = value
        send[4 * pair : 4 * pair + 4] = value.astype(BF16)

    delta_t = face_ref[...].reshape(512, 128).T
    for pair in range(14):
        both = []
        for k in (2 * pair, min(2 * pair + 1, 26)):
            a, b, c = k // 9, k // 3 % 3, k % 3
            window = c2_ref[c, a : a + 8, ROWS[b] : ROWS[b] + 64, :]
            both.append(window.reshape(512, 128))
        got = dot(delta_t, jnp.concatenate(both, axis=1))
        one, two = got[:, :128], got[:, 128:]
        straight = jnp.where(wide_half, one[0:64], two[64:128])
        crossed = jnp.where(wide_half, two[0:64], one[64:128])
        put_gradient(full2_ref, send2_ref, pair, straight + pltpu.roll(crossed, 64, 1))
    for pair in range(14, PAIRS_SECOND):
        put_gradient(full2_ref, send2_ref, pair, jnp.zeros((64, 128), F32))

    def reducer(which, unit, send, parts, line, fin):

        def remote(stage, src, dst, device):
            return pltpu.make_async_remote_copy(
                src_ref=src,
                dst_ref=dst,
                send_sem=sum_send.at[which, stage],
                recv_sem=sum_recv.at[which, stage],
                device_id=device,
                device_id_type=MESH,
            )

        place = pl.ds((core * n_plane + member) * unit, unit)
        parts_whole = parts.at[pl.ds(1, parts.shape[0] - 1)]
        line_whole = line.at[pl.ds(0, nz - 1)]
        fin_whole = fin.at[pl.ds(0, (2 * n_plane - 1) * unit)]
        whole = [
            remote(0, parts_whole, parts_whole, twin),
            remote(1, line_whole, line_whole, twin),
            remote(2, fin_whole, fin_whole, twin),
        ]

        def start_parts(peers):
            for i, (other, at) in enumerate(peers):
                remote(0, send.at[pl.ds(other * unit, unit)], parts.at[i + 1], at).start()

        def start_line(total):
            whole[0].wait_recv()
            for i in range(1, parts.shape[0]):
                total = total + parts[i].astype(F32)
            line[my_z] = total.astype(BF16)
            for at in line_peers:
                remote(1, line.at[my_z], line.at[my_z], at).start()

        def start_back():
            whole[1].wait_recv()
            total = line[0].astype(F32)
            for z in range(1, nz):
                total = total + line[z].astype(F32)
            fin[place] = (total * scale).astype(BF16)
            for _, at in all_peers:
                remote(2, fin.at[place], fin.at[place], at).start()

        def finish():
            whole[2].wait_recv()

        def sent():
            for copy in whole:
                copy.wait_send()

        return start_parts, start_line, start_back, finish, sent

    unit1, unit2 = 4 * per_core1 // n_plane, 4 * per_core2 // n_plane
    sum1 = reducer(0, unit1, send1_ref, parts1_ref, line1_ref, fin1_ref)
    sum2 = reducer(1, unit2, half2_ref, parts2_ref, line2_ref, fin2_ref)
    place1 = pl.ds((core * n_plane + member) * unit1, unit1)

    def half_units(which_core):
        return pl.ds(which_core * 4 * per_core2, 4 * per_core2)

    pair_copy = pltpu.make_async_remote_copy(
        src_ref=send2_ref.at[half_units(1 - core)],
        dst_ref=pair2_ref,
        send_sem=pair_sem.at[0],
        recv_sem=pair_sem.at[1],
        device_id=twin,
        device_id_type=MESH,
    )
    pair_copy.start()

    def start_second():
        pair_copy.wait_recv()
        total = full2_ref[half_units(core)] + pair2_ref[...].astype(F32)
        mine2_ref[...] = total
        half2_ref[...] = total.astype(BF16)
        sum2[0](plane_peers)

    third = functools.partial(windows_second, c3_ref)
    layer(2, c3_ref, store_second, split_second(), first_half, third, weight_back, dot_nt, 0, back_of, start_second)
    delta_t = face_ref[...].reshape(512, 128).T
    for pair in range(PAIRS_FIRST):
        both = []
        for block in (2 * pair, min(2 * pair + 1, 14)):
            a, r = block // 5, ROWS_FIRST[block % 5]
            both.append(c1_ref[a : a + 8, r : r + 64, :].reshape(512, 128))
        got = dot(delta_t, jnp.concatenate(both, axis=1))
        one, two = got[:, :128], got[:, 128:]
        straight = jnp.where(wide_quarter, one[0:64], two[64:128])
        crossed = jnp.where(wide_quarter, two[0:64], one[64:128])
        swapped = jnp.where(wide_quarter, pltpu.roll(crossed, 96, 1), pltpu.roll(crossed, 32, 1))
        put_gradient(full1_ref, send1_ref, pair, straight + swapped)
    sum1[0](all_peers)
    sum2[1](mine2_ref[pl.ds(member * unit2, unit2)])
    sum1[1](full1_ref[place1])
    sum2[2]()
    sum1[2]()
    sum2[3]()
    for pair in range(14):
        value = fin2_ref[4 * pair : 4 * pair + 4].reshape(64, 128).T.astype(F32)
        g2_ref[2 * pair] = value[0:64]
        if pair < 13:
            g2_ref[2 * pair + 1] = value[64:128]
    sum1[3]()
    pair_copy.wait_send()
    sum2[4]()
    sum1[4]()
    halo_sent(0)


def unpack_kernel(block_ref, fin_ref, g2_ref, out_hbm, g1_hbm, g2_hbm, g1_ref, sem):
    block_copy = pltpu.make_async_copy(block_ref, out_hbm, sem.at[0])
    second_copies = [
        pltpu.make_async_copy(g2_ref.at[pl.ds(k, 9)], g2_hbm.at[pl.ds(k, 9)], sem.at[3 + k // 9])
        for k in (0, 9, 18)
    ]
    first_copy = pltpu.make_async_copy(g1_ref, g1_hbm, sem.at[2])
    for copy in second_copies:
        copy.start()
    block_copy.start()
    for pair in range(PAIRS_FIRST):
        value = fin_ref[4 * pair : 4 * pair + 4].reshape(64, 128).T.astype(F32)
        for j in range(2):
            block = 2 * pair + j
            if block > 14:
                continue
            a, kind = block // 5, block % 5
            if kind < 3:
                offsets = (9 * a + 3 * kind, 9 * a + 3 * kind + 2)
            elif kind == 3:
                offsets = (9 * a + 1, 9 * a + 7)
            else:
                offsets = (9 * a + 4,)
            for i, k in enumerate(offsets):
                g1_ref[k] = value[64 * i + 32 * j : 64 * i + 32 * j + 32]
    first_copy.start()
    for copy in second_copies:
        copy.wait()
    block_copy.wait()
    first_copy.wait()


def solution(mesh):
    n_region, n_rep = mesh.shape["region"], mesh.shape["rep"]
    nx, ny = (4, 4) if n_region == 32 else (2, n_rep // 2)
    nz = n_region // nx
    sizes = (nx, nz, ny)
    n_plane = nx * ny
    core1, core2 = 2 * PAIRS_FIRST, 2 * PAIRS_SECOND
    unit1, unit2 = core1 // n_plane, core2 // n_plane
    vmem = pl.BlockSpec(memory_space=pltpu.VMEM)
    smem = pl.BlockSpec(memory_space=pltpu.SMEM)
    hbm = pl.BlockSpec(memory_space=pltpu.HBM)
    anywhere = pl.BlockSpec(memory_space=pl.ANY)
    dma = pltpu.SemaphoreType.DMA

    def body(features, weight_first, weight_second, cotangent, neighbours, voxel_mask):
        scale = 1.0 / math.sqrt(n_rep * 2 * n_region * 512)
        block, fin1, g2 = pl.pallas_call(
            functools.partial(main_kernel, sizes, scale),
            out_shape=(
                jax.ShapeDtypeStruct((512, 128), BF16),
                jax.ShapeDtypeStruct((2 * core1, 16, 128), BF16),
                jax.ShapeDtypeStruct((27, 64, 64), F32),
            ),
            in_specs=[hbm, hbm, hbm, hbm, smem, hbm],
            out_specs=(vmem, vmem, vmem),
            scratch_shapes=[
                pltpu.VMEM((64, 512), BF16),
                pltpu.VMEM((27, 32, 64), BF16),
                pltpu.VMEM((27, 64, 64), BF16),
                pltpu.VMEM((512, 128), BF16),
                pltpu.VMEM((2, 512), jnp.int32),
                pltpu.VMEM((8, 64, 128), F32),
                pltpu.VMEM((8, 64, 128), F32),
                pltpu.VMEM((8, 64, 128), BF16),
                pltpu.VMEM((3, 2, 64, 128), BF16),
                pltpu.VMEM((2, 3, 64, 128), BF16),
                pltpu.VMEM((2, 3, 64, 128), BF16),
                pltpu.VMEM((2, 3, 272, 128), BF16),
                pltpu.VMEM((3, 8, 64, 128), F32),
                pltpu.VMEM((2, 3, 64, 128), F32),
                pltpu.VMEM((10, 272, 128), BF16),
                pltpu.VMEM((3, 10, 144, 128), BF16),
                pltpu.VMEM((3, 10, 144, 128), BF16),
                pltpu.VMEM((3, 5, 128, 128), BF16),
                pltpu.VMEM((27, 128, 128), BF16),
                pltpu.VMEM((512, 128), F32),
                pltpu.VMEM((8, 64, 128), F32),
                pltpu.VMEM((2 * core1, 16, 128), F32),
                pltpu.VMEM((2 * core2, 16, 128), F32),
                pltpu.VMEM((2 * core1, 16, 128), BF16),
                pltpu.VMEM((2 * core2, 16, 128), BF16),
                pltpu.VMEM((core2, 16, 128), BF16),
                pltpu.VMEM((core2, 16, 128), BF16),
                pltpu.VMEM((core2, 16, 128), F32),
                pltpu.VMEM((2 * n_plane, unit1, 16, 128), BF16),
                pltpu.VMEM((n_plane, unit2, 16, 128), BF16),
                pltpu.VMEM((nz, unit1, 16, 128), BF16),
                pltpu.VMEM((nz, unit2, 16, 128), BF16),
                pltpu.VMEM((2 * core2, 16, 128), BF16),
                dma((5,)),
                dma((3, 2)),
                dma((3, 2)),
                dma((2,)),
                dma((2, 3)),
                dma((2, 3)),
            ],
            compiler_params=pltpu.CompilerParams(
                collective_id=0, has_side_effects=True, vmem_limit_bytes=40 * 2**20
            ),
        )(
            *(
                pltpu.with_memory_space_constraint(x, pltpu.HBM)
                for x in (
                    jnp.swapaxes(features, 1, 2).reshape(64, 512),
                    weight_first,
                    weight_second,
                    cotangent.reshape(512, 128),
                    neighbours.reshape(2, 27),
                    voxel_mask.reshape(2, 512),
                )
            )
        )
        out, g1, g2 = pl.pallas_call(
            unpack_kernel,
            out_shape=(
                jax.ShapeDtypeStruct((512, 128), BF16),
                jax.ShapeDtypeStruct((27, 32, 64), F32),
                jax.ShapeDtypeStruct((27, 64, 64), F32),
            ),
            in_specs=[vmem, vmem, vmem],
            out_specs=(anywhere, anywhere, anywhere),
            scratch_shapes=[
                pltpu.VMEM((27, 32, 64), F32),
                dma((6,)),
            ],
            compiler_params=pltpu.CompilerParams(vmem_limit_bytes=40 * 2**20),
        )(block, fin1, g2)
        return out.reshape(1, 512, 128), g1, g2

    in_specs = (
        P("rep", None, "region"),
        P(),
        P(),
        P("rep", None, "region"),
        P("rep", "region", None),
        P("rep", "region", None),
    )
    out_specs = (P("rep", None, "region"), P(), P())
    return jax.shard_map(body, mesh=mesh, in_specs=in_specs, out_specs=out_specs, check_vma=False)
```

```python
import functools
import math

import jax
import jax.numpy as jnp
from jax import lax
from jax.experimental import pallas as pl
from jax.experimental.pallas import tpu as pltpu
from jax.sharding import PartitionSpec as P

MESH = pl.DeviceIdType.MESH
F32 = jnp.float32
BF16 = jnp.bfloat16
ROWS = (0, 80, 16)
ROWS_FIRST = (0, 80, 16, 144, 208)
PAIRS_SECOND = 16
PAIRS_FIRST = 8


def iota(shape, axis):
    return lax.broadcasted_iota(jnp.int32, shape, axis)


def dot(a, b):
    return jnp.dot(a, b, preferred_element_type=F32)


def dot_nt(a, b):
    return lax.dot_general(a, b, (((1,), (1,)), ((), ())), preferred_element_type=F32)


def places(sizes):
    nx, nz, ny = sizes
    region = lax.axis_index("region")
    rep = lax.axis_index("rep")
    return region // nz, lax.rem(region, nz), rep // 2, lax.rem(rep, 2), region, rep


def main_kernel(
    sizes,
    scale,
    feat_hbm,
    w1_hbm,
    w2_hbm,
    cot_hbm,
    nbr_ref,
    mask_hbm,
    out_ref,
    fin1_ref,
    g2_ref,
    feat_ref,
    w1_ref,
    w2_ref,
    cot_ref,
    mask_ref,
    live_ref,
    field_ref,
    face_ref,
    halo_ref,
    edge_ref,
    rim_ref,
    ext_ref,
    side_ref,
    far_ref,
    c1_ref,
    c2_ref,
    c3_ref,
    w1b_ref,
    w2b_ref,
    acc_ref,
    slope_ref,
    full1_ref,
    full2_ref,
    send1_ref,
    send2_ref,
    pair2_ref,
    half2_ref,
    mine2_ref,
    parts1_ref,
    parts2_ref,
    line1_ref,
    line2_ref,
    fin2_ref,
    load_sem,
    halo_send,
    halo_recv,
    pair_sem,
    sum_send,
    sum_recv,
):
    nx, nz, ny = sizes
    n_region, n_plane = nx * nz, nx * ny
    my_x, my_z, my_y, core, region, rep = places(sizes)
    member = my_x * ny + my_y
    right = lax.rem(region + 1, n_region)
    left = lax.rem(region + n_region - 1, n_region)
    twin = {"region": region, "rep": my_y * 2 + 1 - core}

    def apart(offset, size):
        return min(offset, size - offset)

    offsets = sorted(
        ((dx, dy, dc) for dx in range(nx) for dy in range(ny) for dc in range(2)),
        key=lambda d: (-apart(d[0], nx) - apart(d[1], ny), d),
    )
    plane_peers, all_peers = [], []
    for dx, dy, dc in offsets:
        if (dx, dy, dc) == (0, 0, 0):
            continue
        x, y, c = lax.rem(my_x + dx, nx), lax.rem(my_y + dy, ny), lax.rem(core + dc, 2)
        at = {"region": x * nz + my_z, "rep": y * 2 + c}
        all_peers.append((c * n_plane + x * ny + y, at))
        if dc == 0:
            plane_peers.append((x * ny + y, at))
    line_peers = [
        {"region": my_x * nz + lax.rem(my_z + step, nz), "rep": rep}
        for step in sorted(range(1, nz), key=lambda d: -apart(d, nz))
    ]

    halo_ref[...] = jnp.zeros((3, 2, 64, 128), BF16)
    rim_ref[...] = jnp.zeros((2, 3, 64, 128), BF16)

    barrier = pltpu.get_barrier_semaphore()
    partners = [{"region": right, "rep": rep}, {"region": left, "rep": rep}]
    partners += [at for _, at in all_peers] + line_peers
    for at in partners[:2]:
        pl.semaphore_signal(barrier, inc=1, device_id=at, device_id_type=MESH)
    loads = [
        pltpu.make_async_copy(src, dst, load_sem.at[i])
        for i, (src, dst) in enumerate(
            (
                (mask_hbm, mask_ref),
                (feat_hbm, feat_ref),
                (w1_hbm, w1_ref),
                (w2_hbm, w2_ref),
                (cot_hbm, cot_ref),
            )
        )
    ]
    for load in loads:
        load.start()
    for at in partners[2:]:
        pl.semaphore_signal(barrier, inc=1, device_id=at, device_id_type=MESH)
    loads[0].wait()
    loads[1].wait()

    mask = jnp.concatenate([mask_ref[...].astype(F32), jnp.zeros((6, 512), F32)], axis=0).T
    tile_of = (iota((8, 128), 1) // 64 == iota((8, 128), 0)).astype(F32)
    tile_of_first = (lax.rem(iota((8, 128), 1) // 32, 2) == iota((8, 128), 0)).astype(F32)
    live_ref[...] = dot(mask, tile_of).reshape(8, 64, 128)
    twice = (iota((64, 128), 0) == lax.rem(iota((64, 128), 1), 64)).astype(BF16)
    spread = dot(feat_ref[...].T, twice) * dot(mask, tile_of_first)
    field_ref[...] = spread.reshape(8, 64, 128)
    face_ref[...] = spread.astype(BF16).reshape(8, 64, 128)

    def halo_copy(which, side):
        return pltpu.make_async_remote_copy(
            src_ref=edge_ref.at[side] if which == 0 else face_ref.at[7 if side == 0 else 0],
            dst_ref=rim_ref.at[side] if which == 0 else halo_ref.at[which, side],
            send_sem=halo_send.at[which, side],
            recv_sem=halo_recv.at[which, side],
            device_id={"region": right if side == 0 else left, "rep": rep},
            device_id_type=MESH,
        )

    has_right, has_left = region < n_region - 1, region > 0

    def halo_start(which):
        pl.when(has_right)(lambda: halo_copy(which, 0).start())
        pl.when(has_left)(lambda: halo_copy(which, 1).start())

    def halo_wait(which):
        @pl.when(has_left)
        def _():
            halo_copy(which, 0).wait_recv()

        @pl.when(has_right)
        def _():
            halo_copy(which, 1).wait_recv()

    def halo_sent(which):
        pl.when(has_right)(lambda: halo_copy(which, 0).wait_send())
        pl.when(has_left)(lambda: halo_copy(which, 1).wait_send())

    wide_half = iota((64, 128), 1) < 64
    wide_quarter = lax.rem(iota((64, 128), 1) // 32, 2) == 0
    one_lane = wide_quarter[0:1]
    links = []
    for s in range(2):
        for k in range(9):
            named = [(nbr_ref[t, 9 + k] == 2 + s).astype(F32) for t in range(2)]
            links.append(jnp.where(one_lane, named[0], named[1]))
        links.append(jnp.zeros((23, 128), F32))
    links = jnp.concatenate(links, axis=0).astype(BF16)
    for side, face, inside in ((0, 7, 6), (1, 0, 1)):
        edge_ref[side, 0] = jnp.where(wide_half, face_ref[face], face_ref[inside])
        edge_ref[side, 1] = live_ref[face].astype(BF16)
        edge_ref[side, 2] = links
    pl.semaphore_wait(barrier, len(partners))
    halo_start(0)

    loads[2].wait()
    plain = w1_ref[...].reshape(3, 3, 3, 32, 64)
    none = jnp.zeros((3, 3, 3, 32, 64), BF16)
    top = jnp.concatenate([plain, none], axis=-1)
    low = jnp.concatenate([none, plain], axis=-1)
    for b in range(3):
        for at, c in ((0, 0), (64, 2)):
            w1b_ref[:, b, at : at + 32, :] = top[:, b, c]
            w1b_ref[:, b, at + 32 : at + 64, :] = low[:, b, c]
    for at, b in ((0, 0), (64, 2)):
        w1b_ref[:, 3, at : at + 32, :] = top[:, b, 1]
        w1b_ref[:, 3, at + 32 : at + 64, :] = low[:, b, 1]
    w1b_ref[:, 4, 0:32, :] = top[:, 1, 1]
    w1b_ref[:, 4, 32:64, :] = low[:, 1, 1]
    w1b_ref[:, 4, 64:128, :] = jnp.zeros((3, 64, 128), BF16)
    side_ref[2] = jnp.zeros((8, 64, 128), F32)
    far_ref[:, 2] = jnp.zeros((2, 64, 128), F32)
    lane = iota((8, 128), 1)
    first_half = lane < 64
    even_quarter = lax.rem(lane // 32, 2) == 0
    z_row = iota((8, 128), 0)
    z_first, z_last = z_row == 0, z_row == 7

    def rows_of(masked, count):
        return jnp.concatenate([masked] * count, axis=0) if count > 1 else masked

    def split_first():
        source, target = iota((128, 256), 0), iota((128, 256), 1)
        return (source == (target // 128) * 32 + lax.rem(target, 32)).astype(BF16)

    def split_second():
        source, target = iota((128, 256), 0), iota((128, 256), 1)
        return (source == (target // 128) * 64 + lax.rem(target, 64)).astype(BF16)

    def shifted(middle, load, tile_lane):
        ext = []
        for c in range(3):
            groups = [load(0, c, 56, 64)]
            if c == 1 and middle is not None:
                mid = middle
            else:
                mid = load(1, c, 0, 64)
            groups += [mid[8 * y : 8 * y + 8] for y in range(8)]
            groups.append(load(2, c, 0, 8))
            ext.append(groups)
        down = [pltpu.roll(jnp.where(z_last, ext[0][y], ext[1][y]), 1, 0) for y in range(10)]
        up = [pltpu.roll(jnp.where(z_first, ext[2][y], ext[1][y]), 7, 0) for y in range(10)]
        return down, ext[1], up

    def store_first(c_ref, slab, down, mid, up):
        both = [jnp.where(first_half, d, u) for d, u in zip(down, up)]
        c_ref[slab, 0:80, :] = jnp.concatenate(both, axis=0).astype(BF16)
        c_ref[slab, 80:144, :] = jnp.concatenate(both[1:9], axis=0).astype(BF16)
        ends = [jnp.where(first_half, mid[y], mid[y + 2]) for y in range(8)]
        c_ref[slab, 144:208, :] = jnp.concatenate(ends, axis=0).astype(BF16)
        c_ref[slab, 208:272, :] = jnp.concatenate(mid[1:9], axis=0).astype(BF16)

    def store_second(c_ref, slab, down, mid, up):
        for c, groups in enumerate((down, mid, up)):
            c_ref[c, slab, 0:80, :] = jnp.concatenate(groups, axis=0).astype(BF16)
            c_ref[c, slab, 80:144, :] = jnp.concatenate(groups[1:9], axis=0).astype(BF16)

    def build_inner(c_ref, store, splitter, tile_lane):
        whole = dot(face_ref[...].reshape(512, 128), splitter)
        side_ref[0] = whole[:, :128].reshape(8, 64, 128)
        side_ref[1] = whole[:, 128:].reshape(8, 64, 128)
        named = [
            [jnp.minimum(jnp.maximum(nbr_ref[t, 9 + k] - 2, 0), 2) for k in range(9)]
            for t in range(2)
        ]

        @pl.loop(0, 8, unroll=4)
        def _(x):
            def load(b, c, start, stop):
                k = 3 * b + c
                return jnp.where(
                    rows_of(tile_lane, (stop - start) // 8),
                    side_ref[named[0][k], x, start:stop, :],
                    side_ref[named[1][k], x, start:stop, :],
                )

            store(c_ref, x + 1, *shifted(field_ref[x], load, tile_lane))

    def build_faces(which, c_ref, store, splitter, tile_lane):
        source = rim_ref[:, 0] if which == 0 else halo_ref[which]
        whole = dot(source.reshape(128, 128), splitter)
        for side in range(2):
            far_ref[side, 0] = whole[64 * side : 64 * side + 64, :128]
            far_ref[side, 1] = whole[64 * side : 64 * side + 64, 128:]
            named = [
                [
                    jnp.minimum(jnp.maximum(nbr_ref[t, 18 * side + k] - 4 * side, 0), 2)
                    for k in range(9)
                ]
                for t in range(2)
            ]

            def load(b, c, start, stop):
                k = 3 * b + c
                return jnp.where(
                    rows_of(tile_lane, (stop - start) // 8),
                    far_ref[side, named[0][k], start:stop, :],
                    far_ref[side, named[1][k], start:stop, :],
                )

            store(c_ref, 9 * side, *shifted(None, load, tile_lane))

    def build_cross():
        for side, x, base, code in ((0, 0, 18, 0), (1, 7, 0, 4)):
            named = []
            for s in range(2):
                row = []
                for k in range(9):
                    link = [nbr_ref[t, 26 - base - k] == code + s for t in range(2)]
                    row.append(jnp.where(link[0], 0, jnp.where(link[1], 1, 2)))
                named.append(row)

            def load(b, c, start, stop):
                k = 3 * b + c
                return jnp.where(
                    rows_of(even_quarter, (stop - start) // 8),
                    side_ref[named[0][k], x, start:stop, :],
                    side_ref[named[1][k], x, start:stop, :],
                )

            store_first(ext_ref.at[side], 2 - 2 * side, *shifted(None, load, even_quarter))

    def build_rim():
        source, target = iota((128, 384), 0), iota((128, 384), 1)
        group, lane_in = target // 128, lax.rem(target, 128)
        wanted = jnp.where(group == 0, lax.rem(lane_in, 64), (group - 1) * 32 + lax.rem(lane_in, 32))
        for inside in range(2):
            spread_out = (source == wanted + 64 * inside).astype(BF16)
            whole = dot(rim_ref[:, 0].reshape(128, 128), spread_out)
            for side in range(2):
                part = whole[64 * side : 64 * side + 64]
                table = rim_ref[side, 2].astype(F32)

                def load(b, c, start, stop):
                    k = 3 * b + c
                    first = table[k : k + 1] * part[start:stop, 128:256]
                    return first + table[32 + k : 33 + k] * part[start:stop, 256:384]

                slab = 1 if inside == 0 else 2 * side
                store_first(ext_ref.at[side], slab, *shifted(part[:, 0:128], load, even_quarter))

    def hidden_beside():
        windows = []
        for a in range(3):
            for r in ROWS_FIRST:
                windows.append(ext_ref[:, a, r : r + 64, :].reshape(128, 128))
        pre = dot(jnp.concatenate(windows, axis=1), w1b_ref[...].reshape(15 * 128, 128))
        live = rim_ref[:, 1].reshape(128, 128).astype(F32)
        hidden = (live * pre * jax.nn.sigmoid(pre)).astype(BF16)
        halo_ref[1] = hidden.reshape(2, 64, 128)

    def windows_first(start, count):
        return [
            c1_ref[start : start + count, r : r + 64, :].reshape(count * 64, 128)
            for r in ROWS_FIRST
        ]

    def windows_second(c_ref, start, count):
        return [
            c_ref[c, start : start + count, ROWS[b] : ROWS[b] + 64, :].reshape(count * 64, 128)
            for b in range(3)
            for c in range(3)
        ]

    def conv_inner(windows, weight, product=dot, columns=1):
        weights = jnp.concatenate([weight(0), weight(2), weight(1)], axis=columns)
        got = product(jnp.concatenate(windows(1, 8), axis=1), weights)
        acc_ref[...] = got[:, 256:384]
        acc_ref[64:512] += got[0:448, 0:128]
        acc_ref[0:448] += got[64:512, 128:256]

    def conv_faces(windows, weight, product=dot, columns=1):
        weights = jnp.concatenate([weight(0), weight(2)], axis=columns)
        rows = [jnp.concatenate(both, axis=0) for both in zip(windows(0, 1), windows(9, 1))]
        got = product(jnp.concatenate(rows, axis=1), weights)
        acc_ref[0:64] += got[0:64, 0:128]
        acc_ref[448:512] += got[64:128, 128:256]

    def weight_first(a):
        return w1b_ref[a].reshape(5 * 128, 128)

    def weight_second(a):
        return w2b_ref[9 * a : 9 * a + 9].reshape(9 * 128, 128)

    def weight_back(a):
        return jnp.concatenate([w2b_ref[26 - k] for k in range(9 * a, 9 * a + 9)], axis=1)

    def conv_whole(windows, weight):
        weights = jnp.concatenate([weight(0), weight(2), weight(1)], axis=1)
        got = dot(jnp.concatenate(windows(0, 10), axis=1), weights)
        acc_ref[...] = got[0:512, 0:128] + got[64:576, 256:384] + got[128:640, 128:256]

    def layer(which, c_ref, store, splitter, tile_lane, windows, weight, product, columns, activate, between=None):
        build_inner(c_ref, store, splitter, tile_lane)
        conv_inner(windows, weight, product, columns)
        if which == 0:
            build_cross()
        if between is not None:
            between()
        pl.loop(1, 7, unroll=3)(activate)
        halo_wait(which)
        build_faces(which, c_ref, store, splitter, tile_lane)
        if which == 0:
            build_rim()
            hidden_beside()
        conv_faces(windows, weight, product, columns)
        if which == 2:
            halo_sent(2)
        pl.loop(0, 2, unroll=2)(lambda i: activate(7 * i))

    def hidden_of(x):
        rows = pl.ds(pl.multiple_of(x * 64, 64), 64)
        pre = acc_ref[rows, :]
        live = live_ref[x]
        sig = jax.nn.sigmoid(pre)
        hidden = (live * pre * sig).astype(BF16)
        face_ref[x] = hidden
        field_ref[x] = hidden.astype(F32)
        slope_ref[x] = live * sig * (1.0 + pre * (1.0 - sig))

    def outputs_of(x):
        rows = pl.ds(pl.multiple_of(x * 64, 64), 64)
        pre = acc_ref[rows, :]
        live = live_ref[x]
        sig = jax.nn.sigmoid(pre)
        out_ref[rows, :] = (live * pre * sig).astype(BF16)
        upstream = cot_ref[rows, :].astype(F32)
        delta = (upstream * live * sig * (1.0 + pre * (1.0 - sig))).astype(BF16)
        face_ref[x] = delta
        field_ref[x] = delta.astype(F32)

    def back_of(x):
        rows = pl.ds(pl.multiple_of(x * 64, 64), 64)
        face_ref[x] = (acc_ref[rows, :] * slope_ref[x]).astype(BF16)

    layer(0, c1_ref, store_first, split_first(), even_quarter, windows_first, weight_first, dot, 1, hidden_of)

    loads[3].wait()
    none = jnp.zeros((27, 64, 64), BF16)
    w2b_ref[:, 0:64, :] = jnp.concatenate([w2_ref[...], none], axis=-1)
    w2b_ref[:, 64:128, :] = jnp.concatenate([none, w2_ref[...]], axis=-1)
    second = functools.partial(windows_second, c2_ref)
    loads[4].wait()
    build_inner(c2_ref, store_second, split_second(), first_half)
    build_faces(1, c2_ref, store_second, split_second(), first_half)
    conv_whole(second, weight_second)
    pl.loop(0, 2, unroll=2)(lambda i: outputs_of(7 * i))
    halo_start(2)
    pl.loop(1, 7, unroll=3)(outputs_of)

    wide_half = iota((64, 128), 1) < 64
    wide_quarter = lax.rem(iota((64, 128), 1) // 32, 2) == 0
    per_core1, per_core2 = PAIRS_FIRST // 2, PAIRS_SECOND // 2

    def put_gradient(full, send, pair, value):
        value = value.reshape(4, 16, 128)
        full[4 * pair : 4 * pair + 4] = value
        send[4 * pair : 4 * pair + 4] = value.astype(BF16)

    delta_t = face_ref[...].reshape(512, 128).T
    for pair in range(14):
        both = []
        for k in (2 * pair, min(2 * pair + 1, 26)):
            a, b, c = k // 9, k // 3 % 3, k % 3
            window = c2_ref[c, a : a + 8, ROWS[b] : ROWS[b] + 64, :]
            both.append(window.reshape(512, 128))
        got = dot(delta_t, jnp.concatenate(both, axis=1))
        one, two = got[:, :128], got[:, 128:]
        straight = jnp.where(wide_half, one[0:64], two[64:128])
        crossed = jnp.where(wide_half, two[0:64], one[64:128])
        put_gradient(full2_ref, send2_ref, pair, straight + pltpu.roll(crossed, 64, 1))
    for pair in range(14, PAIRS_SECOND):
        put_gradient(full2_ref, send2_ref, pair, jnp.zeros((64, 128), F32))

    def reducer(which, unit, send, parts, line, fin):

        def remote(stage, src, dst, device):
            return pltpu.make_async_remote_copy(
                src_ref=src,
                dst_ref=dst,
                send_sem=sum_send.at[which, stage],
                recv_sem=sum_recv.at[which, stage],
                device_id=device,
                device_id_type=MESH,
            )

        place = pl.ds((core * n_plane + member) * unit, unit)
        parts_whole = parts.at[pl.ds(1, parts.shape[0] - 1)]
        line_whole = line.at[pl.ds(0, nz - 1)]
        fin_whole = fin.at[pl.ds(0, (2 * n_plane - 1) * unit)]
        whole = [
            remote(0, parts_whole, parts_whole, twin),
            remote(1, line_whole, line_whole, twin),
            remote(2, fin_whole, fin_whole, twin),
        ]

        def start_parts(peers):
            for i, (other, at) in enumerate(peers):
                remote(0, send.at[pl.ds(other * unit, unit)], parts.at[i + 1], at).start()

        def start_line(total):
            whole[0].wait_recv()
            for i in range(1, parts.shape[0]):
                total = total + parts[i].astype(F32)
            line[my_z] = total.astype(BF16)
            for at in line_peers:
                remote(1, line.at[my_z], line.at[my_z], at).start()

        def start_back():
            whole[1].wait_recv()
            total = line[0].astype(F32)
            for z in range(1, nz):
                total = total + line[z].astype(F32)
            fin[place] = (total * scale).astype(BF16)
            for _, at in all_peers:
                remote(2, fin.at[place], fin.at[place], at).start()

        def finish():
            whole[2].wait_recv()

        def sent():
            for copy in whole:
                copy.wait_send()

        return start_parts, start_line, start_back, finish, sent

    unit1, unit2 = 4 * per_core1 // n_plane, 4 * per_core2 // n_plane
    sum1 = reducer(0, unit1, send1_ref, parts1_ref, line1_ref, fin1_ref)
    sum2 = reducer(1, unit2, half2_ref, parts2_ref, line2_ref, fin2_ref)
    place1 = pl.ds((core * n_plane + member) * unit1, unit1)

    def half_units(which_core):
        return pl.ds(which_core * 4 * per_core2, 4 * per_core2)

    pair_copy = pltpu.make_async_remote_copy(
        src_ref=send2_ref.at[half_units(1 - core)],
        dst_ref=pair2_ref,
        send_sem=pair_sem.at[0],
        recv_sem=pair_sem.at[1],
        device_id=twin,
        device_id_type=MESH,
    )
    pair_copy.start()

    def start_second():
        pair_copy.wait_recv()
        total = full2_ref[half_units(core)] + pair2_ref[...].astype(F32)
        mine2_ref[...] = total
        half2_ref[...] = total.astype(BF16)
        sum2[0](plane_peers)

    third = functools.partial(windows_second, c3_ref)
    layer(2, c3_ref, store_second, split_second(), first_half, third, weight_back, dot_nt, 0, back_of, start_second)
    delta_t = face_ref[...].reshape(512, 128).T
    for pair in range(PAIRS_FIRST):
        both = []
        for block in (2 * pair, min(2 * pair + 1, 14)):
            a, r = block // 5, ROWS_FIRST[block % 5]
            both.append(c1_ref[a : a + 8, r : r + 64, :].reshape(512, 128))
        got = dot(delta_t, jnp.concatenate(both, axis=1))
        one, two = got[:, :128], got[:, 128:]
        straight = jnp.where(wide_quarter, one[0:64], two[64:128])
        crossed = jnp.where(wide_quarter, two[0:64], one[64:128])
        swapped = jnp.where(wide_quarter, pltpu.roll(crossed, 96, 1), pltpu.roll(crossed, 32, 1))
        put_gradient(full1_ref, send1_ref, pair, straight + swapped)
    sum1[0](all_peers)
    sum2[1](mine2_ref[pl.ds(member * unit2, unit2)])
    sum1[1](full1_ref[place1])
    sum2[2]()
    sum1[2]()
    sum2[3]()
    for pair in range(14):
        value = fin2_ref[4 * pair : 4 * pair + 4].reshape(64, 128).T.astype(F32)
        g2_ref[2 * pair] = value[0:64]
        if pair < 13:
            g2_ref[2 * pair + 1] = value[64:128]
    sum1[3]()
    pair_copy.wait_send()
    sum2[4]()
    sum1[4]()
    halo_sent(0)


def unpack_kernel(block_ref, fin_ref, g2_ref, out_hbm, g1_hbm, g2_hbm, g1_ref, sem):
    block_copy = pltpu.make_async_copy(block_ref, out_hbm, sem.at[0])
    second_copies = [
        pltpu.make_async_copy(g2_ref.at[pl.ds(k, 9)], g2_hbm.at[pl.ds(k, 9)], sem.at[3 + k // 9])
        for k in (0, 9, 18)
    ]
    first_copies = [
        pltpu.make_async_copy(g1_ref.at[pl.ds(k, 9)], g1_hbm.at[pl.ds(k, 9)], sem.at[6 + k // 9])
        for k in (0, 9, 18)
    ]
    for copy in second_copies:
        copy.start()
    block_copy.start()
    for pair in range(PAIRS_FIRST):
        value = fin_ref[4 * pair : 4 * pair + 4].reshape(64, 128).T.astype(F32)
        for j in range(2):
            block = 2 * pair + j
            if block > 14:
                continue
            a, kind = block // 5, block % 5
            if kind < 3:
                offsets = (9 * a + 3 * kind, 9 * a + 3 * kind + 2)
            elif kind == 3:
                offsets = (9 * a + 1, 9 * a + 7)
            else:
                offsets = (9 * a + 4,)
            for i, k in enumerate(offsets):
                g1_ref[k] = value[64 * i + 32 * j : 64 * i + 32 * j + 32]
        if pair in (2, 4, 7):
            first_copies[pair // 3].start()
    for copy in second_copies:
        copy.wait()
    block_copy.wait()
    for copy in first_copies:
        copy.wait()


def solution(mesh):
    n_region, n_rep = mesh.shape["region"], mesh.shape["rep"]
    nx, ny = (4, 4) if n_region == 32 else (2, n_rep // 2)
    nz = n_region // nx
    sizes = (nx, nz, ny)
    n_plane = nx * ny
    core1, core2 = 2 * PAIRS_FIRST, 2 * PAIRS_SECOND
    unit1, unit2 = core1 // n_plane, core2 // n_plane
    vmem = pl.BlockSpec(memory_space=pltpu.VMEM)
    smem = pl.BlockSpec(memory_space=pltpu.SMEM)
    hbm = pl.BlockSpec(memory_space=pltpu.HBM)
    anywhere = pl.BlockSpec(memory_space=pl.ANY)
    dma = pltpu.SemaphoreType.DMA

    def body(features, weight_first, weight_second, cotangent, neighbours, voxel_mask):
        scale = 1.0 / math.sqrt(n_rep * 2 * n_region * 512)
        block, fin1, g2 = pl.pallas_call(
            functools.partial(main_kernel, sizes, scale),
            out_shape=(
                jax.ShapeDtypeStruct((512, 128), BF16),
                jax.ShapeDtypeStruct((2 * core1, 16, 128), BF16),
                jax.ShapeDtypeStruct((27, 64, 64), F32),
            ),
            in_specs=[hbm, hbm, hbm, hbm, smem, hbm],
            out_specs=(vmem, vmem, vmem),
            scratch_shapes=[
                pltpu.VMEM((64, 512), BF16),
                pltpu.VMEM((27, 32, 64), BF16),
                pltpu.VMEM((27, 64, 64), BF16),
                pltpu.VMEM((512, 128), BF16),
                pltpu.VMEM((2, 512), jnp.int32),
                pltpu.VMEM((8, 64, 128), F32),
                pltpu.VMEM((8, 64, 128), F32),
                pltpu.VMEM((8, 64, 128), BF16),
                pltpu.VMEM((3, 2, 64, 128), BF16),
                pltpu.VMEM((2, 3, 64, 128), BF16),
                pltpu.VMEM((2, 3, 64, 128), BF16),
                pltpu.VMEM((2, 3, 272, 128), BF16),
                pltpu.VMEM((3, 8, 64, 128), F32),
                pltpu.VMEM((2, 3, 64, 128), F32),
                pltpu.VMEM((10, 272, 128), BF16),
                pltpu.VMEM((3, 10, 144, 128), BF16),
                pltpu.VMEM((3, 10, 144, 128), BF16),
                pltpu.VMEM((3, 5, 128, 128), BF16),
                pltpu.VMEM((27, 128, 128), BF16),
                pltpu.VMEM((512, 128), F32),
                pltpu.VMEM((8, 64, 128), F32),
                pltpu.VMEM((2 * core1, 16, 128), F32),
                pltpu.VMEM((2 * core2, 16, 128), F32),
                pltpu.VMEM((2 * core1, 16, 128), BF16),
                pltpu.VMEM((2 * core2, 16, 128), BF16),
                pltpu.VMEM((core2, 16, 128), BF16),
                pltpu.VMEM((core2, 16, 128), BF16),
                pltpu.VMEM((core2, 16, 128), F32),
                pltpu.VMEM((2 * n_plane, unit1, 16, 128), BF16),
                pltpu.VMEM((n_plane, unit2, 16, 128), BF16),
                pltpu.VMEM((nz, unit1, 16, 128), BF16),
                pltpu.VMEM((nz, unit2, 16, 128), BF16),
                pltpu.VMEM((2 * core2, 16, 128), BF16),
                dma((5,)),
                dma((3, 2)),
                dma((3, 2)),
                dma((2,)),
                dma((2, 3)),
                dma((2, 3)),
            ],
            compiler_params=pltpu.CompilerParams(
                collective_id=0, has_side_effects=True, vmem_limit_bytes=40 * 2**20
            ),
        )(
            *(
                pltpu.with_memory_space_constraint(x, pltpu.HBM)
                for x in (
                    jnp.swapaxes(features, 1, 2).reshape(64, 512),
                    weight_first,
                    weight_second,
                    cotangent.reshape(512, 128),
                    neighbours.reshape(2, 27),
                    voxel_mask.reshape(2, 512),
                )
            )
        )
        out, g1, g2 = pl.pallas_call(
            unpack_kernel,
            out_shape=(
                jax.ShapeDtypeStruct((512, 128), BF16),
                jax.ShapeDtypeStruct((27, 32, 64), F32),
                jax.ShapeDtypeStruct((27, 64, 64), F32),
            ),
            in_specs=[vmem, vmem, vmem],
            out_specs=(anywhere, anywhere, anywhere),
            scratch_shapes=[
                pltpu.VMEM((27, 32, 64), F32),
                dma((9,)),
            ],
            compiler_params=pltpu.CompilerParams(vmem_limit_bytes=40 * 2**20),
        )(block, fin1, g2)
        return out.reshape(1, 512, 128), g1, g2

    in_specs = (
        P("rep", None, "region"),
        P(),
        P(),
        P("rep", None, "region"),
        P("rep", "region", None),
        P("rep", "region", None),
    )
    out_specs = (P("rep", None, "region"), P(), P())
    return jax.shard_map(body, mesh=mesh, in_specs=in_specs, out_specs=out_specs, check_vma=False)
```

```python
import functools
import math

import jax
import jax.numpy as jnp
from jax import lax
from jax.experimental import pallas as pl
from jax.experimental.pallas import tpu as pltpu
from jax.sharding import PartitionSpec as P

MESH = pl.DeviceIdType.MESH
F32 = jnp.float32
BF16 = jnp.bfloat16
ROWS = (0, 80, 16)
ROWS_FIRST = (0, 80, 16, 144, 208)
PAIRS_SECOND = 16
PAIRS_FIRST = 8


def iota(shape, axis):
    return lax.broadcasted_iota(jnp.int32, shape, axis)


def dot(a, b):
    return jnp.dot(a, b, preferred_element_type=F32)


def dot_nt(a, b):
    return lax.dot_general(a, b, (((1,), (1,)), ((), ())), preferred_element_type=F32)


def places(sizes):
    nx, nz, ny = sizes
    region = lax.axis_index("region")
    rep = lax.axis_index("rep")
    return region // nz, lax.rem(region, nz), rep // 2, lax.rem(rep, 2), region, rep


def main_kernel(
    sizes,
    scale,
    feat_hbm,
    w1_hbm,
    w2_hbm,
    cot_hbm,
    nbr_ref,
    mask_hbm,
    out_ref,
    fin1_ref,
    g2_ref,
    feat_ref,
    w1_ref,
    w2_ref,
    cot_ref,
    mask_ref,
    live_ref,
    field_ref,
    face_ref,
    halo_ref,
    edge_ref,
    rim_ref,
    ext_ref,
    side_ref,
    far_ref,
    c1_ref,
    c2_ref,
    c3_ref,
    w1b_ref,
    w2b_ref,
    acc_ref,
    slope_ref,
    full1_ref,
    full2_ref,
    send1_ref,
    send2_ref,
    pair2_ref,
    half2_ref,
    mine2_ref,
    parts1_ref,
    parts2_ref,
    line1_ref,
    line2_ref,
    fin2_ref,
    load_sem,
    halo_send,
    halo_recv,
    pair_sem,
    sum_send,
    sum_recv,
):
    nx, nz, ny = sizes
    n_region, n_plane = nx * nz, nx * ny
    my_x, my_z, my_y, core, region, rep = places(sizes)
    member = my_x * ny + my_y
    right = lax.rem(region + 1, n_region)
    left = lax.rem(region + n_region - 1, n_region)
    twin = {"region": region, "rep": my_y * 2 + 1 - core}

    def apart(offset, size):
        return min(offset, size - offset)

    offsets = sorted(
        ((dx, dy, dc) for dx in range(nx) for dy in range(ny) for dc in range(2)),
        key=lambda d: (-apart(d[0], nx) - apart(d[1], ny), d),
    )
    plane_peers, all_peers = [], []
    for dx, dy, dc in offsets:
        if (dx, dy, dc) == (0, 0, 0):
            continue
        x, y, c = lax.rem(my_x + dx, nx), lax.rem(my_y + dy, ny), lax.rem(core + dc, 2)
        at = {"region": x * nz + my_z, "rep": y * 2 + c}
        all_peers.append((c * n_plane + x * ny + y, at))
        if dc == 0:
            plane_peers.append((x * ny + y, at))
    line_peers = [
        {"region": my_x * nz + lax.rem(my_z + step, nz), "rep": rep}
        for step in sorted(range(1, nz), key=lambda d: -apart(d, nz))
    ]

    halo_ref[...] = jnp.zeros((3, 2, 64, 128), BF16)
    rim_ref[...] = jnp.zeros((2, 3, 64, 128), BF16)

    barrier = pltpu.get_barrier_semaphore()
    partners = [{"region": right, "rep": rep}, {"region": left, "rep": rep}]
    partners += [at for _, at in all_peers] + line_peers
    for at in partners[:2]:
        pl.semaphore_signal(barrier, inc=1, device_id=at, device_id_type=MESH)
    loads = [
        pltpu.make_async_copy(src, dst, load_sem.at[i])
        for i, (src, dst) in enumerate(
            (
                (mask_hbm, mask_ref),
                (feat_hbm, feat_ref),
                (w1_hbm, w1_ref),
                (w2_hbm, w2_ref),
                (cot_hbm, cot_ref),
            )
        )
    ]
    for load in loads:
        load.start()
    for at in partners[2:]:
        pl.semaphore_signal(barrier, inc=1, device_id=at, device_id_type=MESH)
    loads[0].wait()
    loads[1].wait()

    mask = jnp.concatenate([mask_ref[...].astype(F32), jnp.zeros((6, 512), F32)], axis=0).T
    tile_of = (iota((8, 128), 1) // 64 == iota((8, 128), 0)).astype(F32)
    tile_of_first = (lax.rem(iota((8, 128), 1) // 32, 2) == iota((8, 128), 0)).astype(F32)
    live_ref[...] = dot(mask, tile_of).reshape(8, 64, 128)
    twice = (iota((64, 128), 0) == lax.rem(iota((64, 128), 1), 64)).astype(BF16)
    spread = dot(feat_ref[...].T, twice) * dot(mask, tile_of_first)
    field_ref[...] = spread.reshape(8, 64, 128)
    face_ref[...] = spread.astype(BF16).reshape(8, 64, 128)

    def halo_copy(which, side):
        return pltpu.make_async_remote_copy(
            src_ref=edge_ref.at[side] if which == 0 else face_ref.at[7 if side == 0 else 0],
            dst_ref=rim_ref.at[side] if which == 0 else halo_ref.at[which, side],
            send_sem=halo_send.at[which, side],
            recv_sem=halo_recv.at[which, side],
            device_id={"region": right if side == 0 else left, "rep": rep},
            device_id_type=MESH,
        )

    has_right, has_left = region < n_region - 1, region > 0

    def halo_start(which):
        pl.when(has_right)(lambda: halo_copy(which, 0).start())
        pl.when(has_left)(lambda: halo_copy(which, 1).start())

    def halo_wait(which):
        @pl.when(has_left)
        def _():
            halo_copy(which, 0).wait_recv()

        @pl.when(has_right)
        def _():
            halo_copy(which, 1).wait_recv()

    def halo_sent(which):
        pl.when(has_right)(lambda: halo_copy(which, 0).wait_send())
        pl.when(has_left)(lambda: halo_copy(which, 1).wait_send())

    wide_half = iota((64, 128), 1) < 64
    wide_quarter = lax.rem(iota((64, 128), 1) // 32, 2) == 0
    one_lane = wide_quarter[0:1]
    links = []
    for s in range(2):
        for k in range(9):
            named = [(nbr_ref[t, 9 + k] == 2 + s).astype(F32) for t in range(2)]
            links.append(jnp.where(one_lane, named[0], named[1]))
        links.append(jnp.zeros((23, 128), F32))
    links = jnp.concatenate(links, axis=0).astype(BF16)
    for side, face, inside in ((0, 7, 6), (1, 0, 1)):
        edge_ref[side, 0] = jnp.where(wide_half, face_ref[face], face_ref[inside])
        edge_ref[side, 1] = live_ref[face].astype(BF16)
        edge_ref[side, 2] = links
    pl.semaphore_wait(barrier, len(partners))
    halo_start(0)

    loads[2].wait()
    plain = w1_ref[...].reshape(3, 3, 3, 32, 64)
    none = jnp.zeros((3, 3, 3, 32, 64), BF16)
    top = jnp.concatenate([plain, none], axis=-1)
    low = jnp.concatenate([none, plain], axis=-1)
    for b in range(3):
        for at, c in ((0, 0), (64, 2)):
            w1b_ref[:, b, at : at + 32, :] = top[:, b, c]
            w1b_ref[:, b, at + 32 : at + 64, :] = low[:, b, c]
    for at, b in ((0, 0), (64, 2)):
        w1b_ref[:, 3, at : at + 32, :] = top[:, b, 1]
        w1b_ref[:, 3, at + 32 : at + 64, :] = low[:, b, 1]
    w1b_ref[:, 4, 0:32, :] = top[:, 1, 1]
    w1b_ref[:, 4, 32:64, :] = low[:, 1, 1]
    w1b_ref[:, 4, 64:128, :] = jnp.zeros((3, 64, 128), BF16)
    side_ref[2] = jnp.zeros((8, 64, 128), F32)
    far_ref[:, 2] = jnp.zeros((2, 64, 128), F32)
    lane = iota((8, 128), 1)
    first_half = lane < 64
    even_quarter = lax.rem(lane // 32, 2) == 0
    z_row = iota((8, 128), 0)
    z_first, z_last = z_row == 0, z_row == 7

    def rows_of(masked, count):
        return jnp.concatenate([masked] * count, axis=0) if count > 1 else masked

    def split_first():
        source, target = iota((128, 256), 0), iota((128, 256), 1)
        return (source == (target // 128) * 32 + lax.rem(target, 32)).astype(BF16)

    def split_second():
        source, target = iota((128, 256), 0), iota((128, 256), 1)
        return (source == (target // 128) * 64 + lax.rem(target, 64)).astype(BF16)

    def shifted(middle, load, tile_lane):
        ext = []
        for c in range(3):
            groups = [load(0, c, 56, 64)]
            if c == 1 and middle is not None:
                mid = middle
            else:
                mid = load(1, c, 0, 64)
            groups += [mid[8 * y : 8 * y + 8] for y in range(8)]
            groups.append(load(2, c, 0, 8))
            ext.append(groups)
        down = [pltpu.roll(jnp.where(z_last, ext[0][y], ext[1][y]), 1, 0) for y in range(10)]
        up = [pltpu.roll(jnp.where(z_first, ext[2][y], ext[1][y]), 7, 0) for y in range(10)]
        return down, ext[1], up

    def store_first(c_ref, slab, down, mid, up):
        both = [jnp.where(first_half, d, u) for d, u in zip(down, up)]
        c_ref[slab, 0:80, :] = jnp.concatenate(both, axis=0).astype(BF16)
        c_ref[slab, 80:144, :] = jnp.concatenate(both[1:9], axis=0).astype(BF16)
        ends = [jnp.where(first_half, mid[y], mid[y + 2]) for y in range(8)]
        c_ref[slab, 144:208, :] = jnp.concatenate(ends, axis=0).astype(BF16)
        c_ref[slab, 208:272, :] = jnp.concatenate(mid[1:9], axis=0).astype(BF16)

    def store_second(c_ref, slab, down, mid, up):
        for c, groups in enumerate((down, mid, up)):
            c_ref[c, slab, 0:80, :] = jnp.concatenate(groups, axis=0).astype(BF16)
            c_ref[c, slab, 80:144, :] = jnp.concatenate(groups[1:9], axis=0).astype(BF16)

    def build_inner(c_ref, store, splitter, tile_lane):
        whole = dot(face_ref[...].reshape(512, 128), splitter)
        side_ref[0] = whole[:, :128].reshape(8, 64, 128)
        side_ref[1] = whole[:, 128:].reshape(8, 64, 128)
        named = [
            [jnp.minimum(jnp.maximum(nbr_ref[t, 9 + k] - 2, 0), 2) for k in range(9)]
            for t in range(2)
        ]

        @pl.loop(0, 8, unroll=4)
        def _(x):
            def load(b, c, start, stop):
                k = 3 * b + c
                return jnp.where(
                    rows_of(tile_lane, (stop - start) // 8),
                    side_ref[named[0][k], x, start:stop, :],
                    side_ref[named[1][k], x, start:stop, :],
                )

            store(c_ref, x + 1, *shifted(field_ref[x], load, tile_lane))

    def build_faces(which, c_ref, store, splitter, tile_lane):
        source = rim_ref[:, 0] if which == 0 else halo_ref[which]
        whole = dot(source.reshape(128, 128), splitter)
        for side in range(2):
            far_ref[side, 0] = whole[64 * side : 64 * side + 64, :128]
            far_ref[side, 1] = whole[64 * side : 64 * side + 64, 128:]
            named = [
                [
                    jnp.minimum(jnp.maximum(nbr_ref[t, 18 * side + k] - 4 * side, 0), 2)
                    for k in range(9)
                ]
                for t in range(2)
            ]

            def load(b, c, start, stop):
                k = 3 * b + c
                return jnp.where(
                    rows_of(tile_lane, (stop - start) // 8),
                    far_ref[side, named[0][k], start:stop, :],
                    far_ref[side, named[1][k], start:stop, :],
                )

            store(c_ref, 9 * side, *shifted(None, load, tile_lane))

    def build_cross():
        for side, x, base, code in ((0, 0, 18, 0), (1, 7, 0, 4)):
            named = []
            for s in range(2):
                row = []
                for k in range(9):
                    link = [nbr_ref[t, 26 - base - k] == code + s for t in range(2)]
                    row.append(jnp.where(link[0], 0, jnp.where(link[1], 1, 2)))
                named.append(row)

            def load(b, c, start, stop):
                k = 3 * b + c
                return jnp.where(
                    rows_of(even_quarter, (stop - start) // 8),
                    side_ref[named[0][k], x, start:stop, :],
                    side_ref[named[1][k], x, start:stop, :],
                )

            store_first(ext_ref.at[side], 2 - 2 * side, *shifted(None, load, even_quarter))

    def build_rim():
        source, target = iota((128, 384), 0), iota((128, 384), 1)
        group, lane_in = target // 128, lax.rem(target, 128)
        wanted = jnp.where(group == 0, lax.rem(lane_in, 64), (group - 1) * 32 + lax.rem(lane_in, 32))
        for inside in range(2):
            spread_out = (source == wanted + 64 * inside).astype(BF16)
            whole = dot(rim_ref[:, 0].reshape(128, 128), spread_out)
            for side in range(2):
                part = whole[64 * side : 64 * side + 64]
                table = rim_ref[side, 2].astype(F32)

                def load(b, c, start, stop):
                    k = 3 * b + c
                    first = table[k : k + 1] * part[start:stop, 128:256]
                    return first + table[32 + k : 33 + k] * part[start:stop, 256:384]

                slab = 1 if inside == 0 else 2 * side
                store_first(ext_ref.at[side], slab, *shifted(part[:, 0:128], load, even_quarter))

    def hidden_beside():
        windows = []
        for a in range(3):
            for r in ROWS_FIRST:
                windows.append(ext_ref[:, a, r : r + 64, :].reshape(128, 128))
        pre = dot(jnp.concatenate(windows, axis=1), w1b_ref[...].reshape(15 * 128, 128))
        live = rim_ref[:, 1].reshape(128, 128).astype(F32)
        hidden = (live * pre * jax.nn.sigmoid(pre)).astype(BF16)
        halo_ref[1] = hidden.reshape(2, 64, 128)

    def windows_first(start, count):
        return [
            c1_ref[start : start + count, r : r + 64, :].reshape(count * 64, 128)
            for r in ROWS_FIRST
        ]

    def windows_second(c_ref, start, count):
        return [
            c_ref[c, start : start + count, ROWS[b] : ROWS[b] + 64, :].reshape(count * 64, 128)
            for b in range(3)
            for c in range(3)
        ]

    def conv_inner(windows, weight, product=dot, columns=1):
        weights = jnp.concatenate([weight(0), weight(2), weight(1)], axis=columns)
        got = product(jnp.concatenate(windows(1, 8), axis=1), weights)
        acc_ref[...] = got[:, 256:384]
        acc_ref[64:512] += got[0:448, 0:128]
        acc_ref[0:448] += got[64:512, 128:256]

    def conv_faces(windows, weight, product=dot, columns=1):
        weights = jnp.concatenate([weight(0), weight(2)], axis=columns)
        rows = [jnp.concatenate(both, axis=0) for both in zip(windows(0, 1), windows(9, 1))]
        got = product(jnp.concatenate(rows, axis=1), weights)
        acc_ref[0:64] += got[0:64, 0:128]
        acc_ref[448:512] += got[64:128, 128:256]

    def weight_first(a):
        return w1b_ref[a].reshape(5 * 128, 128)

    def weight_second(a):
        return w2b_ref[9 * a : 9 * a + 9].reshape(9 * 128, 128)

    def weight_back(a):
        return jnp.concatenate([w2b_ref[26 - k] for k in range(9 * a, 9 * a + 9)], axis=1)

    def conv_whole(windows, weight):
        weights = jnp.concatenate([weight(0), weight(2), weight(1)], axis=1)
        got = dot(jnp.concatenate(windows(0, 10), axis=1), weights)
        acc_ref[...] = got[0:512, 0:128] + got[64:576, 256:384] + got[128:640, 128:256]

    def layer(which, c_ref, store, splitter, tile_lane, windows, weight, product, columns, activate, between=None):
        build_inner(c_ref, store, splitter, tile_lane)
        conv_inner(windows, weight, product, columns)
        if which == 0:
            build_cross()
        if between is not None:
            between()
        pl.loop(1, 7, unroll=3)(activate)
        halo_wait(which)
        build_faces(which, c_ref, store, splitter, tile_lane)
        if which == 0:
            build_rim()
            hidden_beside()
        conv_faces(windows, weight, product, columns)
        if which == 2:
            halo_sent(2)
        pl.loop(0, 2, unroll=2)(lambda i: activate(7 * i))

    def hidden_of(x):
        rows = pl.ds(pl.multiple_of(x * 64, 64), 64)
        pre = acc_ref[rows, :]
        live = live_ref[x]
        sig = jax.nn.sigmoid(pre)
        hidden = (live * pre * sig).astype(BF16)
        face_ref[x] = hidden
        field_ref[x] = hidden.astype(F32)
        slope_ref[x] = live * sig * (1.0 + pre * (1.0 - sig))

    def outputs_of(x):
        rows = pl.ds(pl.multiple_of(x * 64, 64), 64)
        pre = acc_ref[rows, :]
        live = live_ref[x]
        sig = jax.nn.sigmoid(pre)
        out_ref[rows, :] = (live * pre * sig).astype(BF16)
        upstream = cot_ref[rows, :].astype(F32)
        delta = (upstream * live * sig * (1.0 + pre * (1.0 - sig))).astype(BF16)
        face_ref[x] = delta
        field_ref[x] = delta.astype(F32)

    def back_of(x):
        rows = pl.ds(pl.multiple_of(x * 64, 64), 64)
        face_ref[x] = (acc_ref[rows, :] * slope_ref[x]).astype(BF16)

    layer(0, c1_ref, store_first, split_first(), even_quarter, windows_first, weight_first, dot, 1, hidden_of)

    loads[3].wait()
    none = jnp.zeros((27, 64, 64), BF16)
    w2b_ref[:, 0:64, :] = jnp.concatenate([w2_ref[...], none], axis=-1)
    w2b_ref[:, 64:128, :] = jnp.concatenate([none, w2_ref[...]], axis=-1)
    second = functools.partial(windows_second, c2_ref)
    loads[4].wait()
    build_inner(c2_ref, store_second, split_second(), first_half)
    build_faces(1, c2_ref, store_second, split_second(), first_half)
    conv_whole(second, weight_second)
    pl.loop(0, 2, unroll=2)(lambda i: outputs_of(7 * i))
    halo_start(2)
    pl.loop(1, 7, unroll=3)(outputs_of)

    wide_half = iota((64, 128), 1) < 64
    wide_quarter = lax.rem(iota((64, 128), 1) // 32, 2) == 0
    per_core1, per_core2 = PAIRS_FIRST // 2, PAIRS_SECOND // 2

    def put_gradient(full, send, pair, value):
        value = value.reshape(4, 16, 128)
        full[4 * pair : 4 * pair + 4] = value
        send[4 * pair : 4 * pair + 4] = value.astype(BF16)

    delta_t = face_ref[...].reshape(512, 128).T
    for pair in range(14):
        both = []
        for k in (2 * pair, min(2 * pair + 1, 26)):
            a, b, c = k // 9, k // 3 % 3, k % 3
            window = c2_ref[c, a : a + 8, ROWS[b] : ROWS[b] + 64, :]
            both.append(window.reshape(512, 128))
        got = dot(delta_t, jnp.concatenate(both, axis=1))
        one, two = got[:, :128], got[:, 128:]
        straight = jnp.where(wide_half, one[0:64], two[64:128])
        crossed = jnp.where(wide_half, two[0:64], one[64:128])
        put_gradient(full2_ref, send2_ref, pair, straight + pltpu.roll(crossed, 64, 1))
    for pair in range(14, PAIRS_SECOND):
        put_gradient(full2_ref, send2_ref, pair, jnp.zeros((64, 128), F32))

    def reducer(which, unit, send, parts, line, fin, back_peers):

        def remote(stage, src, dst, device):
            return pltpu.make_async_remote_copy(
                src_ref=src,
                dst_ref=dst,
                send_sem=sum_send.at[which, stage],
                recv_sem=sum_recv.at[which, stage],
                device_id=device,
                device_id_type=MESH,
            )

        place = pl.ds((core * n_plane + member) * unit, unit)
        parts_whole = parts.at[pl.ds(1, parts.shape[0] - 1)]
        line_whole = line.at[pl.ds(0, nz - 1)]
        fin_whole = fin.at[pl.ds(0, len(back_peers) * unit)]
        fin_half = fin.at[pl.ds(core * n_plane * unit, n_plane * unit)]
        whole = [
            remote(0, parts_whole, parts_whole, twin),
            remote(1, line_whole, line_whole, twin),
            remote(2, fin_whole, fin_whole, twin),
        ]

        def start_parts(peers):
            for i, (other, at) in enumerate(peers):
                remote(0, send.at[pl.ds(other * unit, unit)], parts.at[i + 1], at).start()

        def start_line(total):
            whole[0].wait_recv()
            for i in range(1, parts.shape[0]):
                total = total + parts[i].astype(F32)
            line[my_z] = total.astype(BF16)
            for at in line_peers:
                remote(1, line.at[my_z], line.at[my_z], at).start()

        def start_back():
            whole[1].wait_recv()
            total = line[0].astype(F32)
            for z in range(1, nz):
                total = total + line[z].astype(F32)
            fin[place] = (total * scale).astype(BF16)
            for _, at in back_peers:
                remote(2, fin.at[place], fin.at[place], at).start()

        def finish():
            whole[2].wait_recv()

        def twin_copy():
            return remote(3, fin_half, fin_half, twin)

        def sent():
            for copy in whole:
                copy.wait_send()

        return start_parts, start_line, start_back, finish, sent, twin_copy

    unit1, unit2 = 4 * per_core1 // n_plane, 4 * per_core2 // n_plane
    sum1 = reducer(0, unit1, send1_ref, parts1_ref, line1_ref, fin1_ref, all_peers)
    sum2 = reducer(1, unit2, half2_ref, parts2_ref, line2_ref, fin2_ref, plane_peers)
    place1 = pl.ds((core * n_plane + member) * unit1, unit1)

    def half_units(which_core):
        return pl.ds(which_core * 4 * per_core2, 4 * per_core2)

    pair_copy = pltpu.make_async_remote_copy(
        src_ref=send2_ref.at[half_units(1 - core)],
        dst_ref=pair2_ref,
        send_sem=pair_sem.at[0],
        recv_sem=pair_sem.at[1],
        device_id=twin,
        device_id_type=MESH,
    )
    pair_copy.start()

    def start_second():
        pair_copy.wait_recv()
        total = full2_ref[half_units(core)] + pair2_ref[...].astype(F32)
        mine2_ref[...] = total
        half2_ref[...] = total.astype(BF16)
        sum2[0](plane_peers)

    third = functools.partial(windows_second, c3_ref)
    layer(2, c3_ref, store_second, split_second(), first_half, third, weight_back, dot_nt, 0, back_of, start_second)
    delta_t = face_ref[...].reshape(512, 128).T
    for pair in range(PAIRS_FIRST):
        both = []
        for block in (2 * pair, min(2 * pair + 1, 14)):
            a, r = block // 5, ROWS_FIRST[block % 5]
            both.append(c1_ref[a : a + 8, r : r + 64, :].reshape(512, 128))
        got = dot(delta_t, jnp.concatenate(both, axis=1))
        one, two = got[:, :128], got[:, 128:]
        straight = jnp.where(wide_quarter, one[0:64], two[64:128])
        crossed = jnp.where(wide_quarter, two[0:64], one[64:128])
        swapped = jnp.where(wide_quarter, pltpu.roll(crossed, 96, 1), pltpu.roll(crossed, 32, 1))
        put_gradient(full1_ref, send1_ref, pair, straight + swapped)
    sum1[0](all_peers)
    sum2[1](mine2_ref[pl.ds(member * unit2, unit2)])
    sum1[1](full1_ref[place1])
    sum2[2]()
    sum1[2]()
    sum2[3]()
    sum2[5]().start()

    def unpack_half(which_core):
        for i in range(per_core2):
            pair = which_core * per_core2 + i
            value = fin2_ref[pl.ds(4 * pair, 4)].reshape(64, 128).T.astype(F32)
            g2_ref[pl.ds(2 * pair, 2)] = value.reshape(2, 64, 64)

    unpack_half(core)
    sum2[5]().wait_recv()
    unpack_half(1 - core)
    sum1[3]()
    pair_copy.wait_send()
    sum2[4]()
    sum2[5]().wait_send()
    sum1[4]()
    halo_sent(0)


def unpack_kernel(block_ref, fin_ref, g2_ref, out_hbm, g1_hbm, g2_hbm, g1_ref, sem):
    block_copy = pltpu.make_async_copy(block_ref, out_hbm, sem.at[0])
    second_copies = [
        pltpu.make_async_copy(g2_ref.at[pl.ds(k, 9)], g2_hbm.at[pl.ds(k, 9)], sem.at[3 + k // 9])
        for k in (0, 9, 18)
    ]
    first_copies = [
        pltpu.make_async_copy(g1_ref.at[pl.ds(k, 9)], g1_hbm.at[pl.ds(k, 9)], sem.at[6 + k // 9])
        for k in (0, 9, 18)
    ]
    for copy in second_copies:
        copy.start()
    block_copy.start()
    for pair in range(PAIRS_FIRST):
        value = fin_ref[4 * pair : 4 * pair + 4].reshape(64, 128).T.astype(F32)
        for j in range(2):
            block = 2 * pair + j
            if block > 14:
                continue
            a, kind = block // 5, block % 5
            if kind < 3:
                offsets = (9 * a + 3 * kind, 9 * a + 3 * kind + 2)
            elif kind == 3:
                offsets = (9 * a + 1, 9 * a + 7)
            else:
                offsets = (9 * a + 4,)
            for i, k in enumerate(offsets):
                g1_ref[k] = value[64 * i + 32 * j : 64 * i + 32 * j + 32]
        if pair in (2, 4, 7):
            first_copies[pair // 3].start()
    for copy in second_copies:
        copy.wait()
    block_copy.wait()
    for copy in first_copies:
        copy.wait()


def solution(mesh):
    n_region, n_rep = mesh.shape["region"], mesh.shape["rep"]
    nx, ny = (4, 4) if n_region == 32 else (2, n_rep // 2)
    nz = n_region // nx
    sizes = (nx, nz, ny)
    n_plane = nx * ny
    core1, core2 = 2 * PAIRS_FIRST, 2 * PAIRS_SECOND
    unit1, unit2 = core1 // n_plane, core2 // n_plane
    vmem = pl.BlockSpec(memory_space=pltpu.VMEM)
    smem = pl.BlockSpec(memory_space=pltpu.SMEM)
    hbm = pl.BlockSpec(memory_space=pltpu.HBM)
    anywhere = pl.BlockSpec(memory_space=pl.ANY)
    dma = pltpu.SemaphoreType.DMA

    def body(features, weight_first, weight_second, cotangent, neighbours, voxel_mask):
        scale = 1.0 / math.sqrt(n_rep * 2 * n_region * 512)
        block, fin1, g2 = pl.pallas_call(
            functools.partial(main_kernel, sizes, scale),
            out_shape=(
                jax.ShapeDtypeStruct((512, 128), BF16),
                jax.ShapeDtypeStruct((2 * core1, 16, 128), BF16),
                jax.ShapeDtypeStruct((2 * PAIRS_SECOND, 64, 64), F32),
            ),
            in_specs=[hbm, hbm, hbm, hbm, smem, hbm],
            out_specs=(vmem, vmem, vmem),
            scratch_shapes=[
                pltpu.VMEM((64, 512), BF16),
                pltpu.VMEM((27, 32, 64), BF16),
                pltpu.VMEM((27, 64, 64), BF16),
                pltpu.VMEM((512, 128), BF16),
                pltpu.VMEM((2, 512), jnp.int32),
                pltpu.VMEM((8, 64, 128), F32),
                pltpu.VMEM((8, 64, 128), F32),
                pltpu.VMEM((8, 64, 128), BF16),
                pltpu.VMEM((3, 2, 64, 128), BF16),
                pltpu.VMEM((2, 3, 64, 128), BF16),
                pltpu.VMEM((2, 3, 64, 128), BF16),
                pltpu.VMEM((2, 3, 272, 128), BF16),
                pltpu.VMEM((3, 8, 64, 128), F32),
                pltpu.VMEM((2, 3, 64, 128), F32),
                pltpu.VMEM((10, 272, 128), BF16),
                pltpu.VMEM((3, 10, 144, 128), BF16),
                pltpu.VMEM((3, 10, 144, 128), BF16),
                pltpu.VMEM((3, 5, 128, 128), BF16),
                pltpu.VMEM((27, 128, 128), BF16),
                pltpu.VMEM((512, 128), F32),
                pltpu.VMEM((8, 64, 128), F32),
                pltpu.VMEM((2 * core1, 16, 128), F32),
                pltpu.VMEM((2 * core2, 16, 128), F32),
                pltpu.VMEM((2 * core1, 16, 128), BF16),
                pltpu.VMEM((2 * core2, 16, 128), BF16),
                pltpu.VMEM((core2, 16, 128), BF16),
                pltpu.VMEM((core2, 16, 128), BF16),
                pltpu.VMEM((core2, 16, 128), F32),
                pltpu.VMEM((2 * n_plane, unit1, 16, 128), BF16),
                pltpu.VMEM((n_plane, unit2, 16, 128), BF16),
                pltpu.VMEM((nz, unit1, 16, 128), BF16),
                pltpu.VMEM((nz, unit2, 16, 128), BF16),
                pltpu.VMEM((2 * core2, 16, 128), BF16),
                dma((5,)),
                dma((3, 2)),
                dma((3, 2)),
                dma((2,)),
                dma((2, 4)),
                dma((2, 4)),
            ],
            compiler_params=pltpu.CompilerParams(
                collective_id=0, has_side_effects=True, vmem_limit_bytes=40 * 2**20
            ),
        )(
            *(
                pltpu.with_memory_space_constraint(x, pltpu.HBM)
                for x in (
                    jnp.swapaxes(features, 1, 2).reshape(64, 512),
                    weight_first,
                    weight_second,
                    cotangent.reshape(512, 128),
                    neighbours.reshape(2, 27),
                    voxel_mask.reshape(2, 512),
                )
            )
        )
        out, g1, g2 = pl.pallas_call(
            unpack_kernel,
            out_shape=(
                jax.ShapeDtypeStruct((512, 128), BF16),
                jax.ShapeDtypeStruct((27, 32, 64), F32),
                jax.ShapeDtypeStruct((27, 64, 64), F32),
            ),
            in_specs=[vmem, vmem, vmem],
            out_specs=(anywhere, anywhere, anywhere),
            scratch_shapes=[
                pltpu.VMEM((27, 32, 64), F32),
                dma((9,)),
            ],
            compiler_params=pltpu.CompilerParams(vmem_limit_bytes=40 * 2**20),
        )(block, fin1, g2)
        return out.reshape(1, 512, 128), g1, g2

    in_specs = (
        P("rep", None, "region"),
        P(),
        P(),
        P("rep", None, "region"),
        P("rep", "region", None),
        P("rep", "region", None),
    )
    out_specs = (P("rep", None, "region"), P(), P())
    return jax.shard_map(body, mesh=mesh, in_specs=in_specs, out_specs=out_specs, check_vma=False)
```

```python
import functools
import math

import jax
import jax.numpy as jnp
from jax import lax
from jax.experimental import pallas as pl
from jax.experimental.pallas import tpu as pltpu
from jax.sharding import PartitionSpec as P

MESH = pl.DeviceIdType.MESH
F32 = jnp.float32
BF16 = jnp.bfloat16
ROWS = (0, 80, 16)
ROWS_FIRST = (0, 80, 16, 144, 208)
PAIRS_SECOND = 16
PAIRS_FIRST = 8


def iota(shape, axis):
    return lax.broadcasted_iota(jnp.int32, shape, axis)


def dot(a, b):
    return jnp.dot(a, b, preferred_element_type=F32)


def dot_nt(a, b):
    return lax.dot_general(a, b, (((1,), (1,)), ((), ())), preferred_element_type=F32)


def places(sizes):
    nx, nz, ny = sizes
    region = lax.axis_index("region")
    rep = lax.axis_index("rep")
    return region // nz, lax.rem(region, nz), rep // 2, lax.rem(rep, 2), region, rep


def main_kernel(
    sizes,
    scale,
    feat_hbm,
    w1_hbm,
    w2_hbm,
    cot_hbm,
    nbr_ref,
    mask_hbm,
    out_ref,
    fin1_ref,
    g2_ref,
    feat_ref,
    w1_ref,
    w2_ref,
    cot_ref,
    mask_ref,
    live_ref,
    field_ref,
    face_ref,
    halo_ref,
    edge_ref,
    rim_ref,
    ext_ref,
    side_ref,
    far_ref,
    c1_ref,
    c2_ref,
    c3_ref,
    w1b_ref,
    w2b_ref,
    acc_ref,
    slope_ref,
    full1_ref,
    full2_ref,
    send1_ref,
    send2_ref,
    pair2_ref,
    half2_ref,
    mine2_ref,
    parts1_ref,
    parts2_ref,
    line1_ref,
    line2_ref,
    fin2_ref,
    load_sem,
    halo_send,
    halo_recv,
    pair_sem,
    sum_send,
    sum_recv,
):
    nx, nz, ny = sizes
    n_region, n_plane = nx * nz, nx * ny
    my_x, my_z, my_y, core, region, rep = places(sizes)
    member = my_x * ny + my_y
    right = lax.rem(region + 1, n_region)
    left = lax.rem(region + n_region - 1, n_region)
    twin = {"region": region, "rep": my_y * 2 + 1 - core}

    def apart(offset, size):
        return min(offset, size - offset)

    offsets = sorted(
        ((dx, dy, dc) for dx in range(nx) for dy in range(ny) for dc in range(2)),
        key=lambda d: (-apart(d[0], nx) - apart(d[1], ny), d),
    )
    plane_peers, all_peers = [], []
    for dx, dy, dc in offsets:
        if (dx, dy, dc) == (0, 0, 0):
            continue
        x, y, c = lax.rem(my_x + dx, nx), lax.rem(my_y + dy, ny), lax.rem(core + dc, 2)
        at = {"region": x * nz + my_z, "rep": y * 2 + c}
        all_peers.append((c * n_plane + x * ny + y, at))
        if dc == 0:
            plane_peers.append((x * ny + y, at))
    line_peers = [
        {"region": my_x * nz + lax.rem(my_z + step, nz), "rep": rep}
        for step in sorted(range(1, nz), key=lambda d: -apart(d, nz))
    ]

    halo_ref[...] = jnp.zeros((3, 2, 64, 128), BF16)
    rim_ref[...] = jnp.zeros((2, 3, 64, 128), BF16)

    barrier = pltpu.get_barrier_semaphore()
    partners = [{"region": right, "rep": rep}, {"region": left, "rep": rep}]
    partners += [at for _, at in all_peers] + line_peers
    for at in partners[:2]:
        pl.semaphore_signal(barrier, inc=1, device_id=at, device_id_type=MESH)
    loads = [
        pltpu.make_async_copy(src, dst, load_sem.at[i])
        for i, (src, dst) in enumerate(
            (
                (mask_hbm, mask_ref),
                (feat_hbm, feat_ref),
                (w1_hbm, w1_ref),
                (w2_hbm, w2_ref),
                (cot_hbm, cot_ref),
            )
        )
    ]
    for load in loads:
        load.start()
    for at in partners[2:]:
        pl.semaphore_signal(barrier, inc=1, device_id=at, device_id_type=MESH)
    loads[0].wait()
    loads[1].wait()

    mask = jnp.concatenate([mask_ref[...].astype(F32), jnp.zeros((6, 512), F32)], axis=0).T
    tile_of = (iota((8, 128), 1) // 64 == iota((8, 128), 0)).astype(F32)
    tile_of_first = (lax.rem(iota((8, 128), 1) // 32, 2) == iota((8, 128), 0)).astype(F32)
    live_ref[...] = dot(mask, tile_of).reshape(8, 64, 128)
    twice = (iota((64, 128), 0) == lax.rem(iota((64, 128), 1), 64)).astype(BF16)
    spread = dot(feat_ref[...].T, twice) * dot(mask, tile_of_first)
    field_ref[...] = spread.reshape(8, 64, 128)
    face_ref[...] = spread.astype(BF16).reshape(8, 64, 128)

    def halo_copy(which, side):
        return pltpu.make_async_remote_copy(
            src_ref=edge_ref.at[side] if which == 0 else face_ref.at[7 if side == 0 else 0],
            dst_ref=rim_ref.at[side] if which == 0 else halo_ref.at[which, side],
            send_sem=halo_send.at[which, side],
            recv_sem=halo_recv.at[which, side],
            device_id={"region": right if side == 0 else left, "rep": rep},
            device_id_type=MESH,
        )

    has_right, has_left = region < n_region - 1, region > 0

    def halo_start(which):
        pl.when(has_right)(lambda: halo_copy(which, 0).start())
        pl.when(has_left)(lambda: halo_copy(which, 1).start())

    def halo_wait(which):
        @pl.when(has_left)
        def _():
            halo_copy(which, 0).wait_recv()

        @pl.when(has_right)
        def _():
            halo_copy(which, 1).wait_recv()

    def halo_sent(which):
        pl.when(has_right)(lambda: halo_copy(which, 0).wait_send())
        pl.when(has_left)(lambda: halo_copy(which, 1).wait_send())

    wide_half = iota((64, 128), 1) < 64
    wide_quarter = lax.rem(iota((64, 128), 1) // 32, 2) == 0
    one_lane = wide_quarter[0:1]
    links = []
    for s in range(2):
        for k in range(9):
            named = [(nbr_ref[t, 9 + k] == 2 + s).astype(F32) for t in range(2)]
            links.append(jnp.where(one_lane, named[0], named[1]))
        links.append(jnp.zeros((23, 128), F32))
    links = jnp.concatenate(links, axis=0).astype(BF16)
    for side, face, inside in ((0, 7, 6), (1, 0, 1)):
        edge_ref[side, 0] = jnp.where(wide_half, face_ref[face], face_ref[inside])
        edge_ref[side, 1] = live_ref[face].astype(BF16)
        edge_ref[side, 2] = links
    pl.semaphore_wait(barrier, len(partners))
    halo_start(0)

    loads[2].wait()
    plain = w1_ref[...].reshape(3, 3, 3, 32, 64)
    none = jnp.zeros((3, 3, 3, 32, 64), BF16)
    top = jnp.concatenate([plain, none], axis=-1)
    low = jnp.concatenate([none, plain], axis=-1)
    for b in range(3):
        for at, c in ((0, 0), (64, 2)):
            w1b_ref[:, b, at : at + 32, :] = top[:, b, c]
            w1b_ref[:, b, at + 32 : at + 64, :] = low[:, b, c]
    for at, b in ((0, 0), (64, 2)):
        w1b_ref[:, 3, at : at + 32, :] = top[:, b, 1]
        w1b_ref[:, 3, at + 32 : at + 64, :] = low[:, b, 1]
    w1b_ref[:, 4, 0:32, :] = top[:, 1, 1]
    w1b_ref[:, 4, 32:64, :] = low[:, 1, 1]
    w1b_ref[:, 4, 64:128, :] = jnp.zeros((3, 64, 128), BF16)
    side_ref[2] = jnp.zeros((8, 64, 128), F32)
    far_ref[:, 2] = jnp.zeros((2, 64, 128), F32)
    lane = iota((8, 128), 1)
    first_half = lane < 64
    even_quarter = lax.rem(lane // 32, 2) == 0
    z_row = iota((8, 128), 0)
    z_first, z_last = z_row == 0, z_row == 7

    def rows_of(masked, count):
        return jnp.concatenate([masked] * count, axis=0) if count > 1 else masked

    def split_first():
        source, target = iota((128, 256), 0), iota((128, 256), 1)
        return (source == (target // 128) * 32 + lax.rem(target, 32)).astype(BF16)

    def split_second():
        source, target = iota((128, 256), 0), iota((128, 256), 1)
        return (source == (target // 128) * 64 + lax.rem(target, 64)).astype(BF16)

    def shifted(middle, load, tile_lane):
        ext = []
        for c in range(3):
            groups = [load(0, c, 56, 64)]
            if c == 1 and middle is not None:
                mid = middle
            else:
                mid = load(1, c, 0, 64)
            groups += [mid[8 * y : 8 * y + 8] for y in range(8)]
            groups.append(load(2, c, 0, 8))
            ext.append(groups)
        down = [pltpu.roll(jnp.where(z_last, ext[0][y], ext[1][y]), 1, 0) for y in range(10)]
        up = [pltpu.roll(jnp.where(z_first, ext[2][y], ext[1][y]), 7, 0) for y in range(10)]
        return down, ext[1], up

    def store_first(c_ref, slab, down, mid, up):
        both = [jnp.where(first_half, d, u) for d, u in zip(down, up)]
        c_ref[slab, 0:80, :] = jnp.concatenate(both, axis=0).astype(BF16)
        c_ref[slab, 80:144, :] = jnp.concatenate(both[1:9], axis=0).astype(BF16)
        ends = [jnp.where(first_half, mid[y], mid[y + 2]) for y in range(8)]
        c_ref[slab, 144:208, :] = jnp.concatenate(ends, axis=0).astype(BF16)
        c_ref[slab, 208:272, :] = jnp.concatenate(mid[1:9], axis=0).astype(BF16)

    def store_second(c_ref, slab, down, mid, up):
        for c, groups in enumerate((down, mid, up)):
            c_ref[c, slab, 0:80, :] = jnp.concatenate(groups, axis=0).astype(BF16)
            c_ref[c, slab, 80:144, :] = jnp.concatenate(groups[1:9], axis=0).astype(BF16)

    def build_inner(c_ref, store, splitter, tile_lane):
        whole = dot(face_ref[...].reshape(512, 128), splitter)
        side_ref[0] = whole[:, :128].reshape(8, 64, 128)
        side_ref[1] = whole[:, 128:].reshape(8, 64, 128)
        named = [
            [jnp.minimum(jnp.maximum(nbr_ref[t, 9 + k] - 2, 0), 2) for k in range(9)]
            for t in range(2)
        ]

        @pl.loop(0, 8, unroll=4)
        def _(x):
            def load(b, c, start, stop):
                k = 3 * b + c
                return jnp.where(
                    rows_of(tile_lane, (stop - start) // 8),
                    side_ref[named[0][k], x, start:stop, :],
                    side_ref[named[1][k], x, start:stop, :],
                )

            store(c_ref, x + 1, *shifted(field_ref[x], load, tile_lane))

    def build_faces(which, c_ref, store, splitter, tile_lane):
        source = rim_ref[:, 0] if which == 0 else halo_ref[which]
        whole = dot(source.reshape(128, 128), splitter)
        for side in range(2):
            far_ref[side, 0] = whole[64 * side : 64 * side + 64, :128]
            far_ref[side, 1] = whole[64 * side : 64 * side + 64, 128:]
            named = [
                [
                    jnp.minimum(jnp.maximum(nbr_ref[t, 18 * side + k] - 4 * side, 0), 2)
                    for k in range(9)
                ]
                for t in range(2)
            ]

            def load(b, c, start, stop):
                k = 3 * b + c
                return jnp.where(
                    rows_of(tile_lane, (stop - start) // 8),
                    far_ref[side, named[0][k], start:stop, :],
                    far_ref[side, named[1][k], start:stop, :],
                )

            store(c_ref, 9 * side, *shifted(None, load, tile_lane))

    def build_cross():
        for side, x, base, code in ((0, 0, 18, 0), (1, 7, 0, 4)):
            named = []
            for s in range(2):
                row = []
                for k in range(9):
                    link = [nbr_ref[t, 26 - base - k] == code + s for t in range(2)]
                    row.append(jnp.where(link[0], 0, jnp.where(link[1], 1, 2)))
                named.append(row)

            def load(b, c, start, stop):
                k = 3 * b + c
                return jnp.where(
                    rows_of(even_quarter, (stop - start) // 8),
                    side_ref[named[0][k], x, start:stop, :],
                    side_ref[named[1][k], x, start:stop, :],
                )

            store_first(ext_ref.at[side], 2 - 2 * side, *shifted(None, load, even_quarter))

    def build_rim():
        source, target = iota((128, 384), 0), iota((128, 384), 1)
        group, lane_in = target // 128, lax.rem(target, 128)
        wanted = jnp.where(group == 0, lax.rem(lane_in, 64), (group - 1) * 32 + lax.rem(lane_in, 32))
        for inside in range(2):
            spread_out = (source == wanted + 64 * inside).astype(BF16)
            whole = dot(rim_ref[:, 0].reshape(128, 128), spread_out)
            for side in range(2):
                part = whole[64 * side : 64 * side + 64]
                table = rim_ref[side, 2].astype(F32)

                def load(b, c, start, stop):
                    k = 3 * b + c
                    first = table[k : k + 1] * part[start:stop, 128:256]
                    return first + table[32 + k : 33 + k] * part[start:stop, 256:384]

                slab = 1 if inside == 0 else 2 * side
                store_first(ext_ref.at[side], slab, *shifted(part[:, 0:128], load, even_quarter))

    def hidden_beside():
        windows = []
        for a in range(3):
            for r in ROWS_FIRST:
                windows.append(ext_ref[:, a, r : r + 64, :].reshape(128, 128))
        pre = dot(jnp.concatenate(windows, axis=1), w1b_ref[...].reshape(15 * 128, 128))
        live = rim_ref[:, 1].reshape(128, 128).astype(F32)
        hidden = (live * pre * jax.nn.sigmoid(pre)).astype(BF16)
        halo_ref[1] = hidden.reshape(2, 64, 128)

    def windows_first(start, count):
        return [
            c1_ref[start : start + count, r : r + 64, :].reshape(count * 64, 128)
            for r in ROWS_FIRST
        ]

    def windows_second(c_ref, start, count):
        return [
            c_ref[c, start : start + count, ROWS[b] : ROWS[b] + 64, :].reshape(count * 64, 128)
            for b in range(3)
            for c in range(3)
        ]

    def conv_inner(windows, weight, product=dot, columns=1):
        weights = jnp.concatenate([weight(0), weight(2), weight(1)], axis=columns)
        got = product(jnp.concatenate(windows(1, 8), axis=1), weights)
        acc_ref[...] = got[:, 256:384]
        acc_ref[64:512] += got[0:448, 0:128]
        acc_ref[0:448] += got[64:512, 128:256]

    def conv_faces(windows, weight, product=dot, columns=1):
        weights = jnp.concatenate([weight(0), weight(2)], axis=columns)
        rows = [jnp.concatenate(both, axis=0) for both in zip(windows(0, 1), windows(9, 1))]
        got = product(jnp.concatenate(rows, axis=1), weights)
        acc_ref[0:64] += got[0:64, 0:128]
        acc_ref[448:512] += got[64:128, 128:256]

    def weight_first(a):
        return w1b_ref[a].reshape(5 * 128, 128)

    def weight_second(a):
        return w2b_ref[9 * a : 9 * a + 9].reshape(9 * 128, 128)

    def weight_back(a):
        return jnp.concatenate([w2b_ref[26 - k] for k in range(9 * a, 9 * a + 9)], axis=1)

    def conv_whole(windows, weight):
        weights = jnp.concatenate([weight(0), weight(2), weight(1)], axis=1)
        got = dot(jnp.concatenate(windows(0, 10), axis=1), weights)
        acc_ref[...] = got[0:512, 0:128] + got[64:576, 256:384] + got[128:640, 128:256]

    def layer(which, c_ref, store, splitter, tile_lane, windows, weight, product, columns, activate, between=None):
        build_inner(c_ref, store, splitter, tile_lane)
        conv_inner(windows, weight, product, columns)
        if which == 0:
            build_cross()
        if between is not None:
            between()
        pl.loop(1, 7, unroll=3)(activate)
        halo_wait(which)
        build_faces(which, c_ref, store, splitter, tile_lane)
        if which == 0:
            build_rim()
            hidden_beside()
        conv_faces(windows, weight, product, columns)
        if which == 2:
            halo_sent(2)
        pl.loop(0, 2, unroll=2)(lambda i: activate(7 * i))

    def hidden_of(x):
        rows = pl.ds(pl.multiple_of(x * 64, 64), 64)
        pre = acc_ref[rows, :]
        live = live_ref[x]
        sig = jax.nn.sigmoid(pre)
        hidden = (live * pre * sig).astype(BF16)
        face_ref[x] = hidden
        field_ref[x] = hidden.astype(F32)
        slope_ref[x] = live * sig * (1.0 + pre * (1.0 - sig))

    def outputs_of(x):
        rows = pl.ds(pl.multiple_of(x * 64, 64), 64)
        pre = acc_ref[rows, :]
        live = live_ref[x]
        sig = jax.nn.sigmoid(pre)
        out_ref[rows, :] = (live * pre * sig).astype(BF16)
        upstream = cot_ref[rows, :].astype(F32)
        delta = (upstream * live * sig * (1.0 + pre * (1.0 - sig))).astype(BF16)
        face_ref[x] = delta
        field_ref[x] = delta.astype(F32)

    def back_of(x):
        rows = pl.ds(pl.multiple_of(x * 64, 64), 64)
        face_ref[x] = (acc_ref[rows, :] * slope_ref[x]).astype(BF16)

    layer(0, c1_ref, store_first, split_first(), even_quarter, windows_first, weight_first, dot, 1, hidden_of)

    loads[3].wait()
    none = jnp.zeros((27, 64, 64), BF16)
    w2b_ref[:, 0:64, :] = jnp.concatenate([w2_ref[...], none], axis=-1)
    w2b_ref[:, 64:128, :] = jnp.concatenate([none, w2_ref[...]], axis=-1)
    second = functools.partial(windows_second, c2_ref)
    loads[4].wait()
    build_inner(c2_ref, store_second, split_second(), first_half)
    build_faces(1, c2_ref, store_second, split_second(), first_half)
    conv_whole(second, weight_second)
    pl.loop(0, 2, unroll=2)(lambda i: outputs_of(7 * i))
    halo_start(2)
    pl.loop(1, 7, unroll=3)(outputs_of)

    wide_half = iota((64, 128), 1) < 64
    wide_quarter = lax.rem(iota((64, 128), 1) // 32, 2) == 0
    per_core1, per_core2 = PAIRS_FIRST // 2, PAIRS_SECOND // 2

    def put_gradient(full, send, pair, value):
        value = value.reshape(4, 16, 128)
        full[4 * pair : 4 * pair + 4] = value
        send[4 * pair : 4 * pair + 4] = value.astype(BF16)

    delta_t = face_ref[...].reshape(512, 128).T
    for pair in range(14):
        both = []
        for k in (2 * pair, min(2 * pair + 1, 26)):
            a, b, c = k // 9, k // 3 % 3, k % 3
            window = c2_ref[c, a : a + 8, ROWS[b] : ROWS[b] + 64, :]
            both.append(window.reshape(512, 128))
        got = dot(delta_t, jnp.concatenate(both, axis=1))
        one, two = got[:, :128], got[:, 128:]
        straight = jnp.where(wide_half, one[0:64], two[64:128])
        crossed = jnp.where(wide_half, two[0:64], one[64:128])
        put_gradient(full2_ref, send2_ref, pair, straight + pltpu.roll(crossed, 64, 1))
    for pair in range(14, PAIRS_SECOND):
        put_gradient(full2_ref, send2_ref, pair, jnp.zeros((64, 128), F32))

    def reducer(which, unit, send, parts, line, fin):

        def remote(stage, src, dst, device):
            return pltpu.make_async_remote_copy(
                src_ref=src,
                dst_ref=dst,
                send_sem=sum_send.at[which, stage],
                recv_sem=sum_recv.at[which, stage],
                device_id=device,
                device_id_type=MESH,
            )

        place = pl.ds((core * n_plane + member) * unit, unit)
        parts_whole = parts.at[pl.ds(1, parts.shape[0] - 1)]
        line_whole = line.at[pl.ds(0, nz - 1)]
        fin_whole = fin.at[pl.ds(0, (2 * n_plane - 1) * unit)]
        whole = [
            remote(0, parts_whole, parts_whole, twin),
            remote(1, line_whole, line_whole, twin),
            remote(2, fin_whole, fin_whole, twin),
        ]

        def start_parts(peers):
            for i, (other, at) in enumerate(peers):
                remote(0, send.at[pl.ds(other * unit, unit)], parts.at[i + 1], at).start()

        def start_line(total):
            whole[0].wait_recv()
            for i in range(1, parts.shape[0]):
                total = total + parts[i].astype(F32)
            line[my_z] = total.astype(BF16)
            for at in line_peers:
                remote(1, line.at[my_z], line.at[my_z], at).start()

        def start_back():
            whole[1].wait_recv()
            total = line[0].astype(F32)
            for z in range(1, nz):
                total = total + line[z].astype(F32)
            fin[place] = (total * scale).astype(BF16)
            for _, at in all_peers:
                remote(2, fin.at[place], fin.at[place], at).start()

        def finish():
            whole[2].wait_recv()

        def sent():
            for copy in whole:
                copy.wait_send()

        return start_parts, start_line, start_back, finish, sent

    unit1, unit2 = 4 * per_core1 // n_plane, 4 * per_core2 // n_plane
    sum1 = reducer(0, unit1, send1_ref, parts1_ref, line1_ref, fin1_ref)
    sum2 = reducer(1, unit2, half2_ref, parts2_ref, line2_ref, fin2_ref)
    place1 = pl.ds((core * n_plane + member) * unit1, unit1)

    def half_units(which_core):
        return pl.ds(which_core * 4 * per_core2, 4 * per_core2)

    pair_copy = pltpu.make_async_remote_copy(
        src_ref=send2_ref.at[half_units(1 - core)],
        dst_ref=pair2_ref,
        send_sem=pair_sem.at[0],
        recv_sem=pair_sem.at[1],
        device_id=twin,
        device_id_type=MESH,
    )
    pair_copy.start()

    def start_second():
        pair_copy.wait_recv()
        total = full2_ref[half_units(core)] + pair2_ref[...].astype(F32)
        mine2_ref[...] = total
        half2_ref[...] = total.astype(BF16)
        sum2[0](plane_peers)

    third = functools.partial(windows_second, c3_ref)
    layer(2, c3_ref, store_second, split_second(), first_half, third, weight_back, dot_nt, 0, back_of, start_second)
    delta_t = face_ref[...].reshape(512, 128).T
    for pair in range(PAIRS_FIRST):
        both = []
        for block in (2 * pair, min(2 * pair + 1, 14)):
            a, r = block // 5, ROWS_FIRST[block % 5]
            both.append(c1_ref[a : a + 8, r : r + 64, :].reshape(512, 128))
        got = dot(delta_t, jnp.concatenate(both, axis=1))
        one, two = got[:, :128], got[:, 128:]
        straight = jnp.where(wide_quarter, one[0:64], two[64:128])
        crossed = jnp.where(wide_quarter, two[0:64], one[64:128])
        swapped = jnp.where(wide_quarter, pltpu.roll(crossed, 96, 1), pltpu.roll(crossed, 32, 1))
        put_gradient(full1_ref, send1_ref, pair, straight + swapped)
    sum1[0](all_peers)
    sum2[1](mine2_ref[pl.ds(member * unit2, unit2)])
    sum1[1](full1_ref[place1])
    sum2[2]()
    sum1[2]()
    sum2[3]()
    for pair in range(14):
        value = fin2_ref[4 * pair : 4 * pair + 4].reshape(64, 128).T.astype(F32)
        g2_ref[2 * pair] = value[0:64]
        if pair < 13:
            g2_ref[2 * pair + 1] = value[64:128]
    sum1[3]()
    pair_copy.wait_send()
    sum2[4]()
    sum1[4]()
    halo_sent(0)


def unpack_kernel(block_ref, fin_ref, g2_ref, out_hbm, g1_hbm, g2_hbm, g1_ref, sem):
    block_copy = pltpu.make_async_copy(block_ref, out_hbm, sem.at[0])
    second_copy = pltpu.make_async_copy(g2_ref, g2_hbm, sem.at[1])
    first_copy = pltpu.make_async_copy(g1_ref, g1_hbm, sem.at[2])
    second_copy.start()
    block_copy.start()
    for pair in range(PAIRS_FIRST):
        value = fin_ref[4 * pair : 4 * pair + 4].reshape(64, 128).T.astype(F32)
        for j in range(2):
            block = 2 * pair + j
            if block > 14:
                continue
            a, kind = block // 5, block % 5
            if kind < 3:
                offsets = (9 * a + 3 * kind, 9 * a + 3 * kind + 2)
            elif kind == 3:
                offsets = (9 * a + 1, 9 * a + 7)
            else:
                offsets = (9 * a + 4,)
            for i, k in enumerate(offsets):
                g1_ref[k] = value[64 * i + 32 * j : 64 * i + 32 * j + 32]
    first_copy.start()
    second_copy.wait()
    block_copy.wait()
    first_copy.wait()


def solution(mesh):
    n_region, n_rep = mesh.shape["region"], mesh.shape["rep"]
    nx, ny = (4, 4) if n_region == 32 else (2, n_rep // 2)
    nz = n_region // nx
    sizes = (nx, nz, ny)
    n_plane = nx * ny
    core1, core2 = 2 * PAIRS_FIRST, 2 * PAIRS_SECOND
    unit1, unit2 = core1 // n_plane, core2 // n_plane
    vmem = pl.BlockSpec(memory_space=pltpu.VMEM)
    smem = pl.BlockSpec(memory_space=pltpu.SMEM)
    hbm = pl.BlockSpec(memory_space=pltpu.HBM)
    anywhere = pl.BlockSpec(memory_space=pl.ANY)
    dma = pltpu.SemaphoreType.DMA

    def body(features, weight_first, weight_second, cotangent, neighbours, voxel_mask):
        scale = 1.0 / math.sqrt(n_rep * 2 * n_region * 512)
        block, fin1, g2 = pl.pallas_call(
            functools.partial(main_kernel, sizes, scale),
            out_shape=(
                jax.ShapeDtypeStruct((512, 128), BF16),
                jax.ShapeDtypeStruct((2 * core1, 16, 128), BF16),
                jax.ShapeDtypeStruct((27, 64, 64), F32),
            ),
            in_specs=[hbm, hbm, hbm, hbm, smem, hbm],
            out_specs=(vmem, vmem, vmem),
            scratch_shapes=[
                pltpu.VMEM((64, 512), BF16),
                pltpu.VMEM((27, 32, 64), BF16),
                pltpu.VMEM((27, 64, 64), BF16),
                pltpu.VMEM((512, 128), BF16),
                pltpu.VMEM((2, 512), jnp.int32),
                pltpu.VMEM((8, 64, 128), F32),
                pltpu.VMEM((8, 64, 128), F32),
                pltpu.VMEM((8, 64, 128), BF16),
                pltpu.VMEM((3, 2, 64, 128), BF16),
                pltpu.VMEM((2, 3, 64, 128), BF16),
                pltpu.VMEM((2, 3, 64, 128), BF16),
                pltpu.VMEM((2, 3, 272, 128), BF16),
                pltpu.VMEM((3, 8, 64, 128), F32),
                pltpu.VMEM((2, 3, 64, 128), F32),
                pltpu.VMEM((10, 272, 128), BF16),
                pltpu.VMEM((3, 10, 144, 128), BF16),
                pltpu.VMEM((3, 10, 144, 128), BF16),
                pltpu.VMEM((3, 5, 128, 128), BF16),
                pltpu.VMEM((27, 128, 128), BF16),
                pltpu.VMEM((512, 128), F32),
                pltpu.VMEM((8, 64, 128), F32),
                pltpu.VMEM((2 * core1, 16, 128), F32),
                pltpu.VMEM((2 * core2, 16, 128), F32),
                pltpu.VMEM((2 * core1, 16, 128), BF16),
                pltpu.VMEM((2 * core2, 16, 128), BF16),
                pltpu.VMEM((core2, 16, 128), BF16),
                pltpu.VMEM((core2, 16, 128), BF16),
                pltpu.VMEM((core2, 16, 128), F32),
                pltpu.VMEM((2 * n_plane, unit1, 16, 128), BF16),
                pltpu.VMEM((n_plane, unit2, 16, 128), BF16),
                pltpu.VMEM((nz, unit1, 16, 128), BF16),
                pltpu.VMEM((nz, unit2, 16, 128), BF16),
                pltpu.VMEM((2 * core2, 16, 128), BF16),
                dma((5,)),
                dma((3, 2)),
                dma((3, 2)),
                dma((2,)),
                dma((2, 3)),
                dma((2, 3)),
            ],
            compiler_params=pltpu.CompilerParams(
                collective_id=0, has_side_effects=True, vmem_limit_bytes=40 * 2**20
            ),
        )(
            *(
                pltpu.with_memory_space_constraint(x, pltpu.HBM)
                for x in (
                    jnp.swapaxes(features, 1, 2).reshape(64, 512),
                    weight_first,
                    weight_second,
                    cotangent.reshape(512, 128),
                    neighbours.reshape(2, 27),
                    voxel_mask.reshape(2, 512),
                )
            )
        )
        out, g1, g2 = pl.pallas_call(
            unpack_kernel,
            out_shape=(
                jax.ShapeDtypeStruct((512, 128), BF16),
                jax.ShapeDtypeStruct((27, 32, 64), F32),
                jax.ShapeDtypeStruct((27, 64, 64), F32),
            ),
            in_specs=[vmem, vmem, vmem],
            out_specs=(anywhere, anywhere, anywhere),
            scratch_shapes=[
                pltpu.VMEM((27, 32, 64), F32),
                dma((3,)),
            ],
            compiler_params=pltpu.CompilerParams(vmem_limit_bytes=40 * 2**20),
        )(block, fin1, g2)
        return out.reshape(1, 512, 128), g1, g2

    in_specs = (
        P("rep", None, "region"),
        P(),
        P(),
        P("rep", None, "region"),
        P("rep", "region", None),
        P("rep", "region", None),
    )
    out_specs = (P("rep", None, "region"), P(), P())
    return jax.shard_map(body, mesh=mesh, in_specs=in_specs, out_specs=out_specs, check_vma=False)
```
